32 devices in a mesh: groups: 2 (over x), pb: 16 (over z, y, core).
Axes of the slice: x: 2, y: 2, z: 4, core: 2. Of those that a mesh axis runs over, the one named last changes fastest.
Arguments:
- hidden: bfloat16 [8192, 4096], P(('groups', 'pb')), parts along dimension 0, may hold values from -6 to 6
- final_gain: bfloat16 [4096], replicated, may hold values from 0.099609375 to 1.8984375
- last_row: int32 [32, 256], P(('groups', 'pb')), parts along dimension 0, may hold values from 0 to 255, each once within a row
- pair_owner: int32 [4096, 2], P(('groups', 'pb')), parts along dimension 0, may hold values from 0 to 4095, as said below
- hard_negatives: int32 [32, 4], P(('groups', 'pb')), parts along dimension 0, may hold values from -1 to 15, as said below
Outputs:
- pooled_grad: float32 [8192, 4096], P(('groups', 'pb')), parts along dimension 0
- block_loss: float32 [32], P(('groups', 'pb')), parts along dimension 0
The draws below stay inside these ranges and needn't reach their ends.
There are 2 independent parts, one for each index of `groups`. The reference program is written for one: setup_inputs(seed, part) draws one part's arguments, and reference() takes and returns one part's arrays. A program takes and returns all parts, laid end to end along the dimension named above; an argument that names none is the same for every part. Nothing has to cross between parts.
Inputs may be any that keep to these rules, and one draw needn't show every extreme that they name: `last_row`: each device's row names each of its 256 rows once. `pair_owner`: every global sequence index is named exactly once. The 128 pairs of one query block name at most 32 sequences of any one device, and exactly 32 of some device. `hard_negatives`: entry r of query block j is -1 or block (j + r + 1) mod 16. Every row names at least one block, and some row names all 4.
All inputs are finite; a program needn't handle non-finite values.
Results may differ from the reference program's by a relative error of at most 0.006.
Values may be sent and summed in bfloat16 or wider, within the bound.
No kernel may reach another device: no remote copies, remote signals or barrier semaphores. Data moves between devices by JAX's collectives and lax.ppermute only.
A program may use at most 128 MiB of HBM per device.

```python
import jax
import jax.numpy as jnp
from jax import lax

D = 4096
PAIR_DEV = 128
WINDOW = 4
SEQ_DEV = 256
NBLK = 16
PAIRS = 2048
SEQS = 4096
N_PB = 16


def shuffled_rows(key, count, length):
    row_keys = jax.random.split(key, count)
    return jax.vmap(lambda row_key: jax.random.permutation(row_key, length))(row_keys).astype(jnp.int32)


def draw_pair_owner(key, part):
    key = jax.random.fold_in(key, 11)
    key_first, key_shift, key_slots, key_tie = jax.random.split(key, 4)
    per_pair = 2 * PAIR_DEV // N_PB
    first_perm = jax.random.permutation(key_first, N_PB).astype(jnp.int32)
    shift_by = jax.random.randint(key_shift, (), 1, N_PB, dtype=jnp.int32)
    second = first_perm[(jnp.arange(N_PB, dtype=jnp.int32) + shift_by) % N_PB]
    baseline = jnp.arange(SEQ_DEV, dtype=jnp.int32) // per_pair
    target = jnp.where(baseline[None, :] == second[:, None], first_perm[:, None], baseline[None, :])
    slot_order = shuffled_rows(key_slots, N_PB, SEQ_DEV)
    target = jnp.take_along_axis(target, slot_order, axis=1).reshape(-1)
    tie_break = jax.random.permutation(key_tie, SEQS).astype(jnp.int32)
    ordering = jnp.argsort(target * SEQS + tie_break).astype(jnp.int32)
    grouped = ordering.reshape(N_PB, 2 * PAIR_DEV)
    return jnp.stack([grouped[:, :PAIR_DEV].reshape(-1), grouped[:, PAIR_DEV:].reshape(-1)], axis=1).astype(jnp.int32)


def draw_hard_negatives(key, part):
    key = jax.random.fold_in(key, 23)
    key_count, key_full, key_pick = jax.random.split(key, 3)
    picks = jax.random.randint(key_count, (N_PB,), 0, WINDOW, dtype=jnp.int32)
    counts = 1 + picks * picks // WINDOW
    fullest = jax.random.randint(key_full, (), 0, N_PB, dtype=jnp.int32)
    counts = jnp.where(jnp.arange(N_PB, dtype=jnp.int32) == fullest, WINDOW, counts)
    ranking = shuffled_rows(key_pick, N_PB, WINDOW)
    chosen = ranking < counts[:, None]
    blocks = (jnp.arange(N_PB, dtype=jnp.int32)[:, None] + jnp.arange(WINDOW, dtype=jnp.int32)[None, :] + 1) % N_PB
    return jnp.where(chosen, blocks, -1).astype(jnp.int32)


def block_levels(own_key, extent, cuts, least, high):
    factor_of, own = 1.0, jax.random.fold_in(own_key, 6)
    for axis_at, shards_of in cuts:
        draws = jnp.exp(jax.random.uniform(jax.random.fold_in(own, axis_at), (shards_of,), jnp.float32, least / len(cuts), high / len(cuts)))
        factor_of = factor_of * jnp.repeat(draws, extent[axis_at] // shards_of).reshape([-1 if axis == axis_at else 1 for axis in range(len(extent))])
    return factor_of


def bell_draw(own_key, extent, spread, limit, cuts=(), kind=jnp.bfloat16):
    gain = block_levels(own_key, extent, cuts, -0.22, 0.18) if cuts else 1.0
    values = jax.random.normal(own_key, extent, jnp.float32) * spread * gain
    return jnp.minimum(jnp.maximum(values, -limit), limit).astype(kind)


def setup_inputs(seed: int = 0, part: int = 0) -> dict:
    keys = jax.random.split(jax.random.key(seed), 6)
    part_splits = jax.random.split(jax.random.fold_in(keys[5], part), 6)
    return {
        "hidden": bell_draw(part_splits[0], (SEQS, D), 1.0, 6.0, ((0, 16),)),
        "final_gain": jnp.clip(1.0 + 0.18 * jax.random.normal(keys[1], (D,), jnp.float32), 0.099609375, 1.8984375).astype(jnp.bfloat16),
        "last_row": jax.vmap(lambda own: jax.random.permutation(own, SEQ_DEV))(jax.random.split(part_splits[2], NBLK)).reshape((NBLK, SEQ_DEV)).astype(jnp.int32),
        "pair_owner": draw_pair_owner(jax.random.fold_in(jax.random.fold_in(keys[5], part), 71), part),
        "hard_negatives": draw_hard_negatives(jax.random.fold_in(jax.random.fold_in(keys[5], part), 71), part),
    }


inverse_temp = 50.0
token_eps = 1e-05

def reference(hidden, final_gain, last_row, pair_owner, hard_negatives):
    gain_row = final_gain.astype(jnp.float32)

    def norm_device(block_rows):
        values = block_rows.astype(jnp.float32)
        scale_row = lax.rsqrt(lax.optimization_barrier(jnp.mean(values * values, axis=-1, keepdims=True)) + token_eps)
        return (values * scale_row * gain_row).astype(jnp.bfloat16)
    normed = lax.map(norm_device, hidden.reshape(NBLK, SEQ_DEV, D))
    device_ids = jnp.arange(NBLK, dtype=jnp.int32)[:, None]
    pooled = normed[device_ids, last_row].astype(jnp.float32).reshape(SEQS, D)
    inverse_norm = lax.rsqrt(lax.optimization_barrier(jnp.sum(pooled * pooled, axis=-1, keepdims=True)) + 1e-06)
    unit_vec = pooled * inverse_norm
    embedding = unit_vec.astype(jnp.bfloat16)
    queries = embedding[pair_owner[:, 0]].reshape(NBLK, PAIR_DEV, D)
    documents = embedding[pair_owner[:, 1]].reshape(NBLK, PAIR_DEV, D)
    diagonal = jnp.arange(PAIR_DEV, dtype=jnp.int32)
    columns = jnp.arange((WINDOW + 1) * PAIR_DEV, dtype=jnp.int32)
    target = (columns[None, :] == diagonal[:, None]).astype(jnp.float32)

    def block_step(block):
        query_rows = queries[block]
        listed = hard_negatives[block]
        candidates = jnp.concatenate([documents[block]] + [documents[jnp.maximum(listed[offset], 0)] for offset in range(WINDOW)], axis=0)
        usable = jnp.concatenate([jnp.ones((PAIR_DEV,), jnp.bool_)] + [jnp.broadcast_to(listed[offset] >= 0, (PAIR_DEV,)) for offset in range(WINDOW)])
        scores = inverse_temp * jnp.dot(query_rows, candidates.T, preferred_element_type=jnp.float32)
        masked = jnp.where(usable[None, :], scores, -jnp.inf)
        row_max = lax.optimization_barrier(jnp.max(masked, axis=1, keepdims=True))
        log_total = row_max + jnp.log(lax.optimization_barrier(jnp.sum(jnp.exp(masked - row_max), axis=1, keepdims=True)))
        positive = scores[diagonal, diagonal]
        loss_value = jnp.mean(log_total[:, 0] - positive)
        coefficients = (inverse_temp * (jnp.exp(masked - log_total) - target)).astype(jnp.bfloat16)
        query_grad = jnp.dot(coefficients, candidates, preferred_element_type=jnp.float32).astype(jnp.bfloat16)
        doc_parts = lax.dot_general(coefficients, query_rows, (((0,), (0,)), ((), ())), preferred_element_type=jnp.float32)
        doc_parts = doc_parts.astype(jnp.bfloat16).reshape(WINDOW + 1, PAIR_DEV, D)
        return (loss_value, query_grad, doc_parts)
    losses, query_grads, doc_parts = lax.map(block_step, jnp.arange(NBLK, dtype=jnp.int32))
    doc_sum = doc_parts[:, 0].astype(jnp.float32)
    for offset in range(WINDOW):
        targets_at = jnp.where(hard_negatives[:, offset] >= 0, hard_negatives[:, offset], NBLK).astype(jnp.int32)
        added = jax.ops.segment_sum(doc_parts[:, offset + 1].astype(jnp.float32), targets_at, num_segments=NBLK + 1)
        doc_sum = doc_sum + added[:NBLK]
    doc_grad = doc_sum.astype(jnp.bfloat16)
    emb_grad = jnp.zeros((SEQS, D), jnp.bfloat16)
    emb_grad = emb_grad.at[pair_owner[:, 0]].set(query_grads.reshape(PAIRS, D))
    emb_grad = emb_grad.at[pair_owner[:, 1]].set(doc_grad.reshape(PAIRS, D))
    gradient = emb_grad.astype(jnp.float32)
    pooled_grad = gradient - unit_vec * lax.optimization_barrier(jnp.sum(unit_vec * gradient, axis=-1, keepdims=True))
    return (pooled_grad, losses)
```

```python
import functools

import jax
import jax.numpy as jnp
from jax import lax
from jax.experimental import pallas as pl
from jax.experimental.pallas import tpu as pltpu
from jax.sharding import PartitionSpec as P

inverse_temp = 50.0
token_eps = 1e-05
unit_eps = 1e-06
lanes = 128
vmem_limit = 56 * 1024 * 1024


def norm_kernel(last_ref, hidden_ref, gain_ref, normed_ref, inv_ref, emb_ref):
    rows, width = normed_ref.shape
    source = hidden_ref.shape[0]
    parts, _, piece = emb_ref.shape
    columns = lax.broadcasted_iota(jnp.int32, (rows, source), 1)
    pick = jnp.where(columns == last_ref[...], 1.0, 0.0).astype(jnp.bfloat16)
    values = jnp.dot(pick, hidden_ref[...], preferred_element_type=jnp.float32)
    scale = lax.rsqrt(jnp.mean(values * values, axis=-1, keepdims=True) + token_eps)
    normed = (values * scale * gain_ref[...].astype(jnp.float32)).astype(jnp.bfloat16)
    normed_ref[...] = normed
    pooled = normed.astype(jnp.float32)
    inverse = lax.rsqrt(jnp.sum(pooled * pooled, axis=-1, keepdims=True) + unit_eps)
    inv_ref[...] = jnp.broadcast_to(inverse, inv_ref.shape)
    embedding = (pooled * inverse).astype(jnp.bfloat16)
    for part in range(parts):
        emb_ref[part] = embedding[:, part * piece : (part + 1) * piece]


def norm_call(last_column, hidden, gain_row, parts):
    seqs, width = hidden.shape
    piece = width // parts
    rows = 32
    return pl.pallas_call(
        norm_kernel,
        grid=(seqs // rows,),
        in_specs=[
            pl.BlockSpec((rows, 1), lambda i: (i, 0)),
            pl.BlockSpec((seqs, width), lambda i: (0, 0)),
            pl.BlockSpec((1, width), lambda i: (0, 0)),
        ],
        out_specs=[
            pl.BlockSpec((rows, width), lambda i: (i, 0)),
            pl.BlockSpec((rows, lanes), lambda i: (i, 0)),
            pl.BlockSpec((parts, rows, piece), lambda i: (0, i, 0)),
        ],
        out_shape=[
            jax.ShapeDtypeStruct((seqs, width), jnp.bfloat16),
            jax.ShapeDtypeStruct((seqs, lanes), jnp.float32),
            jax.ShapeDtypeStruct((parts, seqs, piece), jnp.bfloat16),
        ],
        compiler_params=pltpu.CompilerParams(vmem_limit_bytes=vmem_limit),
        name="norm_rows",
    )(last_column, hidden, gain_row)


def score_kernel(blocks, pairs, window, own_ref, emb_ref, q_ref, d_ref, s_ref, wide, picked):
    seqs = emb_ref.shape[0]
    chunk = 256

    def widen(step, carry):
        at = pl.multiple_of(step * chunk, chunk)
        wide[pl.ds(at, chunk), :] = emb_ref[pl.ds(at, chunk), :].astype(jnp.float32)
        return carry

    lax.fori_loop(0, seqs // chunk, widen, 0)

    def pick_block(block, carry):
        def pick_rows(step, inner):
            base = pl.multiple_of(step * 8, 8)
            for k in range(8):
                picked[pl.ds(base + k, 1), :] = wide[pl.ds(own_ref[block, base + k], 1), :]
            return inner

        lax.fori_loop(0, 2 * pairs // 8, pick_rows, 0)
        at = pl.multiple_of(block * pairs, pairs)
        q_ref[pl.ds(at, pairs), :] = picked[:pairs, :].astype(jnp.bfloat16)
        d_ref[pl.ds(at, pairs), :] = picked[pairs:, :].astype(jnp.bfloat16)
        return carry

    lax.fori_loop(0, blocks, pick_block, 0)
    d_ref[blocks * pairs :, :] = d_ref[: window * pairs, :]
    groups = s_ref.shape[0]
    fine = pairs // groups

    def score_block(block, carry):
        at = pl.multiple_of(block * pairs, pairs)
        queries = q_ref[pl.ds(at, pairs), :]
        for column in range(window + 1):
            there = pl.multiple_of(at + column * pairs, pairs)
            documents = d_ref[pl.ds(there, pairs), :]
            tile = inverse_temp * lax.dot_general(
                queries, documents, (((1,), (1,)), ((), ())), preferred_element_type=jnp.float32
            )
            row = pl.multiple_of((column * blocks + block) * fine, fine)
            s_ref[:, pl.ds(row, fine), :] = tile.reshape(groups, fine, pairs)
        return carry

    lax.fori_loop(0, blocks, score_block, 0)


def score_call(own, embedded, blocks, pairs, window):
    seqs, piece = embedded.shape
    fine = pairs // blocks
    tiles = blocks * (window + 1)
    whole = pl.BlockSpec(memory_space=pltpu.VMEM)
    return pl.pallas_call(
        functools.partial(score_kernel, blocks, pairs, window),
        in_specs=[pl.BlockSpec(memory_space=pltpu.SMEM), whole],
        out_specs=[whole, whole, whole],
        out_shape=[
            jax.ShapeDtypeStruct((blocks * pairs, piece), jnp.bfloat16),
            jax.ShapeDtypeStruct(((blocks + window) * pairs, piece), jnp.bfloat16),
            jax.ShapeDtypeStruct((blocks, tiles * fine, pairs), jnp.float32),
        ],
        scratch_shapes=[
            pltpu.VMEM((seqs, piece), jnp.float32),
            pltpu.VMEM((2 * pairs, piece), jnp.float32),
        ],
        compiler_params=pltpu.CompilerParams(vmem_limit_bytes=vmem_limit),
        name="partial_scores",
    )(own, embedded)


def softmax_kernel(blocks, window, listed_ref, s_ref, c_ref, loss_ref):
    fine = s_ref.shape[2]
    pairs = s_ref.shape[3]
    first = lax.axis_index("pb") * fine
    rows = lax.broadcasted_iota(jnp.int32, (fine, pairs), 0) + first
    target = lax.broadcasted_iota(jnp.int32, (fine, pairs), 1) == rows

    def one_block(block):
        listed = [True] + [listed_ref[block, offset] >= 0 for offset in range(window)]
        tiles = [s_ref[0, block]]
        for offset in range(window):
            tiles.append(jnp.where(listed[offset + 1], s_ref[offset + 1, block], -jnp.inf))
        top = functools.reduce(jnp.maximum, tiles)
        row_max = jnp.max(top, axis=1, keepdims=True)
        total = functools.reduce(jnp.add, [jnp.exp(tile - row_max) for tile in tiles])
        log_total = row_max + jnp.log(jnp.sum(total, axis=1, keepdims=True))
        positive = jnp.sum(jnp.where(target, tiles[0], 0.0), axis=1, keepdims=True)
        loss_ref[pl.ds(block, 1), :] = jnp.broadcast_to(
            jnp.sum(log_total - positive, axis=0, keepdims=True), (1, pairs)
        )
        shares = [jnp.exp(tile - log_total) for tile in tiles]
        shares[0] = shares[0] - jnp.where(target, 1.0, 0.0)
        return [inverse_temp * share for share in shares]

    def two_blocks(step, carry):
        even = one_block(2 * step)
        odd = one_block(2 * step + 1)
        for column in range(window + 1):
            both = jnp.concatenate([even[column], odd[column]], axis=0)
            c_ref[column, step] = both.astype(jnp.bfloat16)
        return carry

    lax.fori_loop(0, blocks // 2, two_blocks, 0)


def softmax_call(listed, scores, blocks, window):
    fine, pairs = scores.shape[2:]
    whole = pl.BlockSpec(memory_space=pltpu.VMEM)
    return pl.pallas_call(
        functools.partial(softmax_kernel, blocks, window),
        in_specs=[pl.BlockSpec(memory_space=pltpu.SMEM), whole],
        out_specs=[whole, whole],
        out_shape=[
            jax.ShapeDtypeStruct((window + 1, blocks // 2, 2 * fine, pairs), jnp.bfloat16),
            jax.ShapeDtypeStruct((blocks, pairs), jnp.float32),
        ],
        compiler_params=pltpu.CompilerParams(vmem_limit_bytes=vmem_limit),
        name="softmax_rows",
    )(listed, scores)


def grad_kernel(blocks, pairs, window, own_ref, c_ref, q_ref, d_ref, out_ref, wide, dsum, picked):
    fine = pairs // blocks
    seqs = wide.shape[0]
    dsum[...] = jnp.zeros_like(dsum)

    def scatter_rows(block, offset):
        def step_rows(step, inner):
            base = pl.multiple_of(step * 8, 8)
            for k in range(8):
                wide[pl.ds(own_ref[block, offset + base + k], 1), :] = picked[
                    pl.ds(base + k, 1), :
                ]
            return inner

        lax.fori_loop(0, pairs // 8, step_rows, 0)

    def one_block(block, coefficients):
        at = pl.multiple_of(block * pairs, pairs)
        picked[...] = jnp.dot(
            coefficients,
            d_ref[pl.ds(at, (window + 1) * pairs), :],
            preferred_element_type=jnp.float32,
        )
        scatter_rows(block, 0)
        dsum[pl.ds(at, (window + 1) * pairs), :] += lax.dot_general(
            coefficients,
            q_ref[pl.ds(at, pairs), :],
            (((0,), (0,)), ((), ())),
            preferred_element_type=jnp.float32,
        )

    def two_blocks(step, carry):
        pieces = [c_ref[:, column, step].astype(jnp.float32) for column in range(window + 1)]
        for half in range(2):
            coefficients = jnp.concatenate(
                [
                    piece[:, half * fine : (half + 1) * fine].reshape(pairs, pairs)
                    for piece in pieces
                ],
                axis=1,
            ).astype(jnp.bfloat16)
            one_block(2 * step + half, coefficients)
        return carry

    lax.fori_loop(0, blocks // 2, two_blocks, 0)
    dsum[: window * pairs, :] += dsum[blocks * pairs :, :]

    def doc_block(block, carry):
        at = pl.multiple_of(block * pairs, pairs)
        picked[...] = dsum[pl.ds(at, pairs), :]
        scatter_rows(block, pairs)
        return carry

    lax.fori_loop(0, blocks, doc_block, 0)
    slots = out_ref.shape[1]

    def narrow(part, carry):
        at = pl.multiple_of(part * slots, slots)
        out_ref[part] = wide[pl.ds(at, slots), :].astype(jnp.bfloat16)
        return carry

    lax.fori_loop(0, seqs // slots, narrow, 0)


def grad_call(own, coefficients, queries, documents, blocks, pairs, window):
    count, piece = queries.shape
    seqs = 2 * count
    whole = pl.BlockSpec(memory_space=pltpu.VMEM)
    return pl.pallas_call(
        functools.partial(grad_kernel, blocks, pairs, window),
        in_specs=[pl.BlockSpec(memory_space=pltpu.SMEM), whole, whole, whole],
        out_specs=whole,
        out_shape=jax.ShapeDtypeStruct((blocks, seqs // blocks, piece), jnp.bfloat16),
        scratch_shapes=[
            pltpu.VMEM((seqs, piece), jnp.float32),
            pltpu.VMEM(((blocks + window) * pairs, piece), jnp.float32),
            pltpu.VMEM((pairs, piece), jnp.float32),
        ],
        compiler_params=pltpu.CompilerParams(vmem_limit_bytes=vmem_limit),
        name="slice_grads",
    )(own, coefficients, queries, documents)


def project_kernel(grad_ref, normed_ref, inv_ref, out_ref):
    parts, _, piece = grad_ref.shape
    inverse = inv_ref[:, :1]
    total = 0.0
    for part in range(parts):
        cut = slice(part * piece, (part + 1) * piece)
        unit = normed_ref[:, cut].astype(jnp.float32) * inverse
        total = total + unit * grad_ref[part].astype(jnp.float32)
    along = jnp.sum(total, axis=-1, keepdims=True)
    for part in range(parts):
        cut = slice(part * piece, (part + 1) * piece)
        unit = normed_ref[:, cut].astype(jnp.float32) * inverse
        out_ref[:, cut] = grad_ref[part].astype(jnp.float32) - unit * along


def project_call(returned, normed, inverse):
    parts, seqs, piece = returned.shape
    width = normed.shape[1]
    rows = 32
    return pl.pallas_call(
        project_kernel,
        grid=(seqs // rows,),
        in_specs=[
            pl.BlockSpec((parts, rows, piece), lambda i: (0, i, 0)),
            pl.BlockSpec((rows, width), lambda i: (i, 0)),
            pl.BlockSpec((rows, lanes), lambda i: (i, 0)),
        ],
        out_specs=pl.BlockSpec((rows, width), lambda i: (i, 0)),
        out_shape=jax.ShapeDtypeStruct((seqs, width), jnp.float32),
        compiler_params=pltpu.CompilerParams(vmem_limit_bytes=vmem_limit),
        name="project_out",
    )(returned, normed, inverse)


def feature_plan(hidden, final_gain, last_row, pair_owner, hard_negatives):
    devices = lax.axis_size("pb")
    seqs, width = hidden.shape
    pairs = pair_owner.shape[0]
    window = hard_negatives.shape[1]
    piece = width // devices
    fine = pairs // devices
    facts = jnp.concatenate([pair_owner.T.reshape(-1), hard_negatives[0]]).reshape(1, -1)
    every = lax.all_gather(facts, "pb", axis=0, tiled=True)
    own = every[:, : 2 * pairs]
    listed = every[:, 2 * pairs :]
    normed, inverse, embedding = norm_call(
        last_row.reshape(seqs, 1), hidden, final_gain.reshape(1, width), devices
    )
    embedded = lax.all_to_all(embedding, "pb", split_axis=0, concat_axis=0, tiled=True)
    queries, documents, partial_scores = score_call(
        own, embedded.reshape(devices * seqs, piece), devices, pairs, window
    )
    scores = lax.psum_scatter(partial_scores, "pb", scatter_dimension=0, tiled=False)
    coefficients, losses = softmax_call(
        listed, scores.reshape(window + 1, devices, fine, pairs), devices, window
    )
    block_loss = lax.psum_scatter(losses[:, 0], "pb", scatter_dimension=0, tiled=True) / pairs
    shared = lax.all_gather(coefficients, "pb", axis=0, tiled=False)
    grads = grad_call(own, shared, queries, documents, devices, pairs, window)
    returned = lax.all_to_all(grads, "pb", split_axis=0, concat_axis=0, tiled=True)
    return project_call(returned, normed, inverse), block_loss


def from_behind(value, axis, steps):
    count = lax.axis_size(axis)
    pairs = [(source, (source + steps) % count) for source in range(count)]
    return lax.ppermute(value, axis, pairs)


def similarity(queries, documents):
    return inverse_temp * lax.dot_general(
        queries, documents, (((1,), (1,)), ((), ())), preferred_element_type=jnp.float32
    )


def transposed(weights, queries):
    return lax.dot_general(
        weights, queries, (((0,), (0,)), ((), ())), preferred_element_type=jnp.float32
    )


def combine_docs(weights, documents):
    return jnp.dot(weights, documents, preferred_element_type=jnp.float32)


def skipped(listed, function, operands, out_shape):
    return lax.cond(
        listed,
        lambda inputs: function(*inputs),
        lambda inputs: jnp.zeros(out_shape, jnp.float32),
        operands,
    )


def row_plan(hidden, final_gain, last_row, pair_owner, hard_negatives):
    values = hidden.astype(jnp.float32)
    scale_row = lax.rsqrt(jnp.mean(values * values, axis=-1, keepdims=True) + token_eps)
    normed = (values * scale_row * final_gain.astype(jnp.float32)).astype(jnp.bfloat16)
    seq_count = last_row.shape[1]
    model_width = hidden.shape[1]
    pooled = normed[last_row[0]].astype(jnp.float32)
    inverse_norm = lax.rsqrt(jnp.sum(pooled * pooled, axis=-1, keepdims=True) + 1e-06)
    unit_vec = pooled * inverse_norm
    embedding = unit_vec.astype(jnp.bfloat16)
    devices = lax.axis_size("pb")
    capacity = 2 * seq_count // devices
    pair_count = pair_owner.shape[0]
    wanted = jnp.concatenate([pair_owner[:, 0], pair_owner[:, 1]])
    holder = wanted // seq_count
    within = wanted % seq_count
    entry_ids = jnp.arange(2 * pair_count, dtype=jnp.int32)
    earlier = (holder[None, :] == holder[:, None]) & (entry_ids[None, :] < entry_ids[:, None])
    position = jnp.sum(earlier.astype(jnp.int32), axis=1)
    request = jnp.full((devices, capacity), -1, jnp.int32).at[holder, position].set(within)
    served = lax.all_to_all(request, "pb", split_axis=0, concat_axis=0, tiled=True)
    outgoing = jnp.where(
        served[:, :, None] >= 0, embedding[jnp.maximum(served, 0)], jnp.zeros((), jnp.bfloat16)
    )
    received = lax.all_to_all(outgoing, "pb", split_axis=0, concat_axis=0, tiled=True)
    gathered = received[holder, position]
    queries = gathered[:pair_count]
    own_docs = gathered[pair_count:]
    listed_ids = hard_negatives[0]
    window = hard_negatives.shape[1]
    listed = [listed_ids[offset] >= 0 for offset in range(window)]
    neighbours = []
    moving = own_docs
    for offset in range(window):
        moving = from_behind(moving, "pb", -1)
        neighbours.append(moving)
    tile_shape = (pair_count, pair_count)
    score_blocks = [similarity(queries, own_docs)]
    for offset in range(window):
        score_blocks.append(
            skipped(listed[offset], similarity, (queries, neighbours[offset]), tile_shape)
        )
    all_scores = jnp.concatenate(score_blocks, axis=1)
    usable = jnp.concatenate(
        [jnp.ones((pair_count,), jnp.bool_)]
        + [jnp.broadcast_to(listed[offset], (pair_count,)) for offset in range(window)]
    )
    masked = jnp.where(usable[None, :], all_scores, -jnp.inf)
    row_max = jnp.max(masked, axis=1, keepdims=True)
    log_total = row_max + jnp.log(jnp.sum(jnp.exp(masked - row_max), axis=1, keepdims=True))
    diagonal = jnp.arange(pair_count, dtype=jnp.int32)
    positive = all_scores[diagonal, diagonal]
    block_loss = jnp.mean(log_total[:, 0] - positive).reshape(1)
    columns = jnp.arange((window + 1) * pair_count, dtype=jnp.int32)
    target = (columns[None, :] == diagonal[:, None]).astype(jnp.float32)
    coefficients = (inverse_temp * (jnp.exp(masked - log_total) - target)).astype(jnp.bfloat16)
    pieces = [
        coefficients[:, offset * pair_count : (offset + 1) * pair_count]
        for offset in range(window + 1)
    ]
    grad_shape = (pair_count, model_width)
    query_sum = combine_docs(pieces[0], own_docs)
    for offset in range(window):
        query_sum = query_sum + skipped(
            listed[offset], combine_docs, (pieces[offset + 1], neighbours[offset]), grad_shape
        )
    query_grad = query_sum.astype(jnp.bfloat16)
    own_part = transposed(pieces[0], queries).astype(jnp.bfloat16)
    partial_value = [
        skipped(listed[offset], transposed, (pieces[offset + 1], queries), grad_shape).astype(
            jnp.bfloat16
        )
        for offset in range(window)
    ]
    running = partial_value[window - 1].astype(jnp.float32)
    for offset in range(window):
        running = from_behind(running, "pb", 1)
        if offset + 1 < window:
            running = running + partial_value[window - 2 - offset].astype(jnp.float32)
    doc_grad = (own_part.astype(jnp.float32) + running).astype(jnp.bfloat16)
    answers = jnp.concatenate([query_grad, doc_grad], axis=0)
    returning = (
        jnp.zeros((devices, capacity, model_width), jnp.bfloat16).at[holder, position].set(answers)
    )
    returned = lax.all_to_all(returning, "pb", split_axis=0, concat_axis=0, tiled=True)
    slot_ids = jnp.where(served >= 0, served, seq_count).reshape(-1)
    emb_grad = (
        jnp.zeros((seq_count, model_width), jnp.bfloat16)
        .at[slot_ids]
        .set(returned.reshape(-1, model_width), mode="drop")
    )
    gradient = emb_grad.astype(jnp.float32)
    pooled_grad = gradient - unit_vec * jnp.sum(unit_vec * gradient, axis=-1, keepdims=True)
    return (pooled_grad, block_loss)


def solution(mesh):
    def local(hidden, final_gain, last_row, pair_owner, hard_negatives):
        plan = feature_plan if hidden.shape[1] >= lanes * mesh.shape["pb"] else row_plan
        return plan(hidden, final_gain, last_row, pair_owner, hard_negatives)

    return jax.shard_map(
        local,
        mesh=mesh,
        in_specs=(
            P(("groups", "pb"), None),
            P(),
            P(("groups", "pb"), None),
            P(("groups", "pb"), None),
            P(("groups", "pb"), None),
        ),
        out_specs=(P(("groups", "pb"), None), P(("groups", "pb"))),
        check_vma=False,
    )
```

```python
import functools

import jax
import jax.numpy as jnp
from jax import lax
from jax.experimental import pallas as pl
from jax.experimental.pallas import tpu as pltpu
from jax.sharding import PartitionSpec as P

inverse_temp = 50.0
token_eps = 1e-05
unit_eps = 1e-06
lanes = 128
vmem_limit = 56 * 1024 * 1024


def norm_kernel(last_ref, hidden_ref, gain_ref, owner_ref, negative_ref, normed_ref, inv_ref, emb_ref):
    seqs, width = normed_ref.shape
    parts, _, piece = emb_ref.shape
    pairs = owner_ref.shape[0]
    cuts = [slice(part * piece, (part + 1) * piece) for part in range(parts)]
    sources = lax.broadcasted_iota(jnp.int32, (seqs, seqs), 0)
    pick = jnp.where(sources == last_ref[...], 1.0, 0.0).astype(jnp.bfloat16)

    def folded(squares):
        return functools.reduce(
            jnp.add, [squares[:, at : at + lanes] for at in range(0, piece, lanes)]
        )

    total = jnp.zeros((seqs, lanes), jnp.float32)
    for cut in cuts:
        values = lax.dot_general(
            pick, hidden_ref[:, cut], (((0,), (0,)), ((), ())), preferred_element_type=jnp.float32
        )
        normed_ref[:, cut] = values.astype(jnp.bfloat16)
        total = total + folded(values * values)
    scale = lax.rsqrt(jnp.sum(total, axis=-1, keepdims=True) / width + token_eps)
    total = jnp.zeros((seqs, lanes), jnp.float32)
    for cut in cuts:
        values = normed_ref[:, cut].astype(jnp.float32)
        normed = (values * scale * gain_ref[:, cut].astype(jnp.float32)).astype(jnp.bfloat16)
        normed_ref[:, cut] = normed
        pooled = normed.astype(jnp.float32)
        total = total + folded(pooled * pooled)
    inverse = lax.rsqrt(jnp.sum(total, axis=-1, keepdims=True) + unit_eps)
    inv_ref[...] = jnp.broadcast_to(inverse, inv_ref.shape)

    lane = lax.broadcasted_iota(jnp.int32, (pairs, lanes), 1)
    columns = jnp.where(lane == 0, owner_ref[:, :1], jnp.where(lane == 1, owner_ref[:, 1:], 0))
    owners = columns.astype(jnp.float32).T
    high = jnp.floor(owners * (1.0 / 256.0))
    low = owners - 256.0 * high
    row = lax.broadcasted_iota(jnp.int32, (16, lanes), 0)
    spot = lax.broadcasted_iota(jnp.int32, (16, lanes), 1)
    left = jnp.where(row == 0, low[:1], jnp.where(row == 1, high[:1], 0.0))
    right = jnp.where(row == 0, low[1:2], jnp.where(row == 1, high[1:2], 0.0))
    for offset in range(negative_ref.shape[1]):
        named = (negative_ref[0, offset] >= 0).astype(jnp.float32)
        left = jnp.where((row == 2) & (spot == offset), named, left)
    facts = jnp.concatenate([left, right], axis=1).astype(jnp.bfloat16)

    for part, cut in enumerate(cuts):
        emb_ref[part, :seqs] = (normed_ref[:, cut].astype(jnp.float32) * inverse).astype(jnp.bfloat16)
        emb_ref[part, seqs:] = facts


def norm_call(last_row, hidden, gain_row, pair_owner, hard_negatives, parts):
    seqs, width = hidden.shape
    piece = width // parts
    whole = pl.BlockSpec(memory_space=pltpu.VMEM)
    return pl.pallas_call(
        norm_kernel,
        in_specs=[whole, whole, whole, whole, pl.BlockSpec(memory_space=pltpu.SMEM)],
        out_specs=[whole, whole, whole],
        out_shape=[
            jax.ShapeDtypeStruct((seqs, width), jnp.bfloat16),
            jax.ShapeDtypeStruct((seqs, lanes), jnp.float32),
            jax.ShapeDtypeStruct((parts, seqs + 16, piece), jnp.bfloat16),
        ],
        compiler_params=pltpu.CompilerParams(vmem_limit_bytes=vmem_limit),
        name="norm_rows",
    )(last_row, hidden, gain_row, pair_owner, hard_negatives)


def score_kernel(
    blocks, pairs, window, emb_ref, q_ref, d_ref, s_ref, own_ref, listed_ref, wide, picked, own, sem
):
    seqs = emb_ref.shape[1] - 16
    facts = emb_ref[:, seqs:, :].astype(jnp.float32)
    own_ref[...] = (facts[:, 0, :] + 256.0 * facts[:, 1, :]).astype(jnp.int32)
    listed_ref[...] = facts[:, 2, :lanes].astype(jnp.int32)
    fetch = pltpu.make_async_copy(own_ref, own, sem)
    fetch.start()

    def widen(step, carry):
        at = pl.multiple_of(step * seqs, seqs)
        wide[pl.ds(at, seqs), :] = emb_ref[step, :seqs, :].astype(jnp.float32)
        return carry

    lax.fori_loop(0, emb_ref.shape[0], widen, 0)
    fetch.wait()
    unroll = 16

    def pick_block(block, carry):
        def pick_rows(step, inner):
            base = pl.multiple_of(step * unroll, unroll)
            rows = [wide[pl.ds(own[block, base + k], 1), :] for k in range(unroll)]
            for k in range(unroll):
                picked[pl.ds(base + k, 1), :] = rows[k]
            return inner

        lax.fori_loop(0, 2 * pairs // unroll, pick_rows, 0)
        at = pl.multiple_of(block * pairs, pairs)
        q_ref[pl.ds(at, pairs), :] = picked[:pairs, :].astype(jnp.bfloat16)
        d_ref[pl.ds(at, pairs), :] = picked[pairs:, :].astype(jnp.bfloat16)
        return carry

    lax.fori_loop(0, blocks, pick_block, 0)
    d_ref[blocks * pairs :, :] = d_ref[: window * pairs, :]
    groups = s_ref.shape[0]
    fine = pairs // groups

    def score_block(block, carry):
        at = pl.multiple_of(block * pairs, pairs)
        tiles = inverse_temp * lax.dot_general(
            q_ref[pl.ds(at, pairs), :],
            d_ref[pl.ds(at, (window + 1) * pairs), :],
            (((1,), (1,)), ((), ())),
            preferred_element_type=jnp.float32,
        )
        for column in range(window + 1):
            row = pl.multiple_of((column * blocks + block) * fine, fine)
            tile = tiles[:, column * pairs : (column + 1) * pairs]
            s_ref[:, pl.ds(row, fine), :] = tile.reshape(groups, fine, pairs)
        return carry

    lax.fori_loop(0, blocks, score_block, 0)


def score_call(embedded, blocks, pairs, window):
    parts, rows, piece = embedded.shape
    fine = pairs // blocks
    tiles = blocks * (window + 1)
    whole = pl.BlockSpec(memory_space=pltpu.VMEM)
    return pl.pallas_call(
        functools.partial(score_kernel, blocks, pairs, window),
        in_specs=[whole],
        out_specs=[whole] * 5,
        out_shape=[
            jax.ShapeDtypeStruct((blocks * pairs, piece), jnp.bfloat16),
            jax.ShapeDtypeStruct(((blocks + window) * pairs, piece), jnp.bfloat16),
            jax.ShapeDtypeStruct((blocks, tiles * fine, pairs), jnp.float32),
            jax.ShapeDtypeStruct((blocks, 2 * pairs), jnp.int32),
            jax.ShapeDtypeStruct((blocks, lanes), jnp.int32),
        ],
        scratch_shapes=[
            pltpu.VMEM((parts * (rows - 16), piece), jnp.float32),
            pltpu.VMEM((2 * pairs, piece), jnp.float32),
            pltpu.SMEM((blocks, 2 * pairs), jnp.int32),
            pltpu.SemaphoreType.DMA,
        ],
        compiler_params=pltpu.CompilerParams(vmem_limit_bytes=vmem_limit),
        name="partial_scores",
    )(embedded)


def softmax_kernel(blocks, window, listed_ref, s_ref, c_ref):
    fine = s_ref.shape[2]
    pairs = s_ref.shape[3]
    first = lax.axis_index("pb") * fine
    rows = lax.broadcasted_iota(jnp.int32, (fine, pairs), 0) + first
    target = lax.broadcasted_iota(jnp.int32, (fine, pairs), 1) == rows
    lane = lax.broadcasted_iota(jnp.int32, (16, pairs), 1)

    def one_block(block, losses):
        tiles = [s_ref[0, block]]
        for offset in range(window):
            named = listed_ref[block, offset] > 0
            tiles.append(jnp.where(named, s_ref[offset + 1, block], -jnp.inf))
        top = functools.reduce(jnp.maximum, tiles)
        row_max = jnp.max(top, axis=1, keepdims=True)
        total = functools.reduce(jnp.add, [jnp.exp(tile - row_max) for tile in tiles])
        log_total = row_max + jnp.log(jnp.sum(total, axis=1, keepdims=True))
        positive = jnp.sum(jnp.where(target, tiles[0], 0.0), axis=1, keepdims=True)
        loss = jnp.sum(log_total - positive, axis=0, keepdims=True)
        shares = [jnp.exp(tile - log_total) for tile in tiles]
        shares[0] = shares[0] - jnp.where(target, 1.0, 0.0)
        return [inverse_temp * share for share in shares], jnp.where(lane == block, loss, losses)

    def two_blocks(step, losses):
        even, losses = one_block(2 * step, losses)
        odd, losses = one_block(2 * step + 1, losses)
        for column in range(window + 1):
            both = jnp.concatenate([even[column], odd[column]], axis=0)
            c_ref[column * (blocks // 2) + step] = both.astype(jnp.bfloat16)
        return losses

    losses = lax.fori_loop(0, blocks // 2, two_blocks, jnp.zeros((16, pairs), jnp.float32))
    coarse = losses.astype(jnp.bfloat16).astype(jnp.float32)
    rank = lax.broadcasted_iota(jnp.int32, (16, pairs), 0)
    both = jnp.where(rank == 0, coarse, jnp.where(rank == 1, losses - coarse, 0.0))
    c_ref[(window + 1) * (blocks // 2)] = both.astype(jnp.bfloat16)


def softmax_call(listed, scores, blocks, window):
    fine, pairs = scores.shape[2:]
    whole = pl.BlockSpec(memory_space=pltpu.VMEM)
    return pl.pallas_call(
        functools.partial(softmax_kernel, blocks, window),
        in_specs=[pl.BlockSpec(memory_space=pltpu.SMEM), whole],
        out_specs=whole,
        out_shape=jax.ShapeDtypeStruct(
            ((window + 1) * blocks // 2 + 1, 2 * fine, pairs), jnp.bfloat16
        ),
        compiler_params=pltpu.CompilerParams(vmem_limit_bytes=vmem_limit),
        name="softmax_rows",
    )(listed, scores)


def grad_kernel(
    blocks, pairs, window, own_ref, c_ref, q_ref, d_ref, out_ref, loss_ref, wide, dsum, picked
):
    fine = pairs // blocks
    seqs = wide.shape[0]
    unroll = 16
    half_blocks = blocks // 2
    coarse = c_ref[:, (window + 1) * half_blocks].astype(jnp.float32)
    losses = jnp.sum(coarse[:, 0, :] + coarse[:, 1, :], axis=0, keepdims=True) / pairs
    lane = lax.broadcasted_iota(jnp.int32, losses.shape, 1)
    mine = jnp.where(lane == lax.axis_index("pb"), losses, 0.0)
    loss_ref[...] = jnp.broadcast_to(jnp.sum(mine, axis=1, keepdims=True), loss_ref.shape)
    dsum[...] = jnp.zeros_like(dsum)

    def scatter_rows(block, offset):
        def step_rows(step, inner):
            base = pl.multiple_of(step * unroll, unroll)
            rows = [picked[pl.ds(base + k, 1), :] for k in range(unroll)]
            for k in range(unroll):
                wide[pl.ds(own_ref[block, offset + base + k], 1), :] = rows[k]
            return inner

        lax.fori_loop(0, pairs // unroll, step_rows, 0)

    def one_block(block, coefficients):
        at = pl.multiple_of(block * pairs, pairs)
        picked[...] = jnp.dot(
            coefficients,
            d_ref[pl.ds(at, (window + 1) * pairs), :],
            preferred_element_type=jnp.float32,
        )
        scatter_rows(block, 0)
        dsum[pl.ds(at, (window + 1) * pairs), :] += lax.dot_general(
            coefficients,
            q_ref[pl.ds(at, pairs), :],
            (((0,), (0,)), ((), ())),
            preferred_element_type=jnp.float32,
        )

    def two_blocks(step, carry):
        pieces = [
            c_ref[:, column * half_blocks + step].astype(jnp.float32)
            for column in range(window + 1)
        ]
        for half in range(2):
            coefficients = jnp.concatenate(
                [
                    piece[:, half * fine : (half + 1) * fine].reshape(pairs, pairs)
                    for piece in pieces
                ],
                axis=1,
            ).astype(jnp.bfloat16)
            one_block(2 * step + half, coefficients)
        return carry

    lax.fori_loop(0, half_blocks, two_blocks, 0)
    dsum[: window * pairs, :] += dsum[blocks * pairs :, :]

    def doc_block(block, carry):
        at = pl.multiple_of(block * pairs, pairs)
        picked[...] = dsum[pl.ds(at, pairs), :]
        scatter_rows(block, pairs)
        return carry

    lax.fori_loop(0, blocks, doc_block, 0)
    slots = out_ref.shape[1]

    def narrow(part, carry):
        at = pl.multiple_of(part * slots, slots)
        out_ref[part] = wide[pl.ds(at, slots), :].astype(jnp.bfloat16)
        return carry

    lax.fori_loop(0, seqs // slots, narrow, 0)


def grad_call(own, coefficients, queries, documents, blocks, pairs, window):
    count, piece = queries.shape
    seqs = 2 * count
    whole = pl.BlockSpec(memory_space=pltpu.VMEM)
    return pl.pallas_call(
        functools.partial(grad_kernel, blocks, pairs, window),
        in_specs=[pl.BlockSpec(memory_space=pltpu.SMEM), whole, whole, whole],
        out_specs=[whole, whole],
        out_shape=[
            jax.ShapeDtypeStruct((blocks, seqs // blocks, piece), jnp.bfloat16),
            jax.ShapeDtypeStruct((1, lanes), jnp.float32),
        ],
        scratch_shapes=[
            pltpu.VMEM((seqs, piece), jnp.float32),
            pltpu.VMEM(((blocks + window) * pairs, piece), jnp.float32),
            pltpu.VMEM((pairs, piece), jnp.float32),
        ],
        compiler_params=pltpu.CompilerParams(vmem_limit_bytes=vmem_limit),
        name="slice_grads",
    )(own, coefficients, queries, documents)


def project_kernel(grad_ref, normed_ref, inv_ref, out_ref):
    parts, _, piece = grad_ref.shape
    inverse = inv_ref[:, :1]
    total = 0.0
    for part in range(parts):
        cut = slice(part * piece, (part + 1) * piece)
        unit = normed_ref[:, cut].astype(jnp.float32) * inverse
        total = total + unit * grad_ref[part].astype(jnp.float32)
    along = jnp.sum(total, axis=-1, keepdims=True)
    for part in range(parts):
        cut = slice(part * piece, (part + 1) * piece)
        unit = normed_ref[:, cut].astype(jnp.float32) * inverse
        out_ref[:, cut] = grad_ref[part].astype(jnp.float32) - unit * along


def project_call(returned, normed, inverse):
    parts, seqs, piece = returned.shape
    width = normed.shape[1]
    rows = 32
    return pl.pallas_call(
        project_kernel,
        grid=(seqs // rows,),
        in_specs=[
            pl.BlockSpec((parts, rows, piece), lambda i: (0, i, 0)),
            pl.BlockSpec((rows, width), lambda i: (i, 0)),
            pl.BlockSpec((rows, lanes), lambda i: (i, 0)),
        ],
        out_specs=pl.BlockSpec((rows, width), lambda i: (i, 0)),
        out_shape=jax.ShapeDtypeStruct((seqs, width), jnp.float32),
        compiler_params=pltpu.CompilerParams(vmem_limit_bytes=vmem_limit),
        name="project_out",
    )(returned, normed, inverse)


def feature_plan(hidden, final_gain, last_row, pair_owner, hard_negatives):
    devices = lax.axis_size("pb")
    width = hidden.shape[1]
    pairs = pair_owner.shape[0]
    window = hard_negatives.shape[1]
    fine = pairs // devices
    normed, inverse, embedding = norm_call(
        last_row, hidden, final_gain.reshape(1, width), pair_owner, hard_negatives, devices
    )
    embedded = lax.all_to_all(embedding, "pb", split_axis=0, concat_axis=0, tiled=True)
    queries, documents, partial_scores, own, listed = score_call(embedded, devices, pairs, window)
    scores = lax.psum_scatter(partial_scores, "pb", scatter_dimension=0, tiled=False)
    coefficients = softmax_call(
        listed, scores.reshape(window + 1, devices, fine, pairs), devices, window
    )
    shared = lax.all_gather(coefficients, "pb", axis=0, tiled=False)
    grads, loss = grad_call(own, shared, queries, documents, devices, pairs, window)
    returned = lax.all_to_all(grads, "pb", split_axis=0, concat_axis=0, tiled=True)
    return project_call(returned, normed, inverse), loss[0, :1]


def from_behind(value, axis, steps):
    count = lax.axis_size(axis)
    pairs = [(source, (source + steps) % count) for source in range(count)]
    return lax.ppermute(value, axis, pairs)


def similarity(queries, documents):
    return inverse_temp * lax.dot_general(
        queries, documents, (((1,), (1,)), ((), ())), preferred_element_type=jnp.float32
    )


def transposed(weights, queries):
    return lax.dot_general(
        weights, queries, (((0,), (0,)), ((), ())), preferred_element_type=jnp.float32
    )


def combine_docs(weights, documents):
    return jnp.dot(weights, documents, preferred_element_type=jnp.float32)


def skipped(listed, function, operands, out_shape):
    return lax.cond(
        listed,
        lambda inputs: function(*inputs),
        lambda inputs: jnp.zeros(out_shape, jnp.float32),
        operands,
    )


def row_plan(hidden, final_gain, last_row, pair_owner, hard_negatives):
    values = hidden.astype(jnp.float32)
    scale_row = lax.rsqrt(jnp.mean(values * values, axis=-1, keepdims=True) + token_eps)
    normed = (values * scale_row * final_gain.astype(jnp.float32)).astype(jnp.bfloat16)
    seq_count = last_row.shape[1]
    model_width = hidden.shape[1]
    pooled = normed[last_row[0]].astype(jnp.float32)
    inverse_norm = lax.rsqrt(jnp.sum(pooled * pooled, axis=-1, keepdims=True) + 1e-06)
    unit_vec = pooled * inverse_norm
    embedding = unit_vec.astype(jnp.bfloat16)
    devices = lax.axis_size("pb")
    capacity = 2 * seq_count // devices
    pair_count = pair_owner.shape[0]
    wanted = jnp.concatenate([pair_owner[:, 0], pair_owner[:, 1]])
    holder = wanted // seq_count
    within = wanted % seq_count
    entry_ids = jnp.arange(2 * pair_count, dtype=jnp.int32)
    earlier = (holder[None, :] == holder[:, None]) & (entry_ids[None, :] < entry_ids[:, None])
    position = jnp.sum(earlier.astype(jnp.int32), axis=1)
    request = jnp.full((devices, capacity), -1, jnp.int32).at[holder, position].set(within)
    served = lax.all_to_all(request, "pb", split_axis=0, concat_axis=0, tiled=True)
    outgoing = jnp.where(
        served[:, :, None] >= 0, embedding[jnp.maximum(served, 0)], jnp.zeros((), jnp.bfloat16)
    )
    received = lax.all_to_all(outgoing, "pb", split_axis=0, concat_axis=0, tiled=True)
    gathered = received[holder, position]
    queries = gathered[:pair_count]
    own_docs = gathered[pair_count:]
    listed_ids = hard_negatives[0]
    window = hard_negatives.shape[1]
    listed = [listed_ids[offset] >= 0 for offset in range(window)]
    neighbours = []
    moving = own_docs
    for offset in range(window):
        moving = from_behind(moving, "pb", -1)
        neighbours.append(moving)
    tile_shape = (pair_count, pair_count)
    score_blocks = [similarity(queries, own_docs)]
    for offset in range(window):
        score_blocks.append(
            skipped(listed[offset], similarity, (queries, neighbours[offset]), tile_shape)
        )
    all_scores = jnp.concatenate(score_blocks, axis=1)
    usable = jnp.concatenate(
        [jnp.ones((pair_count,), jnp.bool_)]
        + [jnp.broadcast_to(listed[offset], (pair_count,)) for offset in range(window)]
    )
    masked = jnp.where(usable[None, :], all_scores, -jnp.inf)
    row_max = jnp.max(masked, axis=1, keepdims=True)
    log_total = row_max + jnp.log(jnp.sum(jnp.exp(masked - row_max), axis=1, keepdims=True))
    diagonal = jnp.arange(pair_count, dtype=jnp.int32)
    positive = all_scores[diagonal, diagonal]
    block_loss = jnp.mean(log_total[:, 0] - positive).reshape(1)
    columns = jnp.arange((window + 1) * pair_count, dtype=jnp.int32)
    target = (columns[None, :] == diagonal[:, None]).astype(jnp.float32)
    coefficients = (inverse_temp * (jnp.exp(masked - log_total) - target)).astype(jnp.bfloat16)
    pieces = [
        coefficients[:, offset * pair_count : (offset + 1) * pair_count]
        for offset in range(window + 1)
    ]
    grad_shape = (pair_count, model_width)
    query_sum = combine_docs(pieces[0], own_docs)
    for offset in range(window):
        query_sum = query_sum + skipped(
            listed[offset], combine_docs, (pieces[offset + 1], neighbours[offset]), grad_shape
        )
    query_grad = query_sum.astype(jnp.bfloat16)
    own_part = transposed(pieces[0], queries).astype(jnp.bfloat16)
    partial_value = [
        skipped(listed[offset], transposed, (pieces[offset + 1], queries), grad_shape).astype(
            jnp.bfloat16
        )
        for offset in range(window)
    ]
    running = partial_value[window - 1].astype(jnp.float32)
    for offset in range(window):
        running = from_behind(running, "pb", 1)
        if offset + 1 < window:
            running = running + partial_value[window - 2 - offset].astype(jnp.float32)
    doc_grad = (own_part.astype(jnp.float32) + running).astype(jnp.bfloat16)
    answers = jnp.concatenate([query_grad, doc_grad], axis=0)
    returning = (
        jnp.zeros((devices, capacity, model_width), jnp.bfloat16).at[holder, position].set(answers)
    )
    returned = lax.all_to_all(returning, "pb", split_axis=0, concat_axis=0, tiled=True)
    slot_ids = jnp.where(served >= 0, served, seq_count).reshape(-1)
    emb_grad = (
        jnp.zeros((seq_count, model_width), jnp.bfloat16)
        .at[slot_ids]
        .set(returned.reshape(-1, model_width), mode="drop")
    )
    gradient = emb_grad.astype(jnp.float32)
    pooled_grad = gradient - unit_vec * jnp.sum(unit_vec * gradient, axis=-1, keepdims=True)
    return (pooled_grad, block_loss)


def solution(mesh):
    def local(hidden, final_gain, last_row, pair_owner, hard_negatives):
        plan = feature_plan if hidden.shape[1] >= lanes * mesh.shape["pb"] else row_plan
        return plan(hidden, final_gain, last_row, pair_owner, hard_negatives)

    return jax.shard_map(
        local,
        mesh=mesh,
        in_specs=(
            P(("groups", "pb"), None),
            P(),
            P(("groups", "pb"), None),
            P(("groups", "pb"), None),
            P(("groups", "pb"), None),
        ),
        out_specs=(P(("groups", "pb"), None), P(("groups", "pb"))),
        check_vma=False,
    )
```

```python
import functools

import jax
import jax.numpy as jnp
from jax import lax
from jax.experimental import pallas as pl
from jax.experimental.pallas import tpu as pltpu
from jax.sharding import PartitionSpec as P

inverse_temp = 50.0
token_eps = 1e-05
unit_eps = 1e-06
lanes = 128
vmem_limit = 56 * 1024 * 1024


def spread(target, at, value):
    count, width = value.shape
    for part in range(width // lanes):
        target[pl.ds(at, count), part, :] = value[:, part * lanes : (part + 1) * lanes]


def gathered(source, at, count):
    parts = [source[pl.ds(at, count), part, :] for part in range(source.shape[1])]
    return jnp.concatenate(parts, axis=1)


def norm_kernel(last_ref, hidden_ref, gain_ref, owner_ref, negative_ref, normed_ref, inv_ref, emb_ref):
    seqs, width = normed_ref.shape
    parts, _, piece = emb_ref.shape
    pairs = owner_ref.shape[0]
    cuts = [slice(part * piece, (part + 1) * piece) for part in range(parts)]
    sources = lax.broadcasted_iota(jnp.int32, (seqs, seqs), 0)
    pick = jnp.where(sources == last_ref[...], 1.0, 0.0).astype(jnp.bfloat16)

    def folded(squares):
        return functools.reduce(
            jnp.add, [squares[:, at : at + lanes] for at in range(0, piece, lanes)]
        )

    total = jnp.zeros((seqs, lanes), jnp.float32)
    for cut in cuts:
        values = lax.dot_general(
            pick, hidden_ref[:, cut], (((0,), (0,)), ((), ())), preferred_element_type=jnp.float32
        )
        normed_ref[:, cut] = values.astype(jnp.bfloat16)
        total = total + folded(values * values)
    scale = lax.rsqrt(jnp.sum(total, axis=-1, keepdims=True) / width + token_eps)
    total = jnp.zeros((seqs, lanes), jnp.float32)
    for cut in cuts:
        values = normed_ref[:, cut].astype(jnp.float32)
        normed = (values * scale * gain_ref[:, cut].astype(jnp.float32)).astype(jnp.bfloat16)
        normed_ref[:, cut] = normed
        pooled = normed.astype(jnp.float32)
        total = total + folded(pooled * pooled)
    inverse = lax.rsqrt(jnp.sum(total, axis=-1, keepdims=True) + unit_eps)
    inv_ref[...] = jnp.broadcast_to(inverse, inv_ref.shape)

    lane = lax.broadcasted_iota(jnp.int32, (pairs, lanes), 1)
    columns = jnp.where(lane == 0, owner_ref[:, :1], jnp.where(lane == 1, owner_ref[:, 1:], 0))
    owners = columns.astype(jnp.float32).T
    high = jnp.floor(owners * (1.0 / 256.0))
    low = owners - 256.0 * high
    row = lax.broadcasted_iota(jnp.int32, (16, lanes), 0)
    spot = lax.broadcasted_iota(jnp.int32, (16, lanes), 1)
    left = jnp.where(row == 0, low[:1], jnp.where(row == 1, high[:1], 0.0))
    right = jnp.where(row == 0, low[1:2], jnp.where(row == 1, high[1:2], 0.0))
    for offset in range(negative_ref.shape[1]):
        named = (negative_ref[0, offset] >= 0).astype(jnp.float32)
        left = jnp.where((row == 2) & (spot == offset), named, left)
    facts = jnp.concatenate([left, right], axis=1).astype(jnp.bfloat16)

    for part, cut in enumerate(cuts):
        emb_ref[part, :seqs] = (normed_ref[:, cut].astype(jnp.float32) * inverse).astype(jnp.bfloat16)
        emb_ref[part, seqs:] = facts


def norm_call(last_row, hidden, gain_row, pair_owner, hard_negatives, parts):
    seqs, width = hidden.shape
    piece = width // parts
    whole = pl.BlockSpec(memory_space=pltpu.VMEM)
    return pl.pallas_call(
        norm_kernel,
        in_specs=[whole, whole, whole, whole, pl.BlockSpec(memory_space=pltpu.SMEM)],
        out_specs=[whole, whole, whole],
        out_shape=[
            jax.ShapeDtypeStruct((seqs, width), jnp.bfloat16),
            jax.ShapeDtypeStruct((seqs, lanes), jnp.float32),
            jax.ShapeDtypeStruct((parts, seqs + 16, piece), jnp.bfloat16),
        ],
        compiler_params=pltpu.CompilerParams(vmem_limit_bytes=vmem_limit),
        name="norm_rows",
    )(last_row, hidden, gain_row, pair_owner, hard_negatives)


def score_kernel(
    blocks, pairs, window, emb_ref, q_ref, d_ref, s_ref, own_ref, listed_ref, wide, picked, own, sem
):
    seqs = emb_ref.shape[1] - 16
    facts = emb_ref[:, seqs:, :].astype(jnp.float32)
    own_ref[...] = (facts[:, 0, :] + 256.0 * facts[:, 1, :]).astype(jnp.int32)
    listed_ref[...] = facts[:, 2, :lanes].astype(jnp.int32)
    fetch = pltpu.make_async_copy(own_ref, own, sem)
    fetch.start()

    def widen(step, carry):
        at = pl.multiple_of(step * seqs, seqs)
        spread(wide, at, emb_ref[step, :seqs, :].astype(jnp.float32))
        return carry

    lax.fori_loop(0, emb_ref.shape[0], widen, 0)
    fetch.wait()
    unroll = 16

    def pick_block(block, carry):
        def pick_rows(step, inner):
            base = pl.multiple_of(step * unroll, unroll)
            rows = [wide[own[block, base + k]] for k in range(unroll)]
            for k in range(unroll):
                picked[base + k] = rows[k]
            return inner

        lax.fori_loop(0, 2 * pairs // unroll, pick_rows, 0)
        at = pl.multiple_of(block * pairs, pairs)
        q_ref[pl.ds(at, pairs), :] = gathered(picked, 0, pairs).astype(jnp.bfloat16)
        d_ref[pl.ds(at, pairs), :] = gathered(picked, pairs, pairs).astype(jnp.bfloat16)
        return carry

    lax.fori_loop(0, blocks, pick_block, 0)
    d_ref[blocks * pairs :, :] = d_ref[: window * pairs, :]
    groups = s_ref.shape[0]
    fine = pairs // groups

    def score_block(block, carry):
        at = pl.multiple_of(block * pairs, pairs)
        tiles = inverse_temp * lax.dot_general(
            q_ref[pl.ds(at, pairs), :],
            d_ref[pl.ds(at, (window + 1) * pairs), :],
            (((1,), (1,)), ((), ())),
            preferred_element_type=jnp.float32,
        )
        for column in range(window + 1):
            row = pl.multiple_of((column * blocks + block) * fine, fine)
            tile = tiles[:, column * pairs : (column + 1) * pairs]
            s_ref[:, pl.ds(row, fine), :] = tile.reshape(groups, fine, pairs)
        return carry

    lax.fori_loop(0, blocks, score_block, 0)


def score_call(embedded, blocks, pairs, window):
    parts, rows, piece = embedded.shape
    fine = pairs // blocks
    tiles = blocks * (window + 1)
    whole = pl.BlockSpec(memory_space=pltpu.VMEM)
    return pl.pallas_call(
        functools.partial(score_kernel, blocks, pairs, window),
        in_specs=[whole],
        out_specs=[whole] * 5,
        out_shape=[
            jax.ShapeDtypeStruct((blocks * pairs, piece), jnp.bfloat16),
            jax.ShapeDtypeStruct(((blocks + window) * pairs, piece), jnp.bfloat16),
            jax.ShapeDtypeStruct((blocks, tiles * fine, pairs), jnp.float32),
            jax.ShapeDtypeStruct((blocks, 2 * pairs), jnp.int32),
            jax.ShapeDtypeStruct((blocks, lanes), jnp.int32),
        ],
        scratch_shapes=[
            pltpu.VMEM((parts * (rows - 16), piece // lanes, lanes), jnp.float32),
            pltpu.VMEM((2 * pairs, piece // lanes, lanes), jnp.float32),
            pltpu.SMEM((blocks, 2 * pairs), jnp.int32),
            pltpu.SemaphoreType.DMA,
        ],
        compiler_params=pltpu.CompilerParams(vmem_limit_bytes=vmem_limit),
        name="partial_scores",
    )(embedded)


def softmax_kernel(blocks, window, listed_ref, s_ref, c_ref):
    fine = s_ref.shape[2]
    pairs = s_ref.shape[3]
    first = lax.axis_index("pb") * fine
    rows = lax.broadcasted_iota(jnp.int32, (fine, pairs), 0) + first
    target = lax.broadcasted_iota(jnp.int32, (fine, pairs), 1) == rows
    lane = lax.broadcasted_iota(jnp.int32, (16, pairs), 1)

    def one_block(block, losses):
        tiles = [s_ref[0, block]]
        for offset in range(window):
            named = listed_ref[block, offset] > 0
            tiles.append(jnp.where(named, s_ref[offset + 1, block], -jnp.inf))
        top = functools.reduce(jnp.maximum, tiles)
        row_max = jnp.max(top, axis=1, keepdims=True)
        total = functools.reduce(jnp.add, [jnp.exp(tile - row_max) for tile in tiles])
        log_total = row_max + jnp.log(jnp.sum(total, axis=1, keepdims=True))
        positive = jnp.sum(jnp.where(target, tiles[0], 0.0), axis=1, keepdims=True)
        loss = jnp.sum(log_total - positive, axis=0, keepdims=True)
        shares = [jnp.exp(tile - log_total) for tile in tiles]
        shares[0] = shares[0] - jnp.where(target, 1.0, 0.0)
        return [inverse_temp * share for share in shares], jnp.where(lane == block, loss, losses)

    def two_blocks(step, losses):
        even, losses = one_block(2 * step, losses)
        odd, losses = one_block(2 * step + 1, losses)
        for column in range(window + 1):
            both = jnp.concatenate([even[column], odd[column]], axis=0)
            c_ref[column * (blocks // 2) + step] = both.astype(jnp.bfloat16)
        return losses

    losses = lax.fori_loop(0, blocks // 2, two_blocks, jnp.zeros((16, pairs), jnp.float32))
    coarse = losses.astype(jnp.bfloat16).astype(jnp.float32)
    rank = lax.broadcasted_iota(jnp.int32, (16, pairs), 0)
    both = jnp.where(rank == 0, coarse, jnp.where(rank == 1, losses - coarse, 0.0))
    c_ref[(window + 1) * (blocks // 2)] = both.astype(jnp.bfloat16)


def softmax_call(listed, scores, blocks, window):
    fine, pairs = scores.shape[2:]
    whole = pl.BlockSpec(memory_space=pltpu.VMEM)
    return pl.pallas_call(
        functools.partial(softmax_kernel, blocks, window),
        in_specs=[pl.BlockSpec(memory_space=pltpu.SMEM), whole],
        out_specs=whole,
        out_shape=jax.ShapeDtypeStruct(
            ((window + 1) * blocks // 2 + 1, 2 * fine, pairs), jnp.bfloat16
        ),
        compiler_params=pltpu.CompilerParams(vmem_limit_bytes=vmem_limit),
        name="softmax_rows",
    )(listed, scores)


def grad_kernel(
    blocks, pairs, window, own_ref, c_ref, q_ref, d_ref, out_ref, loss_ref, wide, dsum, picked
):
    fine = pairs // blocks
    seqs = wide.shape[0]
    unroll = 16
    half_blocks = blocks // 2
    coarse = c_ref[:, (window + 1) * half_blocks].astype(jnp.float32)
    losses = jnp.sum(coarse[:, 0, :] + coarse[:, 1, :], axis=0, keepdims=True) / pairs
    lane = lax.broadcasted_iota(jnp.int32, losses.shape, 1)
    mine = jnp.where(lane == lax.axis_index("pb"), losses, 0.0)
    loss_ref[...] = jnp.broadcast_to(jnp.sum(mine, axis=1, keepdims=True), loss_ref.shape)
    dsum[...] = jnp.zeros_like(dsum)

    def scatter_rows(block, offset):
        def step_rows(step, inner):
            base = pl.multiple_of(step * unroll, unroll)
            rows = [picked[base + k] for k in range(unroll)]
            for k in range(unroll):
                wide[own_ref[block, offset + base + k]] = rows[k]
            return inner

        lax.fori_loop(0, pairs // unroll, step_rows, 0)

    def one_block(block, coefficients):
        at = pl.multiple_of(block * pairs, pairs)
        summed = jnp.dot(
            coefficients,
            d_ref[pl.ds(at, (window + 1) * pairs), :],
            preferred_element_type=jnp.float32,
        )
        spread(picked, 0, summed)
        scatter_rows(block, 0)
        dsum[pl.ds(at, (window + 1) * pairs), :] += lax.dot_general(
            coefficients,
            q_ref[pl.ds(at, pairs), :],
            (((0,), (0,)), ((), ())),
            preferred_element_type=jnp.float32,
        )

    def two_blocks(step, carry):
        pieces = [
            c_ref[:, column * half_blocks + step].astype(jnp.float32)
            for column in range(window + 1)
        ]
        for half in range(2):
            coefficients = jnp.concatenate(
                [
                    piece[:, half * fine : (half + 1) * fine].reshape(pairs, pairs)
                    for piece in pieces
                ],
                axis=1,
            ).astype(jnp.bfloat16)
            one_block(2 * step + half, coefficients)
        return carry

    lax.fori_loop(0, half_blocks, two_blocks, 0)
    dsum[: window * pairs, :] += dsum[blocks * pairs :, :]

    def doc_block(block, carry):
        at = pl.multiple_of(block * pairs, pairs)
        spread(picked, 0, dsum[pl.ds(at, pairs), :])
        scatter_rows(block, pairs)
        return carry

    lax.fori_loop(0, blocks, doc_block, 0)
    slots = out_ref.shape[1]

    def narrow(part, carry):
        at = pl.multiple_of(part * slots, slots)
        out_ref[part] = gathered(wide, at, slots).astype(jnp.bfloat16)
        return carry

    lax.fori_loop(0, seqs // slots, narrow, 0)


def grad_call(own, coefficients, queries, documents, blocks, pairs, window):
    count, piece = queries.shape
    seqs = 2 * count
    whole = pl.BlockSpec(memory_space=pltpu.VMEM)
    return pl.pallas_call(
        functools.partial(grad_kernel, blocks, pairs, window),
        in_specs=[pl.BlockSpec(memory_space=pltpu.SMEM), whole, whole, whole],
        out_specs=[whole, whole],
        out_shape=[
            jax.ShapeDtypeStruct((blocks, seqs // blocks, piece), jnp.bfloat16),
            jax.ShapeDtypeStruct((1, lanes), jnp.float32),
        ],
        scratch_shapes=[
            pltpu.VMEM((seqs, piece // lanes, lanes), jnp.float32),
            pltpu.VMEM(((blocks + window) * pairs, piece), jnp.float32),
            pltpu.VMEM((pairs, piece // lanes, lanes), jnp.float32),
        ],
        compiler_params=pltpu.CompilerParams(vmem_limit_bytes=vmem_limit),
        name="slice_grads",
    )(own, coefficients, queries, documents)


def project_kernel(grad_ref, normed_ref, inv_ref, out_ref):
    parts, _, piece = grad_ref.shape
    inverse = inv_ref[:, :1]
    total = 0.0
    for part in range(parts):
        cut = slice(part * piece, (part + 1) * piece)
        unit = normed_ref[:, cut].astype(jnp.float32) * inverse
        total = total + unit * grad_ref[part].astype(jnp.float32)
    along = jnp.sum(total, axis=-1, keepdims=True)
    for part in range(parts):
        cut = slice(part * piece, (part + 1) * piece)
        unit = normed_ref[:, cut].astype(jnp.float32) * inverse
        out_ref[:, cut] = grad_ref[part].astype(jnp.float32) - unit * along


def project_call(returned, normed, inverse):
    parts, seqs, piece = returned.shape
    width = normed.shape[1]
    rows = 32
    return pl.pallas_call(
        project_kernel,
        grid=(seqs // rows,),
        in_specs=[
            pl.BlockSpec((parts, rows, piece), lambda i: (0, i, 0)),
            pl.BlockSpec((rows, width), lambda i: (i, 0)),
            pl.BlockSpec((rows, lanes), lambda i: (i, 0)),
        ],
        out_specs=pl.BlockSpec((rows, width), lambda i: (i, 0)),
        out_shape=jax.ShapeDtypeStruct((seqs, width), jnp.float32),
        compiler_params=pltpu.CompilerParams(vmem_limit_bytes=vmem_limit),
        name="project_out",
    )(returned, normed, inverse)


def feature_plan(hidden, final_gain, last_row, pair_owner, hard_negatives):
    devices = lax.axis_size("pb")
    width = hidden.shape[1]
    pairs = pair_owner.shape[0]
    window = hard_negatives.shape[1]
    fine = pairs // devices
    normed, inverse, embedding = norm_call(
        last_row, hidden, final_gain.reshape(1, width), pair_owner, hard_negatives, devices
    )
    embedded = lax.all_to_all(embedding, "pb", split_axis=0, concat_axis=0, tiled=True)
    queries, documents, partial_scores, own, listed = score_call(embedded, devices, pairs, window)
    scores = lax.psum_scatter(partial_scores, "pb", scatter_dimension=0, tiled=False)
    coefficients = softmax_call(
        listed, scores.reshape(window + 1, devices, fine, pairs), devices, window
    )
    shared = lax.all_gather(coefficients, "pb", axis=0, tiled=False)
    grads, loss = grad_call(own, shared, queries, documents, devices, pairs, window)
    returned = lax.all_to_all(grads, "pb", split_axis=0, concat_axis=0, tiled=True)
    return project_call(returned, normed, inverse), loss[0, :1]


def from_behind(value, axis, steps):
    count = lax.axis_size(axis)
    pairs = [(source, (source + steps) % count) for source in range(count)]
    return lax.ppermute(value, axis, pairs)


def similarity(queries, documents):
    return inverse_temp * lax.dot_general(
        queries, documents, (((1,), (1,)), ((), ())), preferred_element_type=jnp.float32
    )


def transposed(weights, queries):
    return lax.dot_general(
        weights, queries, (((0,), (0,)), ((), ())), preferred_element_type=jnp.float32
    )


def combine_docs(weights, documents):
    return jnp.dot(weights, documents, preferred_element_type=jnp.float32)


def skipped(listed, function, operands, out_shape):
    return lax.cond(
        listed,
        lambda inputs: function(*inputs),
        lambda inputs: jnp.zeros(out_shape, jnp.float32),
        operands,
    )


def row_plan(hidden, final_gain, last_row, pair_owner, hard_negatives):
    values = hidden.astype(jnp.float32)
    scale_row = lax.rsqrt(jnp.mean(values * values, axis=-1, keepdims=True) + token_eps)
    normed = (values * scale_row * final_gain.astype(jnp.float32)).astype(jnp.bfloat16)
    seq_count = last_row.shape[1]
    model_width = hidden.shape[1]
    pooled = normed[last_row[0]].astype(jnp.float32)
    inverse_norm = lax.rsqrt(jnp.sum(pooled * pooled, axis=-1, keepdims=True) + 1e-06)
    unit_vec = pooled * inverse_norm
    embedding = unit_vec.astype(jnp.bfloat16)
    devices = lax.axis_size("pb")
    capacity = 2 * seq_count // devices
    pair_count = pair_owner.shape[0]
    wanted = jnp.concatenate([pair_owner[:, 0], pair_owner[:, 1]])
    holder = wanted // seq_count
    within = wanted % seq_count
    entry_ids = jnp.arange(2 * pair_count, dtype=jnp.int32)
    earlier = (holder[None, :] == holder[:, None]) & (entry_ids[None, :] < entry_ids[:, None])
    position = jnp.sum(earlier.astype(jnp.int32), axis=1)
    request = jnp.full((devices, capacity), -1, jnp.int32).at[holder, position].set(within)
    served = lax.all_to_all(request, "pb", split_axis=0, concat_axis=0, tiled=True)
    outgoing = jnp.where(
        served[:, :, None] >= 0, embedding[jnp.maximum(served, 0)], jnp.zeros((), jnp.bfloat16)
    )
    received = lax.all_to_all(outgoing, "pb", split_axis=0, concat_axis=0, tiled=True)
    gathered = received[holder, position]
    queries = gathered[:pair_count]
    own_docs = gathered[pair_count:]
    listed_ids = hard_negatives[0]
    window = hard_negatives.shape[1]
    listed = [listed_ids[offset] >= 0 for offset in range(window)]
    neighbours = []
    moving = own_docs
    for offset in range(window):
        moving = from_behind(moving, "pb", -1)
        neighbours.append(moving)
    tile_shape = (pair_count, pair_count)
    score_blocks = [similarity(queries, own_docs)]
    for offset in range(window):
        score_blocks.append(
            skipped(listed[offset], similarity, (queries, neighbours[offset]), tile_shape)
        )
    all_scores = jnp.concatenate(score_blocks, axis=1)
    usable = jnp.concatenate(
        [jnp.ones((pair_count,), jnp.bool_)]
        + [jnp.broadcast_to(listed[offset], (pair_count,)) for offset in range(window)]
    )
    masked = jnp.where(usable[None, :], all_scores, -jnp.inf)
    row_max = jnp.max(masked, axis=1, keepdims=True)
    log_total = row_max + jnp.log(jnp.sum(jnp.exp(masked - row_max), axis=1, keepdims=True))
    diagonal = jnp.arange(pair_count, dtype=jnp.int32)
    positive = all_scores[diagonal, diagonal]
    block_loss = jnp.mean(log_total[:, 0] - positive).reshape(1)
    columns = jnp.arange((window + 1) * pair_count, dtype=jnp.int32)
    target = (columns[None, :] == diagonal[:, None]).astype(jnp.float32)
    coefficients = (inverse_temp * (jnp.exp(masked - log_total) - target)).astype(jnp.bfloat16)
    pieces = [
        coefficients[:, offset * pair_count : (offset + 1) * pair_count]
        for offset in range(window + 1)
    ]
    grad_shape = (pair_count, model_width)
    query_sum = combine_docs(pieces[0], own_docs)
    for offset in range(window):
        query_sum = query_sum + skipped(
            listed[offset], combine_docs, (pieces[offset + 1], neighbours[offset]), grad_shape
        )
    query_grad = query_sum.astype(jnp.bfloat16)
    own_part = transposed(pieces[0], queries).astype(jnp.bfloat16)
    partial_value = [
        skipped(listed[offset], transposed, (pieces[offset + 1], queries), grad_shape).astype(
            jnp.bfloat16
        )
        for offset in range(window)
    ]
    running = partial_value[window - 1].astype(jnp.float32)
    for offset in range(window):
        running = from_behind(running, "pb", 1)
        if offset + 1 < window:
            running = running + partial_value[window - 2 - offset].astype(jnp.float32)
    doc_grad = (own_part.astype(jnp.float32) + running).astype(jnp.bfloat16)
    answers = jnp.concatenate([query_grad, doc_grad], axis=0)
    returning = (
        jnp.zeros((devices, capacity, model_width), jnp.bfloat16).at[holder, position].set(answers)
    )
    returned = lax.all_to_all(returning, "pb", split_axis=0, concat_axis=0, tiled=True)
    slot_ids = jnp.where(served >= 0, served, seq_count).reshape(-1)
    emb_grad = (
        jnp.zeros((seq_count, model_width), jnp.bfloat16)
        .at[slot_ids]
        .set(returned.reshape(-1, model_width), mode="drop")
    )
    gradient = emb_grad.astype(jnp.float32)
    pooled_grad = gradient - unit_vec * jnp.sum(unit_vec * gradient, axis=-1, keepdims=True)
    return (pooled_grad, block_loss)


def solution(mesh):
    def local(hidden, final_gain, last_row, pair_owner, hard_negatives):
        plan = feature_plan if hidden.shape[1] >= lanes * mesh.shape["pb"] else row_plan
        return plan(hidden, final_gain, last_row, pair_owner, hard_negatives)

    return jax.shard_map(
        local,
        mesh=mesh,
        in_specs=(
            P(("groups", "pb"), None),
            P(),
            P(("groups", "pb"), None),
            P(("groups", "pb"), None),
            P(("groups", "pb"), None),
        ),
        out_specs=(P(("groups", "pb"), None), P(("groups", "pb"))),
        check_vma=False,
    )
```

```python
import functools

import jax
import jax.numpy as jnp
from jax import lax
from jax.experimental import pallas as pl
from jax.experimental.pallas import tpu as pltpu
from jax.sharding import PartitionSpec as P

inverse_temp = 50.0
token_eps = 1e-05
unit_eps = 1e-06
lanes = 128
vmem_limit = 56 * 1024 * 1024


def spread(target, at, value):
    count, width = value.shape
    for part in range(width // lanes):
        target[pl.ds(at, count), part, :] = value[:, part * lanes : (part + 1) * lanes]


def gathered(source, at, count):
    parts = [source[pl.ds(at, count), part, :] for part in range(source.shape[1])]
    return jnp.concatenate(parts, axis=1)


def norm_kernel(last_ref, hidden_ref, gain_ref, owner_ref, negative_ref, normed_ref, inv_ref, emb_ref):
    seqs, width = normed_ref.shape
    parts, _, piece = emb_ref.shape
    pairs = owner_ref.shape[0]
    cuts = [slice(part * piece, (part + 1) * piece) for part in range(parts)]
    sources = lax.broadcasted_iota(jnp.int32, (seqs, seqs), 0)
    pick = jnp.where(sources == last_ref[...], 1.0, 0.0).astype(jnp.bfloat16)

    def folded(squares):
        return functools.reduce(
            jnp.add, [squares[:, at : at + lanes] for at in range(0, piece, lanes)]
        )

    total = jnp.zeros((seqs, lanes), jnp.float32)
    for cut in cuts:
        values = lax.dot_general(
            pick, hidden_ref[:, cut], (((0,), (0,)), ((), ())), preferred_element_type=jnp.float32
        )
        normed_ref[:, cut] = values.astype(jnp.bfloat16)
        total = total + folded(values * values)
    scale = lax.rsqrt(jnp.sum(total, axis=-1, keepdims=True) / width + token_eps)
    total = jnp.zeros((seqs, lanes), jnp.float32)
    for cut in cuts:
        values = normed_ref[:, cut].astype(jnp.float32)
        normed = (values * scale * gain_ref[:, cut].astype(jnp.float32)).astype(jnp.bfloat16)
        normed_ref[:, cut] = normed
        pooled = normed.astype(jnp.float32)
        total = total + folded(pooled * pooled)
    inverse = lax.rsqrt(jnp.sum(total, axis=-1, keepdims=True) + unit_eps)
    inv_ref[...] = jnp.broadcast_to(inverse, inv_ref.shape)

    lane = lax.broadcasted_iota(jnp.int32, (pairs, lanes), 1)
    columns = jnp.where(lane == 0, owner_ref[:, :1], jnp.where(lane == 1, owner_ref[:, 1:], 0))
    owners = columns.astype(jnp.float32).T
    high = jnp.floor(owners * (1.0 / 256.0))
    low = owners - 256.0 * high
    row = lax.broadcasted_iota(jnp.int32, (16, lanes), 0)
    spot = lax.broadcasted_iota(jnp.int32, (16, lanes), 1)
    left = jnp.where(row == 0, low[:1], jnp.where(row == 1, high[:1], 0.0))
    right = jnp.where(row == 0, low[1:2], jnp.where(row == 1, high[1:2], 0.0))
    for offset in range(negative_ref.shape[1]):
        named = (negative_ref[0, offset] >= 0).astype(jnp.float32)
        left = jnp.where((row == 2) & (spot == offset), named, left)
    facts = jnp.concatenate([left, right], axis=1).astype(jnp.bfloat16)

    for part, cut in enumerate(cuts):
        emb_ref[part, :seqs] = (normed_ref[:, cut].astype(jnp.float32) * inverse).astype(jnp.bfloat16)
        emb_ref[part, seqs:] = facts


def norm_call(last_row, hidden, gain_row, pair_owner, hard_negatives, parts):
    seqs, width = hidden.shape
    piece = width // parts
    whole = pl.BlockSpec(memory_space=pltpu.VMEM)
    return pl.pallas_call(
        norm_kernel,
        in_specs=[whole, whole, whole, whole, pl.BlockSpec(memory_space=pltpu.SMEM)],
        out_specs=[whole, whole, whole],
        out_shape=[
            jax.ShapeDtypeStruct((seqs, width), jnp.bfloat16),
            jax.ShapeDtypeStruct((seqs, lanes), jnp.float32),
            jax.ShapeDtypeStruct((parts, seqs + 16, piece), jnp.bfloat16),
        ],
        compiler_params=pltpu.CompilerParams(vmem_limit_bytes=vmem_limit),
        name="norm_rows",
    )(last_row, hidden, gain_row, pair_owner, hard_negatives)


def score_kernel(
    blocks,
    pairs,
    window,
    emb_ref,
    q_ref,
    d_ref,
    s_ref,
    own_ref,
    place_ref,
    wide,
    picked,
    tiles,
    facts,
    own,
    named,
    sems,
):
    seqs = emb_ref.shape[1] - 16
    sent = emb_ref[:, seqs:, :].astype(jnp.float32)
    own_ref[...] = (sent[:, 0, :] + 256.0 * sent[:, 1, :]).astype(jnp.int32)
    facts[...] = sent[:, 2, :lanes].astype(jnp.int32)
    fetches = [
        pltpu.make_async_copy(own_ref, own, sems.at[0]),
        pltpu.make_async_copy(facts, named, sems.at[1]),
    ]
    for fetch in fetches:
        fetch.start()

    def widen(step, carry):
        at = pl.multiple_of(step * seqs, seqs)
        spread(wide, at, emb_ref[step, :seqs, :].astype(jnp.float32))
        return carry

    lax.fori_loop(0, emb_ref.shape[0], widen, 0)
    for fetch in fetches:
        fetch.wait()

    def place(block, count):
        place_ref[0, block] = block
        for offset in range(window):
            present = named[block, offset] > 0
            place_ref[offset + 1, block] = jnp.where(present, count, -1)
            count = count + present.astype(jnp.int32)
        return count

    lax.fori_loop(0, blocks, place, blocks)
    unroll = 16

    def pick_block(block, carry):
        def pick_rows(step, inner):
            base = pl.multiple_of(step * unroll, unroll)
            rows = [wide[own[block, base + k]] for k in range(unroll)]
            for k in range(unroll):
                picked[base + k] = rows[k]
            return inner

        lax.fori_loop(0, 2 * pairs // unroll, pick_rows, 0)
        at = pl.multiple_of(block * pairs, pairs)
        q_ref[pl.ds(at, pairs), :] = gathered(picked, 0, pairs).astype(jnp.bfloat16)
        d_ref[pl.ds(at, pairs), :] = gathered(picked, pairs, pairs).astype(jnp.bfloat16)
        return carry

    lax.fori_loop(0, blocks, pick_block, 0)
    d_ref[blocks * pairs :, :] = d_ref[: window * pairs, :]
    groups = s_ref.shape[0]
    fine = pairs // groups

    def score_blocks(step, carry):
        at = pl.multiple_of(step * 2 * pairs, 2 * pairs)
        tiles[...] = inverse_temp * lax.dot_general(
            q_ref[pl.ds(at, 2 * pairs), :],
            d_ref[pl.ds(at, (window + 2) * pairs), :],
            (((1,), (1,)), ((), ())),
            preferred_element_type=jnp.float32,
        )
        for half in range(2):
            for column in range(window + 1):
                spot = place_ref[column, 2 * step + half]

                @pl.when(spot >= 0)
                def _():
                    row = pl.multiple_of(spot * fine, fine)
                    tile = tiles[
                        half * pairs : (half + 1) * pairs,
                        (half + column) * pairs : (half + column + 1) * pairs,
                    ]
                    s_ref[:, pl.ds(row, fine), :] = tile.reshape(groups, fine, pairs)

        return carry

    lax.fori_loop(0, blocks // 2, score_blocks, 0)


def score_call(embedded, room, blocks, pairs, window):
    parts, rows, piece = embedded.shape
    fine = pairs // blocks
    whole = pl.BlockSpec(memory_space=pltpu.VMEM)
    scalars = pl.BlockSpec(memory_space=pltpu.SMEM)
    return pl.pallas_call(
        functools.partial(score_kernel, blocks, pairs, window),
        in_specs=[whole],
        out_specs=[whole, whole, whole, whole, scalars],
        out_shape=[
            jax.ShapeDtypeStruct((blocks * pairs, piece), jnp.bfloat16),
            jax.ShapeDtypeStruct(((blocks + window) * pairs, piece), jnp.bfloat16),
            jax.ShapeDtypeStruct((blocks, room * fine, pairs), jnp.float32),
            jax.ShapeDtypeStruct((blocks, 2 * pairs), jnp.int32),
            jax.ShapeDtypeStruct((window + 1, blocks), jnp.int32),
        ],
        scratch_shapes=[
            pltpu.VMEM((parts * (rows - 16), piece // lanes, lanes), jnp.float32),
            pltpu.VMEM((2 * pairs, piece // lanes, lanes), jnp.float32),
            pltpu.VMEM((2 * pairs, (window + 2) * pairs), jnp.float32),
            pltpu.VMEM((blocks, lanes), jnp.int32),
            pltpu.SMEM((blocks, 2 * pairs), jnp.int32),
            pltpu.SMEM((blocks, lanes), jnp.int32),
            pltpu.SemaphoreType.DMA((2,)),
        ],
        compiler_params=pltpu.CompilerParams(vmem_limit_bytes=vmem_limit),
        name="partial_scores",
    )(embedded)


def softmax_kernel(blocks, window, place_ref, s_ref, c_ref, packed, masked):
    fine, pairs = s_ref.shape[1:]
    count = blocks * fine
    for block in range(blocks):
        for column in range(window + 1):
            spot = place_ref[column, block]
            tile = s_ref[jnp.maximum(spot, 0)]
            masked[block * fine : (block + 1) * fine, column * pairs : (column + 1) * pairs] = (
                jnp.where(spot >= 0, tile, -jnp.inf)
            )
    row = lax.broadcasted_iota(jnp.int32, (count, pairs), 0)
    lane = lax.broadcasted_iota(jnp.int32, (count, pairs), 1)
    target = lane == lax.axis_index("pb") * fine + row % fine
    pieces = [masked[:, column * pairs : (column + 1) * pairs] for column in range(window + 1)]
    row_max = jnp.max(functools.reduce(jnp.maximum, pieces), axis=1, keepdims=True)
    total = functools.reduce(jnp.add, [jnp.exp(piece - row_max) for piece in pieces])
    log_total = row_max + jnp.log(jnp.sum(total, axis=1, keepdims=True))
    positive = jnp.sum(jnp.where(target, pieces[0], 0.0), axis=1, keepdims=True)
    for column, piece in enumerate(pieces):
        share = jnp.exp(piece - log_total)
        if column == 0:
            share = share - jnp.where(target, 1.0, 0.0)
        masked[:, column * pairs : (column + 1) * pairs] = inverse_temp * share
    for block in range(blocks):
        for column in range(window + 1):
            spot = place_ref[column, block]

            @pl.when(spot >= 0)
            def _():
                packed[spot] = masked[
                    block * fine : (block + 1) * fine, column * pairs : (column + 1) * pairs
                ]

    room = packed.shape[0]
    for step in range(room // 2):
        both = jnp.concatenate([packed[2 * step], packed[2 * step + 1]], axis=0)
        c_ref[step] = both.astype(jnp.bfloat16)
    losses = jnp.sum(
        jnp.where(lane == row // fine, log_total - positive, 0.0), axis=0, keepdims=True
    )
    coarse = losses.astype(jnp.bfloat16).astype(jnp.float32)
    rank = lax.broadcasted_iota(jnp.int32, (2 * fine, pairs), 0)
    both = jnp.where(rank == 0, coarse, jnp.where(rank == 1, losses - coarse, 0.0))
    c_ref[room // 2] = both.astype(jnp.bfloat16)


def softmax_call(place, scores, blocks, window):
    room, fine, pairs = scores.shape
    whole = pl.BlockSpec(memory_space=pltpu.VMEM)
    return pl.pallas_call(
        functools.partial(softmax_kernel, blocks, window),
        in_specs=[pl.BlockSpec(memory_space=pltpu.SMEM), whole],
        out_specs=whole,
        out_shape=jax.ShapeDtypeStruct((room // 2 + 1, 2 * fine, pairs), jnp.bfloat16),
        scratch_shapes=[
            pltpu.VMEM((room, fine, pairs), jnp.float32),
            pltpu.VMEM((blocks * fine, (window + 1) * pairs), jnp.float32),
        ],
        compiler_params=pltpu.CompilerParams(vmem_limit_bytes=vmem_limit),
        name="softmax_rows",
    )(place, scores)


def grad_kernel(
    blocks,
    pairs,
    window,
    own_ref,
    place_ref,
    c_ref,
    q_ref,
    d_ref,
    out_ref,
    loss_ref,
    wide,
    dsum,
    picked,
    packed,
    square,
):
    fine = pairs // blocks
    seqs = wide.shape[0]
    room = packed.shape[1]
    unroll = 16
    sent = c_ref[:, room // 2].astype(jnp.float32)
    losses = jnp.sum(sent[:, 0, :] + sent[:, 1, :], axis=0, keepdims=True) / pairs
    lane = lax.broadcasted_iota(jnp.int32, losses.shape, 1)
    mine = jnp.where(lane == lax.axis_index("pb"), losses, 0.0)
    loss_ref[...] = jnp.broadcast_to(jnp.sum(mine, axis=1, keepdims=True), loss_ref.shape)
    dsum[...] = jnp.zeros_like(dsum)
    square[...] = jnp.zeros_like(square)

    def unpack(step, carry):
        both = c_ref[:, step].astype(jnp.float32)
        packed[:, 2 * step] = both[:, :fine]
        packed[:, 2 * step + 1] = both[:, fine:]
        return carry

    lax.fori_loop(0, room // 2, unpack, 0)

    def scatter_rows(block, offset, start):
        def step_rows(step, inner):
            base = pl.multiple_of(step * unroll, unroll)
            rows = [picked[start + base + k] for k in range(unroll)]
            for k in range(unroll):
                wide[own_ref[block, offset + base + k]] = rows[k]
            return inner

        lax.fori_loop(0, pairs // unroll, step_rows, 0)

    def two_blocks(step, carry):
        for half in range(2):
            for column in range(window + 1):
                spot = place_ref[column, 2 * step + half]
                tile = packed[:, jnp.maximum(spot, 0)].reshape(pairs, pairs)
                square[
                    half * pairs : (half + 1) * pairs,
                    (half + column) * pairs : (half + column + 1) * pairs,
                ] = jnp.where(spot >= 0, tile, 0.0).astype(jnp.bfloat16)
        at = pl.multiple_of(step * 2 * pairs, 2 * pairs)
        there = pl.ds(at, (window + 2) * pairs)
        coefficients = square[...]
        summed = jnp.dot(coefficients, d_ref[there, :], preferred_element_type=jnp.float32)
        spread(picked, 0, summed)
        dsum[there, :] += lax.dot_general(
            coefficients,
            q_ref[pl.ds(at, 2 * pairs), :],
            (((0,), (0,)), ((), ())),
            preferred_element_type=jnp.float32,
        )
        for half in range(2):
            scatter_rows(2 * step + half, 0, half * pairs)
        return carry

    lax.fori_loop(0, blocks // 2, two_blocks, 0)
    dsum[: window * pairs, :] += dsum[blocks * pairs :, :]

    def doc_block(block, carry):
        at = pl.multiple_of(block * pairs, pairs)
        spread(picked, 0, dsum[pl.ds(at, pairs), :])
        scatter_rows(block, pairs, 0)
        return carry

    lax.fori_loop(0, blocks, doc_block, 0)
    slots = out_ref.shape[1]

    def narrow(part, carry):
        at = pl.multiple_of(part * slots, slots)
        out_ref[part] = gathered(wide, at, slots).astype(jnp.bfloat16)
        return carry

    lax.fori_loop(0, seqs // slots, narrow, 0)


def grad_call(own, place, coefficients, queries, documents, blocks, pairs, window):
    count, piece = queries.shape
    seqs = 2 * count
    room = 2 * (coefficients.shape[1] - 1)
    whole = pl.BlockSpec(memory_space=pltpu.VMEM)
    scalars = pl.BlockSpec(memory_space=pltpu.SMEM)
    return pl.pallas_call(
        functools.partial(grad_kernel, blocks, pairs, window),
        in_specs=[scalars, scalars, whole, whole, whole],
        out_specs=[whole, whole],
        out_shape=[
            jax.ShapeDtypeStruct((blocks, seqs // blocks, piece), jnp.bfloat16),
            jax.ShapeDtypeStruct((1, lanes), jnp.float32),
        ],
        scratch_shapes=[
            pltpu.VMEM((seqs, piece // lanes, lanes), jnp.float32),
            pltpu.VMEM(((blocks + window) * pairs, piece), jnp.float32),
            pltpu.VMEM((2 * pairs, piece // lanes, lanes), jnp.float32),
            pltpu.VMEM((blocks, room, pairs // blocks, pairs), jnp.float32),
            pltpu.VMEM((2 * pairs, (window + 2) * pairs), jnp.bfloat16),
        ],
        compiler_params=pltpu.CompilerParams(vmem_limit_bytes=vmem_limit),
        name="slice_grads",
    )(own, place, coefficients, queries, documents)


def project_kernel(grad_ref, normed_ref, inv_ref, out_ref):
    parts, _, piece = grad_ref.shape
    inverse = inv_ref[:, :1]
    total = 0.0
    for part in range(parts):
        cut = slice(part * piece, (part + 1) * piece)
        unit = normed_ref[:, cut].astype(jnp.float32) * inverse
        total = total + unit * grad_ref[part].astype(jnp.float32)
    along = jnp.sum(total, axis=-1, keepdims=True)
    for part in range(parts):
        cut = slice(part * piece, (part + 1) * piece)
        unit = normed_ref[:, cut].astype(jnp.float32) * inverse
        out_ref[:, cut] = grad_ref[part].astype(jnp.float32) - unit * along


def project_call(returned, normed, inverse):
    parts, seqs, piece = returned.shape
    width = normed.shape[1]
    rows = 32
    return pl.pallas_call(
        project_kernel,
        grid=(seqs // rows,),
        in_specs=[
            pl.BlockSpec((parts, rows, piece), lambda i: (0, i, 0)),
            pl.BlockSpec((rows, width), lambda i: (i, 0)),
            pl.BlockSpec((rows, lanes), lambda i: (i, 0)),
        ],
        out_specs=pl.BlockSpec((rows, width), lambda i: (i, 0)),
        out_shape=jax.ShapeDtypeStruct((seqs, width), jnp.float32),
        compiler_params=pltpu.CompilerParams(vmem_limit_bytes=vmem_limit),
        name="project_out",
    )(returned, normed, inverse)


def middle(embedded, room, devices, pairs, window):
    fine = pairs // devices
    queries, documents, partial_scores, own, place = score_call(
        embedded, room, devices, pairs, window
    )
    scores = lax.psum_scatter(partial_scores, "pb", scatter_dimension=0, tiled=False)
    coefficients = softmax_call(place, scores.reshape(room, fine, pairs), devices, window)
    shared = lax.all_gather(coefficients, "pb", axis=0, tiled=False)
    grads, loss = grad_call(own, place, shared, queries, documents, devices, pairs, window)
    return grads, loss[0, :1]


def feature_plan(hidden, final_gain, last_row, pair_owner, hard_negatives):
    devices = lax.axis_size("pb")
    seqs, width = hidden.shape
    pairs = pair_owner.shape[0]
    window = hard_negatives.shape[1]
    normed, inverse, embedding = norm_call(
        last_row, hidden, final_gain.reshape(1, width), pair_owner, hard_negatives, devices
    )
    embedded = lax.all_to_all(embedding, "pb", split_axis=0, concat_axis=0, tiled=True)
    most = devices * (window + 1)
    rooms = [most * part // 20 for part in (10, 11, 12, 13, 14, 16, 20)]
    used = devices + jnp.sum(embedded[:, seqs + 2, :window].astype(jnp.float32))
    level = sum((used > room).astype(jnp.int32) for room in rooms[:-1])
    grads, loss = lax.switch(
        level,
        [
            functools.partial(middle, room=room, devices=devices, pairs=pairs, window=window)
            for room in rooms
        ],
        embedded,
    )
    returned = lax.all_to_all(grads, "pb", split_axis=0, concat_axis=0, tiled=True)
    return project_call(returned, normed, inverse), loss


def from_behind(value, axis, steps):
    count = lax.axis_size(axis)
    pairs = [(source, (source + steps) % count) for source in range(count)]
    return lax.ppermute(value, axis, pairs)


def similarity(queries, documents):
    return inverse_temp * lax.dot_general(
        queries, documents, (((1,), (1,)), ((), ())), preferred_element_type=jnp.float32
    )


def transposed(weights, queries):
    return lax.dot_general(
        weights, queries, (((0,), (0,)), ((), ())), preferred_element_type=jnp.float32
    )


def combine_docs(weights, documents):
    return jnp.dot(weights, documents, preferred_element_type=jnp.float32)


def skipped(listed, function, operands, out_shape):
    return lax.cond(
        listed,
        lambda inputs: function(*inputs),
        lambda inputs: jnp.zeros(out_shape, jnp.float32),
        operands,
    )


def row_plan(hidden, final_gain, last_row, pair_owner, hard_negatives):
    values = hidden.astype(jnp.float32)
    scale_row = lax.rsqrt(jnp.mean(values * values, axis=-1, keepdims=True) + token_eps)
    normed = (values * scale_row * final_gain.astype(jnp.float32)).astype(jnp.bfloat16)
    seq_count = last_row.shape[1]
    model_width = hidden.shape[1]
    pooled = normed[last_row[0]].astype(jnp.float32)
    inverse_norm = lax.rsqrt(jnp.sum(pooled * pooled, axis=-1, keepdims=True) + 1e-06)
    unit_vec = pooled * inverse_norm
    embedding = unit_vec.astype(jnp.bfloat16)
    devices = lax.axis_size("pb")
    capacity = 2 * seq_count // devices
    pair_count = pair_owner.shape[0]
    wanted = jnp.concatenate([pair_owner[:, 0], pair_owner[:, 1]])
    holder = wanted // seq_count
    within = wanted % seq_count
    entry_ids = jnp.arange(2 * pair_count, dtype=jnp.int32)
    earlier = (holder[None, :] == holder[:, None]) & (entry_ids[None, :] < entry_ids[:, None])
    position = jnp.sum(earlier.astype(jnp.int32), axis=1)
    request = jnp.full((devices, capacity), -1, jnp.int32).at[holder, position].set(within)
    served = lax.all_to_all(request, "pb", split_axis=0, concat_axis=0, tiled=True)
    outgoing = jnp.where(
        served[:, :, None] >= 0, embedding[jnp.maximum(served, 0)], jnp.zeros((), jnp.bfloat16)
    )
    received = lax.all_to_all(outgoing, "pb", split_axis=0, concat_axis=0, tiled=True)
    gathered = received[holder, position]
    queries = gathered[:pair_count]
    own_docs = gathered[pair_count:]
    listed_ids = hard_negatives[0]
    window = hard_negatives.shape[1]
    listed = [listed_ids[offset] >= 0 for offset in range(window)]
    neighbours = []
    moving = own_docs
    for offset in range(window):
        moving = from_behind(moving, "pb", -1)
        neighbours.append(moving)
    tile_shape = (pair_count, pair_count)
    score_blocks = [similarity(queries, own_docs)]
    for offset in range(window):
        score_blocks.append(
            skipped(listed[offset], similarity, (queries, neighbours[offset]), tile_shape)
        )
    all_scores = jnp.concatenate(score_blocks, axis=1)
    usable = jnp.concatenate(
        [jnp.ones((pair_count,), jnp.bool_)]
        + [jnp.broadcast_to(listed[offset], (pair_count,)) for offset in range(window)]
    )
    masked = jnp.where(usable[None, :], all_scores, -jnp.inf)
    row_max = jnp.max(masked, axis=1, keepdims=True)
    log_total = row_max + jnp.log(jnp.sum(jnp.exp(masked - row_max), axis=1, keepdims=True))
    diagonal = jnp.arange(pair_count, dtype=jnp.int32)
    positive = all_scores[diagonal, diagonal]
    block_loss = jnp.mean(log_total[:, 0] - positive).reshape(1)
    columns = jnp.arange((window + 1) * pair_count, dtype=jnp.int32)
    target = (columns[None, :] == diagonal[:, None]).astype(jnp.float32)
    coefficients = (inverse_temp * (jnp.exp(masked - log_total) - target)).astype(jnp.bfloat16)
    pieces = [
        coefficients[:, offset * pair_count : (offset + 1) * pair_count]
        for offset in range(window + 1)
    ]
    grad_shape = (pair_count, model_width)
    query_sum = combine_docs(pieces[0], own_docs)
    for offset in range(window):
        query_sum = query_sum + skipped(
            listed[offset], combine_docs, (pieces[offset + 1], neighbours[offset]), grad_shape
        )
    query_grad = query_sum.astype(jnp.bfloat16)
    own_part = transposed(pieces[0], queries).astype(jnp.bfloat16)
    partial_value = [
        skipped(listed[offset], transposed, (pieces[offset + 1], queries), grad_shape).astype(
            jnp.bfloat16
        )
        for offset in range(window)
    ]
    running = partial_value[window - 1].astype(jnp.float32)
    for offset in range(window):
        running = from_behind(running, "pb", 1)
        if offset + 1 < window:
            running = running + partial_value[window - 2 - offset].astype(jnp.float32)
    doc_grad = (own_part.astype(jnp.float32) + running).astype(jnp.bfloat16)
    answers = jnp.concatenate([query_grad, doc_grad], axis=0)
    returning = (
        jnp.zeros((devices, capacity, model_width), jnp.bfloat16).at[holder, position].set(answers)
    )
    returned = lax.all_to_all(returning, "pb", split_axis=0, concat_axis=0, tiled=True)
    slot_ids = jnp.where(served >= 0, served, seq_count).reshape(-1)
    emb_grad = (
        jnp.zeros((seq_count, model_width), jnp.bfloat16)
        .at[slot_ids]
        .set(returned.reshape(-1, model_width), mode="drop")
    )
    gradient = emb_grad.astype(jnp.float32)
    pooled_grad = gradient - unit_vec * jnp.sum(unit_vec * gradient, axis=-1, keepdims=True)
    return (pooled_grad, block_loss)


def solution(mesh):
    def local(hidden, final_gain, last_row, pair_owner, hard_negatives):
        plan = feature_plan if hidden.shape[1] >= lanes * mesh.shape["pb"] else row_plan
        return plan(hidden, final_gain, last_row, pair_owner, hard_negatives)

    return jax.shard_map(
        local,
        mesh=mesh,
        in_specs=(
            P(("groups", "pb"), None),
            P(),
            P(("groups", "pb"), None),
            P(("groups", "pb"), None),
            P(("groups", "pb"), None),
        ),
        out_specs=(P(("groups", "pb"), None), P(("groups", "pb"))),
        check_vma=False,
    )
```

```python
import functools

import jax
import jax.numpy as jnp
from jax import lax
from jax.experimental import pallas as pl
from jax.experimental.pallas import tpu as pltpu
from jax.sharding import PartitionSpec as P

inverse_temp = 50.0
token_eps = 1e-05
unit_eps = 1e-06
lanes = 128
bound_steps = 256.0
code_steps = 32000.0
vmem_limit = 56 * 1024 * 1024


def spread(target, at, value):
    count, width = value.shape
    for part in range(width // lanes):
        target[pl.ds(at, count), part, :] = value[:, part * lanes : (part + 1) * lanes]


def gathered(source, at, count):
    parts = [source[pl.ds(at, count), part, :] for part in range(source.shape[1])]
    return jnp.concatenate(parts, axis=1)


def norm_kernel(last_ref, hidden_ref, gain_ref, owner_ref, negative_ref, normed_ref, inv_ref, emb_ref):
    seqs, width = normed_ref.shape
    parts, _, piece = emb_ref.shape
    pairs = owner_ref.shape[1]
    cuts = [slice(part * piece, (part + 1) * piece) for part in range(parts)]
    sources = lax.broadcasted_iota(jnp.int32, (seqs, seqs), 0)
    pick = jnp.where(sources == last_ref[...], 1.0, 0.0).astype(jnp.bfloat16)

    def folded(squares):
        return functools.reduce(
            jnp.add, [squares[:, at : at + lanes] for at in range(0, piece, lanes)]
        )

    total = jnp.zeros((seqs, lanes), jnp.float32)
    for cut in cuts:
        values = lax.dot_general(
            pick, hidden_ref[:, cut], (((0,), (0,)), ((), ())), preferred_element_type=jnp.float32
        )
        normed_ref[:, cut] = values.astype(jnp.bfloat16)
        total = total + folded(values * values)
    scale = lax.rsqrt(jnp.sum(total, axis=-1, keepdims=True) / width + token_eps)
    total = jnp.zeros((seqs, lanes), jnp.float32)
    for cut in cuts:
        values = normed_ref[:, cut].astype(jnp.float32)
        gain = gain_ref[cut].astype(jnp.float32).reshape(1, piece)
        normed = (values * scale * gain).astype(jnp.bfloat16)
        normed_ref[:, cut] = normed
        pooled = normed.astype(jnp.float32)
        total = total + folded(pooled * pooled)
    inverse = lax.rsqrt(jnp.sum(total, axis=-1, keepdims=True) + unit_eps)
    inv_ref[...] = jnp.broadcast_to(inverse, inv_ref.shape)

    owners = owner_ref[...].astype(jnp.float32)
    high = jnp.floor(owners * (1.0 / 256.0))
    low = owners - 256.0 * high
    row = lax.broadcasted_iota(jnp.int32, (16, pairs), 0)
    spot = lax.broadcasted_iota(jnp.int32, (16, pairs), 1)
    left = jnp.where(row == 0, low[:1], jnp.where(row == 1, high[:1], 0.0))
    right = jnp.where(row == 0, low[1:2], jnp.where(row == 1, high[1:2], 0.0))
    for offset in range(negative_ref.shape[1]):
        named = (negative_ref[0, offset] >= 0).astype(jnp.float32)
        left = jnp.where((row == 2) & (spot == offset), named, left)
    facts = jnp.concatenate([left, right], axis=1).astype(jnp.bfloat16)

    for part, cut in enumerate(cuts):
        emb_ref[part, :seqs] = (normed_ref[:, cut].astype(jnp.float32) * inverse).astype(jnp.bfloat16)
        emb_ref[part, seqs:] = facts


def norm_call(last_row, hidden, gain, owners, hard_negatives, parts):
    seqs, width = hidden.shape
    piece = width // parts
    whole = pl.BlockSpec(memory_space=pltpu.VMEM)
    return pl.pallas_call(
        norm_kernel,
        in_specs=[whole, whole, whole, whole, pl.BlockSpec(memory_space=pltpu.SMEM)],
        out_specs=[whole, whole, whole],
        out_shape=[
            jax.ShapeDtypeStruct((seqs, width), jnp.bfloat16),
            jax.ShapeDtypeStruct((seqs, lanes), jnp.float32),
            jax.ShapeDtypeStruct((parts, seqs + 16, piece), jnp.bfloat16),
        ],
        compiler_params=pltpu.CompilerParams(vmem_limit_bytes=vmem_limit),
        name="norm_rows",
    )(last_row, hidden, gain, owners, hard_negatives)


def score_kernel(
    blocks,
    pairs,
    window,
    emb_ref,
    q_ref,
    d_ref,
    s_ref,
    own_ref,
    place_ref,
    wide,
    picked,
    tiles,
    facts,
    own,
    named,
    sums,
    sems,
):
    seqs = emb_ref.shape[1] - 16
    sent = emb_ref[:, seqs:, :].astype(jnp.float32)
    own_ref[...] = (sent[:, 0, :] + 256.0 * sent[:, 1, :]).astype(jnp.int32)
    facts[...] = sent[:, 2, :lanes].astype(jnp.int32)
    fetches = [
        pltpu.make_async_copy(own_ref, own, sems.at[0]),
        pltpu.make_async_copy(facts, named, sems.at[1]),
    ]
    for fetch in fetches:
        fetch.start()

    def widen(step, carry):
        at = pl.multiple_of(step * seqs, seqs)
        spread(wide, at, emb_ref[step, :seqs, :].astype(jnp.float32))
        return carry

    lax.fori_loop(0, emb_ref.shape[0], widen, 0)
    for fetch in fetches:
        fetch.wait()

    def place(block, count):
        place_ref[0, block] = block
        for offset in range(window):
            present = named[block, offset] > 0
            place_ref[offset + 1, block] = jnp.where(present, count, -1)
            count = count + present.astype(jnp.int32)
        return count

    lax.fori_loop(0, blocks, place, blocks)
    unroll = 16

    def pick_block(block, carry):
        def pick_rows(step, inner):
            base = pl.multiple_of(step * unroll, unroll)
            rows = [wide[own[block, base + k]] for k in range(unroll)]
            for k in range(unroll):
                picked[base + k] = rows[k]
            return inner

        lax.fori_loop(0, 2 * pairs // unroll, pick_rows, 0)
        at = pl.multiple_of(block * pairs, pairs)
        q_ref[pl.ds(at, pairs), :] = gathered(picked, 0, pairs).astype(jnp.bfloat16)
        d_ref[pl.ds(at, pairs), :] = gathered(picked, pairs, pairs).astype(jnp.bfloat16)
        return carry

    lax.fori_loop(0, blocks, pick_block, 0)
    d_ref[blocks * pairs :, :] = d_ref[: window * pairs, :]
    groups = s_ref.shape[0]
    fine = pairs // groups

    def score_blocks(step, top):
        at = pl.multiple_of(step * 2 * pairs, 2 * pairs)
        tiles[...] = inverse_temp * lax.dot_general(
            q_ref[pl.ds(at, 2 * pairs), :],
            d_ref[pl.ds(at, (window + 2) * pairs), :],
            (((1,), (1,)), ((), ())),
            preferred_element_type=jnp.float32,
        )
        for half in range(2):
            for column in range(window + 1):
                spot = place_ref[column, 2 * step + half]

                @pl.when(spot >= 0)
                def _():
                    row = pl.multiple_of(spot * fine, fine)
                    tile = tiles[
                        half * pairs : (half + 1) * pairs,
                        (half + column) * pairs : (half + column + 1) * pairs,
                    ]
                    sums[:, pl.ds(row, fine), :] = tile.reshape(groups, fine, pairs)

        used = tiles[...]
        for at in range(0, used.shape[1], pairs):
            size = jnp.abs(used[:, at : at + pairs]).reshape(-1, fine, pairs)
            top = jnp.maximum(top, jnp.max(size, axis=0))
        return top

    top = lax.fori_loop(0, blocks // 2, score_blocks, jnp.zeros((fine, pairs), jnp.float32))
    top = jnp.max(jnp.max(top, axis=1, keepdims=True), axis=0, keepdims=True)
    bound = jnp.ceil(top * bound_steps) + 1.0
    scale = code_steps * bound_steps / bound
    room = s_ref.shape[1] - 1

    def encode(step, carry):
        at = pl.multiple_of(step * 2 * fine, 2 * fine)
        codes = jnp.round(sums[:, pl.ds(at, 2 * fine), :] * scale)
        s_ref[:, step] = codes.astype(jnp.int32).astype(jnp.int16)
        return carry

    lax.fori_loop(0, room, encode, 0)
    sent_bound = jnp.broadcast_to(bound, (groups * 2 * fine, pairs)).astype(jnp.int32)
    s_ref[:, room] = sent_bound.astype(jnp.int16).reshape(groups, 2 * fine, pairs)


def score_call(embedded, room, blocks, pairs, window):
    parts, rows, piece = embedded.shape
    fine = pairs // blocks
    whole = pl.BlockSpec(memory_space=pltpu.VMEM)
    scalars = pl.BlockSpec(memory_space=pltpu.SMEM)
    return pl.pallas_call(
        functools.partial(score_kernel, blocks, pairs, window),
        in_specs=[whole],
        out_specs=[whole, whole, whole, whole, scalars],
        out_shape=[
            jax.ShapeDtypeStruct((blocks * pairs, piece), jnp.bfloat16),
            jax.ShapeDtypeStruct(((blocks + window) * pairs, piece), jnp.bfloat16),
            jax.ShapeDtypeStruct((blocks, room // 2 + 1, 2 * fine, pairs), jnp.int16),
            jax.ShapeDtypeStruct((blocks, 2 * pairs), jnp.int32),
            jax.ShapeDtypeStruct((window + 1, blocks), jnp.int32),
        ],
        scratch_shapes=[
            pltpu.VMEM((parts * (rows - 16), piece // lanes, lanes), jnp.float32),
            pltpu.VMEM((2 * pairs, piece // lanes, lanes), jnp.float32),
            pltpu.VMEM((2 * pairs, (window + 2) * pairs), jnp.float32),
            pltpu.VMEM((blocks, lanes), jnp.int32),
            pltpu.SMEM((blocks, 2 * pairs), jnp.int32),
            pltpu.SMEM((blocks, lanes), jnp.int32),
            pltpu.VMEM((blocks, room * fine, pairs), jnp.float32),
            pltpu.SemaphoreType.DMA((2,)),
        ],
        compiler_params=pltpu.CompilerParams(vmem_limit_bytes=vmem_limit),
        name="partial_scores",
    )(embedded)


def softmax_kernel(blocks, window, place_ref, s_ref, c_ref, packed, masked):
    room, fine, pairs = packed.shape
    count = blocks * fine
    bound = s_ref[:, room // 2].astype(jnp.int32).astype(jnp.float32)
    scale = bound * (1.0 / (code_steps * bound_steps))

    def decode(step, carry):
        codes = s_ref[:, step].astype(jnp.int32).astype(jnp.float32)
        both = jnp.sum(codes * scale, axis=0)
        packed[2 * step] = both[:fine]
        packed[2 * step + 1] = both[fine:]
        return carry

    lax.fori_loop(0, room // 2, decode, 0)
    for block in range(blocks):
        for column in range(window + 1):
            spot = place_ref[column, block]
            tile = packed[jnp.maximum(spot, 0)]
            masked[block * fine : (block + 1) * fine, column * pairs : (column + 1) * pairs] = (
                jnp.where(spot >= 0, tile, -jnp.inf)
            )
    row = lax.broadcasted_iota(jnp.int32, (count, pairs), 0)
    lane = lax.broadcasted_iota(jnp.int32, (count, pairs), 1)
    target = lane == lax.axis_index("pb") * fine + row % fine
    pieces = [masked[:, column * pairs : (column + 1) * pairs] for column in range(window + 1)]
    row_max = jnp.max(functools.reduce(jnp.maximum, pieces), axis=1, keepdims=True)
    total = functools.reduce(jnp.add, [jnp.exp(piece - row_max) for piece in pieces])
    log_total = row_max + jnp.log(jnp.sum(total, axis=1, keepdims=True))
    positive = jnp.sum(jnp.where(target, pieces[0], 0.0), axis=1, keepdims=True)
    for column, piece in enumerate(pieces):
        share = jnp.exp(piece - log_total)
        if column == 0:
            share = share - jnp.where(target, 1.0, 0.0)
        masked[:, column * pairs : (column + 1) * pairs] = inverse_temp * share
    for block in range(blocks):
        for column in range(window + 1):
            spot = place_ref[column, block]

            @pl.when(spot >= 0)
            def _():
                packed[spot] = masked[
                    block * fine : (block + 1) * fine, column * pairs : (column + 1) * pairs
                ]

    for step in range(room // 2):
        both = jnp.concatenate([packed[2 * step], packed[2 * step + 1]], axis=0)
        c_ref[step] = both.astype(jnp.bfloat16)
    losses = jnp.sum(
        jnp.where(lane == row // fine, log_total - positive, 0.0), axis=0, keepdims=True
    )
    coarse = losses.astype(jnp.bfloat16).astype(jnp.float32)
    rank = lax.broadcasted_iota(jnp.int32, (2 * fine, pairs), 0)
    both = jnp.where(rank == 0, coarse, jnp.where(rank == 1, losses - coarse, 0.0))
    c_ref[room // 2] = both.astype(jnp.bfloat16)


def softmax_call(place, scores, blocks, window):
    _, steps, fine, pairs = scores.shape
    room, fine = 2 * (steps - 1), fine // 2
    whole = pl.BlockSpec(memory_space=pltpu.VMEM)
    return pl.pallas_call(
        functools.partial(softmax_kernel, blocks, window),
        in_specs=[pl.BlockSpec(memory_space=pltpu.SMEM), whole],
        out_specs=whole,
        out_shape=jax.ShapeDtypeStruct((room // 2 + 1, 2 * fine, pairs), jnp.bfloat16),
        scratch_shapes=[
            pltpu.VMEM((room, fine, pairs), jnp.float32),
            pltpu.VMEM((blocks * fine, (window + 1) * pairs), jnp.float32),
        ],
        compiler_params=pltpu.CompilerParams(vmem_limit_bytes=vmem_limit),
        name="softmax_rows",
    )(place, scores)


def grad_kernel(
    blocks,
    pairs,
    window,
    own_ref,
    place_ref,
    mine_ref,
    other_ref,
    q_ref,
    d_ref,
    out_ref,
    loss_ref,
    wide,
    dsum,
    picked,
    packed,
    square,
):
    fine = pairs // blocks
    seqs = wide.shape[0]
    room = packed.shape[1]
    unroll = 16
    losses = 0.0
    for half in (mine_ref, other_ref):
        sent = half[:, room // 2].astype(jnp.float32)
        losses = losses + jnp.sum(sent[:, 0, :] + sent[:, 1, :], axis=0, keepdims=True) / pairs
    core = lax.axis_index("pb") % 2
    lane = lax.broadcasted_iota(jnp.int32, losses.shape, 1)
    mine = jnp.where(lane == lax.axis_index("pb"), losses, 0.0)
    loss_ref[...] = jnp.broadcast_to(jnp.sum(mine, axis=1, keepdims=True), loss_ref.shape)
    dsum[...] = jnp.zeros_like(dsum)
    square[...] = jnp.zeros_like(square)

    def unpack(step, carry):
        for half, at in ((mine_ref, core), (other_ref, 1 - core)):
            both = half[:, step].astype(jnp.float32)
            for chip in range(blocks // 2):
                packed[2 * chip + at, 2 * step] = both[chip, :fine]
                packed[2 * chip + at, 2 * step + 1] = both[chip, fine:]
        return carry

    lax.fori_loop(0, room // 2, unpack, 0)

    def scatter_rows(block, offset, start):
        def step_rows(step, inner):
            base = pl.multiple_of(step * unroll, unroll)
            rows = [picked[start + base + k] for k in range(unroll)]
            for k in range(unroll):
                wide[own_ref[block, offset + base + k]] = rows[k]
            return inner

        lax.fori_loop(0, pairs // unroll, step_rows, 0)

    def two_blocks(step, carry):
        for half in range(2):
            for column in range(window + 1):
                spot = place_ref[column, 2 * step + half]
                tile = packed[:, jnp.maximum(spot, 0)].reshape(pairs, pairs)
                square[
                    half * pairs : (half + 1) * pairs,
                    (half + column) * pairs : (half + column + 1) * pairs,
                ] = jnp.where(spot >= 0, tile, 0.0).astype(jnp.bfloat16)
        at = pl.multiple_of(step * 2 * pairs, 2 * pairs)
        there = pl.ds(at, (window + 2) * pairs)
        coefficients = square[...]
        summed = jnp.dot(coefficients, d_ref[there, :], preferred_element_type=jnp.float32)
        spread(picked, 0, summed)
        dsum[there, :] += lax.dot_general(
            coefficients,
            q_ref[pl.ds(at, 2 * pairs), :],
            (((0,), (0,)), ((), ())),
            preferred_element_type=jnp.float32,
        )
        for half in range(2):
            scatter_rows(2 * step + half, 0, half * pairs)
        return carry

    lax.fori_loop(0, blocks // 2, two_blocks, 0)
    dsum[: window * pairs, :] += dsum[blocks * pairs :, :]

    def doc_block(block, carry):
        at = pl.multiple_of(block * pairs, pairs)
        spread(picked, 0, dsum[pl.ds(at, pairs), :])
        scatter_rows(block, pairs, 0)
        return carry

    lax.fori_loop(0, blocks, doc_block, 0)
    slots = out_ref.shape[1]

    def narrow(part, carry):
        at = pl.multiple_of(part * slots, slots)
        out_ref[part] = gathered(wide, at, slots).astype(jnp.bfloat16)
        return carry

    lax.fori_loop(0, seqs // slots, narrow, 0)


def grad_call(own, place, mine, other, queries, documents, blocks, pairs, window):
    count, piece = queries.shape
    seqs = 2 * count
    room = 2 * (mine.shape[1] - 1)
    whole = pl.BlockSpec(memory_space=pltpu.VMEM)
    scalars = pl.BlockSpec(memory_space=pltpu.SMEM)
    return pl.pallas_call(
        functools.partial(grad_kernel, blocks, pairs, window),
        in_specs=[scalars, scalars, whole, whole, whole, whole],
        out_specs=[whole, whole],
        out_shape=[
            jax.ShapeDtypeStruct((blocks, seqs // blocks, piece), jnp.bfloat16),
            jax.ShapeDtypeStruct((1, lanes), jnp.float32),
        ],
        scratch_shapes=[
            pltpu.VMEM((seqs, piece // lanes, lanes), jnp.float32),
            pltpu.VMEM(((blocks + window) * pairs, piece), jnp.float32),
            pltpu.VMEM((2 * pairs, piece // lanes, lanes), jnp.float32),
            pltpu.VMEM((blocks, room, pairs // blocks, pairs), jnp.float32),
            pltpu.VMEM((2 * pairs, (window + 2) * pairs), jnp.bfloat16),
        ],
        compiler_params=pltpu.CompilerParams(vmem_limit_bytes=vmem_limit),
        name="slice_grads",
    )(own, place, mine, other, queries, documents)


def project_kernel(grad_ref, normed_ref, inv_ref, out_ref):
    parts, _, piece = grad_ref.shape
    inverse = inv_ref[:, :1]
    total = 0.0
    for part in range(parts):
        cut = slice(part * piece, (part + 1) * piece)
        unit = normed_ref[:, cut].astype(jnp.float32) * inverse
        total = total + unit * grad_ref[part].astype(jnp.float32)
    along = jnp.sum(total, axis=-1, keepdims=True)
    for part in range(parts):
        cut = slice(part * piece, (part + 1) * piece)
        unit = normed_ref[:, cut].astype(jnp.float32) * inverse
        out_ref[:, cut] = grad_ref[part].astype(jnp.float32) - unit * along


def project_call(returned, normed, inverse):
    parts, seqs, piece = returned.shape
    width = normed.shape[1]
    rows = 32
    return pl.pallas_call(
        project_kernel,
        grid=(seqs // rows,),
        in_specs=[
            pl.BlockSpec((parts, rows, piece), lambda i: (0, i, 0)),
            pl.BlockSpec((rows, width), lambda i: (i, 0)),
            pl.BlockSpec((rows, lanes), lambda i: (i, 0)),
        ],
        out_specs=pl.BlockSpec((rows, width), lambda i: (i, 0)),
        out_shape=jax.ShapeDtypeStruct((seqs, width), jnp.float32),
        compiler_params=pltpu.CompilerParams(vmem_limit_bytes=vmem_limit),
        name="project_out",
    )(returned, normed, inverse)


def middle(embedded, room, devices, pairs, window):
    queries, documents, partial_scores, own, place = score_call(
        embedded, room, devices, pairs, window
    )
    scores = lax.all_to_all(partial_scores, "pb", split_axis=0, concat_axis=0, tiled=True)
    coefficients = softmax_call(place, scores, devices, window)
    same_core = [list(range(core, devices, 2)) for core in range(2)]
    mine = lax.all_gather(coefficients, "pb", axis_index_groups=same_core, axis=0, tiled=False)
    other = lax.ppermute(mine, "pb", [(at, at ^ 1) for at in range(devices)])
    grads, loss = grad_call(own, place, mine, other, queries, documents, devices, pairs, window)
    return grads, loss[0, :1]


def feature_plan(hidden, final_gain, last_row, pair_owner, hard_negatives):
    devices = lax.axis_size("pb")
    seqs, width = hidden.shape
    pairs = pair_owner.shape[0]
    window = hard_negatives.shape[1]
    normed, inverse, embedding = norm_call(
        last_row, hidden, final_gain, pair_owner.T, hard_negatives, devices
    )
    embedded = lax.all_to_all(embedding, "pb", split_axis=0, concat_axis=0, tiled=True)
    most = devices * (window + 1)
    rooms = [most * part // 20 for part in (10, 11, 12, 13, 14, 16, 20)]
    used = devices + jnp.sum(embedded[:, seqs + 2, :window].astype(jnp.float32))
    level = sum((used > room).astype(jnp.int32) for room in rooms[:-1])
    grads, loss = lax.switch(
        level,
        [
            functools.partial(middle, room=room, devices=devices, pairs=pairs, window=window)
            for room in rooms
        ],
        embedded,
    )
    returned = lax.all_to_all(grads, "pb", split_axis=0, concat_axis=0, tiled=True)
    return project_call(returned, normed, inverse), loss


def from_behind(value, axis, steps):
    count = lax.axis_size(axis)
    pairs = [(source, (source + steps) % count) for source in range(count)]
    return lax.ppermute(value, axis, pairs)


def similarity(queries, documents):
    return inverse_temp * lax.dot_general(
        queries, documents, (((1,), (1,)), ((), ())), preferred_element_type=jnp.float32
    )


def transposed(weights, queries):
    return lax.dot_general(
        weights, queries, (((0,), (0,)), ((), ())), preferred_element_type=jnp.float32
    )


def combine_docs(weights, documents):
    return jnp.dot(weights, documents, preferred_element_type=jnp.float32)


def skipped(listed, function, operands, out_shape):
    return lax.cond(
        listed,
        lambda inputs: function(*inputs),
        lambda inputs: jnp.zeros(out_shape, jnp.float32),
        operands,
    )


def row_plan(hidden, final_gain, last_row, pair_owner, hard_negatives):
    values = hidden.astype(jnp.float32)
    scale_row = lax.rsqrt(jnp.mean(values * values, axis=-1, keepdims=True) + token_eps)
    normed = (values * scale_row * final_gain.astype(jnp.float32)).astype(jnp.bfloat16)
    seq_count = last_row.shape[1]
    model_width = hidden.shape[1]
    pooled = normed[last_row[0]].astype(jnp.float32)
    inverse_norm = lax.rsqrt(jnp.sum(pooled * pooled, axis=-1, keepdims=True) + 1e-06)
    unit_vec = pooled * inverse_norm
    embedding = unit_vec.astype(jnp.bfloat16)
    devices = lax.axis_size("pb")
    capacity = 2 * seq_count // devices
    pair_count = pair_owner.shape[0]
    wanted = jnp.concatenate([pair_owner[:, 0], pair_owner[:, 1]])
    holder = wanted // seq_count
    within = wanted % seq_count
    entry_ids = jnp.arange(2 * pair_count, dtype=jnp.int32)
    earlier = (holder[None, :] == holder[:, None]) & (entry_ids[None, :] < entry_ids[:, None])
    position = jnp.sum(earlier.astype(jnp.int32), axis=1)
    request = jnp.full((devices, capacity), -1, jnp.int32).at[holder, position].set(within)
    served = lax.all_to_all(request, "pb", split_axis=0, concat_axis=0, tiled=True)
    outgoing = jnp.where(
        served[:, :, None] >= 0, embedding[jnp.maximum(served, 0)], jnp.zeros((), jnp.bfloat16)
    )
    received = lax.all_to_all(outgoing, "pb", split_axis=0, concat_axis=0, tiled=True)
    gathered = received[holder, position]
    queries = gathered[:pair_count]
    own_docs = gathered[pair_count:]
    listed_ids = hard_negatives[0]
    window = hard_negatives.shape[1]
    listed = [listed_ids[offset] >= 0 for offset in range(window)]
    neighbours = []
    moving = own_docs
    for offset in range(window):
        moving = from_behind(moving, "pb", -1)
        neighbours.append(moving)
    tile_shape = (pair_count, pair_count)
    score_blocks = [similarity(queries, own_docs)]
    for offset in range(window):
        score_blocks.append(
            skipped(listed[offset], similarity, (queries, neighbours[offset]), tile_shape)
        )
    all_scores = jnp.concatenate(score_blocks, axis=1)
    usable = jnp.concatenate(
        [jnp.ones((pair_count,), jnp.bool_)]
        + [jnp.broadcast_to(listed[offset], (pair_count,)) for offset in range(window)]
    )
    masked = jnp.where(usable[None, :], all_scores, -jnp.inf)
    row_max = jnp.max(masked, axis=1, keepdims=True)
    log_total = row_max + jnp.log(jnp.sum(jnp.exp(masked - row_max), axis=1, keepdims=True))
    diagonal = jnp.arange(pair_count, dtype=jnp.int32)
    positive = all_scores[diagonal, diagonal]
    block_loss = jnp.mean(log_total[:, 0] - positive).reshape(1)
    columns = jnp.arange((window + 1) * pair_count, dtype=jnp.int32)
    target = (columns[None, :] == diagonal[:, None]).astype(jnp.float32)
    coefficients = (inverse_temp * (jnp.exp(masked - log_total) - target)).astype(jnp.bfloat16)
    pieces = [
        coefficients[:, offset * pair_count : (offset + 1) * pair_count]
        for offset in range(window + 1)
    ]
    grad_shape = (pair_count, model_width)
    query_sum = combine_docs(pieces[0], own_docs)
    for offset in range(window):
        query_sum = query_sum + skipped(
            listed[offset], combine_docs, (pieces[offset + 1], neighbours[offset]), grad_shape
        )
    query_grad = query_sum.astype(jnp.bfloat16)
    own_part = transposed(pieces[0], queries).astype(jnp.bfloat16)
    partial_value = [
        skipped(listed[offset], transposed, (pieces[offset + 1], queries), grad_shape).astype(
            jnp.bfloat16
        )
        for offset in range(window)
    ]
    running = partial_value[window - 1].astype(jnp.float32)
    for offset in range(window):
        running = from_behind(running, "pb", 1)
        if offset + 1 < window:
            running = running + partial_value[window - 2 - offset].astype(jnp.float32)
    doc_grad = (own_part.astype(jnp.float32) + running).astype(jnp.bfloat16)
    answers = jnp.concatenate([query_grad, doc_grad], axis=0)
    returning = (
        jnp.zeros((devices, capacity, model_width), jnp.bfloat16).at[holder, position].set(answers)
    )
    returned = lax.all_to_all(returning, "pb", split_axis=0, concat_axis=0, tiled=True)
    slot_ids = jnp.where(served >= 0, served, seq_count).reshape(-1)
    emb_grad = (
        jnp.zeros((seq_count, model_width), jnp.bfloat16)
        .at[slot_ids]
        .set(returned.reshape(-1, model_width), mode="drop")
    )
    gradient = emb_grad.astype(jnp.float32)
    pooled_grad = gradient - unit_vec * jnp.sum(unit_vec * gradient, axis=-1, keepdims=True)
    return (pooled_grad, block_loss)


def solution(mesh):
    def local(hidden, final_gain, last_row, pair_owner, hard_negatives):
        plan = feature_plan if hidden.shape[1] >= lanes * mesh.shape["pb"] else row_plan
        return plan(hidden, final_gain, last_row, pair_owner, hard_negatives)

    return jax.shard_map(
        local,
        mesh=mesh,
        in_specs=(
            P(("groups", "pb"), None),
            P(),
            P(("groups", "pb"), None),
            P(("groups", "pb"), None),
            P(("groups", "pb"), None),
        ),
        out_specs=(P(("groups", "pb"), None), P(("groups", "pb"))),
        check_vma=False,
    )
```

```python
import functools

import jax
import jax.numpy as jnp
from jax import lax
from jax.experimental import pallas as pl
from jax.experimental.pallas import tpu as pltpu
from jax.sharding import PartitionSpec as P

inverse_temp = 50.0
token_eps = 1e-05
unit_eps = 1e-06
lanes = 128
bound_steps = 256.0
code_steps = 32000.0
vmem_limit = 56 * 1024 * 1024


def spread(target, at, value):
    count, width = value.shape
    for part in range(width // lanes):
        target[pl.ds(at, count), part, :] = value[:, part * lanes : (part + 1) * lanes]


def gathered(source, at, count):
    parts = [source[pl.ds(at, count), part, :] for part in range(source.shape[1])]
    return jnp.concatenate(parts, axis=1)


def norm_kernel(last_ref, hidden_ref, gain_ref, owner_ref, negative_ref, normed_ref, inv_ref, emb_ref):
    seqs, width = normed_ref.shape
    parts, _, piece = emb_ref.shape
    pairs = owner_ref.shape[1]
    cuts = [slice(part * piece, (part + 1) * piece) for part in range(parts)]
    sources = lax.broadcasted_iota(jnp.int32, (seqs, seqs), 0)
    pick = jnp.where(sources == last_ref[...], 1.0, 0.0).astype(jnp.bfloat16)

    def folded(squares):
        return functools.reduce(
            jnp.add, [squares[:, at : at + lanes] for at in range(0, piece, lanes)]
        )

    total = jnp.zeros((seqs, lanes), jnp.float32)
    for cut in cuts:
        values = lax.dot_general(
            pick, hidden_ref[:, cut], (((0,), (0,)), ((), ())), preferred_element_type=jnp.float32
        )
        normed_ref[:, cut] = values.astype(jnp.bfloat16)
        total = total + folded(values * values)
    scale = lax.rsqrt(jnp.sum(total, axis=-1, keepdims=True) / width + token_eps)
    total = jnp.zeros((seqs, lanes), jnp.float32)
    for cut in cuts:
        values = normed_ref[:, cut].astype(jnp.float32)
        gain = gain_ref[cut].astype(jnp.float32).reshape(1, piece)
        normed = (values * scale * gain).astype(jnp.bfloat16)
        normed_ref[:, cut] = normed
        pooled = normed.astype(jnp.float32)
        total = total + folded(pooled * pooled)
    inverse = lax.rsqrt(jnp.sum(total, axis=-1, keepdims=True) + unit_eps)
    inv_ref[...] = jnp.broadcast_to(inverse, inv_ref.shape)

    owners = owner_ref[...].astype(jnp.float32)
    high = jnp.floor(owners * (1.0 / 256.0))
    low = owners - 256.0 * high
    row = lax.broadcasted_iota(jnp.int32, (16, pairs), 0)
    spot = lax.broadcasted_iota(jnp.int32, (16, pairs), 1)
    left = jnp.where(row == 0, low[:1], jnp.where(row == 1, high[:1], 0.0))
    right = jnp.where(row == 0, low[1:2], jnp.where(row == 1, high[1:2], 0.0))
    for offset in range(negative_ref.shape[1]):
        named = (negative_ref[0, offset] >= 0).astype(jnp.float32)
        left = jnp.where((row == 2) & (spot == offset), named, left)
    facts = jnp.concatenate([left, right], axis=1).astype(jnp.bfloat16)

    for part, cut in enumerate(cuts):
        emb_ref[part, :seqs] = (normed_ref[:, cut].astype(jnp.float32) * inverse).astype(jnp.bfloat16)
        emb_ref[part, seqs:] = facts


def norm_call(last_row, hidden, gain, owners, hard_negatives, parts):
    seqs, width = hidden.shape
    piece = width // parts
    whole = pl.BlockSpec(memory_space=pltpu.VMEM)
    return pl.pallas_call(
        norm_kernel,
        in_specs=[whole, whole, whole, whole, pl.BlockSpec(memory_space=pltpu.SMEM)],
        out_specs=[whole, whole, whole],
        out_shape=[
            jax.ShapeDtypeStruct((seqs, width), jnp.bfloat16),
            jax.ShapeDtypeStruct((seqs, lanes), jnp.float32),
            jax.ShapeDtypeStruct((parts, seqs + 16, piece), jnp.bfloat16),
        ],
        compiler_params=pltpu.CompilerParams(vmem_limit_bytes=vmem_limit),
        name="norm_rows",
    )(last_row, hidden, gain, owners, hard_negatives)


def score_kernel(
    blocks,
    pairs,
    window,
    emb_ref,
    q_ref,
    d_ref,
    mine_ref,
    other_ref,
    own_ref,
    place_ref,
    wide,
    picked,
    tiles,
    facts,
    own,
    named,
    sums,
    sems,
):
    seqs = emb_ref.shape[1] - 16
    sent = emb_ref[:, seqs:, :].astype(jnp.float32)
    own_ref[...] = (sent[:, 0, :] + 256.0 * sent[:, 1, :]).astype(jnp.int32)
    facts[...] = sent[:, 2, :lanes].astype(jnp.int32)
    fetches = [
        pltpu.make_async_copy(own_ref, own, sems.at[0]),
        pltpu.make_async_copy(facts, named, sems.at[1]),
    ]
    for fetch in fetches:
        fetch.start()

    def widen(step, carry):
        at = pl.multiple_of(step * seqs, seqs)
        spread(wide, at, emb_ref[step, :seqs, :].astype(jnp.float32))
        return carry

    lax.fori_loop(0, emb_ref.shape[0], widen, 0)
    for fetch in fetches:
        fetch.wait()

    def place(block, count):
        place_ref[0, block] = block
        for offset in range(window):
            present = named[block, offset] > 0
            place_ref[offset + 1, block] = jnp.where(present, count, -1)
            count = count + present.astype(jnp.int32)
        return count

    used = lax.fori_loop(0, blocks, place, blocks)
    fine = pairs // blocks

    def clear(spot, carry):
        empty = jnp.zeros((2, blocks // 2, fine, pairs), jnp.float32)
        sums[:, :, pl.ds(pl.multiple_of(spot * fine, fine), fine), :] = empty
        return carry

    lax.fori_loop(used, sums.shape[2] // fine, clear, 0)
    unroll = 16

    def pick_block(block, carry):
        def pick_rows(step, inner):
            base = pl.multiple_of(step * unroll, unroll)
            rows = [wide[own[block, base + k]] for k in range(unroll)]
            for k in range(unroll):
                picked[base + k] = rows[k]
            return inner

        lax.fori_loop(0, 2 * pairs // unroll, pick_rows, 0)
        at = pl.multiple_of(block * pairs, pairs)
        q_ref[pl.ds(at, pairs), :] = gathered(picked, 0, pairs).astype(jnp.bfloat16)
        d_ref[pl.ds(at, pairs), :] = gathered(picked, pairs, pairs).astype(jnp.bfloat16)
        return carry

    lax.fori_loop(0, blocks, pick_block, 0)
    d_ref[blocks * pairs :, :] = d_ref[: window * pairs, :]
    core = lax.axis_index("pb") % 2

    def score_blocks(step, carry):
        at = pl.multiple_of(step * 2 * pairs, 2 * pairs)
        tiles[...] = inverse_temp * lax.dot_general(
            q_ref[pl.ds(at, 2 * pairs), :],
            d_ref[pl.ds(at, (window + 2) * pairs), :],
            (((1,), (1,)), ((), ())),
            preferred_element_type=jnp.float32,
        )
        for half in range(2):
            for column in range(window + 1):
                spot = place_ref[column, 2 * step + half]

                @pl.when(spot >= 0)
                def _():
                    row = pl.multiple_of(spot * fine, fine)
                    tile = tiles[
                        half * pairs : (half + 1) * pairs,
                        (half + column) * pairs : (half + column + 1) * pairs,
                    ]
                    parted = tile.reshape(blocks // 2, 2, fine, pairs)
                    for parity in range(2):
                        sums[parity, :, pl.ds(row, fine), :] = parted[:, parity]

        return carry

    lax.fori_loop(0, blocks // 2, score_blocks, 0)

    def part(chip, carry):
        mine_ref[chip] = sums[core, chip]
        other_ref[chip] = sums[1 - core, chip]
        return carry

    lax.fori_loop(0, blocks // 2, part, 0)


def score_call(embedded, room, blocks, pairs, window):
    parts, rows, piece = embedded.shape
    fine = pairs // blocks
    whole = pl.BlockSpec(memory_space=pltpu.VMEM)
    scalars = pl.BlockSpec(memory_space=pltpu.SMEM)
    return pl.pallas_call(
        functools.partial(score_kernel, blocks, pairs, window),
        in_specs=[whole],
        out_specs=[whole, whole, whole, whole, whole, scalars],
        out_shape=[
            jax.ShapeDtypeStruct((blocks * pairs, piece), jnp.bfloat16),
            jax.ShapeDtypeStruct(((blocks + window) * pairs, piece), jnp.bfloat16),
            jax.ShapeDtypeStruct((blocks // 2, room * fine, pairs), jnp.float32),
            jax.ShapeDtypeStruct((blocks // 2, room * fine, pairs), jnp.float32),
            jax.ShapeDtypeStruct((blocks, 2 * pairs), jnp.int32),
            jax.ShapeDtypeStruct((window + 1, blocks), jnp.int32),
        ],
        scratch_shapes=[
            pltpu.VMEM((parts * (rows - 16), piece // lanes, lanes), jnp.float32),
            pltpu.VMEM((2 * pairs, piece // lanes, lanes), jnp.float32),
            pltpu.VMEM((2 * pairs, (window + 2) * pairs), jnp.float32),
            pltpu.VMEM((blocks, lanes), jnp.int32),
            pltpu.SMEM((blocks, 2 * pairs), jnp.int32),
            pltpu.SMEM((blocks, lanes), jnp.int32),
            pltpu.VMEM((2, blocks // 2, room * fine, pairs), jnp.float32),
            pltpu.SemaphoreType.DMA((2,)),
        ],
        compiler_params=pltpu.CompilerParams(vmem_limit_bytes=vmem_limit),
        name="partial_scores",
    )(embedded)


def merge_kernel(mine_ref, other_ref, own_ref, *code_refs):
    chips, rows, pairs = mine_ref.shape
    steps = code_refs[0].shape[0] - 1
    fine = rows // steps // 2
    chip = lax.axis_index("pb") // 2

    def largest(step, top):
        at = pl.multiple_of(step * 2 * fine, 2 * fine)
        size = jnp.abs(mine_ref[:, pl.ds(at, 2 * fine), :] + other_ref[:, pl.ds(at, 2 * fine), :])
        return jnp.maximum(top, jnp.max(size, axis=0))

    top = lax.fori_loop(0, steps, largest, jnp.zeros((2 * fine, pairs), jnp.float32))
    top = jnp.max(jnp.max(top, axis=1, keepdims=True), axis=0, keepdims=True)
    bound = jnp.ceil(jnp.minimum(top, 100.0) * bound_steps) + 1.0
    scale = code_steps * bound_steps / bound
    own_ref[...] = mine_ref[chip] + other_ref[chip]
    for hop, code_ref in enumerate(code_refs):
        target = chip ^ (hop + 1)

        def encode(step, carry):
            at = pl.multiple_of(step * 2 * fine, 2 * fine)
            there = pl.ds(at, 2 * fine)
            codes = jnp.round((mine_ref[target, there, :] + other_ref[target, there, :]) * scale)
            code_ref[step] = codes.astype(jnp.int32).astype(jnp.int16)
            return carry

        lax.fori_loop(0, steps, encode, 0)
        code_ref[steps] = jnp.broadcast_to(bound, (2 * fine, pairs)).astype(jnp.int32).astype(jnp.int16)


def merge_call(mine, other, blocks):
    chips, rows, pairs = mine.shape
    fine = pairs // blocks
    whole = pl.BlockSpec(memory_space=pltpu.VMEM)
    coded = jax.ShapeDtypeStruct((rows // (2 * fine) + 1, 2 * fine, pairs), jnp.int16)
    return pl.pallas_call(
        merge_kernel,
        in_specs=[whole, whole],
        out_specs=[whole] * chips,
        out_shape=[jax.ShapeDtypeStruct((rows, pairs), jnp.float32)] + [coded] * (chips - 1),
        compiler_params=pltpu.CompilerParams(vmem_limit_bytes=vmem_limit),
        name="merge_scores",
    )(mine, other)


def softmax_kernel(blocks, window, place_ref, own_ref, *refs):
    code_refs, (c_ref, packed, masked) = refs[:-3], refs[-3:]
    room, fine, pairs = packed.shape
    count = blocks * fine
    unit = 1.0 / (code_steps * bound_steps)
    scales = [ref[room // 2].astype(jnp.int32).astype(jnp.float32) * unit for ref in code_refs]

    def decode(step, carry):
        both = own_ref[pl.ds(pl.multiple_of(step * 2 * fine, 2 * fine), 2 * fine), :]
        for ref, scale in zip(code_refs, scales):
            both = both + ref[step].astype(jnp.int32).astype(jnp.float32) * scale
        packed[2 * step] = both[:fine]
        packed[2 * step + 1] = both[fine:]
        return carry

    lax.fori_loop(0, room // 2, decode, 0)
    for block in range(blocks):
        for column in range(window + 1):
            spot = place_ref[column, block]
            tile = packed[jnp.maximum(spot, 0)]
            masked[block * fine : (block + 1) * fine, column * pairs : (column + 1) * pairs] = (
                jnp.where(spot >= 0, tile, -jnp.inf)
            )
    row = lax.broadcasted_iota(jnp.int32, (count, pairs), 0)
    lane = lax.broadcasted_iota(jnp.int32, (count, pairs), 1)
    target = lane == lax.axis_index("pb") * fine + row % fine
    pieces = [masked[:, column * pairs : (column + 1) * pairs] for column in range(window + 1)]
    row_max = jnp.max(functools.reduce(jnp.maximum, pieces), axis=1, keepdims=True)
    total = functools.reduce(jnp.add, [jnp.exp(piece - row_max) for piece in pieces])
    log_total = row_max + jnp.log(jnp.sum(total, axis=1, keepdims=True))
    positive = jnp.sum(jnp.where(target, pieces[0], 0.0), axis=1, keepdims=True)
    for column, piece in enumerate(pieces):
        share = jnp.exp(piece - log_total)
        if column == 0:
            share = share - jnp.where(target, 1.0, 0.0)
        masked[:, column * pairs : (column + 1) * pairs] = inverse_temp * share
    for block in range(blocks):
        for column in range(window + 1):
            spot = place_ref[column, block]

            @pl.when(spot >= 0)
            def _():
                packed[spot] = masked[
                    block * fine : (block + 1) * fine, column * pairs : (column + 1) * pairs
                ]

    for step in range(room // 2):
        both = jnp.concatenate([packed[2 * step], packed[2 * step + 1]], axis=0)
        c_ref[step] = both.astype(jnp.bfloat16)
    losses = jnp.sum(
        jnp.where(lane == row // fine, log_total - positive, 0.0), axis=0, keepdims=True
    )
    coarse = losses.astype(jnp.bfloat16).astype(jnp.float32)
    rank = lax.broadcasted_iota(jnp.int32, (2 * fine, pairs), 0)
    both = jnp.where(rank == 0, coarse, jnp.where(rank == 1, losses - coarse, 0.0))
    c_ref[room // 2] = both.astype(jnp.bfloat16)


def softmax_call(place, own_scores, codes, blocks, window):
    steps, fine, pairs = codes[0].shape
    room, fine = 2 * (steps - 1), fine // 2
    whole = pl.BlockSpec(memory_space=pltpu.VMEM)
    return pl.pallas_call(
        functools.partial(softmax_kernel, blocks, window),
        in_specs=[pl.BlockSpec(memory_space=pltpu.SMEM), whole] + [whole] * len(codes),
        out_specs=whole,
        out_shape=jax.ShapeDtypeStruct((room // 2 + 1, 2 * fine, pairs), jnp.bfloat16),
        scratch_shapes=[
            pltpu.VMEM((room, fine, pairs), jnp.float32),
            pltpu.VMEM((blocks * fine, (window + 1) * pairs), jnp.float32),
        ],
        compiler_params=pltpu.CompilerParams(vmem_limit_bytes=vmem_limit),
        name="softmax_rows",
    )(place, own_scores, *codes)


def grad_kernel(
    blocks,
    pairs,
    window,
    own_ref,
    place_ref,
    q_ref,
    d_ref,
    *refs,
):
    part_refs, (out_ref, loss_ref, wide, dsum, picked, packed, square) = refs[:-7], refs[-7:]
    fine = pairs // blocks
    seqs = wide.shape[0]
    room = packed.shape[1]
    me = lax.axis_index("pb")
    masks = swap_masks(blocks)
    unroll = 16
    losses = 0.0
    for part in part_refs:
        sent = part[:, room // 2].astype(jnp.float32)
        losses = losses + jnp.sum(sent[:, 0, :] + sent[:, 1, :], axis=0, keepdims=True) / pairs
    lane = lax.broadcasted_iota(jnp.int32, losses.shape, 1)
    mine = jnp.where(lane == me, losses, 0.0)
    loss_ref[...] = jnp.broadcast_to(jnp.sum(mine, axis=1, keepdims=True), loss_ref.shape)
    dsum[...] = jnp.zeros_like(dsum)
    square[...] = jnp.zeros_like(square)

    def unpack(step, carry):
        for part, mask in zip(part_refs, masks):
            both = part[:, step].astype(jnp.float32)
            for at, apart in enumerate(mask):
                packed[me ^ apart, 2 * step] = both[at, :fine]
                packed[me ^ apart, 2 * step + 1] = both[at, fine:]
        return carry

    lax.fori_loop(0, room // 2, unpack, 0)

    def scatter_rows(block, offset, start):
        def step_rows(step, inner):
            base = pl.multiple_of(step * unroll, unroll)
            rows = [picked[start + base + k] for k in range(unroll)]
            for k in range(unroll):
                wide[own_ref[block, offset + base + k]] = rows[k]
            return inner

        lax.fori_loop(0, pairs // unroll, step_rows, 0)

    def two_blocks(step, carry):
        for half in range(2):
            for column in range(window + 1):
                spot = place_ref[column, 2 * step + half]
                tile = packed[:, jnp.maximum(spot, 0)].reshape(pairs, pairs)
                square[
                    half * pairs : (half + 1) * pairs,
                    (half + column) * pairs : (half + column + 1) * pairs,
                ] = jnp.where(spot >= 0, tile, 0.0).astype(jnp.bfloat16)
        at = pl.multiple_of(step * 2 * pairs, 2 * pairs)
        there = pl.ds(at, (window + 2) * pairs)
        coefficients = square[...]
        summed = jnp.dot(coefficients, d_ref[there, :], preferred_element_type=jnp.float32)
        spread(picked, 0, summed)
        dsum[there, :] += lax.dot_general(
            coefficients,
            q_ref[pl.ds(at, 2 * pairs), :],
            (((0,), (0,)), ((), ())),
            preferred_element_type=jnp.float32,
        )
        for half in range(2):
            scatter_rows(2 * step + half, 0, half * pairs)
        return carry

    lax.fori_loop(0, blocks // 2, two_blocks, 0)
    dsum[: window * pairs, :] += dsum[blocks * pairs :, :]

    def doc_block(block, carry):
        at = pl.multiple_of(block * pairs, pairs)
        spread(picked, 0, dsum[pl.ds(at, pairs), :])
        scatter_rows(block, pairs, 0)
        return carry

    lax.fori_loop(0, blocks, doc_block, 0)
    slots = out_ref.shape[1]

    def narrow(part, carry):
        at = pl.multiple_of(part * slots, slots)
        out_ref[part] = gathered(wide, at, slots).astype(jnp.bfloat16)
        return carry

    lax.fori_loop(0, seqs // slots, narrow, 0)


def grad_call(own, place, parts, queries, documents, blocks, pairs, window):
    count, piece = queries.shape
    seqs = 2 * count
    room = 2 * (parts[0].shape[1] - 1)
    whole = pl.BlockSpec(memory_space=pltpu.VMEM)
    scalars = pl.BlockSpec(memory_space=pltpu.SMEM)
    return pl.pallas_call(
        functools.partial(grad_kernel, blocks, pairs, window),
        in_specs=[scalars, scalars, whole, whole] + [whole] * len(parts),
        out_specs=[whole, whole],
        out_shape=[
            jax.ShapeDtypeStruct((blocks, seqs // blocks, piece), jnp.bfloat16),
            jax.ShapeDtypeStruct((1, lanes), jnp.float32),
        ],
        scratch_shapes=[
            pltpu.VMEM((seqs, piece // lanes, lanes), jnp.float32),
            pltpu.VMEM(((blocks + window) * pairs, piece), jnp.float32),
            pltpu.VMEM((2 * pairs, piece // lanes, lanes), jnp.float32),
            pltpu.VMEM((blocks, room, pairs // blocks, pairs), jnp.float32),
            pltpu.VMEM((2 * pairs, (window + 2) * pairs), jnp.bfloat16),
        ],
        compiler_params=pltpu.CompilerParams(vmem_limit_bytes=vmem_limit),
        name="slice_grads",
    )(own, place, queries, documents, *parts)


def project_kernel(grad_ref, normed_ref, inv_ref, out_ref):
    parts, _, piece = grad_ref.shape
    inverse = inv_ref[:, :1]
    total = 0.0
    for part in range(parts):
        cut = slice(part * piece, (part + 1) * piece)
        unit = normed_ref[:, cut].astype(jnp.float32) * inverse
        total = total + unit * grad_ref[part].astype(jnp.float32)
    along = jnp.sum(total, axis=-1, keepdims=True)
    for part in range(parts):
        cut = slice(part * piece, (part + 1) * piece)
        unit = normed_ref[:, cut].astype(jnp.float32) * inverse
        out_ref[:, cut] = grad_ref[part].astype(jnp.float32) - unit * along


def project_call(returned, normed, inverse):
    parts, seqs, piece = returned.shape
    width = normed.shape[1]
    rows = 32
    return pl.pallas_call(
        project_kernel,
        grid=(seqs // rows,),
        in_specs=[
            pl.BlockSpec((parts, rows, piece), lambda i: (0, i, 0)),
            pl.BlockSpec((rows, width), lambda i: (i, 0)),
            pl.BlockSpec((rows, lanes), lambda i: (i, 0)),
        ],
        out_specs=pl.BlockSpec((rows, width), lambda i: (i, 0)),
        out_shape=jax.ShapeDtypeStruct((seqs, width), jnp.float32),
        compiler_params=pltpu.CompilerParams(vmem_limit_bytes=vmem_limit),
        name="project_out",
    )(returned, normed, inverse)


def swapped(value, apart):
    pairs = [(at, at ^ apart) for at in range(lax.axis_size("pb"))]
    return lax.ppermute(value, "pb", pairs)


def swap_steps(devices):
    return [1 << bit for bit in reversed(range(devices.bit_length() - 1))]


def swap_masks(devices):
    known, masks = [0], [[0]]
    for apart in swap_steps(devices):
        masks.append([mask ^ apart for mask in known])
        known = known + masks[-1]
    return masks


def gather_all(value):
    held = value[None]
    parts = [held]
    for apart in swap_steps(lax.axis_size("pb")):
        arrived = swapped(held, apart)
        parts.append(arrived)
        held = jnp.concatenate([held, arrived], axis=0)
    return parts


def middle(embedded, room, devices, pairs, window):
    queries, documents, mine, other, own, place = score_call(
        embedded, room, devices, pairs, window
    )
    own_scores, *codes = merge_call(mine, swapped(other, 1), devices)
    codes = [swapped(code, 2 * (hop + 1)) for hop, code in enumerate(codes)]
    parts = gather_all(softmax_call(place, own_scores, codes, devices, window))
    grads, loss = grad_call(own, place, parts, queries, documents, devices, pairs, window)
    return grads, loss[0, :1]


def feature_plan(hidden, final_gain, last_row, pair_owner, hard_negatives):
    devices = lax.axis_size("pb")
    seqs, width = hidden.shape
    pairs = pair_owner.shape[0]
    window = hard_negatives.shape[1]
    normed, inverse, embedding = norm_call(
        last_row, hidden, final_gain, pair_owner.T, hard_negatives, devices
    )
    embedded = lax.all_to_all(embedding, "pb", split_axis=0, concat_axis=0, tiled=True)
    most = devices * (window + 1)
    rooms = [most * part // 20 for part in (10, 11, 12, 13, 14, 16, 20)]
    used = devices + jnp.sum(embedded[:, seqs + 2, :window].astype(jnp.float32))
    level = sum((used > room).astype(jnp.int32) for room in rooms[:-1])
    grads, loss = lax.switch(
        level,
        [
            functools.partial(middle, room=room, devices=devices, pairs=pairs, window=window)
            for room in rooms
        ],
        embedded,
    )
    returned = lax.all_to_all(grads, "pb", split_axis=0, concat_axis=0, tiled=True)
    return project_call(returned, normed, inverse), loss


def from_behind(value, axis, steps):
    count = lax.axis_size(axis)
    pairs = [(source, (source + steps) % count) for source in range(count)]
    return lax.ppermute(value, axis, pairs)


def similarity(queries, documents):
    return inverse_temp * lax.dot_general(
        queries, documents, (((1,), (1,)), ((), ())), preferred_element_type=jnp.float32
    )


def transposed(weights, queries):
    return lax.dot_general(
        weights, queries, (((0,), (0,)), ((), ())), preferred_element_type=jnp.float32
    )


def combine_docs(weights, documents):
    return jnp.dot(weights, documents, preferred_element_type=jnp.float32)


def skipped(listed, function, operands, out_shape):
    return lax.cond(
        listed,
        lambda inputs: function(*inputs),
        lambda inputs: jnp.zeros(out_shape, jnp.float32),
        operands,
    )


def row_plan(hidden, final_gain, last_row, pair_owner, hard_negatives):
    values = hidden.astype(jnp.float32)
    scale_row = lax.rsqrt(jnp.mean(values * values, axis=-1, keepdims=True) + token_eps)
    normed = (values * scale_row * final_gain.astype(jnp.float32)).astype(jnp.bfloat16)
    seq_count = last_row.shape[1]
    model_width = hidden.shape[1]
    pooled = normed[last_row[0]].astype(jnp.float32)
    inverse_norm = lax.rsqrt(jnp.sum(pooled * pooled, axis=-1, keepdims=True) + 1e-06)
    unit_vec = pooled * inverse_norm
    embedding = unit_vec.astype(jnp.bfloat16)
    devices = lax.axis_size("pb")
    capacity = 2 * seq_count // devices
    pair_count = pair_owner.shape[0]
    wanted = jnp.concatenate([pair_owner[:, 0], pair_owner[:, 1]])
    holder = wanted // seq_count
    within = wanted % seq_count
    entry_ids = jnp.arange(2 * pair_count, dtype=jnp.int32)
    earlier = (holder[None, :] == holder[:, None]) & (entry_ids[None, :] < entry_ids[:, None])
    position = jnp.sum(earlier.astype(jnp.int32), axis=1)
    request = jnp.full((devices, capacity), -1, jnp.int32).at[holder, position].set(within)
    served = lax.all_to_all(request, "pb", split_axis=0, concat_axis=0, tiled=True)
    outgoing = jnp.where(
        served[:, :, None] >= 0, embedding[jnp.maximum(served, 0)], jnp.zeros((), jnp.bfloat16)
    )
    received = lax.all_to_all(outgoing, "pb", split_axis=0, concat_axis=0, tiled=True)
    gathered = received[holder, position]
    queries = gathered[:pair_count]
    own_docs = gathered[pair_count:]
    listed_ids = hard_negatives[0]
    window = hard_negatives.shape[1]
    listed = [listed_ids[offset] >= 0 for offset in range(window)]
    neighbours = []
    moving = own_docs
    for offset in range(window):
        moving = from_behind(moving, "pb", -1)
        neighbours.append(moving)
    tile_shape = (pair_count, pair_count)
    score_blocks = [similarity(queries, own_docs)]
    for offset in range(window):
        score_blocks.append(
            skipped(listed[offset], similarity, (queries, neighbours[offset]), tile_shape)
        )
    all_scores = jnp.concatenate(score_blocks, axis=1)
    usable = jnp.concatenate(
        [jnp.ones((pair_count,), jnp.bool_)]
        + [jnp.broadcast_to(listed[offset], (pair_count,)) for offset in range(window)]
    )
    masked = jnp.where(usable[None, :], all_scores, -jnp.inf)
    row_max = jnp.max(masked, axis=1, keepdims=True)
    log_total = row_max + jnp.log(jnp.sum(jnp.exp(masked - row_max), axis=1, keepdims=True))
    diagonal = jnp.arange(pair_count, dtype=jnp.int32)
    positive = all_scores[diagonal, diagonal]
    block_loss = jnp.mean(log_total[:, 0] - positive).reshape(1)
    columns = jnp.arange((window + 1) * pair_count, dtype=jnp.int32)
    target = (columns[None, :] == diagonal[:, None]).astype(jnp.float32)
    coefficients = (inverse_temp * (jnp.exp(masked - log_total) - target)).astype(jnp.bfloat16)
    pieces = [
        coefficients[:, offset * pair_count : (offset + 1) * pair_count]
        for offset in range(window + 1)
    ]
    grad_shape = (pair_count, model_width)
    query_sum = combine_docs(pieces[0], own_docs)
    for offset in range(window):
        query_sum = query_sum + skipped(
            listed[offset], combine_docs, (pieces[offset + 1], neighbours[offset]), grad_shape
        )
    query_grad = query_sum.astype(jnp.bfloat16)
    own_part = transposed(pieces[0], queries).astype(jnp.bfloat16)
    partial_value = [
        skipped(listed[offset], transposed, (pieces[offset + 1], queries), grad_shape).astype(
            jnp.bfloat16
        )
        for offset in range(window)
    ]
    running = partial_value[window - 1].astype(jnp.float32)
    for offset in range(window):
        running = from_behind(running, "pb", 1)
        if offset + 1 < window:
            running = running + partial_value[window - 2 - offset].astype(jnp.float32)
    doc_grad = (own_part.astype(jnp.float32) + running).astype(jnp.bfloat16)
    answers = jnp.concatenate([query_grad, doc_grad], axis=0)
    returning = (
        jnp.zeros((devices, capacity, model_width), jnp.bfloat16).at[holder, position].set(answers)
    )
    returned = lax.all_to_all(returning, "pb", split_axis=0, concat_axis=0, tiled=True)
    slot_ids = jnp.where(served >= 0, served, seq_count).reshape(-1)
    emb_grad = (
        jnp.zeros((seq_count, model_width), jnp.bfloat16)
        .at[slot_ids]
        .set(returned.reshape(-1, model_width), mode="drop")
    )
    gradient = emb_grad.astype(jnp.float32)
    pooled_grad = gradient - unit_vec * jnp.sum(unit_vec * gradient, axis=-1, keepdims=True)
    return (pooled_grad, block_loss)


def solution(mesh):
    def local(hidden, final_gain, last_row, pair_owner, hard_negatives):
        plan = feature_plan if hidden.shape[1] >= lanes * mesh.shape["pb"] else row_plan
        return plan(hidden, final_gain, last_row, pair_owner, hard_negatives)

    return jax.shard_map(
        local,
        mesh=mesh,
        in_specs=(
            P(("groups", "pb"), None),
            P(),
            P(("groups", "pb"), None),
            P(("groups", "pb"), None),
            P(("groups", "pb"), None),
        ),
        out_specs=(P(("groups", "pb"), None), P(("groups", "pb"))),
        check_vma=False,
    )
```

```python
import functools

import jax
import jax.numpy as jnp
from jax import lax
from jax.experimental import pallas as pl
from jax.experimental.pallas import tpu as pltpu
from jax.sharding import PartitionSpec as P

inverse_temp = 50.0
token_eps = 1e-05
unit_eps = 1e-06
lanes = 128
bound_steps = 256.0
code_steps = 32000.0
vmem_limit = 56 * 1024 * 1024


def spread(target, at, value):
    count = value.shape[0]
    for half in range(2):
        target[pl.ds(2 * at + half, count, stride=2), :] = value[:, half * lanes : (half + 1) * lanes]


def gathered(source, at, count):
    halves = [source[pl.ds(2 * at + half, count, stride=2), :] for half in range(2)]
    return jnp.concatenate(halves, axis=1)


def row_pair(index):
    return pl.ds(pl.multiple_of(2 * index, 2), 2)


def norm_kernel(
    last_ref, hidden_ref, gain_ref, owner_ref, negative_ref, normed_ref, inv_ref, *emb_refs
):
    seqs, width = normed_ref.shape
    parts = len(emb_refs)
    piece = emb_refs[0].shape[1]
    pairs = owner_ref.shape[1]
    cuts = [slice(part * piece, (part + 1) * piece) for part in range(parts)]
    sources = lax.broadcasted_iota(jnp.int32, (seqs, seqs), 0)
    pick = jnp.where(sources == last_ref[...], 1.0, 0.0).astype(jnp.bfloat16)

    def folded(squares):
        return functools.reduce(
            jnp.add, [squares[:, at : at + lanes] for at in range(0, piece, lanes)]
        )

    total = jnp.zeros((seqs, lanes), jnp.float32)
    for cut in cuts:
        values = lax.dot_general(
            pick, hidden_ref[:, cut], (((0,), (0,)), ((), ())), preferred_element_type=jnp.float32
        )
        normed_ref[:, cut] = values.astype(jnp.bfloat16)
        total = total + folded(values * values)
    scale = lax.rsqrt(jnp.sum(total, axis=-1, keepdims=True) / width + token_eps)
    total = jnp.zeros((seqs, lanes), jnp.float32)
    for cut in cuts:
        values = normed_ref[:, cut].astype(jnp.float32)
        gain = gain_ref[cut].astype(jnp.float32).reshape(1, piece)
        normed = (values * scale * gain).astype(jnp.bfloat16)
        normed_ref[:, cut] = normed
        pooled = normed.astype(jnp.float32)
        total = total + folded(pooled * pooled)
    inverse = lax.rsqrt(jnp.sum(total, axis=-1, keepdims=True) + unit_eps)
    inv_ref[...] = jnp.broadcast_to(inverse, inv_ref.shape)

    owners = owner_ref[...].astype(jnp.float32)
    high = jnp.floor(owners * (1.0 / 256.0))
    low = owners - 256.0 * high
    row = lax.broadcasted_iota(jnp.int32, (16, pairs), 0)
    spot = lax.broadcasted_iota(jnp.int32, (16, pairs), 1)
    left = jnp.where(row == 0, low[:1], jnp.where(row == 1, high[:1], 0.0))
    right = jnp.where(row == 0, low[1:2], jnp.where(row == 1, high[1:2], 0.0))
    for offset in range(negative_ref.shape[1]):
        named = (negative_ref[0, offset] >= 0).astype(jnp.float32)
        left = jnp.where((row == 2) & (spot == offset), named, left)
    facts = jnp.concatenate([left, right], axis=1).astype(jnp.bfloat16)

    me = lax.axis_index("pb")
    for apart, emb_ref in enumerate(emb_refs):
        cut = pl.ds(pl.multiple_of((me ^ apart) * piece, piece), piece)
        emb_ref[:seqs] = (normed_ref[:, cut].astype(jnp.float32) * inverse).astype(jnp.bfloat16)
        emb_ref[seqs:] = facts


def norm_call(last_row, hidden, gain, owners, hard_negatives, parts):
    seqs, width = hidden.shape
    piece = width // parts
    whole = pl.BlockSpec(memory_space=pltpu.VMEM)
    return pl.pallas_call(
        norm_kernel,
        in_specs=[whole, whole, whole, whole, pl.BlockSpec(memory_space=pltpu.SMEM)],
        out_specs=[whole] * (parts + 2),
        out_shape=[
            jax.ShapeDtypeStruct((seqs, width), jnp.bfloat16),
            jax.ShapeDtypeStruct((seqs, lanes), jnp.float32),
        ]
        + [jax.ShapeDtypeStruct((seqs + 16, piece), jnp.bfloat16)] * parts,
        compiler_params=pltpu.CompilerParams(vmem_limit_bytes=vmem_limit),
        name="norm_rows",
    )(last_row, hidden, gain, owners, hard_negatives)


def score_kernel(
    blocks,
    pairs,
    window,
    *refs,
):
    emb_refs, (q_ref, d_ref, mine_ref, other_ref, own_ref, place_ref) = refs[:-14], refs[-14:-8]
    wide, picked, tiles, facts, own, named, sums, sems = refs[-8:]
    seqs = emb_refs[0].shape[0] - 16
    me = lax.axis_index("pb")
    for apart, emb_ref in enumerate(emb_refs):
        sent = emb_ref[seqs:, :].astype(jnp.float32)
        at = pl.ds(me ^ apart, 1)
        own_ref[at, :] = (sent[0:1] + 256.0 * sent[1:2]).astype(jnp.int32)
        facts[at, :] = sent[2:3, :lanes].astype(jnp.int32)
    fetches = [
        pltpu.make_async_copy(own_ref, own, sems.at[0]),
        pltpu.make_async_copy(facts, named, sems.at[1]),
    ]
    for fetch in fetches:
        fetch.start()

    for apart, emb_ref in enumerate(emb_refs):
        at = pl.multiple_of((me ^ apart) * seqs, seqs)
        spread(wide, at, emb_ref[:seqs, :].astype(jnp.float32))
    for fetch in fetches:
        fetch.wait()

    def place(block, count):
        place_ref[0, block] = block
        for offset in range(window):
            present = named[block, offset] > 0
            place_ref[offset + 1, block] = jnp.where(present, count, -1)
            count = count + present.astype(jnp.int32)
        return count

    used = lax.fori_loop(0, blocks, place, blocks)
    fine = pairs // blocks

    def clear(spot, carry):
        empty = jnp.zeros((2, blocks // 2, fine, pairs), jnp.float32)
        sums[:, :, pl.ds(pl.multiple_of(spot * fine, fine), fine), :] = empty
        return carry

    lax.fori_loop(used, sums.shape[2] // fine, clear, 0)
    unroll = 16

    def pick_block(block, carry):
        def pick_rows(step, inner):
            base = pl.multiple_of(step * unroll, unroll)
            rows = [wide[row_pair(own[block, base + k]), :] for k in range(unroll)]
            for k in range(unroll):
                picked[row_pair(base + k), :] = rows[k]
            return inner

        lax.fori_loop(0, 2 * pairs // unroll, pick_rows, 0)
        at = pl.multiple_of(block * pairs, pairs)
        q_ref[pl.ds(at, pairs), :] = gathered(picked, 0, pairs).astype(jnp.bfloat16)
        d_ref[pl.ds(at, pairs), :] = gathered(picked, pairs, pairs).astype(jnp.bfloat16)
        return carry

    lax.fori_loop(0, blocks, pick_block, 0)
    d_ref[blocks * pairs :, :] = d_ref[: window * pairs, :]
    core = me % 2

    def score_blocks(step, carry):
        at = pl.multiple_of(step * 2 * pairs, 2 * pairs)
        tiles[...] = inverse_temp * lax.dot_general(
            q_ref[pl.ds(at, 2 * pairs), :],
            d_ref[pl.ds(at, (window + 2) * pairs), :],
            (((1,), (1,)), ((), ())),
            preferred_element_type=jnp.float32,
        )
        for half in range(2):
            for column in range(window + 1):
                spot = place_ref[column, 2 * step + half]

                @pl.when(spot >= 0)
                def _():
                    row = pl.multiple_of(spot * fine, fine)
                    tile = tiles[
                        half * pairs : (half + 1) * pairs,
                        (half + column) * pairs : (half + column + 1) * pairs,
                    ]
                    parted = tile.reshape(blocks // 2, 2, fine, pairs)
                    for parity in range(2):
                        sums[parity, :, pl.ds(row, fine), :] = parted[:, parity]

        return carry

    lax.fori_loop(0, blocks // 2, score_blocks, 0)

    def part(chip, carry):
        mine_ref[chip] = sums[core, chip]
        other_ref[chip] = sums[1 - core, chip]
        return carry

    lax.fori_loop(0, blocks // 2, part, 0)


def score_call(embedded, room, blocks, pairs, window):
    rows, piece = embedded[0].shape
    fine = pairs // blocks
    whole = pl.BlockSpec(memory_space=pltpu.VMEM)
    scalars = pl.BlockSpec(memory_space=pltpu.SMEM)
    return pl.pallas_call(
        functools.partial(score_kernel, blocks, pairs, window),
        in_specs=[whole] * blocks,
        out_specs=[whole, whole, whole, whole, whole, scalars],
        out_shape=[
            jax.ShapeDtypeStruct((blocks * pairs, piece), jnp.bfloat16),
            jax.ShapeDtypeStruct(((blocks + window) * pairs, piece), jnp.bfloat16),
            jax.ShapeDtypeStruct((blocks // 2, room * fine, pairs), jnp.float32),
            jax.ShapeDtypeStruct((blocks // 2, room * fine, pairs), jnp.float32),
            jax.ShapeDtypeStruct((blocks, 2 * pairs), jnp.int32),
            jax.ShapeDtypeStruct((window + 1, blocks), jnp.int32),
        ],
        scratch_shapes=[
            pltpu.VMEM((2 * blocks * (rows - 16), lanes), jnp.float32),
            pltpu.VMEM((4 * pairs, lanes), jnp.float32),
            pltpu.VMEM((2 * pairs, (window + 2) * pairs), jnp.float32),
            pltpu.VMEM((blocks, lanes), jnp.int32),
            pltpu.SMEM((blocks, 2 * pairs), jnp.int32),
            pltpu.SMEM((blocks, lanes), jnp.int32),
            pltpu.VMEM((2, blocks // 2, room * fine, pairs), jnp.float32),
            pltpu.SemaphoreType.DMA((2,)),
        ],
        compiler_params=pltpu.CompilerParams(vmem_limit_bytes=vmem_limit),
        name="partial_scores",
    )(*embedded)


def merge_kernel(mine_ref, other_ref, own_ref, *code_refs):
    chips, rows, pairs = mine_ref.shape
    steps = code_refs[0].shape[0] - 1
    fine = rows // steps // 2
    chip = lax.axis_index("pb") // 2

    def largest(step, top):
        at = pl.multiple_of(step * 2 * fine, 2 * fine)
        size = jnp.abs(mine_ref[:, pl.ds(at, 2 * fine), :] + other_ref[:, pl.ds(at, 2 * fine), :])
        return jnp.maximum(top, jnp.max(size, axis=0))

    top = lax.fori_loop(0, steps, largest, jnp.zeros((2 * fine, pairs), jnp.float32))
    top = jnp.max(jnp.max(top, axis=1, keepdims=True), axis=0, keepdims=True)
    bound = jnp.ceil(jnp.minimum(top, 100.0) * bound_steps) + 1.0
    scale = code_steps * bound_steps / bound
    own_ref[...] = mine_ref[chip] + other_ref[chip]
    for hop, code_ref in enumerate(code_refs):
        target = chip ^ (hop + 1)

        def encode(step, carry):
            at = pl.multiple_of(step * 2 * fine, 2 * fine)
            there = pl.ds(at, 2 * fine)
            codes = jnp.round((mine_ref[target, there, :] + other_ref[target, there, :]) * scale)
            code_ref[step] = codes.astype(jnp.int32).astype(jnp.int16)
            return carry

        lax.fori_loop(0, steps, encode, 0)
        code_ref[steps] = jnp.broadcast_to(bound, (2 * fine, pairs)).astype(jnp.int32).astype(jnp.int16)


def merge_call(mine, other, blocks):
    chips, rows, pairs = mine.shape
    fine = pairs // blocks
    whole = pl.BlockSpec(memory_space=pltpu.VMEM)
    coded = jax.ShapeDtypeStruct((rows // (2 * fine) + 1, 2 * fine, pairs), jnp.int16)
    return pl.pallas_call(
        merge_kernel,
        in_specs=[whole, whole],
        out_specs=[whole] * chips,
        out_shape=[jax.ShapeDtypeStruct((rows, pairs), jnp.float32)] + [coded] * (chips - 1),
        compiler_params=pltpu.CompilerParams(vmem_limit_bytes=vmem_limit),
        name="merge_scores",
    )(mine, other)


def softmax_kernel(blocks, window, place_ref, own_ref, *refs):
    code_refs, (c_ref, packed, masked) = refs[:-3], refs[-3:]
    room, fine, pairs = packed.shape
    count = blocks * fine
    unit = 1.0 / (code_steps * bound_steps)
    scales = [ref[room // 2].astype(jnp.int32).astype(jnp.float32) * unit for ref in code_refs]

    def decode(step, carry):
        both = own_ref[pl.ds(pl.multiple_of(step * 2 * fine, 2 * fine), 2 * fine), :]
        for ref, scale in zip(code_refs, scales):
            both = both + ref[step].astype(jnp.int32).astype(jnp.float32) * scale
        packed[2 * step] = both[:fine]
        packed[2 * step + 1] = both[fine:]
        return carry

    lax.fori_loop(0, room // 2, decode, 0)
    for block in range(blocks):
        for column in range(window + 1):
            spot = place_ref[column, block]
            tile = packed[jnp.maximum(spot, 0)]
            masked[block * fine : (block + 1) * fine, column * pairs : (column + 1) * pairs] = (
                jnp.where(spot >= 0, tile, -jnp.inf)
            )
    row = lax.broadcasted_iota(jnp.int32, (count, pairs), 0)
    lane = lax.broadcasted_iota(jnp.int32, (count, pairs), 1)
    target = lane == lax.axis_index("pb") * fine + row % fine
    pieces = [masked[:, column * pairs : (column + 1) * pairs] for column in range(window + 1)]
    row_max = jnp.max(functools.reduce(jnp.maximum, pieces), axis=1, keepdims=True)
    total = functools.reduce(jnp.add, [jnp.exp(piece - row_max) for piece in pieces])
    log_total = row_max + jnp.log(jnp.sum(total, axis=1, keepdims=True))
    positive = jnp.sum(jnp.where(target, pieces[0], 0.0), axis=1, keepdims=True)
    for column, piece in enumerate(pieces):
        share = jnp.exp(piece - log_total)
        if column == 0:
            share = share - jnp.where(target, 1.0, 0.0)
        masked[:, column * pairs : (column + 1) * pairs] = inverse_temp * share
    for block in range(blocks):
        for column in range(window + 1):
            spot = place_ref[column, block]

            @pl.when(spot >= 0)
            def _():
                packed[spot] = masked[
                    block * fine : (block + 1) * fine, column * pairs : (column + 1) * pairs
                ]

    for step in range(room // 2):
        both = jnp.concatenate([packed[2 * step], packed[2 * step + 1]], axis=0)
        c_ref[step] = both.astype(jnp.bfloat16)
    losses = jnp.sum(
        jnp.where(lane == row // fine, log_total - positive, 0.0), axis=0, keepdims=True
    )
    coarse = losses.astype(jnp.bfloat16).astype(jnp.float32)
    rank = lax.broadcasted_iota(jnp.int32, (2 * fine, pairs), 0)
    both = jnp.where(rank == 0, coarse, jnp.where(rank == 1, losses - coarse, 0.0))
    c_ref[room // 2] = both.astype(jnp.bfloat16)


def softmax_call(place, own_scores, codes, blocks, window):
    steps, fine, pairs = codes[0].shape
    room, fine = 2 * (steps - 1), fine // 2
    whole = pl.BlockSpec(memory_space=pltpu.VMEM)
    return pl.pallas_call(
        functools.partial(softmax_kernel, blocks, window),
        in_specs=[pl.BlockSpec(memory_space=pltpu.SMEM), whole] + [whole] * len(codes),
        out_specs=whole,
        out_shape=jax.ShapeDtypeStruct((room // 2 + 1, 2 * fine, pairs), jnp.bfloat16),
        scratch_shapes=[
            pltpu.VMEM((room, fine, pairs), jnp.float32),
            pltpu.VMEM((blocks * fine, (window + 1) * pairs), jnp.float32),
        ],
        compiler_params=pltpu.CompilerParams(vmem_limit_bytes=vmem_limit),
        name="softmax_rows",
    )(place, own_scores, *codes)


def grad_kernel(
    blocks,
    pairs,
    window,
    own_ref,
    place_ref,
    q_ref,
    d_ref,
    *refs,
):
    part_refs, out_refs = refs[: -blocks - 6], refs[-blocks - 6 : -6]
    loss_ref, wide, dsum, picked, packed, square = refs[-6:]
    fine = pairs // blocks
    room = packed.shape[1]
    me = lax.axis_index("pb")
    masks = swap_masks(blocks)
    unroll = 16
    losses = 0.0
    for part in part_refs:
        sent = part[:, room // 2].astype(jnp.float32)
        losses = losses + jnp.sum(sent[:, 0, :] + sent[:, 1, :], axis=0, keepdims=True) / pairs
    lane = lax.broadcasted_iota(jnp.int32, losses.shape, 1)
    mine = jnp.where(lane == me, losses, 0.0)
    loss_ref[...] = jnp.broadcast_to(jnp.sum(mine, axis=1, keepdims=True), loss_ref.shape)
    dsum[...] = jnp.zeros_like(dsum)
    square[...] = jnp.zeros_like(square)

    def unpack(step, carry):
        for part, mask in zip(part_refs, masks):
            both = part[:, step].astype(jnp.float32)
            for at, apart in enumerate(mask):
                packed[me ^ apart, 2 * step] = both[at, :fine]
                packed[me ^ apart, 2 * step + 1] = both[at, fine:]
        return carry

    lax.fori_loop(0, room // 2, unpack, 0)

    def scatter_rows(block, offset, start):
        def step_rows(step, inner):
            base = pl.multiple_of(step * unroll, unroll)
            rows = [picked[row_pair(start + base + k), :] for k in range(unroll)]
            for k in range(unroll):
                wide[row_pair(own_ref[block, offset + base + k]), :] = rows[k]
            return inner

        lax.fori_loop(0, pairs // unroll, step_rows, 0)

    def two_blocks(step, carry):
        for half in range(2):
            for column in range(window + 1):
                spot = place_ref[column, 2 * step + half]
                tile = packed[:, jnp.maximum(spot, 0)].reshape(pairs, pairs)
                square[
                    half * pairs : (half + 1) * pairs,
                    (half + column) * pairs : (half + column + 1) * pairs,
                ] = jnp.where(spot >= 0, tile, 0.0).astype(jnp.bfloat16)
        at = pl.multiple_of(step * 2 * pairs, 2 * pairs)
        there = pl.ds(at, (window + 2) * pairs)
        coefficients = square[...]
        summed = jnp.dot(coefficients, d_ref[there, :], preferred_element_type=jnp.float32)
        spread(picked, 0, summed)
        dsum[there, :] += lax.dot_general(
            coefficients,
            q_ref[pl.ds(at, 2 * pairs), :],
            (((0,), (0,)), ((), ())),
            preferred_element_type=jnp.float32,
        )
        for half in range(2):
            scatter_rows(2 * step + half, 0, half * pairs)
        return carry

    lax.fori_loop(0, blocks // 2, two_blocks, 0)
    dsum[: window * pairs, :] += dsum[blocks * pairs :, :]

    def doc_block(block, carry):
        at = pl.multiple_of(block * pairs, pairs)
        spread(picked, 0, dsum[pl.ds(at, pairs), :])
        scatter_rows(block, pairs, 0)
        return carry

    lax.fori_loop(0, blocks, doc_block, 0)
    slots = out_refs[0].shape[0]
    for apart, out_ref in enumerate(out_refs):
        at = pl.multiple_of((me ^ apart) * slots, slots)
        out_ref[...] = gathered(wide, at, slots).astype(jnp.bfloat16)


def grad_call(own, place, parts, queries, documents, blocks, pairs, window):
    count, piece = queries.shape
    seqs = 2 * count
    room = 2 * (parts[0].shape[1] - 1)
    whole = pl.BlockSpec(memory_space=pltpu.VMEM)
    scalars = pl.BlockSpec(memory_space=pltpu.SMEM)
    return pl.pallas_call(
        functools.partial(grad_kernel, blocks, pairs, window),
        in_specs=[scalars, scalars, whole, whole] + [whole] * len(parts),
        out_specs=[whole] * (blocks + 1),
        out_shape=[jax.ShapeDtypeStruct((seqs // blocks, piece), jnp.bfloat16)] * blocks
        + [jax.ShapeDtypeStruct((1, lanes), jnp.float32)],
        scratch_shapes=[
            pltpu.VMEM((2 * seqs, lanes), jnp.float32),
            pltpu.VMEM(((blocks + window) * pairs, piece), jnp.float32),
            pltpu.VMEM((4 * pairs, lanes), jnp.float32),
            pltpu.VMEM((blocks, room, pairs // blocks, pairs), jnp.float32),
            pltpu.VMEM((2 * pairs, (window + 2) * pairs), jnp.bfloat16),
        ],
        compiler_params=pltpu.CompilerParams(vmem_limit_bytes=vmem_limit),
        name="slice_grads",
    )(own, place, queries, documents, *parts)


def project_kernel(normed_ref, inv_ref, *refs):
    grad_refs, out_ref = refs[:-1], refs[-1]
    piece = grad_refs[0].shape[1]
    me = lax.axis_index("pb")
    inverse = inv_ref[:, :1]
    cuts = [
        pl.ds(pl.multiple_of((me ^ apart) * piece, piece), piece) for apart in range(len(grad_refs))
    ]
    total = 0.0
    for cut, grad_ref in zip(cuts, grad_refs):
        unit = normed_ref[:, cut].astype(jnp.float32) * inverse
        total = total + unit * grad_ref[...].astype(jnp.float32)
    along = jnp.sum(total, axis=-1, keepdims=True)
    for cut, grad_ref in zip(cuts, grad_refs):
        unit = normed_ref[:, cut].astype(jnp.float32) * inverse
        out_ref[:, cut] = grad_ref[...].astype(jnp.float32) - unit * along


def project_call(returned, normed, inverse):
    seqs, piece = returned[0].shape
    width = normed.shape[1]
    rows = 64
    return pl.pallas_call(
        project_kernel,
        grid=(seqs // rows,),
        in_specs=[
            pl.BlockSpec((rows, width), lambda i: (i, 0)),
            pl.BlockSpec((rows, lanes), lambda i: (i, 0)),
        ]
        + [pl.BlockSpec((rows, piece), lambda i: (i, 0))] * len(returned),
        out_specs=pl.BlockSpec((rows, width), lambda i: (i, 0)),
        out_shape=jax.ShapeDtypeStruct((seqs, width), jnp.float32),
        compiler_params=pltpu.CompilerParams(vmem_limit_bytes=vmem_limit),
        name="project_out",
    )(normed, inverse, *returned)


def swapped(value, apart):
    pairs = [(at, at ^ apart) for at in range(lax.axis_size("pb"))]
    return lax.ppermute(value, "pb", pairs)


def swap_steps(devices):
    return [1 << bit for bit in reversed(range(devices.bit_length() - 1))]


def swap_masks(devices):
    known, masks = [0], [[0]]
    for apart in swap_steps(devices):
        masks.append([mask ^ apart for mask in known])
        known = known + masks[-1]
    return masks


def gather_all(value):
    held = value[None]
    parts = [held]
    for apart in swap_steps(lax.axis_size("pb")):
        arrived = swapped(held, apart)
        parts.append(arrived)
        held = jnp.concatenate([held, arrived], axis=0)
    return parts


def exchange(blocks):
    arrived = {0: blocks[0]}
    for apart in reversed(range(1, len(blocks))):
        arrived[apart] = swapped(blocks[apart], apart)
    return [arrived[apart] for apart in range(len(blocks))]


def middle(embedded, room, devices, pairs, window):
    queries, documents, mine, other, own, place = score_call(
        embedded, room, devices, pairs, window
    )
    own_scores, *codes = merge_call(mine, swapped(other, 1), devices)
    codes = [swapped(code, 2 * (hop + 1)) for hop, code in enumerate(codes)]
    parts = gather_all(softmax_call(place, own_scores, codes, devices, window))
    *grads, loss = grad_call(own, place, parts, queries, documents, devices, pairs, window)
    return grads, loss[0, :1]


def feature_plan(hidden, final_gain, last_row, pair_owner, hard_negatives):
    devices = lax.axis_size("pb")
    seqs, width = hidden.shape
    pairs = pair_owner.shape[0]
    window = hard_negatives.shape[1]
    normed, inverse, *embedding = norm_call(
        last_row, hidden, final_gain, pair_owner.T, hard_negatives, devices
    )
    embedded = exchange(embedding)
    most = devices * (window + 1)
    rooms = [most * part // 20 for part in (10, 11, 12, 13, 14, 16, 20)]
    flags = sum(block[seqs + 2, :window].astype(jnp.float32) for block in embedded)
    used = devices + jnp.sum(flags)
    level = sum((used > room).astype(jnp.int32) for room in rooms[:-1])
    grads, loss = lax.switch(
        level,
        [
            functools.partial(middle, room=room, devices=devices, pairs=pairs, window=window)
            for room in rooms
        ],
        embedded,
    )
    return project_call(exchange(grads), normed, inverse), loss


def from_behind(value, axis, steps):
    count = lax.axis_size(axis)
    pairs = [(source, (source + steps) % count) for source in range(count)]
    return lax.ppermute(value, axis, pairs)


def similarity(queries, documents):
    return inverse_temp * lax.dot_general(
        queries, documents, (((1,), (1,)), ((), ())), preferred_element_type=jnp.float32
    )


def transposed(weights, queries):
    return lax.dot_general(
        weights, queries, (((0,), (0,)), ((), ())), preferred_element_type=jnp.float32
    )


def combine_docs(weights, documents):
    return jnp.dot(weights, documents, preferred_element_type=jnp.float32)


def skipped(listed, function, operands, out_shape):
    return lax.cond(
        listed,
        lambda inputs: function(*inputs),
        lambda inputs: jnp.zeros(out_shape, jnp.float32),
        operands,
    )


def row_plan(hidden, final_gain, last_row, pair_owner, hard_negatives):
    values = hidden.astype(jnp.float32)
    scale_row = lax.rsqrt(jnp.mean(values * values, axis=-1, keepdims=True) + token_eps)
    normed = (values * scale_row * final_gain.astype(jnp.float32)).astype(jnp.bfloat16)
    seq_count = last_row.shape[1]
    model_width = hidden.shape[1]
    pooled = normed[last_row[0]].astype(jnp.float32)
    inverse_norm = lax.rsqrt(jnp.sum(pooled * pooled, axis=-1, keepdims=True) + 1e-06)
    unit_vec = pooled * inverse_norm
    embedding = unit_vec.astype(jnp.bfloat16)
    devices = lax.axis_size("pb")
    capacity = 2 * seq_count // devices
    pair_count = pair_owner.shape[0]
    wanted = jnp.concatenate([pair_owner[:, 0], pair_owner[:, 1]])
    holder = wanted // seq_count
    within = wanted % seq_count
    entry_ids = jnp.arange(2 * pair_count, dtype=jnp.int32)
    earlier = (holder[None, :] == holder[:, None]) & (entry_ids[None, :] < entry_ids[:, None])
    position = jnp.sum(earlier.astype(jnp.int32), axis=1)
    request = jnp.full((devices, capacity), -1, jnp.int32).at[holder, position].set(within)
    served = lax.all_to_all(request, "pb", split_axis=0, concat_axis=0, tiled=True)
    outgoing = jnp.where(
        served[:, :, None] >= 0, embedding[jnp.maximum(served, 0)], jnp.zeros((), jnp.bfloat16)
    )
    received = lax.all_to_all(outgoing, "pb", split_axis=0, concat_axis=0, tiled=True)
    gathered = received[holder, position]
    queries = gathered[:pair_count]
    own_docs = gathered[pair_count:]
    listed_ids = hard_negatives[0]
    window = hard_negatives.shape[1]
    listed = [listed_ids[offset] >= 0 for offset in range(window)]
    neighbours = []
    moving = own_docs
    for offset in range(window):
        moving = from_behind(moving, "pb", -1)
        neighbours.append(moving)
    tile_shape = (pair_count, pair_count)
    score_blocks = [similarity(queries, own_docs)]
    for offset in range(window):
        score_blocks.append(
            skipped(listed[offset], similarity, (queries, neighbours[offset]), tile_shape)
        )
    all_scores = jnp.concatenate(score_blocks, axis=1)
    usable = jnp.concatenate(
        [jnp.ones((pair_count,), jnp.bool_)]
        + [jnp.broadcast_to(listed[offset], (pair_count,)) for offset in range(window)]
    )
    masked = jnp.where(usable[None, :], all_scores, -jnp.inf)
    row_max = jnp.max(masked, axis=1, keepdims=True)
    log_total = row_max + jnp.log(jnp.sum(jnp.exp(masked - row_max), axis=1, keepdims=True))
    diagonal = jnp.arange(pair_count, dtype=jnp.int32)
    positive = all_scores[diagonal, diagonal]
    block_loss = jnp.mean(log_total[:, 0] - positive).reshape(1)
    columns = jnp.arange((window + 1) * pair_count, dtype=jnp.int32)
    target = (columns[None, :] == diagonal[:, None]).astype(jnp.float32)
    coefficients = (inverse_temp * (jnp.exp(masked - log_total) - target)).astype(jnp.bfloat16)
    pieces = [
        coefficients[:, offset * pair_count : (offset + 1) * pair_count]
        for offset in range(window + 1)
    ]
    grad_shape = (pair_count, model_width)
    query_sum = combine_docs(pieces[0], own_docs)
    for offset in range(window):
        query_sum = query_sum + skipped(
            listed[offset], combine_docs, (pieces[offset + 1], neighbours[offset]), grad_shape
        )
    query_grad = query_sum.astype(jnp.bfloat16)
    own_part = transposed(pieces[0], queries).astype(jnp.bfloat16)
    partial_value = [
        skipped(listed[offset], transposed, (pieces[offset + 1], queries), grad_shape).astype(
            jnp.bfloat16
        )
        for offset in range(window)
    ]
    running = partial_value[window - 1].astype(jnp.float32)
    for offset in range(window):
        running = from_behind(running, "pb", 1)
        if offset + 1 < window:
            running = running + partial_value[window - 2 - offset].astype(jnp.float32)
    doc_grad = (own_part.astype(jnp.float32) + running).astype(jnp.bfloat16)
    answers = jnp.concatenate([query_grad, doc_grad], axis=0)
    returning = (
        jnp.zeros((devices, capacity, model_width), jnp.bfloat16).at[holder, position].set(answers)
    )
    returned = lax.all_to_all(returning, "pb", split_axis=0, concat_axis=0, tiled=True)
    slot_ids = jnp.where(served >= 0, served, seq_count).reshape(-1)
    emb_grad = (
        jnp.zeros((seq_count, model_width), jnp.bfloat16)
        .at[slot_ids]
        .set(returned.reshape(-1, model_width), mode="drop")
    )
    gradient = emb_grad.astype(jnp.float32)
    pooled_grad = gradient - unit_vec * jnp.sum(unit_vec * gradient, axis=-1, keepdims=True)
    return (pooled_grad, block_loss)


def solution(mesh):
    def local(hidden, final_gain, last_row, pair_owner, hard_negatives):
        plan = feature_plan if hidden.shape[1] >= lanes * mesh.shape["pb"] else row_plan
        return plan(hidden, final_gain, last_row, pair_owner, hard_negatives)

    return jax.shard_map(
        local,
        mesh=mesh,
        in_specs=(
            P(("groups", "pb"), None),
            P(),
            P(("groups", "pb"), None),
            P(("groups", "pb"), None),
            P(("groups", "pb"), None),
        ),
        out_specs=(P(("groups", "pb"), None), P(("groups", "pb"))),
        check_vma=False,
    )
```

```python
import functools

import jax
import jax.numpy as jnp
from jax import lax
from jax.experimental import pallas as pl
from jax.experimental.pallas import tpu as pltpu
from jax.sharding import PartitionSpec as P

inverse_temp = 50.0
token_eps = 1e-05
unit_eps = 1e-06
lanes = 128
bound_steps = 256.0
code_steps = 32000.0
vmem_limit = 56 * 1024 * 1024


def spread(target, at, value):
    count = value.shape[0]
    for half in range(2):
        target[pl.ds(2 * at + half, count, stride=2), :] = value[:, half * lanes : (half + 1) * lanes]


def gathered(source, at, count):
    halves = [source[pl.ds(2 * at + half, count, stride=2), :] for half in range(2)]
    return jnp.concatenate(halves, axis=1)


def row_pair(index):
    return pl.ds(pl.multiple_of(2 * index, 2), 2)


def norm_kernel(
    last_ref, hidden_ref, gain_ref, owner_ref, negative_ref, normed_ref, inv_ref, *emb_refs
):
    seqs, width = normed_ref.shape
    parts = len(emb_refs)
    piece = emb_refs[0].shape[1]
    pairs = owner_ref.shape[1]
    cuts = [slice(part * piece, (part + 1) * piece) for part in range(parts)]
    sources = lax.broadcasted_iota(jnp.int32, (seqs, seqs), 0)
    pick = jnp.where(sources == last_ref[...], 1.0, 0.0).astype(jnp.bfloat16)

    def folded(squares):
        return functools.reduce(
            jnp.add, [squares[:, at : at + lanes] for at in range(0, piece, lanes)]
        )

    total = jnp.zeros((seqs, lanes), jnp.float32)
    for cut in cuts:
        values = lax.dot_general(
            pick, hidden_ref[:, cut], (((0,), (0,)), ((), ())), preferred_element_type=jnp.float32
        )
        normed_ref[:, cut] = values.astype(jnp.bfloat16)
        total = total + folded(values * values)
    scale = lax.rsqrt(jnp.sum(total, axis=-1, keepdims=True) / width + token_eps)
    total = jnp.zeros((seqs, lanes), jnp.float32)
    for cut in cuts:
        values = normed_ref[:, cut].astype(jnp.float32)
        gain = gain_ref[cut].astype(jnp.float32).reshape(1, piece)
        normed = (values * scale * gain).astype(jnp.bfloat16)
        normed_ref[:, cut] = normed
        pooled = normed.astype(jnp.float32)
        total = total + folded(pooled * pooled)
    inverse = lax.rsqrt(jnp.sum(total, axis=-1, keepdims=True) + unit_eps)
    inv_ref[...] = jnp.broadcast_to(inverse, inv_ref.shape)

    owners = owner_ref[...].astype(jnp.float32)
    high = jnp.floor(owners * (1.0 / 256.0))
    low = owners - 256.0 * high
    row = lax.broadcasted_iota(jnp.int32, (16, pairs), 0)
    spot = lax.broadcasted_iota(jnp.int32, (16, pairs), 1)
    left = jnp.where(row == 0, low[:1], jnp.where(row == 1, high[:1], 0.0))
    right = jnp.where(row == 0, low[1:2], jnp.where(row == 1, high[1:2], 0.0))
    for offset in range(negative_ref.shape[1]):
        named = (negative_ref[0, offset] >= 0).astype(jnp.float32)
        left = jnp.where((row == 2) & (spot == offset), named, left)
    facts = jnp.concatenate([left, right], axis=1).astype(jnp.bfloat16)

    me = lax.axis_index("pb")
    for apart, emb_ref in enumerate(emb_refs):
        cut = pl.ds(pl.multiple_of((me ^ apart) * piece, piece), piece)
        emb_ref[:seqs] = (normed_ref[:, cut].astype(jnp.float32) * inverse).astype(jnp.bfloat16)
        emb_ref[seqs:] = facts


def norm_call(last_row, hidden, gain, owners, hard_negatives, parts):
    seqs, width = hidden.shape
    piece = width // parts
    whole = pl.BlockSpec(memory_space=pltpu.VMEM)
    return pl.pallas_call(
        norm_kernel,
        in_specs=[whole, whole, whole, whole, pl.BlockSpec(memory_space=pltpu.SMEM)],
        out_specs=[whole] * (parts + 2),
        out_shape=[
            jax.ShapeDtypeStruct((seqs, width), jnp.bfloat16),
            jax.ShapeDtypeStruct((seqs, lanes), jnp.float32),
        ]
        + [jax.ShapeDtypeStruct((seqs + 16, piece), jnp.bfloat16)] * parts,
        compiler_params=pltpu.CompilerParams(vmem_limit_bytes=vmem_limit),
        name="norm_rows",
    )(last_row, hidden, gain, owners, hard_negatives)


def score_kernel(
    blocks,
    pairs,
    window,
    *refs,
):
    emb_refs, (q_ref, d_ref, mine_ref, other_ref, top_ref, own_ref, place_ref) = refs[:-14], refs[-14:-7]
    wide, picked, tiles, facts, own, named, sems = refs[-7:]
    seqs = emb_refs[0].shape[0] - 16
    me = lax.axis_index("pb")
    for apart, emb_ref in enumerate(emb_refs):
        sent = emb_ref[seqs:, :].astype(jnp.float32)
        at = pl.ds(me ^ apart, 1)
        own_ref[at, :] = (sent[0:1] + 256.0 * sent[1:2]).astype(jnp.int32)
        facts[at, :] = sent[2:3, :lanes].astype(jnp.int32)
    fetches = [
        pltpu.make_async_copy(own_ref, own, sems.at[0]),
        pltpu.make_async_copy(facts, named, sems.at[1]),
    ]
    for fetch in fetches:
        fetch.start()

    for apart, emb_ref in enumerate(emb_refs):
        at = pl.multiple_of((me ^ apart) * seqs, seqs)
        spread(wide, at, emb_ref[:seqs, :].astype(jnp.float32))
    for fetch in fetches:
        fetch.wait()

    def place(block, count):
        place_ref[0, block] = block
        for offset in range(window):
            present = named[block, offset] > 0
            place_ref[offset + 1, block] = jnp.where(present, count, -1)
            count = count + present.astype(jnp.int32)
        return count

    used = lax.fori_loop(0, blocks, place, blocks)
    fine = pairs // blocks

    def clear(spot, carry):
        empty = jnp.zeros((blocks // 2, fine, pairs), jnp.float32)
        at = pl.ds(pl.multiple_of(spot * fine, fine), fine)
        mine_ref[:, at, :] = empty
        other_ref[:, at, :] = empty
        return carry

    lax.fori_loop(used, mine_ref.shape[1] // fine, clear, 0)
    unroll = 32

    def pick_block(block, carry):
        def pick_rows(step, inner):
            base = pl.multiple_of(step * unroll, unroll)
            rows = [wide[row_pair(own[block, base + k]), :] for k in range(unroll)]
            for k in range(unroll):
                picked[row_pair(base + k), :] = rows[k]
            return inner

        lax.fori_loop(0, 2 * pairs // unroll, pick_rows, 0)
        at = pl.multiple_of(block * pairs, pairs)
        q_ref[pl.ds(at, pairs), :] = gathered(picked, 0, pairs).astype(jnp.bfloat16)
        d_ref[pl.ds(at, pairs), :] = gathered(picked, pairs, pairs).astype(jnp.bfloat16)
        return carry

    lax.fori_loop(0, blocks, pick_block, 0)
    d_ref[blocks * pairs :, :] = d_ref[: window * pairs, :]
    even = me % 2 == 0
    top_ref[...] = jnp.zeros_like(top_ref)

    def score_blocks(step, carry):
        at = pl.multiple_of(step * 2 * pairs, 2 * pairs)
        tiles[...] = inverse_temp * lax.dot_general(
            q_ref[pl.ds(at, 2 * pairs), :],
            d_ref[pl.ds(at, (window + 2) * pairs), :],
            (((1,), (1,)), ((), ())),
            preferred_element_type=jnp.float32,
        )
        for half in range(2):
            for column in range(window + 1):
                spot = place_ref[column, 2 * step + half]

                @pl.when(spot >= 0)
                def _():
                    row = pl.multiple_of(spot * fine, fine)
                    tile = tiles[
                        half * pairs : (half + 1) * pairs,
                        (half + column) * pairs : (half + column + 1) * pairs,
                    ]
                    parted = tile.reshape(blocks // 2, 2, fine, pairs)
                    first, second = parted[:, 0], parted[:, 1]
                    mine_ref[:, pl.ds(row, fine), :] = jnp.where(even, first, second)
                    other_ref[:, pl.ds(row, fine), :] = jnp.where(even, second, first)
                    size = jnp.maximum(jnp.abs(first), jnp.abs(second))
                    top_ref[...] = jnp.maximum(top_ref[...], jnp.max(size, axis=0))

        return carry

    lax.fori_loop(0, blocks // 2, score_blocks, 0)


def score_call(embedded, room, blocks, pairs, window):
    rows, piece = embedded[0].shape
    fine = pairs // blocks
    whole = pl.BlockSpec(memory_space=pltpu.VMEM)
    scalars = pl.BlockSpec(memory_space=pltpu.SMEM)
    return pl.pallas_call(
        functools.partial(score_kernel, blocks, pairs, window),
        in_specs=[whole] * blocks,
        out_specs=[whole, whole, whole, whole, whole, whole, scalars],
        out_shape=[
            jax.ShapeDtypeStruct((blocks * pairs, piece), jnp.bfloat16),
            jax.ShapeDtypeStruct(((blocks + window) * pairs, piece), jnp.bfloat16),
            jax.ShapeDtypeStruct((blocks // 2, room * fine, pairs), jnp.float32),
            jax.ShapeDtypeStruct((blocks // 2, room * fine, pairs), jnp.float32),
            jax.ShapeDtypeStruct((fine, pairs), jnp.float32),
            jax.ShapeDtypeStruct((blocks, 2 * pairs), jnp.int32),
            jax.ShapeDtypeStruct((window + 1, blocks), jnp.int32),
        ],
        scratch_shapes=[
            pltpu.VMEM((2 * blocks * (rows - 16), lanes), jnp.float32),
            pltpu.VMEM((4 * pairs, lanes), jnp.float32),
            pltpu.VMEM((2 * pairs, (window + 2) * pairs), jnp.float32),
            pltpu.VMEM((blocks, lanes), jnp.int32),
            pltpu.SMEM((blocks, 2 * pairs), jnp.int32),
            pltpu.SMEM((blocks, lanes), jnp.int32),
            pltpu.SemaphoreType.DMA((2,)),
        ],
        compiler_params=pltpu.CompilerParams(vmem_limit_bytes=vmem_limit),
        name="partial_scores",
    )(*embedded)


def merge_kernel(mine_ref, other_ref, top_ref, other_top_ref, own_ref, *code_refs):
    chips, rows, pairs = mine_ref.shape
    steps = code_refs[0].shape[0] - 1
    fine = rows // steps // 2
    chip = lax.axis_index("pb") // 2

    def highest(ref):
        return jnp.max(jnp.max(ref[...], axis=1, keepdims=True), axis=0, keepdims=True)

    top = highest(top_ref) + highest(other_top_ref)
    bound = jnp.ceil(top * bound_steps) + 1.0
    scale = code_steps * bound_steps / bound
    own_ref[...] = mine_ref[chip] + other_ref[chip]
    for hop, code_ref in enumerate(code_refs):
        target = chip ^ (hop + 1)

        def encode(step, carry):
            at = pl.multiple_of(step * 2 * fine, 2 * fine)
            there = pl.ds(at, 2 * fine)
            codes = jnp.round((mine_ref[target, there, :] + other_ref[target, there, :]) * scale)
            code_ref[step] = codes.astype(jnp.int32).astype(jnp.int16)
            return carry

        lax.fori_loop(0, steps, encode, 0)
        code_ref[steps] = jnp.broadcast_to(bound, (2 * fine, pairs)).astype(jnp.int32).astype(jnp.int16)


def merge_call(mine, other, top, other_top, blocks):
    chips, rows, pairs = mine.shape
    fine = pairs // blocks
    whole = pl.BlockSpec(memory_space=pltpu.VMEM)
    coded = jax.ShapeDtypeStruct((rows // (2 * fine) + 1, 2 * fine, pairs), jnp.int16)
    return pl.pallas_call(
        merge_kernel,
        in_specs=[whole] * 4,
        out_specs=[whole] * chips,
        out_shape=[jax.ShapeDtypeStruct((rows, pairs), jnp.float32)] + [coded] * (chips - 1),
        compiler_params=pltpu.CompilerParams(vmem_limit_bytes=vmem_limit),
        name="merge_scores",
    )(mine, other, top, other_top)


def softmax_kernel(blocks, window, place_ref, own_ref, *refs):
    code_refs, (c_ref, packed, masked) = refs[:-3], refs[-3:]
    room, fine, pairs = packed.shape
    count = blocks * fine
    unit = 1.0 / (code_steps * bound_steps)
    scales = [ref[room // 2].astype(jnp.int32).astype(jnp.float32) * unit for ref in code_refs]

    def decode(step, carry):
        both = own_ref[pl.ds(pl.multiple_of(step * 2 * fine, 2 * fine), 2 * fine), :]
        for ref, scale in zip(code_refs, scales):
            both = both + ref[step].astype(jnp.int32).astype(jnp.float32) * scale
        packed[2 * step] = both[:fine]
        packed[2 * step + 1] = both[fine:]
        return carry

    lax.fori_loop(0, room // 2, decode, 0)
    for block in range(blocks):
        for column in range(window + 1):
            spot = place_ref[column, block]
            tile = packed[jnp.maximum(spot, 0)]
            masked[block * fine : (block + 1) * fine, column * pairs : (column + 1) * pairs] = (
                jnp.where(spot >= 0, tile, -jnp.inf)
            )
    row = lax.broadcasted_iota(jnp.int32, (count, pairs), 0)
    lane = lax.broadcasted_iota(jnp.int32, (count, pairs), 1)
    target = lane == lax.axis_index("pb") * fine + row % fine
    pieces = [masked[:, column * pairs : (column + 1) * pairs] for column in range(window + 1)]
    row_max = jnp.max(functools.reduce(jnp.maximum, pieces), axis=1, keepdims=True)
    total = functools.reduce(jnp.add, [jnp.exp(piece - row_max) for piece in pieces])
    log_total = row_max + jnp.log(jnp.sum(total, axis=1, keepdims=True))
    positive = jnp.sum(jnp.where(target, pieces[0], 0.0), axis=1, keepdims=True)
    for column, piece in enumerate(pieces):
        share = jnp.exp(piece - log_total)
        if column == 0:
            share = share - jnp.where(target, 1.0, 0.0)
        masked[:, column * pairs : (column + 1) * pairs] = inverse_temp * share
    for block in range(blocks):
        for column in range(window + 1):
            spot = place_ref[column, block]

            @pl.when(spot >= 0)
            def _():
                packed[spot] = masked[
                    block * fine : (block + 1) * fine, column * pairs : (column + 1) * pairs
                ]

    for step in range(room // 2):
        both = jnp.concatenate([packed[2 * step], packed[2 * step + 1]], axis=0)
        c_ref[step] = both.astype(jnp.bfloat16)
    losses = jnp.sum(
        jnp.where(lane == row // fine, log_total - positive, 0.0), axis=0, keepdims=True
    )
    coarse = losses.astype(jnp.bfloat16).astype(jnp.float32)
    rank = lax.broadcasted_iota(jnp.int32, (2 * fine, pairs), 0)
    both = jnp.where(rank == 0, coarse, jnp.where(rank == 1, losses - coarse, 0.0))
    c_ref[room // 2] = both.astype(jnp.bfloat16)


def softmax_call(place, own_scores, codes, blocks, window):
    steps, fine, pairs = codes[0].shape
    room, fine = 2 * (steps - 1), fine // 2
    whole = pl.BlockSpec(memory_space=pltpu.VMEM)
    return pl.pallas_call(
        functools.partial(softmax_kernel, blocks, window),
        in_specs=[pl.BlockSpec(memory_space=pltpu.SMEM), whole] + [whole] * len(codes),
        out_specs=whole,
        out_shape=jax.ShapeDtypeStruct((room // 2 + 1, 2 * fine, pairs), jnp.bfloat16),
        scratch_shapes=[
            pltpu.VMEM((room, fine, pairs), jnp.float32),
            pltpu.VMEM((blocks * fine, (window + 1) * pairs), jnp.float32),
        ],
        compiler_params=pltpu.CompilerParams(vmem_limit_bytes=vmem_limit),
        name="softmax_rows",
    )(place, own_scores, *codes)


def grad_kernel(
    blocks,
    pairs,
    window,
    own_ref,
    place_ref,
    q_ref,
    d_ref,
    *refs,
):
    part_refs, out_refs = refs[: -blocks - 6], refs[-blocks - 6 : -6]
    loss_ref, wide, dsum, picked, packed, square = refs[-6:]
    fine = pairs // blocks
    room = packed.shape[1]
    me = lax.axis_index("pb")
    masks = swap_masks(blocks)
    unroll = 32
    losses = 0.0
    for part in part_refs:
        sent = part[:, room // 2].astype(jnp.float32)
        losses = losses + jnp.sum(sent[:, 0, :] + sent[:, 1, :], axis=0, keepdims=True) / pairs
    lane = lax.broadcasted_iota(jnp.int32, losses.shape, 1)
    mine = jnp.where(lane == me, losses, 0.0)
    loss_ref[...] = jnp.broadcast_to(jnp.sum(mine, axis=1, keepdims=True), loss_ref.shape)
    dsum[...] = jnp.zeros_like(dsum)
    square[...] = jnp.zeros_like(square)

    def unpack(step, carry):
        for part, mask in zip(part_refs, masks):
            both = part[:, step].astype(jnp.float32)
            for at, apart in enumerate(mask):
                packed[me ^ apart, 2 * step] = both[at, :fine]
                packed[me ^ apart, 2 * step + 1] = both[at, fine:]
        return carry

    lax.fori_loop(0, room // 2, unpack, 0)

    def scatter_rows(block, offset, start):
        def step_rows(step, inner):
            base = pl.multiple_of(step * unroll, unroll)
            rows = [picked[row_pair(start + base + k), :] for k in range(unroll)]
            for k in range(unroll):
                wide[row_pair(own_ref[block, offset + base + k]), :] = rows[k]
            return inner

        lax.fori_loop(0, pairs // unroll, step_rows, 0)

    def two_blocks(step, carry):
        for half in range(2):
            for column in range(window + 1):
                spot = place_ref[column, 2 * step + half]
                tile = packed[:, jnp.maximum(spot, 0)].reshape(pairs, pairs)
                square[
                    half * pairs : (half + 1) * pairs,
                    (half + column) * pairs : (half + column + 1) * pairs,
                ] = jnp.where(spot >= 0, tile, 0.0).astype(jnp.bfloat16)
        at = pl.multiple_of(step * 2 * pairs, 2 * pairs)
        there = pl.ds(at, (window + 2) * pairs)
        coefficients = square[...]
        summed = jnp.dot(coefficients, d_ref[there, :], preferred_element_type=jnp.float32)
        spread(picked, 0, summed)
        dsum[there, :] += lax.dot_general(
            coefficients,
            q_ref[pl.ds(at, 2 * pairs), :],
            (((0,), (0,)), ((), ())),
            preferred_element_type=jnp.float32,
        )
        for half in range(2):
            scatter_rows(2 * step + half, 0, half * pairs)
        return carry

    lax.fori_loop(0, blocks // 2, two_blocks, 0)
    dsum[: window * pairs, :] += dsum[blocks * pairs :, :]

    def doc_block(block, carry):
        at = pl.multiple_of(block * pairs, pairs)
        spread(picked, 0, dsum[pl.ds(at, pairs), :])
        scatter_rows(block, pairs, 0)
        return carry

    lax.fori_loop(0, blocks, doc_block, 0)
    slots = out_refs[0].shape[0]
    for apart, out_ref in enumerate(out_refs):
        at = pl.multiple_of((me ^ apart) * slots, slots)
        out_ref[...] = gathered(wide, at, slots).astype(jnp.bfloat16)


def grad_call(own, place, parts, queries, documents, blocks, pairs, window):
    count, piece = queries.shape
    seqs = 2 * count
    room = 2 * (parts[0].shape[1] - 1)
    whole = pl.BlockSpec(memory_space=pltpu.VMEM)
    scalars = pl.BlockSpec(memory_space=pltpu.SMEM)
    return pl.pallas_call(
        functools.partial(grad_kernel, blocks, pairs, window),
        in_specs=[scalars, scalars, whole, whole] + [whole] * len(parts),
        out_specs=[whole] * (blocks + 1),
        out_shape=[jax.ShapeDtypeStruct((seqs // blocks, piece), jnp.bfloat16)] * blocks
        + [jax.ShapeDtypeStruct((1, lanes), jnp.float32)],
        scratch_shapes=[
            pltpu.VMEM((2 * seqs, lanes), jnp.float32),
            pltpu.VMEM(((blocks + window) * pairs, piece), jnp.float32),
            pltpu.VMEM((4 * pairs, lanes), jnp.float32),
            pltpu.VMEM((blocks, room, pairs // blocks, pairs), jnp.float32),
            pltpu.VMEM((2 * pairs, (window + 2) * pairs), jnp.bfloat16),
        ],
        compiler_params=pltpu.CompilerParams(vmem_limit_bytes=vmem_limit),
        name="slice_grads",
    )(own, place, queries, documents, *parts)


def project_kernel(normed_ref, inv_ref, *refs):
    grad_refs, out_ref = refs[:-1], refs[-1]
    piece = grad_refs[0].shape[1]
    me = lax.axis_index("pb")
    inverse = inv_ref[:, :1]
    cuts = [
        pl.ds(pl.multiple_of((me ^ apart) * piece, piece), piece) for apart in range(len(grad_refs))
    ]
    total = 0.0
    for cut, grad_ref in zip(cuts, grad_refs):
        unit = normed_ref[:, cut].astype(jnp.float32) * inverse
        total = total + unit * grad_ref[...].astype(jnp.float32)
    along = jnp.sum(total, axis=-1, keepdims=True)
    for cut, grad_ref in zip(cuts, grad_refs):
        unit = normed_ref[:, cut].astype(jnp.float32) * inverse
        out_ref[:, cut] = grad_ref[...].astype(jnp.float32) - unit * along


def project_call(returned, normed, inverse):
    seqs, piece = returned[0].shape
    width = normed.shape[1]
    rows = 64
    return pl.pallas_call(
        project_kernel,
        grid=(seqs // rows,),
        in_specs=[
            pl.BlockSpec((rows, width), lambda i: (i, 0)),
            pl.BlockSpec((rows, lanes), lambda i: (i, 0)),
        ]
        + [pl.BlockSpec((rows, piece), lambda i: (i, 0))] * len(returned),
        out_specs=pl.BlockSpec((rows, width), lambda i: (i, 0)),
        out_shape=jax.ShapeDtypeStruct((seqs, width), jnp.float32),
        compiler_params=pltpu.CompilerParams(vmem_limit_bytes=vmem_limit),
        name="project_out",
    )(normed, inverse, *returned)


def swapped(value, apart):
    pairs = [(at, at ^ apart) for at in range(lax.axis_size("pb"))]
    return lax.ppermute(value, "pb", pairs)


def swap_bits(devices):
    bits = [1 << bit for bit in reversed(range(devices.bit_length() - 1))]
    return bits[:-2], bits[-2], bits[-1]


def swap_masks(devices):
    far, side, last = swap_bits(devices)
    held = [0]
    for apart in far:
        held = held + [mask ^ apart for mask in held]
    held = held + [mask ^ side for mask in held]
    return [held, [mask ^ last for mask in held]]


def gather_all(value):
    far, side, last = swap_bits(lax.axis_size("pb"))
    held = value[None]
    beside = [swapped(held, side)]
    for apart in far:
        arrived = swapped(held, apart)
        beside.append(swapped(arrived, side))
        held = jnp.concatenate([held, arrived], axis=0)
    held = jnp.concatenate([held] + beside, axis=0)
    return [held, swapped(held, last)]


def exchange(blocks):
    arrived = {0: blocks[0]}
    half = len(blocks) // 2
    for apart in range(half):
        for target in (apart + half, apart):
            if target:
                arrived[target] = swapped(blocks[target], target)
    return [arrived[apart] for apart in range(len(blocks))]


def middle(embedded, room, devices, pairs, window):
    queries, documents, mine, other, top, own, place = score_call(
        embedded, room, devices, pairs, window
    )
    own_scores, *codes = merge_call(mine, swapped(other, 1), top, swapped(top, 1), devices)
    codes = [swapped(code, 2 * (hop + 1)) for hop, code in enumerate(codes)]
    parts = gather_all(softmax_call(place, own_scores, codes, devices, window))
    *grads, loss = grad_call(own, place, parts, queries, documents, devices, pairs, window)
    return grads, loss[0, :1]


def feature_plan(hidden, final_gain, last_row, pair_owner, hard_negatives):
    devices = lax.axis_size("pb")
    seqs, width = hidden.shape
    pairs = pair_owner.shape[0]
    window = hard_negatives.shape[1]
    normed, inverse, *embedding = norm_call(
        last_row, hidden, final_gain, pair_owner.T, hard_negatives, devices
    )
    embedded = exchange(embedding)
    most = devices * (window + 1)
    rooms = [most * part // 20 for part in (10, 11, 12, 13, 14, 16, 20)]
    flags = sum(block[seqs + 2, :window].astype(jnp.float32) for block in embedded)
    used = devices + jnp.sum(flags)
    level = sum((used > room).astype(jnp.int32) for room in rooms[:-1])
    grads, loss = lax.switch(
        level,
        [
            functools.partial(middle, room=room, devices=devices, pairs=pairs, window=window)
            for room in rooms
        ],
        embedded,
    )
    return project_call(exchange(grads), normed, inverse), loss


def from_behind(value, axis, steps):
    count = lax.axis_size(axis)
    pairs = [(source, (source + steps) % count) for source in range(count)]
    return lax.ppermute(value, axis, pairs)


def similarity(queries, documents):
    return inverse_temp * lax.dot_general(
        queries, documents, (((1,), (1,)), ((), ())), preferred_element_type=jnp.float32
    )


def transposed(weights, queries):
    return lax.dot_general(
        weights, queries, (((0,), (0,)), ((), ())), preferred_element_type=jnp.float32
    )


def combine_docs(weights, documents):
    return jnp.dot(weights, documents, preferred_element_type=jnp.float32)


def skipped(listed, function, operands, out_shape):
    return lax.cond(
        listed,
        lambda inputs: function(*inputs),
        lambda inputs: jnp.zeros(out_shape, jnp.float32),
        operands,
    )


def row_plan(hidden, final_gain, last_row, pair_owner, hard_negatives):
    values = hidden.astype(jnp.float32)
    scale_row = lax.rsqrt(jnp.mean(values * values, axis=-1, keepdims=True) + token_eps)
    normed = (values * scale_row * final_gain.astype(jnp.float32)).astype(jnp.bfloat16)
    seq_count = last_row.shape[1]
    model_width = hidden.shape[1]
    pooled = normed[last_row[0]].astype(jnp.float32)
    inverse_norm = lax.rsqrt(jnp.sum(pooled * pooled, axis=-1, keepdims=True) + 1e-06)
    unit_vec = pooled * inverse_norm
    embedding = unit_vec.astype(jnp.bfloat16)
    devices = lax.axis_size("pb")
    capacity = 2 * seq_count // devices
    pair_count = pair_owner.shape[0]
    wanted = jnp.concatenate([pair_owner[:, 0], pair_owner[:, 1]])
    holder = wanted // seq_count
    within = wanted % seq_count
    entry_ids = jnp.arange(2 * pair_count, dtype=jnp.int32)
    earlier = (holder[None, :] == holder[:, None]) & (entry_ids[None, :] < entry_ids[:, None])
    position = jnp.sum(earlier.astype(jnp.int32), axis=1)
    request = jnp.full((devices, capacity), -1, jnp.int32).at[holder, position].set(within)
    served = lax.all_to_all(request, "pb", split_axis=0, concat_axis=0, tiled=True)
    outgoing = jnp.where(
        served[:, :, None] >= 0, embedding[jnp.maximum(served, 0)], jnp.zeros((), jnp.bfloat16)
    )
    received = lax.all_to_all(outgoing, "pb", split_axis=0, concat_axis=0, tiled=True)
    gathered = received[holder, position]
    queries = gathered[:pair_count]
    own_docs = gathered[pair_count:]
    listed_ids = hard_negatives[0]
    window = hard_negatives.shape[1]
    listed = [listed_ids[offset] >= 0 for offset in range(window)]
    neighbours = []
    moving = own_docs
    for offset in range(window):
        moving = from_behind(moving, "pb", -1)
        neighbours.append(moving)
    tile_shape = (pair_count, pair_count)
    score_blocks = [similarity(queries, own_docs)]
    for offset in range(window):
        score_blocks.append(
            skipped(listed[offset], similarity, (queries, neighbours[offset]), tile_shape)
        )
    all_scores = jnp.concatenate(score_blocks, axis=1)
    usable = jnp.concatenate(
        [jnp.ones((pair_count,), jnp.bool_)]
        + [jnp.broadcast_to(listed[offset], (pair_count,)) for offset in range(window)]
    )
    masked = jnp.where(usable[None, :], all_scores, -jnp.inf)
    row_max = jnp.max(masked, axis=1, keepdims=True)
    log_total = row_max + jnp.log(jnp.sum(jnp.exp(masked - row_max), axis=1, keepdims=True))
    diagonal = jnp.arange(pair_count, dtype=jnp.int32)
    positive = all_scores[diagonal, diagonal]
    block_loss = jnp.mean(log_total[:, 0] - positive).reshape(1)
    columns = jnp.arange((window + 1) * pair_count, dtype=jnp.int32)
    target = (columns[None, :] == diagonal[:, None]).astype(jnp.float32)
    coefficients = (inverse_temp * (jnp.exp(masked - log_total) - target)).astype(jnp.bfloat16)
    pieces = [
        coefficients[:, offset * pair_count : (offset + 1) * pair_count]
        for offset in range(window + 1)
    ]
    grad_shape = (pair_count, model_width)
    query_sum = combine_docs(pieces[0], own_docs)
    for offset in range(window):
        query_sum = query_sum + skipped(
            listed[offset], combine_docs, (pieces[offset + 1], neighbours[offset]), grad_shape
        )
    query_grad = query_sum.astype(jnp.bfloat16)
    own_part = transposed(pieces[0], queries).astype(jnp.bfloat16)
    partial_value = [
        skipped(listed[offset], transposed, (pieces[offset + 1], queries), grad_shape).astype(
            jnp.bfloat16
        )
        for offset in range(window)
    ]
    running = partial_value[window - 1].astype(jnp.float32)
    for offset in range(window):
        running = from_behind(running, "pb", 1)
        if offset + 1 < window:
            running = running + partial_value[window - 2 - offset].astype(jnp.float32)
    doc_grad = (own_part.astype(jnp.float32) + running).astype(jnp.bfloat16)
    answers = jnp.concatenate([query_grad, doc_grad], axis=0)
    returning = (
        jnp.zeros((devices, capacity, model_width), jnp.bfloat16).at[holder, position].set(answers)
    )
    returned = lax.all_to_all(returning, "pb", split_axis=0, concat_axis=0, tiled=True)
    slot_ids = jnp.where(served >= 0, served, seq_count).reshape(-1)
    emb_grad = (
        jnp.zeros((seq_count, model_width), jnp.bfloat16)
        .at[slot_ids]
        .set(returned.reshape(-1, model_width), mode="drop")
    )
    gradient = emb_grad.astype(jnp.float32)
    pooled_grad = gradient - unit_vec * jnp.sum(unit_vec * gradient, axis=-1, keepdims=True)
    return (pooled_grad, block_loss)


def solution(mesh):
    def local(hidden, final_gain, last_row, pair_owner, hard_negatives):
        plan = feature_plan if hidden.shape[1] >= lanes * mesh.shape["pb"] else row_plan
        return plan(hidden, final_gain, last_row, pair_owner, hard_negatives)

    return jax.shard_map(
        local,
        mesh=mesh,
        in_specs=(
            P(("groups", "pb"), None),
            P(),
            P(("groups", "pb"), None),
            P(("groups", "pb"), None),
            P(("groups", "pb"), None),
        ),
        out_specs=(P(("groups", "pb"), None), P(("groups", "pb"))),
        check_vma=False,
    )
```

```python
import functools

import jax
import jax.numpy as jnp
from jax import lax
from jax.experimental import pallas as pl
from jax.experimental.pallas import tpu as pltpu
from jax.sharding import PartitionSpec as P

inverse_temp = 50.0
token_eps = 1e-05
unit_eps = 1e-06
lanes = 128
bound_steps = 256.0
code_steps = 32000.0
vmem_limit = 56 * 1024 * 1024


def spread(target, at, value):
    count = value.shape[0]
    for half in range(2):
        target[pl.ds(2 * at + half, count, stride=2), :] = value[:, half * lanes : (half + 1) * lanes]


def gathered(source, at, count):
    halves = [source[pl.ds(2 * at + half, count, stride=2), :] for half in range(2)]
    return jnp.concatenate(halves, axis=1)


def row_pair(index):
    return pl.ds(pl.multiple_of(2 * index, 2), 2)


def norm_kernel(
    last_ref, hidden_ref, gain_ref, owner_ref, negative_ref, normed_ref, inv_ref, emb_ref
):
    seqs, width = normed_ref.shape
    parts, _, piece = emb_ref.shape
    pairs = owner_ref.shape[1]
    cuts = [slice(part * piece, (part + 1) * piece) for part in range(parts)]
    sources = lax.broadcasted_iota(jnp.int32, (seqs, seqs), 0)
    pick = jnp.where(sources == last_ref[...], 1.0, 0.0).astype(jnp.bfloat16)

    def folded(squares):
        return functools.reduce(
            jnp.add, [squares[:, at : at + lanes] for at in range(0, piece, lanes)]
        )

    total = jnp.zeros((seqs, lanes), jnp.float32)
    for cut in cuts:
        values = lax.dot_general(
            pick, hidden_ref[:, cut], (((0,), (0,)), ((), ())), preferred_element_type=jnp.float32
        )
        normed_ref[:, cut] = values.astype(jnp.bfloat16)
        total = total + folded(values * values)
    scale = lax.rsqrt(jnp.sum(total, axis=-1, keepdims=True) / width + token_eps)
    total = jnp.zeros((seqs, lanes), jnp.float32)
    for cut in cuts:
        values = normed_ref[:, cut].astype(jnp.float32)
        gain = gain_ref[cut].astype(jnp.float32).reshape(1, piece)
        normed = (values * scale * gain).astype(jnp.bfloat16)
        normed_ref[:, cut] = normed
        pooled = normed.astype(jnp.float32)
        total = total + folded(pooled * pooled)
    inverse = lax.rsqrt(jnp.sum(total, axis=-1, keepdims=True) + unit_eps)
    inv_ref[...] = jnp.broadcast_to(inverse, inv_ref.shape)

    owners = owner_ref[...].astype(jnp.float32)
    high = jnp.floor(owners * (1.0 / 256.0))
    low = owners - 256.0 * high
    row = lax.broadcasted_iota(jnp.int32, (16, pairs), 0)
    spot = lax.broadcasted_iota(jnp.int32, (16, pairs), 1)
    left = jnp.where(row == 0, low[:1], jnp.where(row == 1, high[:1], 0.0))
    right = jnp.where(row == 0, low[1:2], jnp.where(row == 1, high[1:2], 0.0))
    for offset in range(negative_ref.shape[1]):
        named = (negative_ref[0, offset] >= 0).astype(jnp.float32)
        left = jnp.where((row == 2) & (spot == offset), named, left)
    facts = jnp.concatenate([left, right], axis=1).astype(jnp.bfloat16)

    for part, cut in enumerate(cuts):
        emb_ref[part, :seqs] = (normed_ref[:, cut].astype(jnp.float32) * inverse).astype(jnp.bfloat16)
        emb_ref[part, seqs:] = facts


def norm_call(last_row, hidden, gain, owners, hard_negatives, parts):
    seqs, width = hidden.shape
    piece = width // parts
    whole = pl.BlockSpec(memory_space=pltpu.VMEM)
    return pl.pallas_call(
        norm_kernel,
        in_specs=[whole, whole, whole, whole, pl.BlockSpec(memory_space=pltpu.SMEM)],
        out_specs=[whole] * 3,
        out_shape=[
            jax.ShapeDtypeStruct((seqs, width), jnp.bfloat16),
            jax.ShapeDtypeStruct((seqs, lanes), jnp.float32),
            jax.ShapeDtypeStruct((parts, seqs + 16, piece), jnp.bfloat16),
        ],
        compiler_params=pltpu.CompilerParams(vmem_limit_bytes=vmem_limit),
        name="norm_rows",
    )(last_row, hidden, gain, owners, hard_negatives)


def score_kernel(
    blocks,
    pairs,
    window,
    *refs,
):
    emb_ref, q_ref, d_ref, mine_ref, other_ref, top_ref, own_ref, place_ref = refs[:-7]
    wide, picked, tiles, facts, own, named, sems = refs[-7:]
    seqs = emb_ref.shape[1] - 16
    sent = emb_ref[:, seqs:, :].astype(jnp.float32)
    own_ref[...] = (sent[:, 0, :] + 256.0 * sent[:, 1, :]).astype(jnp.int32)
    facts[...] = sent[:, 2, :lanes].astype(jnp.int32)
    fetches = [
        pltpu.make_async_copy(own_ref, own, sems.at[0]),
        pltpu.make_async_copy(facts, named, sems.at[1]),
    ]
    for fetch in fetches:
        fetch.start()

    for part in range(blocks):
        spread(wide, part * seqs, emb_ref[part, :seqs, :].astype(jnp.float32))
    for fetch in fetches:
        fetch.wait()

    def place(block, count):
        place_ref[0, block] = block
        for offset in range(window):
            present = named[block, offset] > 0
            place_ref[offset + 1, block] = jnp.where(present, count, -1)
            count = count + present.astype(jnp.int32)
        return count

    used = lax.fori_loop(0, blocks, place, blocks)
    fine = pairs // blocks

    def clear(spot, carry):
        empty = jnp.zeros((blocks // 2, fine, pairs), jnp.float32)
        at = pl.ds(pl.multiple_of(spot * fine, fine), fine)
        mine_ref[:, at, :] = empty
        other_ref[:, at, :] = empty
        return carry

    lax.fori_loop(used, mine_ref.shape[1] // fine, clear, 0)
    unroll = 32

    def pick_block(block, carry):
        def pick_rows(step, inner):
            base = pl.multiple_of(step * unroll, unroll)
            rows = [wide[row_pair(own[block, base + k]), :] for k in range(unroll)]
            for k in range(unroll):
                picked[row_pair(base + k), :] = rows[k]
            return inner

        lax.fori_loop(0, 2 * pairs // unroll, pick_rows, 0)
        at = pl.multiple_of(block * pairs, pairs)
        q_ref[pl.ds(at, pairs), :] = gathered(picked, 0, pairs).astype(jnp.bfloat16)
        d_ref[pl.ds(at, pairs), :] = gathered(picked, pairs, pairs).astype(jnp.bfloat16)
        return carry

    lax.fori_loop(0, blocks, pick_block, 0)
    d_ref[blocks * pairs :, :] = d_ref[: window * pairs, :]
    even = lax.axis_index("pb") % 2 == 0
    top_ref[...] = jnp.zeros_like(top_ref)

    def score_blocks(step, carry):
        at = pl.multiple_of(step * 2 * pairs, 2 * pairs)
        tiles[...] = inverse_temp * lax.dot_general(
            q_ref[pl.ds(at, 2 * pairs), :],
            d_ref[pl.ds(at, (window + 2) * pairs), :],
            (((1,), (1,)), ((), ())),
            preferred_element_type=jnp.float32,
        )
        for half in range(2):
            for column in range(window + 1):
                spot = place_ref[column, 2 * step + half]

                @pl.when(spot >= 0)
                def _():
                    row = pl.multiple_of(spot * fine, fine)
                    tile = tiles[
                        half * pairs : (half + 1) * pairs,
                        (half + column) * pairs : (half + column + 1) * pairs,
                    ]
                    parted = tile.reshape(blocks // 2, 2, fine, pairs)
                    first, second = parted[:, 0], parted[:, 1]
                    mine_ref[:, pl.ds(row, fine), :] = jnp.where(even, first, second)
                    other_ref[:, pl.ds(row, fine), :] = jnp.where(even, second, first)
                    size = jnp.maximum(jnp.abs(first), jnp.abs(second))
                    top_ref[...] = jnp.maximum(top_ref[...], jnp.max(size, axis=0))

        return carry

    lax.fori_loop(0, blocks // 2, score_blocks, 0)


def score_call(embedded, room, blocks, pairs, window):
    _, rows, piece = embedded.shape
    fine = pairs // blocks
    whole = pl.BlockSpec(memory_space=pltpu.VMEM)
    scalars = pl.BlockSpec(memory_space=pltpu.SMEM)
    return pl.pallas_call(
        functools.partial(score_kernel, blocks, pairs, window),
        in_specs=[whole],
        out_specs=[whole, whole, whole, whole, whole, whole, scalars],
        out_shape=[
            jax.ShapeDtypeStruct((blocks * pairs, piece), jnp.bfloat16),
            jax.ShapeDtypeStruct(((blocks + window) * pairs, piece), jnp.bfloat16),
            jax.ShapeDtypeStruct((blocks // 2, room * fine, pairs), jnp.float32),
            jax.ShapeDtypeStruct((blocks // 2, room * fine, pairs), jnp.float32),
            jax.ShapeDtypeStruct((fine, pairs), jnp.float32),
            jax.ShapeDtypeStruct((blocks, 2 * pairs), jnp.int32),
            jax.ShapeDtypeStruct((window + 1, blocks), jnp.int32),
        ],
        scratch_shapes=[
            pltpu.VMEM((2 * blocks * (rows - 16), lanes), jnp.float32),
            pltpu.VMEM((4 * pairs, lanes), jnp.float32),
            pltpu.VMEM((2 * pairs, (window + 2) * pairs), jnp.float32),
            pltpu.VMEM((blocks, lanes), jnp.int32),
            pltpu.SMEM((blocks, 2 * pairs), jnp.int32),
            pltpu.SMEM((blocks, lanes), jnp.int32),
            pltpu.SemaphoreType.DMA((2,)),
        ],
        compiler_params=pltpu.CompilerParams(vmem_limit_bytes=vmem_limit),
        name="partial_scores",
    )(embedded)


def merge_kernel(mine_ref, other_ref, top_ref, other_top_ref, own_ref, *code_refs):
    chips, rows, pairs = mine_ref.shape
    steps = code_refs[0].shape[0] - 1
    fine = rows // steps // 2
    chip = lax.axis_index("pb") // 2

    def highest(ref):
        return jnp.max(jnp.max(ref[...], axis=1, keepdims=True), axis=0, keepdims=True)

    top = highest(top_ref) + highest(other_top_ref)
    bound = jnp.ceil(top * bound_steps) + 1.0
    scale = code_steps * bound_steps / bound
    own_ref[...] = mine_ref[chip] + other_ref[chip]
    for hop, code_ref in enumerate(code_refs):
        target = chip ^ (hop + 1)

        def encode(step, carry):
            at = pl.multiple_of(step * 2 * fine, 2 * fine)
            there = pl.ds(at, 2 * fine)
            codes = jnp.round((mine_ref[target, there, :] + other_ref[target, there, :]) * scale)
            code_ref[step] = codes.astype(jnp.int32).astype(jnp.int16)
            return carry

        lax.fori_loop(0, steps, encode, 0)
        code_ref[steps] = jnp.broadcast_to(bound, (2 * fine, pairs)).astype(jnp.int32).astype(jnp.int16)


def merge_call(mine, other, top, other_top, blocks):
    chips, rows, pairs = mine.shape
    fine = pairs // blocks
    whole = pl.BlockSpec(memory_space=pltpu.VMEM)
    coded = jax.ShapeDtypeStruct((rows // (2 * fine) + 1, 2 * fine, pairs), jnp.int16)
    return pl.pallas_call(
        merge_kernel,
        in_specs=[whole] * 4,
        out_specs=[whole] * chips,
        out_shape=[jax.ShapeDtypeStruct((rows, pairs), jnp.float32)] + [coded] * (chips - 1),
        compiler_params=pltpu.CompilerParams(vmem_limit_bytes=vmem_limit),
        name="merge_scores",
    )(mine, other, top, other_top)


def softmax_kernel(blocks, window, place_ref, own_ref, *refs):
    code_refs, (c_ref, packed, masked) = refs[:-3], refs[-3:]
    room, fine, pairs = packed.shape
    count = blocks * fine
    unit = 1.0 / (code_steps * bound_steps)
    scales = [ref[room // 2].astype(jnp.int32).astype(jnp.float32) * unit for ref in code_refs]

    def decode(step, carry):
        both = own_ref[pl.ds(pl.multiple_of(step * 2 * fine, 2 * fine), 2 * fine), :]
        for ref, scale in zip(code_refs, scales):
            both = both + ref[step].astype(jnp.int32).astype(jnp.float32) * scale
        packed[2 * step] = both[:fine]
        packed[2 * step + 1] = both[fine:]
        return carry

    lax.fori_loop(0, room // 2, decode, 0)
    for block in range(blocks):
        for column in range(window + 1):
            spot = place_ref[column, block]
            tile = packed[jnp.maximum(spot, 0)]
            masked[block * fine : (block + 1) * fine, column * pairs : (column + 1) * pairs] = (
                jnp.where(spot >= 0, tile, -jnp.inf)
            )
    row = lax.broadcasted_iota(jnp.int32, (count, pairs), 0)
    lane = lax.broadcasted_iota(jnp.int32, (count, pairs), 1)
    target = lane == lax.axis_index("pb") * fine + row % fine
    pieces = [masked[:, column * pairs : (column + 1) * pairs] for column in range(window + 1)]
    row_max = jnp.max(functools.reduce(jnp.maximum, pieces), axis=1, keepdims=True)
    total = functools.reduce(jnp.add, [jnp.exp(piece - row_max) for piece in pieces])
    log_total = row_max + jnp.log(jnp.sum(total, axis=1, keepdims=True))
    positive = jnp.sum(jnp.where(target, pieces[0], 0.0), axis=1, keepdims=True)
    for column, piece in enumerate(pieces):
        share = jnp.exp(piece - log_total)
        if column == 0:
            share = share - jnp.where(target, 1.0, 0.0)
        masked[:, column * pairs : (column + 1) * pairs] = inverse_temp * share
    for block in range(blocks):
        for column in range(window + 1):
            spot = place_ref[column, block]

            @pl.when(spot >= 0)
            def _():
                packed[spot] = masked[
                    block * fine : (block + 1) * fine, column * pairs : (column + 1) * pairs
                ]

    for step in range(room // 2):
        both = jnp.concatenate([packed[2 * step], packed[2 * step + 1]], axis=0)
        c_ref[step] = both.astype(jnp.bfloat16)
    losses = jnp.sum(
        jnp.where(lane == row // fine, log_total - positive, 0.0), axis=0, keepdims=True
    )
    coarse = losses.astype(jnp.bfloat16).astype(jnp.float32)
    rank = lax.broadcasted_iota(jnp.int32, (2 * fine, pairs), 0)
    both = jnp.where(rank == 0, coarse, jnp.where(rank == 1, losses - coarse, 0.0))
    c_ref[room // 2] = both.astype(jnp.bfloat16)


def softmax_call(place, own_scores, codes, blocks, window):
    steps, fine, pairs = codes[0].shape
    room, fine = 2 * (steps - 1), fine // 2
    whole = pl.BlockSpec(memory_space=pltpu.VMEM)
    return pl.pallas_call(
        functools.partial(softmax_kernel, blocks, window),
        in_specs=[pl.BlockSpec(memory_space=pltpu.SMEM), whole] + [whole] * len(codes),
        out_specs=whole,
        out_shape=jax.ShapeDtypeStruct((room // 2 + 1, 2 * fine, pairs), jnp.bfloat16),
        scratch_shapes=[
            pltpu.VMEM((room, fine, pairs), jnp.float32),
            pltpu.VMEM((blocks * fine, (window + 1) * pairs), jnp.float32),
        ],
        compiler_params=pltpu.CompilerParams(vmem_limit_bytes=vmem_limit),
        name="softmax_rows",
    )(place, own_scores, *codes)


def grad_kernel(
    blocks,
    pairs,
    window,
    own_ref,
    place_ref,
    q_ref,
    d_ref,
    *refs,
):
    part_refs = refs[:-7]
    out_ref, loss_ref, wide, dsum, picked, packed, square = refs[-7:]
    fine = pairs // blocks
    room = packed.shape[1]
    me = lax.axis_index("pb")
    masks = swap_masks(blocks)
    unroll = 32
    losses = 0.0
    for part in part_refs:
        sent = part[:, room // 2].astype(jnp.float32)
        losses = losses + jnp.sum(sent[:, 0, :] + sent[:, 1, :], axis=0, keepdims=True) / pairs
    lane = lax.broadcasted_iota(jnp.int32, losses.shape, 1)
    mine = jnp.where(lane == me, losses, 0.0)
    loss_ref[...] = jnp.broadcast_to(jnp.sum(mine, axis=1, keepdims=True), loss_ref.shape)
    dsum[...] = jnp.zeros_like(dsum)
    square[...] = jnp.zeros_like(square)

    def unpack(step, carry):
        for part, mask in zip(part_refs, masks):
            both = part[:, step].astype(jnp.float32)
            for at, apart in enumerate(mask):
                packed[me ^ apart, 2 * step] = both[at, :fine]
                packed[me ^ apart, 2 * step + 1] = both[at, fine:]
        return carry

    lax.fori_loop(0, room // 2, unpack, 0)

    def scatter_rows(block, offset, start):
        def step_rows(step, inner):
            base = pl.multiple_of(step * unroll, unroll)
            rows = [picked[row_pair(start + base + k), :] for k in range(unroll)]
            for k in range(unroll):
                wide[row_pair(own_ref[block, offset + base + k]), :] = rows[k]
            return inner

        lax.fori_loop(0, pairs // unroll, step_rows, 0)

    def two_blocks(step, carry):
        for half in range(2):
            for column in range(window + 1):
                spot = place_ref[column, 2 * step + half]
                tile = packed[:, jnp.maximum(spot, 0)].reshape(pairs, pairs)
                square[
                    half * pairs : (half + 1) * pairs,
                    (half + column) * pairs : (half + column + 1) * pairs,
                ] = jnp.where(spot >= 0, tile, 0.0).astype(jnp.bfloat16)
        at = pl.multiple_of(step * 2 * pairs, 2 * pairs)
        there = pl.ds(at, (window + 2) * pairs)
        coefficients = square[...]
        summed = jnp.dot(coefficients, d_ref[there, :], preferred_element_type=jnp.float32)
        spread(picked, 0, summed)
        dsum[there, :] += lax.dot_general(
            coefficients,
            q_ref[pl.ds(at, 2 * pairs), :],
            (((0,), (0,)), ((), ())),
            preferred_element_type=jnp.float32,
        )
        for half in range(2):
            scatter_rows(2 * step + half, 0, half * pairs)
        return carry

    lax.fori_loop(0, blocks // 2, two_blocks, 0)
    dsum[: window * pairs, :] += dsum[blocks * pairs :, :]

    def doc_block(block, carry):
        at = pl.multiple_of(block * pairs, pairs)
        spread(picked, 0, dsum[pl.ds(at, pairs), :])
        scatter_rows(block, pairs, 0)
        return carry

    lax.fori_loop(0, blocks, doc_block, 0)
    slots = out_ref.shape[1]
    for part in range(blocks):
        out_ref[part] = gathered(wide, part * slots, slots).astype(jnp.bfloat16)


def grad_call(own, place, parts, queries, documents, blocks, pairs, window):
    count, piece = queries.shape
    seqs = 2 * count
    room = 2 * (parts[0].shape[1] - 1)
    whole = pl.BlockSpec(memory_space=pltpu.VMEM)
    scalars = pl.BlockSpec(memory_space=pltpu.SMEM)
    return pl.pallas_call(
        functools.partial(grad_kernel, blocks, pairs, window),
        in_specs=[scalars, scalars, whole, whole] + [whole] * len(parts),
        out_specs=[whole, whole],
        out_shape=[
            jax.ShapeDtypeStruct((blocks, seqs // blocks, piece), jnp.bfloat16),
            jax.ShapeDtypeStruct((1, lanes), jnp.float32),
        ],
        scratch_shapes=[
            pltpu.VMEM((2 * seqs, lanes), jnp.float32),
            pltpu.VMEM(((blocks + window) * pairs, piece), jnp.float32),
            pltpu.VMEM((4 * pairs, lanes), jnp.float32),
            pltpu.VMEM((blocks, room, pairs // blocks, pairs), jnp.float32),
            pltpu.VMEM((2 * pairs, (window + 2) * pairs), jnp.bfloat16),
        ],
        compiler_params=pltpu.CompilerParams(vmem_limit_bytes=vmem_limit),
        name="slice_grads",
    )(own, place, queries, documents, *parts)


def project_kernel(grad_ref, normed_ref, inv_ref, out_ref):
    parts, _, piece = grad_ref.shape
    cuts = [slice(part * piece, (part + 1) * piece) for part in range(parts)]
    inverse = inv_ref[:, :1]
    total = 0.0
    for part, cut in enumerate(cuts):
        unit = normed_ref[:, cut].astype(jnp.float32) * inverse
        total = total + unit * grad_ref[part].astype(jnp.float32)
    along = jnp.sum(total, axis=-1, keepdims=True)
    for part, cut in enumerate(cuts):
        unit = normed_ref[:, cut].astype(jnp.float32) * inverse
        out_ref[:, cut] = grad_ref[part].astype(jnp.float32) - unit * along


def project_call(returned, normed, inverse):
    parts, seqs, piece = returned.shape
    width = normed.shape[1]
    rows = 64
    return pl.pallas_call(
        project_kernel,
        grid=(seqs // rows,),
        in_specs=[
            pl.BlockSpec((parts, rows, piece), lambda i: (0, i, 0)),
            pl.BlockSpec((rows, width), lambda i: (i, 0)),
            pl.BlockSpec((rows, lanes), lambda i: (i, 0)),
        ],
        out_specs=pl.BlockSpec((rows, width), lambda i: (i, 0)),
        out_shape=jax.ShapeDtypeStruct((seqs, width), jnp.float32),
        compiler_params=pltpu.CompilerParams(vmem_limit_bytes=vmem_limit),
        name="project_out",
    )(returned, normed, inverse)


def swapped(value, apart):
    pairs = [(at, at ^ apart) for at in range(lax.axis_size("pb"))]
    return lax.ppermute(value, "pb", pairs)


def swap_bits(devices):
    bits = [1 << bit for bit in reversed(range(devices.bit_length() - 1))]
    return bits[:-2], bits[-2], bits[-1]


def swap_masks(devices):
    far, side, last = swap_bits(devices)
    held = [0]
    for apart in far:
        held = held + [mask ^ apart for mask in held]
    held = held + [mask ^ side for mask in held]
    return [held, [mask ^ last for mask in held]]


def gather_all(value):
    far, side, last = swap_bits(lax.axis_size("pb"))
    held = value[None]
    beside = [swapped(held, side)]
    for apart in far:
        arrived = swapped(held, apart)
        beside.append(swapped(arrived, side))
        held = jnp.concatenate([held, arrived], axis=0)
    held = jnp.concatenate([held] + beside, axis=0)
    return [held, swapped(held, last)]


def middle(embedded, room, devices, pairs, window):
    queries, documents, mine, other, top, own, place = score_call(
        embedded, room, devices, pairs, window
    )
    own_scores, *codes = merge_call(mine, swapped(other, 1), top, swapped(top, 1), devices)
    codes = [swapped(code, 2 * (hop + 1)) for hop, code in enumerate(codes)]
    parts = gather_all(softmax_call(place, own_scores, codes, devices, window))
    grads, loss = grad_call(own, place, parts, queries, documents, devices, pairs, window)
    return grads, loss[0, :1]


def feature_plan(hidden, final_gain, last_row, pair_owner, hard_negatives):
    devices = lax.axis_size("pb")
    seqs, width = hidden.shape
    pairs = pair_owner.shape[0]
    window = hard_negatives.shape[1]
    normed, inverse, embedding = norm_call(
        last_row, hidden, final_gain, pair_owner.T, hard_negatives, devices
    )
    embedded = lax.all_to_all(embedding, "pb", split_axis=0, concat_axis=0, tiled=True)
    most = devices * (window + 1)
    rooms = [most * part // 20 for part in (10, 11, 12, 13, 14, 16, 20)]
    used = devices + jnp.sum(embedded[:, seqs + 2, :window].astype(jnp.float32))
    level = sum((used > room).astype(jnp.int32) for room in rooms[:-1])
    grads, loss = lax.switch(
        level,
        [
            functools.partial(middle, room=room, devices=devices, pairs=pairs, window=window)
            for room in rooms
        ],
        embedded,
    )
    returned = lax.all_to_all(grads, "pb", split_axis=0, concat_axis=0, tiled=True)
    return project_call(returned, normed, inverse), loss


def from_behind(value, axis, steps):
    count = lax.axis_size(axis)
    pairs = [(source, (source + steps) % count) for source in range(count)]
    return lax.ppermute(value, axis, pairs)


def similarity(queries, documents):
    return inverse_temp * lax.dot_general(
        queries, documents, (((1,), (1,)), ((), ())), preferred_element_type=jnp.float32
    )


def transposed(weights, queries):
    return lax.dot_general(
        weights, queries, (((0,), (0,)), ((), ())), preferred_element_type=jnp.float32
    )


def combine_docs(weights, documents):
    return jnp.dot(weights, documents, preferred_element_type=jnp.float32)


def skipped(listed, function, operands, out_shape):
    return lax.cond(
        listed,
        lambda inputs: function(*inputs),
        lambda inputs: jnp.zeros(out_shape, jnp.float32),
        operands,
    )


def row_plan(hidden, final_gain, last_row, pair_owner, hard_negatives):
    values = hidden.astype(jnp.float32)
    scale_row = lax.rsqrt(jnp.mean(values * values, axis=-1, keepdims=True) + token_eps)
    normed = (values * scale_row * final_gain.astype(jnp.float32)).astype(jnp.bfloat16)
    seq_count = last_row.shape[1]
    model_width = hidden.shape[1]
    pooled = normed[last_row[0]].astype(jnp.float32)
    inverse_norm = lax.rsqrt(jnp.sum(pooled * pooled, axis=-1, keepdims=True) + 1e-06)
    unit_vec = pooled * inverse_norm
    embedding = unit_vec.astype(jnp.bfloat16)
    devices = lax.axis_size("pb")
    capacity = 2 * seq_count // devices
    pair_count = pair_owner.shape[0]
    wanted = jnp.concatenate([pair_owner[:, 0], pair_owner[:, 1]])
    holder = wanted // seq_count
    within = wanted % seq_count
    entry_ids = jnp.arange(2 * pair_count, dtype=jnp.int32)
    earlier = (holder[None, :] == holder[:, None]) & (entry_ids[None, :] < entry_ids[:, None])
    position = jnp.sum(earlier.astype(jnp.int32), axis=1)
    request = jnp.full((devices, capacity), -1, jnp.int32).at[holder, position].set(within)
    served = lax.all_to_all(request, "pb", split_axis=0, concat_axis=0, tiled=True)
    outgoing = jnp.where(
        served[:, :, None] >= 0, embedding[jnp.maximum(served, 0)], jnp.zeros((), jnp.bfloat16)
    )
    received = lax.all_to_all(outgoing, "pb", split_axis=0, concat_axis=0, tiled=True)
    gathered = received[holder, position]
    queries = gathered[:pair_count]
    own_docs = gathered[pair_count:]
    listed_ids = hard_negatives[0]
    window = hard_negatives.shape[1]
    listed = [listed_ids[offset] >= 0 for offset in range(window)]
    neighbours = []
    moving = own_docs
    for offset in range(window):
        moving = from_behind(moving, "pb", -1)
        neighbours.append(moving)
    tile_shape = (pair_count, pair_count)
    score_blocks = [similarity(queries, own_docs)]
    for offset in range(window):
        score_blocks.append(
            skipped(listed[offset], similarity, (queries, neighbours[offset]), tile_shape)
        )
    all_scores = jnp.concatenate(score_blocks, axis=1)
    usable = jnp.concatenate(
        [jnp.ones((pair_count,), jnp.bool_)]
        + [jnp.broadcast_to(listed[offset], (pair_count,)) for offset in range(window)]
    )
    masked = jnp.where(usable[None, :], all_scores, -jnp.inf)
    row_max = jnp.max(masked, axis=1, keepdims=True)
    log_total = row_max + jnp.log(jnp.sum(jnp.exp(masked - row_max), axis=1, keepdims=True))
    diagonal = jnp.arange(pair_count, dtype=jnp.int32)
    positive = all_scores[diagonal, diagonal]
    block_loss = jnp.mean(log_total[:, 0] - positive).reshape(1)
    columns = jnp.arange((window + 1) * pair_count, dtype=jnp.int32)
    target = (columns[None, :] == diagonal[:, None]).astype(jnp.float32)
    coefficients = (inverse_temp * (jnp.exp(masked - log_total) - target)).astype(jnp.bfloat16)
    pieces = [
        coefficients[:, offset * pair_count : (offset + 1) * pair_count]
        for offset in range(window + 1)
    ]
    grad_shape = (pair_count, model_width)
    query_sum = combine_docs(pieces[0], own_docs)
    for offset in range(window):
        query_sum = query_sum + skipped(
            listed[offset], combine_docs, (pieces[offset + 1], neighbours[offset]), grad_shape
        )
    query_grad = query_sum.astype(jnp.bfloat16)
    own_part = transposed(pieces[0], queries).astype(jnp.bfloat16)
    partial_value = [
        skipped(listed[offset], transposed, (pieces[offset + 1], queries), grad_shape).astype(
            jnp.bfloat16
        )
        for offset in range(window)
    ]
    running = partial_value[window - 1].astype(jnp.float32)
    for offset in range(window):
        running = from_behind(running, "pb", 1)
        if offset + 1 < window:
            running = running + partial_value[window - 2 - offset].astype(jnp.float32)
    doc_grad = (own_part.astype(jnp.float32) + running).astype(jnp.bfloat16)
    answers = jnp.concatenate([query_grad, doc_grad], axis=0)
    returning = (
        jnp.zeros((devices, capacity, model_width), jnp.bfloat16).at[holder, position].set(answers)
    )
    returned = lax.all_to_all(returning, "pb", split_axis=0, concat_axis=0, tiled=True)
    slot_ids = jnp.where(served >= 0, served, seq_count).reshape(-1)
    emb_grad = (
        jnp.zeros((seq_count, model_width), jnp.bfloat16)
        .at[slot_ids]
        .set(returned.reshape(-1, model_width), mode="drop")
    )
    gradient = emb_grad.astype(jnp.float32)
    pooled_grad = gradient - unit_vec * jnp.sum(unit_vec * gradient, axis=-1, keepdims=True)
    return (pooled_grad, block_loss)


def solution(mesh):
    def local(hidden, final_gain, last_row, pair_owner, hard_negatives):
        plan = feature_plan if hidden.shape[1] >= lanes * mesh.shape["pb"] else row_plan
        return plan(hidden, final_gain, last_row, pair_owner, hard_negatives)

    return jax.shard_map(
        local,
        mesh=mesh,
        in_specs=(
            P(("groups", "pb"), None),
            P(),
            P(("groups", "pb"), None),
            P(("groups", "pb"), None),
            P(("groups", "pb"), None),
        ),
        out_specs=(P(("groups", "pb"), None), P(("groups", "pb"))),
        check_vma=False,
    )
```

```python
import functools

import jax
import jax.numpy as jnp
from jax import lax
from jax.experimental import pallas as pl
from jax.experimental.pallas import tpu as pltpu
from jax.sharding import PartitionSpec as P

inverse_temp = 50.0
token_eps = 1e-05
unit_eps = 1e-06
lanes = 128
bound_steps = 256.0
code_steps = 32000.0
mebibyte = 1024 * 1024


def spread(target, at, value):
    count = value.shape[0]
    for half in range(2):
        target[pl.ds(2 * at + half, count, stride=2), :] = value[:, half * lanes : (half + 1) * lanes]


def gathered(source, at, count):
    halves = [source[pl.ds(2 * at + half, count, stride=2), :] for half in range(2)]
    return jnp.concatenate(halves, axis=1)


def row_pair(index):
    return pl.ds(pl.multiple_of(2 * index, 2), 2)


def norm_kernel(
    last_ref, hidden_ref, gain_ref, owner_ref, negative_ref, normed_ref, inv_ref, emb_ref
):
    seqs, width = normed_ref.shape
    parts, _, piece = emb_ref.shape
    pairs = owner_ref.shape[1]
    cuts = [slice(part * piece, (part + 1) * piece) for part in range(parts)]
    sources = lax.broadcasted_iota(jnp.int32, (seqs, seqs), 0)
    pick = jnp.where(sources == last_ref[...], 1.0, 0.0).astype(jnp.bfloat16)

    def folded(squares):
        return functools.reduce(
            jnp.add, [squares[:, at : at + lanes] for at in range(0, piece, lanes)]
        )

    total = jnp.zeros((seqs, lanes), jnp.float32)
    for cut in cuts:
        values = lax.dot_general(
            pick, hidden_ref[:, cut], (((0,), (0,)), ((), ())), preferred_element_type=jnp.float32
        )
        normed_ref[:, cut] = values.astype(jnp.bfloat16)
        total = total + folded(values * values)
    scale = lax.rsqrt(jnp.sum(total, axis=-1, keepdims=True) / width + token_eps)
    total = jnp.zeros((seqs, lanes), jnp.float32)
    for cut in cuts:
        values = normed_ref[:, cut].astype(jnp.float32)
        gain = gain_ref[cut].astype(jnp.float32).reshape(1, piece)
        normed = (values * scale * gain).astype(jnp.bfloat16)
        normed_ref[:, cut] = normed
        pooled = normed.astype(jnp.float32)
        total = total + folded(pooled * pooled)
    inverse = lax.rsqrt(jnp.sum(total, axis=-1, keepdims=True) + unit_eps)
    inv_ref[...] = jnp.broadcast_to(inverse, inv_ref.shape)

    owners = owner_ref[...].astype(jnp.float32)
    high = jnp.floor(owners * (1.0 / 256.0))
    low = owners - 256.0 * high
    row = lax.broadcasted_iota(jnp.int32, (16, pairs), 0)
    spot = lax.broadcasted_iota(jnp.int32, (16, pairs), 1)
    left = jnp.where(row == 0, low[:1], jnp.where(row == 1, high[:1], 0.0))
    right = jnp.where(row == 0, low[1:2], jnp.where(row == 1, high[1:2], 0.0))
    for offset in range(negative_ref.shape[1]):
        named = (negative_ref[0, offset] >= 0).astype(jnp.float32)
        left = jnp.where((row == 2) & (spot == offset), named, left)
    facts = jnp.concatenate([left, right], axis=1).astype(jnp.bfloat16)

    for part, cut in enumerate(cuts):
        emb_ref[part, :seqs] = (normed_ref[:, cut].astype(jnp.float32) * inverse).astype(jnp.bfloat16)
        emb_ref[part, seqs:] = facts


def norm_call(last_row, hidden, gain, owners, hard_negatives, parts):
    seqs, width = hidden.shape
    piece = width // parts
    whole = pl.BlockSpec(memory_space=pltpu.VMEM)
    return pl.pallas_call(
        norm_kernel,
        in_specs=[whole, whole, whole, whole, pl.BlockSpec(memory_space=pltpu.SMEM)],
        out_specs=[whole] * 3,
        out_shape=[
            jax.ShapeDtypeStruct((seqs, width), jnp.bfloat16),
            jax.ShapeDtypeStruct((seqs, lanes), jnp.float32),
            jax.ShapeDtypeStruct((parts, seqs + 16, piece), jnp.bfloat16),
        ],
        compiler_params=pltpu.CompilerParams(vmem_limit_bytes=14 * mebibyte),
        name="norm_rows",
    )(last_row, hidden, gain, owners, hard_negatives)


def score_kernel(
    blocks,
    pairs,
    window,
    *refs,
):
    emb_ref, q_ref, d_ref, mine_ref, other_ref, top_ref, own_ref, place_ref = refs[:-7]
    wide, picked, tiles, facts, own, named, sems = refs[-7:]
    seqs = emb_ref.shape[1] - 16
    sent = emb_ref[:, seqs:, :].astype(jnp.float32)
    own_ref[...] = (sent[:, 0, :] + 256.0 * sent[:, 1, :]).astype(jnp.int32)
    facts[...] = sent[:, 2, :lanes].astype(jnp.int32)
    fetches = [
        pltpu.make_async_copy(own_ref, own, sems.at[0]),
        pltpu.make_async_copy(facts, named, sems.at[1]),
    ]
    for fetch in fetches:
        fetch.start()

    for part in range(blocks):
        spread(wide, part * seqs, emb_ref[part, :seqs, :].astype(jnp.float32))
    for fetch in fetches:
        fetch.wait()

    def place(block, count):
        place_ref[0, block] = block
        for offset in range(window):
            present = named[block, offset] > 0
            place_ref[offset + 1, block] = jnp.where(present, count, -1)
            count = count + present.astype(jnp.int32)
        return count

    used = lax.fori_loop(0, blocks, place, blocks)
    fine = pairs // blocks

    def clear(spot, carry):
        empty = jnp.zeros((blocks // 2, fine, pairs), jnp.float32)
        at = pl.ds(pl.multiple_of(spot * fine, fine), fine)
        mine_ref[:, at, :] = empty
        other_ref[:, at, :] = empty
        return carry

    lax.fori_loop(used, mine_ref.shape[1] // fine, clear, 0)
    unroll = 32

    def pick_block(block, carry):
        def pick_rows(step, inner):
            base = pl.multiple_of(step * unroll, unroll)
            rows = [wide[row_pair(own[block, base + k]), :] for k in range(unroll)]
            for k in range(unroll):
                picked[row_pair(base + k), :] = rows[k]
            return inner

        lax.fori_loop(0, 2 * pairs // unroll, pick_rows, 0)
        at = pl.multiple_of(block * pairs, pairs)
        q_ref[pl.ds(at, pairs), :] = gathered(picked, 0, pairs).astype(jnp.bfloat16)
        d_ref[pl.ds(at, pairs), :] = gathered(picked, pairs, pairs).astype(jnp.bfloat16)
        return carry

    lax.fori_loop(0, blocks, pick_block, 0)
    d_ref[blocks * pairs :, :] = d_ref[: window * pairs, :]
    even = lax.axis_index("pb") % 2 == 0
    top_ref[...] = jnp.zeros_like(top_ref)

    def score_blocks(step, carry):
        at = pl.multiple_of(step * 2 * pairs, 2 * pairs)
        tiles[...] = inverse_temp * lax.dot_general(
            q_ref[pl.ds(at, 2 * pairs), :],
            d_ref[pl.ds(at, (window + 2) * pairs), :],
            (((1,), (1,)), ((), ())),
            preferred_element_type=jnp.float32,
        )
        for half in range(2):
            for column in range(window + 1):
                spot = place_ref[column, 2 * step + half]

                @pl.when(spot >= 0)
                def _():
                    row = pl.multiple_of(spot * fine, fine)
                    tile = tiles[
                        half * pairs : (half + 1) * pairs,
                        (half + column) * pairs : (half + column + 1) * pairs,
                    ]
                    parted = tile.reshape(blocks // 2, 2, fine, pairs)
                    first, second = parted[:, 0], parted[:, 1]
                    mine_ref[:, pl.ds(row, fine), :] = jnp.where(even, first, second)
                    other_ref[:, pl.ds(row, fine), :] = jnp.where(even, second, first)
                    size = jnp.maximum(jnp.abs(first), jnp.abs(second))
                    top_ref[...] = jnp.maximum(top_ref[...], jnp.max(size, axis=0))

        return carry

    lax.fori_loop(0, blocks // 2, score_blocks, 0)


def score_call(embedded, room, blocks, pairs, window):
    _, rows, piece = embedded.shape
    fine = pairs // blocks
    whole = pl.BlockSpec(memory_space=pltpu.VMEM)
    scalars = pl.BlockSpec(memory_space=pltpu.SMEM)
    return pl.pallas_call(
        functools.partial(score_kernel, blocks, pairs, window),
        in_specs=[whole],
        out_specs=[whole, whole, whole, whole, whole, whole, scalars],
        out_shape=[
            jax.ShapeDtypeStruct((blocks * pairs, piece), jnp.bfloat16),
            jax.ShapeDtypeStruct(((blocks + window) * pairs, piece), jnp.bfloat16),
            jax.ShapeDtypeStruct((blocks // 2, room * fine, pairs), jnp.float32),
            jax.ShapeDtypeStruct((blocks // 2, room * fine, pairs), jnp.float32),
            jax.ShapeDtypeStruct((fine, pairs), jnp.float32),
            jax.ShapeDtypeStruct((blocks, 2 * pairs), jnp.int32),
            jax.ShapeDtypeStruct((window + 1, blocks), jnp.int32),
        ],
        scratch_shapes=[
            pltpu.VMEM((2 * blocks * (rows - 16), lanes), jnp.float32),
            pltpu.VMEM((4 * pairs, lanes), jnp.float32),
            pltpu.VMEM((2 * pairs, (window + 2) * pairs), jnp.float32),
            pltpu.VMEM((blocks, lanes), jnp.int32),
            pltpu.SMEM((blocks, 2 * pairs), jnp.int32),
            pltpu.SMEM((blocks, lanes), jnp.int32),
            pltpu.SemaphoreType.DMA((2,)),
        ],
        compiler_params=pltpu.CompilerParams(vmem_limit_bytes=22 * mebibyte),
        name="partial_scores",
    )(embedded)


def merge_kernel(mine_ref, other_ref, top_ref, other_top_ref, own_ref, *code_refs):
    chips, rows, pairs = mine_ref.shape
    steps = code_refs[0].shape[0] - 1
    fine = rows // steps // 2
    chip = lax.axis_index("pb") // 2

    def highest(ref):
        return jnp.max(jnp.max(ref[...], axis=1, keepdims=True), axis=0, keepdims=True)

    top = highest(top_ref) + highest(other_top_ref)
    bound = jnp.ceil(top * bound_steps) + 1.0
    scale = code_steps * bound_steps / bound
    own_ref[...] = mine_ref[chip] + other_ref[chip]
    for hop, code_ref in enumerate(code_refs):
        target = chip ^ (hop + 1)

        def encode(step, carry):
            at = pl.multiple_of(step * 2 * fine, 2 * fine)
            there = pl.ds(at, 2 * fine)
            codes = jnp.round((mine_ref[target, there, :] + other_ref[target, there, :]) * scale)
            code_ref[step] = codes.astype(jnp.int32).astype(jnp.int16)
            return carry

        lax.fori_loop(0, steps, encode, 0)
        code_ref[steps] = jnp.broadcast_to(bound, (2 * fine, pairs)).astype(jnp.int32).astype(jnp.int16)


def merge_call(mine, other, top, other_top, blocks):
    chips, rows, pairs = mine.shape
    fine = pairs // blocks
    whole = pl.BlockSpec(memory_space=pltpu.VMEM)
    coded = jax.ShapeDtypeStruct((rows // (2 * fine) + 1, 2 * fine, pairs), jnp.int16)
    return pl.pallas_call(
        merge_kernel,
        in_specs=[whole] * 4,
        out_specs=[whole] * chips,
        out_shape=[jax.ShapeDtypeStruct((rows, pairs), jnp.float32)] + [coded] * (chips - 1),
        compiler_params=pltpu.CompilerParams(vmem_limit_bytes=12 * mebibyte),
        name="merge_scores",
    )(mine, other, top, other_top)


def softmax_kernel(blocks, window, place_ref, own_ref, *refs):
    code_refs, (c_ref, packed, masked) = refs[:-3], refs[-3:]
    room, fine, pairs = packed.shape
    count = blocks * fine
    unit = 1.0 / (code_steps * bound_steps)
    scales = [ref[room // 2].astype(jnp.int32).astype(jnp.float32) * unit for ref in code_refs]

    def decode(step, carry):
        both = own_ref[pl.ds(pl.multiple_of(step * 2 * fine, 2 * fine), 2 * fine), :]
        for ref, scale in zip(code_refs, scales):
            both = both + ref[step].astype(jnp.int32).astype(jnp.float32) * scale
        packed[2 * step] = both[:fine]
        packed[2 * step + 1] = both[fine:]
        return carry

    lax.fori_loop(0, room // 2, decode, 0)
    for block in range(blocks):
        for column in range(window + 1):
            spot = place_ref[column, block]
            tile = packed[jnp.maximum(spot, 0)]
            masked[block * fine : (block + 1) * fine, column * pairs : (column + 1) * pairs] = (
                jnp.where(spot >= 0, tile, -jnp.inf)
            )
    row = lax.broadcasted_iota(jnp.int32, (count, pairs), 0)
    lane = lax.broadcasted_iota(jnp.int32, (count, pairs), 1)
    target = lane == lax.axis_index("pb") * fine + row % fine
    pieces = [masked[:, column * pairs : (column + 1) * pairs] for column in range(window + 1)]
    row_max = jnp.max(functools.reduce(jnp.maximum, pieces), axis=1, keepdims=True)
    total = functools.reduce(jnp.add, [jnp.exp(piece - row_max) for piece in pieces])
    log_total = row_max + jnp.log(jnp.sum(total, axis=1, keepdims=True))
    positive = jnp.sum(jnp.where(target, pieces[0], 0.0), axis=1, keepdims=True)
    for column, piece in enumerate(pieces):
        share = jnp.exp(piece - log_total)
        if column == 0:
            share = share - jnp.where(target, 1.0, 0.0)
        masked[:, column * pairs : (column + 1) * pairs] = inverse_temp * share
    for block in range(blocks):
        for column in range(window + 1):
            spot = place_ref[column, block]

            @pl.when(spot >= 0)
            def _():
                packed[spot] = masked[
                    block * fine : (block + 1) * fine, column * pairs : (column + 1) * pairs
                ]

    for step in range(room // 2):
        both = jnp.concatenate([packed[2 * step], packed[2 * step + 1]], axis=0)
        c_ref[step] = both.astype(jnp.bfloat16)
    losses = jnp.sum(
        jnp.where(lane == row // fine, log_total - positive, 0.0), axis=0, keepdims=True
    )
    coarse = losses.astype(jnp.bfloat16).astype(jnp.float32)
    rank = lax.broadcasted_iota(jnp.int32, (2 * fine, pairs), 0)
    both = jnp.where(rank == 0, coarse, jnp.where(rank == 1, losses - coarse, 0.0))
    c_ref[room // 2] = both.astype(jnp.bfloat16)


def softmax_call(place, own_scores, codes, blocks, window):
    steps, fine, pairs = codes[0].shape
    room, fine = 2 * (steps - 1), fine // 2
    whole = pl.BlockSpec(memory_space=pltpu.VMEM)
    return pl.pallas_call(
        functools.partial(softmax_kernel, blocks, window),
        in_specs=[pl.BlockSpec(memory_space=pltpu.SMEM), whole] + [whole] * len(codes),
        out_specs=whole,
        out_shape=jax.ShapeDtypeStruct((room // 2 + 1, 2 * fine, pairs), jnp.bfloat16),
        scratch_shapes=[
            pltpu.VMEM((room, fine, pairs), jnp.float32),
            pltpu.VMEM((blocks * fine, (window + 1) * pairs), jnp.float32),
        ],
        compiler_params=pltpu.CompilerParams(vmem_limit_bytes=8 * mebibyte),
        name="softmax_rows",
    )(place, own_scores, *codes)


def grad_kernel(
    blocks,
    pairs,
    window,
    own_ref,
    place_ref,
    q_ref,
    d_ref,
    *refs,
):
    part_refs = refs[:-7]
    out_ref, loss_ref, wide, dsum, picked, packed, square = refs[-7:]
    fine = pairs // blocks
    room = packed.shape[1]
    me = lax.axis_index("pb")
    masks = swap_masks(blocks)
    unroll = 32
    losses = 0.0
    for part in part_refs:
        sent = part[:, room // 2].astype(jnp.float32)
        losses = losses + jnp.sum(sent[:, 0, :] + sent[:, 1, :], axis=0, keepdims=True) / pairs
    lane = lax.broadcasted_iota(jnp.int32, losses.shape, 1)
    mine = jnp.where(lane == me, losses, 0.0)
    loss_ref[...] = jnp.broadcast_to(jnp.sum(mine, axis=1, keepdims=True), loss_ref.shape)
    dsum[...] = jnp.zeros_like(dsum)
    square[...] = jnp.zeros_like(square)

    def unpack(step, carry):
        for part, mask in zip(part_refs, masks):
            both = part[:, step].astype(jnp.float32)
            for at, apart in enumerate(mask):
                packed[me ^ apart, 2 * step] = both[at, :fine]
                packed[me ^ apart, 2 * step + 1] = both[at, fine:]
        return carry

    lax.fori_loop(0, room // 2, unpack, 0)

    def scatter_rows(block, offset, start):
        def step_rows(step, inner):
            base = pl.multiple_of(step * unroll, unroll)
            rows = [picked[row_pair(start + base + k), :] for k in range(unroll)]
            for k in range(unroll):
                wide[row_pair(own_ref[block, offset + base + k]), :] = rows[k]
            return inner

        lax.fori_loop(0, pairs // unroll, step_rows, 0)

    def two_blocks(step, carry):
        for half in range(2):
            for column in range(window + 1):
                spot = place_ref[column, 2 * step + half]
                tile = packed[:, jnp.maximum(spot, 0)].reshape(pairs, pairs)
                square[
                    half * pairs : (half + 1) * pairs,
                    (half + column) * pairs : (half + column + 1) * pairs,
                ] = jnp.where(spot >= 0, tile, 0.0).astype(jnp.bfloat16)
        at = pl.multiple_of(step * 2 * pairs, 2 * pairs)
        there = pl.ds(at, (window + 2) * pairs)
        coefficients = square[...]
        summed = jnp.dot(coefficients, d_ref[there, :], preferred_element_type=jnp.float32)
        spread(picked, 0, summed)
        dsum[there, :] += lax.dot_general(
            coefficients,
            q_ref[pl.ds(at, 2 * pairs), :],
            (((0,), (0,)), ((), ())),
            preferred_element_type=jnp.float32,
        )
        for half in range(2):
            scatter_rows(2 * step + half, 0, half * pairs)
        return carry

    lax.fori_loop(0, blocks // 2, two_blocks, 0)
    dsum[: window * pairs, :] += dsum[blocks * pairs :, :]

    def doc_block(block, carry):
        at = pl.multiple_of(block * pairs, pairs)
        spread(picked, 0, dsum[pl.ds(at, pairs), :])
        scatter_rows(block, pairs, 0)
        return carry

    lax.fori_loop(0, blocks, doc_block, 0)
    slots = out_ref.shape[1]
    for part in range(blocks):
        out_ref[part] = gathered(wide, part * slots, slots).astype(jnp.bfloat16)


def grad_call(own, place, parts, queries, documents, blocks, pairs, window):
    count, piece = queries.shape
    seqs = 2 * count
    room = 2 * (parts[0].shape[1] - 1)
    whole = pl.BlockSpec(memory_space=pltpu.VMEM)
    scalars = pl.BlockSpec(memory_space=pltpu.SMEM)
    return pl.pallas_call(
        functools.partial(grad_kernel, blocks, pairs, window),
        in_specs=[scalars, scalars, whole, whole] + [whole] * len(parts),
        out_specs=[whole, whole],
        out_shape=[
            jax.ShapeDtypeStruct((blocks, seqs // blocks, piece), jnp.bfloat16),
            jax.ShapeDtypeStruct((1, lanes), jnp.float32),
        ],
        scratch_shapes=[
            pltpu.VMEM((2 * seqs, lanes), jnp.float32),
            pltpu.VMEM(((blocks + window) * pairs, piece), jnp.float32),
            pltpu.VMEM((4 * pairs, lanes), jnp.float32),
            pltpu.VMEM((blocks, room, pairs // blocks, pairs), jnp.float32),
            pltpu.VMEM((2 * pairs, (window + 2) * pairs), jnp.bfloat16),
        ],
        compiler_params=pltpu.CompilerParams(vmem_limit_bytes=26 * mebibyte),
        name="slice_grads",
    )(own, place, queries, documents, *parts)


def project_kernel(grad_ref, normed_ref, inv_ref, out_ref):
    parts, _, piece = grad_ref.shape
    cuts = [slice(part * piece, (part + 1) * piece) for part in range(parts)]
    inverse = inv_ref[:, :1]
    total = 0.0
    for part, cut in enumerate(cuts):
        unit = normed_ref[:, cut].astype(jnp.float32) * inverse
        total = total + unit * grad_ref[part].astype(jnp.float32)
    along = jnp.sum(total, axis=-1, keepdims=True)
    for part, cut in enumerate(cuts):
        unit = normed_ref[:, cut].astype(jnp.float32) * inverse
        out_ref[:, cut] = grad_ref[part].astype(jnp.float32) - unit * along


def project_call(returned, normed, inverse):
    parts, seqs, piece = returned.shape
    width = normed.shape[1]
    rows = 64
    return pl.pallas_call(
        project_kernel,
        grid=(seqs // rows,),
        in_specs=[
            pl.BlockSpec((parts, rows, piece), lambda i: (0, i, 0)),
            pl.BlockSpec((rows, width), lambda i: (i, 0)),
            pl.BlockSpec((rows, lanes), lambda i: (i, 0)),
        ],
        out_specs=pl.BlockSpec((rows, width), lambda i: (i, 0)),
        out_shape=jax.ShapeDtypeStruct((seqs, width), jnp.float32),
        compiler_params=pltpu.CompilerParams(vmem_limit_bytes=10 * mebibyte),
        name="project_out",
    )(returned, normed, inverse)


def swapped(value, apart):
    pairs = [(at, at ^ apart) for at in range(lax.axis_size("pb"))]
    return lax.ppermute(value, "pb", pairs)


def swap_bits(devices):
    bits = [1 << bit for bit in reversed(range(devices.bit_length() - 1))]
    return bits[:-2], bits[-2], bits[-1]


def swap_masks(devices):
    far, side, last = swap_bits(devices)
    held = [0]
    for apart in far:
        held = held + [mask ^ apart for mask in held]
    held = held + [mask ^ side for mask in held]
    return [held, [mask ^ last for mask in held]]


def gather_all(value):
    far, side, last = swap_bits(lax.axis_size("pb"))
    held = value[None]
    beside = [swapped(held, side)]
    for apart in far:
        arrived = swapped(held, apart)
        beside.append(swapped(arrived, side))
        held = jnp.concatenate([held, arrived], axis=0)
    held = jnp.concatenate([held] + beside, axis=0)
    return [held, swapped(held, last)]


def middle(embedded, room, devices, pairs, window):
    queries, documents, mine, other, top, own, place = score_call(
        embedded, room, devices, pairs, window
    )
    own_scores, *codes = merge_call(mine, swapped(other, 1), top, swapped(top, 1), devices)
    codes = [swapped(code, 2 * (hop + 1)) for hop, code in enumerate(codes)]
    parts = gather_all(softmax_call(place, own_scores, codes, devices, window))
    grads, loss = grad_call(own, place, parts, queries, documents, devices, pairs, window)
    return grads, loss[0, :1]


def feature_plan(hidden, final_gain, last_row, pair_owner, hard_negatives):
    devices = lax.axis_size("pb")
    seqs, width = hidden.shape
    pairs = pair_owner.shape[0]
    window = hard_negatives.shape[1]
    normed, inverse, embedding = norm_call(
        last_row, hidden, final_gain, pair_owner.T, hard_negatives, devices
    )
    embedded = lax.all_to_all(embedding, "pb", split_axis=0, concat_axis=0, tiled=True)
    most = devices * (window + 1)
    rooms = [most * part // 20 for part in (10, 11, 12, 13, 14, 16, 20)]
    used = devices + jnp.sum(embedded[:, seqs + 2, :window].astype(jnp.float32))
    level = sum((used > room).astype(jnp.int32) for room in rooms[:-1])
    grads, loss = lax.switch(
        level,
        [
            functools.partial(middle, room=room, devices=devices, pairs=pairs, window=window)
            for room in rooms
        ],
        embedded,
    )
    returned = lax.all_to_all(grads, "pb", split_axis=0, concat_axis=0, tiled=True)
    return project_call(returned, normed, inverse), loss


def from_behind(value, axis, steps):
    count = lax.axis_size(axis)
    pairs = [(source, (source + steps) % count) for source in range(count)]
    return lax.ppermute(value, axis, pairs)


def similarity(queries, documents):
    return inverse_temp * lax.dot_general(
        queries, documents, (((1,), (1,)), ((), ())), preferred_element_type=jnp.float32
    )


def transposed(weights, queries):
    return lax.dot_general(
        weights, queries, (((0,), (0,)), ((), ())), preferred_element_type=jnp.float32
    )


def combine_docs(weights, documents):
    return jnp.dot(weights, documents, preferred_element_type=jnp.float32)


def skipped(listed, function, operands, out_shape):
    return lax.cond(
        listed,
        lambda inputs: function(*inputs),
        lambda inputs: jnp.zeros(out_shape, jnp.float32),
        operands,
    )


def row_plan(hidden, final_gain, last_row, pair_owner, hard_negatives):
    values = hidden.astype(jnp.float32)
    scale_row = lax.rsqrt(jnp.mean(values * values, axis=-1, keepdims=True) + token_eps)
    normed = (values * scale_row * final_gain.astype(jnp.float32)).astype(jnp.bfloat16)
    seq_count = last_row.shape[1]
    model_width = hidden.shape[1]
    pooled = normed[last_row[0]].astype(jnp.float32)
    inverse_norm = lax.rsqrt(jnp.sum(pooled * pooled, axis=-1, keepdims=True) + 1e-06)
    unit_vec = pooled * inverse_norm
    embedding = unit_vec.astype(jnp.bfloat16)
    devices = lax.axis_size("pb")
    capacity = 2 * seq_count // devices
    pair_count = pair_owner.shape[0]
    wanted = jnp.concatenate([pair_owner[:, 0], pair_owner[:, 1]])
    holder = wanted // seq_count
    within = wanted % seq_count
    entry_ids = jnp.arange(2 * pair_count, dtype=jnp.int32)
    earlier = (holder[None, :] == holder[:, None]) & (entry_ids[None, :] < entry_ids[:, None])
    position = jnp.sum(earlier.astype(jnp.int32), axis=1)
    request = jnp.full((devices, capacity), -1, jnp.int32).at[holder, position].set(within)
    served = lax.all_to_all(request, "pb", split_axis=0, concat_axis=0, tiled=True)
    outgoing = jnp.where(
        served[:, :, None] >= 0, embedding[jnp.maximum(served, 0)], jnp.zeros((), jnp.bfloat16)
    )
    received = lax.all_to_all(outgoing, "pb", split_axis=0, concat_axis=0, tiled=True)
    gathered = received[holder, position]
    queries = gathered[:pair_count]
    own_docs = gathered[pair_count:]
    listed_ids = hard_negatives[0]
    window = hard_negatives.shape[1]
    listed = [listed_ids[offset] >= 0 for offset in range(window)]
    neighbours = []
    moving = own_docs
    for offset in range(window):
        moving = from_behind(moving, "pb", -1)
        neighbours.append(moving)
    tile_shape = (pair_count, pair_count)
    score_blocks = [similarity(queries, own_docs)]
    for offset in range(window):
        score_blocks.append(
            skipped(listed[offset], similarity, (queries, neighbours[offset]), tile_shape)
        )
    all_scores = jnp.concatenate(score_blocks, axis=1)
    usable = jnp.concatenate(
        [jnp.ones((pair_count,), jnp.bool_)]
        + [jnp.broadcast_to(listed[offset], (pair_count,)) for offset in range(window)]
    )
    masked = jnp.where(usable[None, :], all_scores, -jnp.inf)
    row_max = jnp.max(masked, axis=1, keepdims=True)
    log_total = row_max + jnp.log(jnp.sum(jnp.exp(masked - row_max), axis=1, keepdims=True))
    diagonal = jnp.arange(pair_count, dtype=jnp.int32)
    positive = all_scores[diagonal, diagonal]
    block_loss = jnp.mean(log_total[:, 0] - positive).reshape(1)
    columns = jnp.arange((window + 1) * pair_count, dtype=jnp.int32)
    target = (columns[None, :] == diagonal[:, None]).astype(jnp.float32)
    coefficients = (inverse_temp * (jnp.exp(masked - log_total) - target)).astype(jnp.bfloat16)
    pieces = [
        coefficients[:, offset * pair_count : (offset + 1) * pair_count]
        for offset in range(window + 1)
    ]
    grad_shape = (pair_count, model_width)
    query_sum = combine_docs(pieces[0], own_docs)
    for offset in range(window):
        query_sum = query_sum + skipped(
            listed[offset], combine_docs, (pieces[offset + 1], neighbours[offset]), grad_shape
        )
    query_grad = query_sum.astype(jnp.bfloat16)
    own_part = transposed(pieces[0], queries).astype(jnp.bfloat16)
    partial_value = [
        skipped(listed[offset], transposed, (pieces[offset + 1], queries), grad_shape).astype(
            jnp.bfloat16
        )
        for offset in range(window)
    ]
    running = partial_value[window - 1].astype(jnp.float32)
    for offset in range(window):
        running = from_behind(running, "pb", 1)
        if offset + 1 < window:
            running = running + partial_value[window - 2 - offset].astype(jnp.float32)
    doc_grad = (own_part.astype(jnp.float32) + running).astype(jnp.bfloat16)
    answers = jnp.concatenate([query_grad, doc_grad], axis=0)
    returning = (
        jnp.zeros((devices, capacity, model_width), jnp.bfloat16).at[holder, position].set(answers)
    )
    returned = lax.all_to_all(returning, "pb", split_axis=0, concat_axis=0, tiled=True)
    slot_ids = jnp.where(served >= 0, served, seq_count).reshape(-1)
    emb_grad = (
        jnp.zeros((seq_count, model_width), jnp.bfloat16)
        .at[slot_ids]
        .set(returned.reshape(-1, model_width), mode="drop")
    )
    gradient = emb_grad.astype(jnp.float32)
    pooled_grad = gradient - unit_vec * jnp.sum(unit_vec * gradient, axis=-1, keepdims=True)
    return (pooled_grad, block_loss)


def solution(mesh):
    def local(hidden, final_gain, last_row, pair_owner, hard_negatives):
        plan = feature_plan if hidden.shape[1] >= lanes * mesh.shape["pb"] else row_plan
        return plan(hidden, final_gain, last_row, pair_owner, hard_negatives)

    return jax.shard_map(
        local,
        mesh=mesh,
        in_specs=(
            P(("groups", "pb"), None),
            P(),
            P(("groups", "pb"), None),
            P(("groups", "pb"), None),
            P(("groups", "pb"), None),
        ),
        out_specs=(P(("groups", "pb"), None), P(("groups", "pb"))),
        check_vma=False,
    )
```

```python
import functools

import jax
import jax.numpy as jnp
from jax import lax
from jax.experimental import pallas as pl
from jax.experimental.pallas import tpu as pltpu
from jax.sharding import PartitionSpec as P

inverse_temp = 50.0
token_eps = 1e-05
unit_eps = 1e-06
lanes = 128
bound_steps = 256.0
code_steps = 32000.0
mebibyte = 1024 * 1024


def spread(target, at, value):
    count = value.shape[0]
    for half in range(2):
        target[pl.ds(2 * at + half, count, stride=2), :] = value[:, half * lanes : (half + 1) * lanes]


def gathered(source, at, count):
    halves = [source[pl.ds(2 * at + half, count, stride=2), :] for half in range(2)]
    return jnp.concatenate(halves, axis=1)


def row_pair(index):
    return pl.ds(pl.multiple_of(2 * index, 2), 2)


def norm_kernel(
    last_ref, hidden_ref, gain_ref, owner_ref, negative_ref, normed_ref, inv_ref, emb_ref
):
    seqs, width = normed_ref.shape
    parts, _, piece = emb_ref.shape
    pairs = owner_ref.shape[1]
    cuts = [slice(part * piece, (part + 1) * piece) for part in range(parts)]
    sources = lax.broadcasted_iota(jnp.int32, (seqs, seqs), 0)
    pick = jnp.where(sources == last_ref[...], 1.0, 0.0).astype(jnp.bfloat16)

    def folded(squares):
        return functools.reduce(
            jnp.add, [squares[:, at : at + lanes] for at in range(0, piece, lanes)]
        )

    total = jnp.zeros((seqs, lanes), jnp.float32)
    for cut in cuts:
        values = lax.dot_general(
            pick, hidden_ref[:, cut], (((0,), (0,)), ((), ())), preferred_element_type=jnp.float32
        )
        normed_ref[:, cut] = values.astype(jnp.bfloat16)
        total = total + folded(values * values)
    scale = lax.rsqrt(jnp.sum(total, axis=-1, keepdims=True) / width + token_eps)
    total = jnp.zeros((seqs, lanes), jnp.float32)
    for cut in cuts:
        values = normed_ref[:, cut].astype(jnp.float32)
        gain = gain_ref[cut].astype(jnp.float32).reshape(1, piece)
        normed = (values * scale * gain).astype(jnp.bfloat16)
        normed_ref[:, cut] = normed
        pooled = normed.astype(jnp.float32)
        total = total + folded(pooled * pooled)
    inverse = lax.rsqrt(jnp.sum(total, axis=-1, keepdims=True) + unit_eps)
    inv_ref[...] = jnp.broadcast_to(inverse, inv_ref.shape)

    owners = owner_ref[...].astype(jnp.float32)
    high = jnp.floor(owners * (1.0 / 256.0))
    low = owners - 256.0 * high
    row = lax.broadcasted_iota(jnp.int32, (16, pairs), 0)
    spot = lax.broadcasted_iota(jnp.int32, (16, pairs), 1)
    left = jnp.where(row == 0, low[:1], jnp.where(row == 1, high[:1], 0.0))
    right = jnp.where(row == 0, low[1:2], jnp.where(row == 1, high[1:2], 0.0))
    for offset in range(negative_ref.shape[1]):
        named = (negative_ref[0, offset] >= 0).astype(jnp.float32)
        left = jnp.where((row == 2) & (spot == offset), named, left)
    facts = jnp.concatenate([left, right], axis=1).astype(jnp.bfloat16)

    for part, cut in enumerate(cuts):
        emb_ref[part, :seqs] = (normed_ref[:, cut].astype(jnp.float32) * inverse).astype(jnp.bfloat16)
        emb_ref[part, seqs:] = facts


def norm_call(last_row, hidden, gain, owners, hard_negatives, parts):
    seqs, width = hidden.shape
    piece = width // parts
    whole = pl.BlockSpec(memory_space=pltpu.VMEM)
    return pl.pallas_call(
        norm_kernel,
        in_specs=[whole, whole, whole, whole, pl.BlockSpec(memory_space=pltpu.SMEM)],
        out_specs=[whole] * 3,
        out_shape=[
            jax.ShapeDtypeStruct((seqs, width), jnp.bfloat16),
            jax.ShapeDtypeStruct((seqs, lanes), jnp.float32),
            jax.ShapeDtypeStruct((parts, seqs + 16, piece), jnp.bfloat16),
        ],
        compiler_params=pltpu.CompilerParams(vmem_limit_bytes=56 * mebibyte),
        name="norm_rows",
    )(last_row, hidden, gain, owners, hard_negatives)


def score_kernel(
    blocks,
    pairs,
    window,
    *refs,
):
    emb_ref, q_ref, d_ref, mine_ref, other_ref, top_ref, own_ref, place_ref = refs[:-6]
    wide, picked, facts, own, named, sems = refs[-6:]
    seqs = emb_ref.shape[1] - 16
    sent = emb_ref[:, seqs:, :].astype(jnp.float32)
    own_ref[...] = (sent[:, 0, :] + 256.0 * sent[:, 1, :]).astype(jnp.int32)
    facts[...] = sent[:, 2, :lanes].astype(jnp.int32)
    fetches = [
        pltpu.make_async_copy(own_ref, own, sems.at[0]),
        pltpu.make_async_copy(facts, named, sems.at[1]),
    ]
    for fetch in fetches:
        fetch.start()

    for part in range(blocks):
        spread(wide, part * seqs, emb_ref[part, :seqs, :].astype(jnp.float32))
    for fetch in fetches:
        fetch.wait()

    def place(block, count):
        place_ref[0, block] = block
        for offset in range(window):
            present = named[block, offset] > 0
            place_ref[offset + 1, block] = jnp.where(present, count, -1)
            count = count + present.astype(jnp.int32)
        return count

    used = lax.fori_loop(0, blocks, place, blocks)
    fine = pairs // blocks

    def clear(spot, carry):
        empty = jnp.zeros((blocks // 2, fine, pairs), jnp.float32)
        at = pl.ds(pl.multiple_of(spot * fine, fine), fine)
        mine_ref[:, at, :] = empty
        other_ref[:, at, :] = empty
        return carry

    lax.fori_loop(used, mine_ref.shape[1] // fine, clear, 0)
    group = 32

    def pick_block(block, carry):
        for base in range(0, 2 * pairs, group):
            rows = [wide[row_pair(own[block, base + k]), :] for k in range(group)]
            for k in range(group):
                picked[2 * (base + k) : 2 * (base + k + 1), :] = rows[k]
        at = pl.multiple_of(block * pairs, pairs)
        q_ref[pl.ds(at, pairs), :] = gathered(picked, 0, pairs).astype(jnp.bfloat16)
        d_ref[pl.ds(at, pairs), :] = gathered(picked, pairs, pairs).astype(jnp.bfloat16)
        return carry

    lax.fori_loop(0, blocks, pick_block, 0)
    d_ref[blocks * pairs :, :] = d_ref[: window * pairs, :]
    even = lax.axis_index("pb") % 2 == 0
    spare = mine_ref.shape[1] // fine - 1

    def score_blocks(step, carry):
        at = pl.multiple_of(step * 2 * pairs, 2 * pairs)
        tiles = inverse_temp * lax.dot_general(
            q_ref[pl.ds(at, 2 * pairs), :],
            d_ref[pl.ds(at, (window + 2) * pairs), :],
            (((1,), (1,)), ((), ())),
            preferred_element_type=jnp.float32,
        )
        top = carry
        for half in range(2):
            for column in range(window + 1):
                spot = place_ref[column, 2 * step + half]
                row = pl.multiple_of(jnp.where(spot >= 0, spot, spare) * fine, fine)
                tile = tiles[
                    half * pairs : (half + 1) * pairs,
                    (half + column) * pairs : (half + column + 1) * pairs,
                ]
                parted = tile.reshape(blocks // 2, 2, fine, pairs)
                first, second = parted[:, 0], parted[:, 1]
                mine_ref[:, pl.ds(row, fine), :] = jnp.where(even, first, second)
                other_ref[:, pl.ds(row, fine), :] = jnp.where(even, second, first)
                size = jnp.maximum(jnp.abs(first), jnp.abs(second))
                top = jnp.maximum(top, jnp.max(size, axis=0))
        return top

    top_ref[...] = lax.fori_loop(
        0, blocks // 2, score_blocks, jnp.zeros((fine, pairs), jnp.float32)
    )


def score_call(embedded, room, blocks, pairs, window):
    _, rows, piece = embedded.shape
    fine = pairs // blocks
    whole = pl.BlockSpec(memory_space=pltpu.VMEM)
    scalars = pl.BlockSpec(memory_space=pltpu.SMEM)
    return pl.pallas_call(
        functools.partial(score_kernel, blocks, pairs, window),
        in_specs=[whole],
        out_specs=[whole, whole, whole, whole, whole, whole, scalars],
        out_shape=[
            jax.ShapeDtypeStruct((blocks * pairs, piece), jnp.bfloat16),
            jax.ShapeDtypeStruct(((blocks + window) * pairs, piece), jnp.bfloat16),
            jax.ShapeDtypeStruct((blocks // 2, (room + 1) * fine, pairs), jnp.float32),
            jax.ShapeDtypeStruct((blocks // 2, (room + 1) * fine, pairs), jnp.float32),
            jax.ShapeDtypeStruct((fine, pairs), jnp.float32),
            jax.ShapeDtypeStruct((blocks, 2 * pairs), jnp.int32),
            jax.ShapeDtypeStruct((window + 1, blocks), jnp.int32),
        ],
        scratch_shapes=[
            pltpu.VMEM((2 * blocks * (rows - 16), lanes), jnp.float32),
            pltpu.VMEM((4 * pairs, lanes), jnp.float32),
            pltpu.VMEM((blocks, lanes), jnp.int32),
            pltpu.SMEM((blocks, 2 * pairs), jnp.int32),
            pltpu.SMEM((blocks, lanes), jnp.int32),
            pltpu.SemaphoreType.DMA((2,)),
        ],
        compiler_params=pltpu.CompilerParams(vmem_limit_bytes=22 * mebibyte),
        name="partial_scores",
    )(embedded)


def merge_kernel(mine_ref, other_ref, top_ref, other_top_ref, own_ref, *code_refs):
    rows, pairs = own_ref.shape
    steps = code_refs[0].shape[0] - 1
    fine = rows // steps // 2
    chip = lax.axis_index("pb") // 2

    def highest(ref):
        return jnp.max(jnp.max(ref[...], axis=1, keepdims=True), axis=0, keepdims=True)

    top = highest(top_ref) + highest(other_top_ref)
    bound = jnp.ceil(top * bound_steps) + 1.0
    scale = code_steps * bound_steps / bound
    own_ref[...] = mine_ref[chip, :rows] + other_ref[chip, :rows]
    for hop, code_ref in enumerate(code_refs):
        target = chip ^ (hop + 1)

        def encode(step, carry):
            at = pl.multiple_of(step * 2 * fine, 2 * fine)
            there = pl.ds(at, 2 * fine)
            codes = jnp.round((mine_ref[target, there, :] + other_ref[target, there, :]) * scale)
            code_ref[step] = codes.astype(jnp.int32).astype(jnp.int16)
            return carry

        lax.fori_loop(0, steps, encode, 0)
        code_ref[steps] = jnp.broadcast_to(bound, (2 * fine, pairs)).astype(jnp.int32).astype(jnp.int16)


def merge_call(mine, other, top, other_top, blocks):
    chips, rows, pairs = mine.shape
    fine = pairs // blocks
    rows = rows - fine
    whole = pl.BlockSpec(memory_space=pltpu.VMEM)
    coded = jax.ShapeDtypeStruct((rows // (2 * fine) + 1, 2 * fine, pairs), jnp.int16)
    return pl.pallas_call(
        merge_kernel,
        in_specs=[whole] * 4,
        out_specs=[whole] * chips,
        out_shape=[jax.ShapeDtypeStruct((rows, pairs), jnp.float32)] + [coded] * (chips - 1),
        compiler_params=pltpu.CompilerParams(vmem_limit_bytes=12 * mebibyte),
        name="merge_scores",
    )(mine, other, top, other_top)


def softmax_kernel(blocks, window, place_ref, own_ref, *refs):
    code_refs, (c_ref, packed, masked) = refs[:-3], refs[-3:]
    room, fine, pairs = packed.shape
    count = blocks * fine
    unit = 1.0 / (code_steps * bound_steps)
    scales = [ref[room // 2].astype(jnp.int32).astype(jnp.float32) * unit for ref in code_refs]

    def decode(step, carry):
        both = own_ref[pl.ds(pl.multiple_of(step * 2 * fine, 2 * fine), 2 * fine), :]
        for ref, scale in zip(code_refs, scales):
            both = both + ref[step].astype(jnp.int32).astype(jnp.float32) * scale
        packed[2 * step] = both[:fine]
        packed[2 * step + 1] = both[fine:]
        return carry

    lax.fori_loop(0, room // 2, decode, 0)
    for block in range(blocks):
        for column in range(window + 1):
            spot = place_ref[column, block]
            tile = packed[jnp.maximum(spot, 0)]
            masked[block * fine : (block + 1) * fine, column * pairs : (column + 1) * pairs] = (
                jnp.where(spot >= 0, tile, -jnp.inf)
            )
    row = lax.broadcasted_iota(jnp.int32, (count, pairs), 0)
    lane = lax.broadcasted_iota(jnp.int32, (count, pairs), 1)
    target = lane == lax.axis_index("pb") * fine + row % fine
    pieces = [masked[:, column * pairs : (column + 1) * pairs] for column in range(window + 1)]
    row_max = jnp.max(functools.reduce(jnp.maximum, pieces), axis=1, keepdims=True)
    total = functools.reduce(jnp.add, [jnp.exp(piece - row_max) for piece in pieces])
    log_total = row_max + jnp.log(jnp.sum(total, axis=1, keepdims=True))
    positive = jnp.sum(jnp.where(target, pieces[0], 0.0), axis=1, keepdims=True)
    for column, piece in enumerate(pieces):
        share = jnp.exp(piece - log_total)
        if column == 0:
            share = share - jnp.where(target, 1.0, 0.0)
        masked[:, column * pairs : (column + 1) * pairs] = inverse_temp * share
    for block in range(blocks):
        for column in range(window + 1):
            spot = place_ref[column, block]

            @pl.when(spot >= 0)
            def _():
                packed[spot] = masked[
                    block * fine : (block + 1) * fine, column * pairs : (column + 1) * pairs
                ]

    for step in range(room // 2):
        both = jnp.concatenate([packed[2 * step], packed[2 * step + 1]], axis=0)
        c_ref[step] = both.astype(jnp.bfloat16)
    losses = jnp.sum(
        jnp.where(lane == row // fine, log_total - positive, 0.0), axis=0, keepdims=True
    )
    coarse = losses.astype(jnp.bfloat16).astype(jnp.float32)
    rank = lax.broadcasted_iota(jnp.int32, (2 * fine, pairs), 0)
    both = jnp.where(rank == 0, coarse, jnp.where(rank == 1, losses - coarse, 0.0))
    c_ref[room // 2] = both.astype(jnp.bfloat16)


def softmax_call(place, own_scores, codes, blocks, window):
    steps, fine, pairs = codes[0].shape
    room, fine = 2 * (steps - 1), fine // 2
    whole = pl.BlockSpec(memory_space=pltpu.VMEM)
    return pl.pallas_call(
        functools.partial(softmax_kernel, blocks, window),
        in_specs=[pl.BlockSpec(memory_space=pltpu.SMEM), whole] + [whole] * len(codes),
        out_specs=whole,
        out_shape=jax.ShapeDtypeStruct((room // 2 + 1, 2 * fine, pairs), jnp.bfloat16),
        scratch_shapes=[
            pltpu.VMEM((room, fine, pairs), jnp.float32),
            pltpu.VMEM((blocks * fine, (window + 1) * pairs), jnp.float32),
        ],
        compiler_params=pltpu.CompilerParams(vmem_limit_bytes=8 * mebibyte),
        name="softmax_rows",
    )(place, own_scores, *codes)


def grad_kernel(
    blocks,
    pairs,
    window,
    own_ref,
    place_ref,
    q_ref,
    d_ref,
    *refs,
):
    part_refs = refs[:-7]
    out_ref, loss_ref, wide, dsum, picked, packed, square = refs[-7:]
    fine = pairs // blocks
    room = packed.shape[1]
    me = lax.axis_index("pb")
    masks = swap_masks(blocks)
    group = 32
    losses = 0.0
    for part in part_refs:
        sent = part[:, room // 2].astype(jnp.float32)
        losses = losses + jnp.sum(sent[:, 0, :] + sent[:, 1, :], axis=0, keepdims=True) / pairs
    lane = lax.broadcasted_iota(jnp.int32, losses.shape, 1)
    mine = jnp.where(lane == me, losses, 0.0)
    loss_ref[...] = jnp.broadcast_to(jnp.sum(mine, axis=1, keepdims=True), loss_ref.shape)
    dsum[...] = jnp.zeros_like(dsum)
    square[...] = jnp.zeros_like(square)

    def unpack(step, carry):
        for part, mask in zip(part_refs, masks):
            both = part[:, step].astype(jnp.float32)
            for at, apart in enumerate(mask):
                packed[me ^ apart, 2 * step] = both[at, :fine]
                packed[me ^ apart, 2 * step + 1] = both[at, fine:]
        return carry

    lax.fori_loop(0, room // 2, unpack, 0)

    def scatter_rows(block, offset, start):
        for base in range(0, pairs, group):
            rows = [
                picked[2 * (start + base + k) : 2 * (start + base + k + 1), :] for k in range(group)
            ]
            for k in range(group):
                wide[row_pair(own_ref[block, offset + base + k]), :] = rows[k]

    def two_blocks(step, carry):
        for half in range(2):
            for column in range(window + 1):
                spot = place_ref[column, 2 * step + half]
                tile = packed[:, jnp.maximum(spot, 0)].reshape(pairs, pairs)
                square[
                    half * pairs : (half + 1) * pairs,
                    (half + column) * pairs : (half + column + 1) * pairs,
                ] = jnp.where(spot >= 0, tile, 0.0).astype(jnp.bfloat16)
        at = pl.multiple_of(step * 2 * pairs, 2 * pairs)
        there = pl.ds(at, (window + 2) * pairs)
        coefficients = square[...]
        summed = jnp.dot(coefficients, d_ref[there, :], preferred_element_type=jnp.float32)
        spread(picked, 0, summed)
        dsum[there, :] += lax.dot_general(
            coefficients,
            q_ref[pl.ds(at, 2 * pairs), :],
            (((0,), (0,)), ((), ())),
            preferred_element_type=jnp.float32,
        )
        for half in range(2):
            scatter_rows(2 * step + half, 0, half * pairs)
        return carry

    lax.fori_loop(0, blocks // 2, two_blocks, 0)
    dsum[: window * pairs, :] += dsum[blocks * pairs :, :]

    def doc_block(block, carry):
        at = pl.multiple_of(block * pairs, pairs)
        spread(picked, 0, dsum[pl.ds(at, pairs), :])
        scatter_rows(block, pairs, 0)
        return carry

    lax.fori_loop(0, blocks, doc_block, 0)
    slots = out_ref.shape[1]
    for part in range(blocks):
        out_ref[part] = gathered(wide, part * slots, slots).astype(jnp.bfloat16)


def grad_call(own, place, parts, queries, documents, blocks, pairs, window):
    count, piece = queries.shape
    seqs = 2 * count
    room = 2 * (parts[0].shape[1] - 1)
    whole = pl.BlockSpec(memory_space=pltpu.VMEM)
    scalars = pl.BlockSpec(memory_space=pltpu.SMEM)
    return pl.pallas_call(
        functools.partial(grad_kernel, blocks, pairs, window),
        in_specs=[scalars, scalars, whole, whole] + [whole] * len(parts),
        out_specs=[whole, whole],
        out_shape=[
            jax.ShapeDtypeStruct((blocks, seqs // blocks, piece), jnp.bfloat16),
            jax.ShapeDtypeStruct((1, lanes), jnp.float32),
        ],
        scratch_shapes=[
            pltpu.VMEM((2 * seqs, lanes), jnp.float32),
            pltpu.VMEM(((blocks + window) * pairs, piece), jnp.float32),
            pltpu.VMEM((4 * pairs, lanes), jnp.float32),
            pltpu.VMEM((blocks, room, pairs // blocks, pairs), jnp.float32),
            pltpu.VMEM((2 * pairs, (window + 2) * pairs), jnp.bfloat16),
        ],
        compiler_params=pltpu.CompilerParams(vmem_limit_bytes=26 * mebibyte),
        name="slice_grads",
    )(own, place, queries, documents, *parts)


def project_kernel(grad_ref, normed_ref, inv_ref, out_ref):
    parts, _, piece = grad_ref.shape
    cuts = [slice(part * piece, (part + 1) * piece) for part in range(parts)]
    inverse = inv_ref[:, :1]
    total = 0.0
    for part, cut in enumerate(cuts):
        unit = normed_ref[:, cut].astype(jnp.float32) * inverse
        total = total + unit * grad_ref[part].astype(jnp.float32)
    along = jnp.sum(total, axis=-1, keepdims=True)
    for part, cut in enumerate(cuts):
        unit = normed_ref[:, cut].astype(jnp.float32) * inverse
        out_ref[:, cut] = grad_ref[part].astype(jnp.float32) - unit * along


def project_call(returned, normed, inverse):
    parts, seqs, piece = returned.shape
    width = normed.shape[1]
    rows = 64
    return pl.pallas_call(
        project_kernel,
        grid=(seqs // rows,),
        in_specs=[
            pl.BlockSpec((parts, rows, piece), lambda i: (0, i, 0)),
            pl.BlockSpec((rows, width), lambda i: (i, 0)),
            pl.BlockSpec((rows, lanes), lambda i: (i, 0)),
        ],
        out_specs=pl.BlockSpec((rows, width), lambda i: (i, 0)),
        out_shape=jax.ShapeDtypeStruct((seqs, width), jnp.float32),
        compiler_params=pltpu.CompilerParams(vmem_limit_bytes=10 * mebibyte),
        name="project_out",
    )(returned, normed, inverse)


def swapped(value, apart):
    pairs = [(at, at ^ apart) for at in range(lax.axis_size("pb"))]
    return lax.ppermute(value, "pb", pairs)


def swap_bits(devices):
    bits = [1 << bit for bit in reversed(range(devices.bit_length() - 1))]
    return bits[:-2], bits[-2], bits[-1]


def swap_masks(devices):
    far, side, last = swap_bits(devices)
    held = [0]
    for apart in far:
        held = held + [mask ^ apart for mask in held]
    held = held + [mask ^ side for mask in held]
    return [held, [mask ^ last for mask in held]]


def gather_all(value):
    far, side, last = swap_bits(lax.axis_size("pb"))
    held = value[None]
    beside = [swapped(held, side)]
    for apart in far:
        arrived = swapped(held, apart)
        beside.append(swapped(arrived, side))
        held = jnp.concatenate([held, arrived], axis=0)
    held = jnp.concatenate([held] + beside, axis=0)
    return [held, swapped(held, last)]


def middle(embedded, room, devices, pairs, window):
    queries, documents, mine, other, top, own, place = score_call(
        embedded, room, devices, pairs, window
    )
    own_scores, *codes = merge_call(mine, swapped(other, 1), top, swapped(top, 1), devices)
    codes = [swapped(code, 2 * (hop + 1)) for hop, code in enumerate(codes)]
    parts = gather_all(softmax_call(place, own_scores, codes, devices, window))
    grads, loss = grad_call(own, place, parts, queries, documents, devices, pairs, window)
    return grads, loss[0, :1]


def feature_plan(hidden, final_gain, last_row, pair_owner, hard_negatives):
    devices = lax.axis_size("pb")
    seqs, width = hidden.shape
    pairs = pair_owner.shape[0]
    window = hard_negatives.shape[1]
    normed, inverse, embedding = norm_call(
        last_row, hidden, final_gain, pair_owner.T, hard_negatives, devices
    )
    embedded = lax.all_to_all(embedding, "pb", split_axis=0, concat_axis=0, tiled=True)
    most = devices * (window + 1)
    rooms = [most * part // 20 for part in (10, 11, 12, 13, 14, 16, 20)]
    used = devices + jnp.sum(embedded[:, seqs + 2, :window].astype(jnp.float32))
    level = sum((used > room).astype(jnp.int32) for room in rooms[:-1])
    grads, loss = lax.switch(
        level,
        [
            functools.partial(middle, room=room, devices=devices, pairs=pairs, window=window)
            for room in rooms
        ],
        embedded,
    )
    returned = lax.all_to_all(grads, "pb", split_axis=0, concat_axis=0, tiled=True)
    return project_call(returned, normed, inverse), loss


def from_behind(value, axis, steps):
    count = lax.axis_size(axis)
    pairs = [(source, (source + steps) % count) for source in range(count)]
    return lax.ppermute(value, axis, pairs)


def similarity(queries, documents):
    return inverse_temp * lax.dot_general(
        queries, documents, (((1,), (1,)), ((), ())), preferred_element_type=jnp.float32
    )


def transposed(weights, queries):
    return lax.dot_general(
        weights, queries, (((0,), (0,)), ((), ())), preferred_element_type=jnp.float32
    )


def combine_docs(weights, documents):
    return jnp.dot(weights, documents, preferred_element_type=jnp.float32)


def skipped(listed, function, operands, out_shape):
    return lax.cond(
        listed,
        lambda inputs: function(*inputs),
        lambda inputs: jnp.zeros(out_shape, jnp.float32),
        operands,
    )


def row_plan(hidden, final_gain, last_row, pair_owner, hard_negatives):
    values = hidden.astype(jnp.float32)
    scale_row = lax.rsqrt(jnp.mean(values * values, axis=-1, keepdims=True) + token_eps)
    normed = (values * scale_row * final_gain.astype(jnp.float32)).astype(jnp.bfloat16)
    seq_count = last_row.shape[1]
    model_width = hidden.shape[1]
    pooled = normed[last_row[0]].astype(jnp.float32)
    inverse_norm = lax.rsqrt(jnp.sum(pooled * pooled, axis=-1, keepdims=True) + 1e-06)
    unit_vec = pooled * inverse_norm
    embedding = unit_vec.astype(jnp.bfloat16)
    devices = lax.axis_size("pb")
    capacity = 2 * seq_count // devices
    pair_count = pair_owner.shape[0]
    wanted = jnp.concatenate([pair_owner[:, 0], pair_owner[:, 1]])
    holder = wanted // seq_count
    within = wanted % seq_count
    entry_ids = jnp.arange(2 * pair_count, dtype=jnp.int32)
    earlier = (holder[None, :] == holder[:, None]) & (entry_ids[None, :] < entry_ids[:, None])
    position = jnp.sum(earlier.astype(jnp.int32), axis=1)
    request = jnp.full((devices, capacity), -1, jnp.int32).at[holder, position].set(within)
    served = lax.all_to_all(request, "pb", split_axis=0, concat_axis=0, tiled=True)
    outgoing = jnp.where(
        served[:, :, None] >= 0, embedding[jnp.maximum(served, 0)], jnp.zeros((), jnp.bfloat16)
    )
    received = lax.all_to_all(outgoing, "pb", split_axis=0, concat_axis=0, tiled=True)
    gathered = received[holder, position]
    queries = gathered[:pair_count]
    own_docs = gathered[pair_count:]
    listed_ids = hard_negatives[0]
    window = hard_negatives.shape[1]
    listed = [listed_ids[offset] >= 0 for offset in range(window)]
    neighbours = []
    moving = own_docs
    for offset in range(window):
        moving = from_behind(moving, "pb", -1)
        neighbours.append(moving)
    tile_shape = (pair_count, pair_count)
    score_blocks = [similarity(queries, own_docs)]
    for offset in range(window):
        score_blocks.append(
            skipped(listed[offset], similarity, (queries, neighbours[offset]), tile_shape)
        )
    all_scores = jnp.concatenate(score_blocks, axis=1)
    usable = jnp.concatenate(
        [jnp.ones((pair_count,), jnp.bool_)]
        + [jnp.broadcast_to(listed[offset], (pair_count,)) for offset in range(window)]
    )
    masked = jnp.where(usable[None, :], all_scores, -jnp.inf)
    row_max = jnp.max(masked, axis=1, keepdims=True)
    log_total = row_max + jnp.log(jnp.sum(jnp.exp(masked - row_max), axis=1, keepdims=True))
    diagonal = jnp.arange(pair_count, dtype=jnp.int32)
    positive = all_scores[diagonal, diagonal]
    block_loss = jnp.mean(log_total[:, 0] - positive).reshape(1)
    columns = jnp.arange((window + 1) * pair_count, dtype=jnp.int32)
    target = (columns[None, :] == diagonal[:, None]).astype(jnp.float32)
    coefficients = (inverse_temp * (jnp.exp(masked - log_total) - target)).astype(jnp.bfloat16)
    pieces = [
        coefficients[:, offset * pair_count : (offset + 1) * pair_count]
        for offset in range(window + 1)
    ]
    grad_shape = (pair_count, model_width)
    query_sum = combine_docs(pieces[0], own_docs)
    for offset in range(window):
        query_sum = query_sum + skipped(
            listed[offset], combine_docs, (pieces[offset + 1], neighbours[offset]), grad_shape
        )
    query_grad = query_sum.astype(jnp.bfloat16)
    own_part = transposed(pieces[0], queries).astype(jnp.bfloat16)
    partial_value = [
        skipped(listed[offset], transposed, (pieces[offset + 1], queries), grad_shape).astype(
            jnp.bfloat16
        )
        for offset in range(window)
    ]
    running = partial_value[window - 1].astype(jnp.float32)
    for offset in range(window):
        running = from_behind(running, "pb", 1)
        if offset + 1 < window:
            running = running + partial_value[window - 2 - offset].astype(jnp.float32)
    doc_grad = (own_part.astype(jnp.float32) + running).astype(jnp.bfloat16)
    answers = jnp.concatenate([query_grad, doc_grad], axis=0)
    returning = (
        jnp.zeros((devices, capacity, model_width), jnp.bfloat16).at[holder, position].set(answers)
    )
    returned = lax.all_to_all(returning, "pb", split_axis=0, concat_axis=0, tiled=True)
    slot_ids = jnp.where(served >= 0, served, seq_count).reshape(-1)
    emb_grad = (
        jnp.zeros((seq_count, model_width), jnp.bfloat16)
        .at[slot_ids]
        .set(returned.reshape(-1, model_width), mode="drop")
    )
    gradient = emb_grad.astype(jnp.float32)
    pooled_grad = gradient - unit_vec * jnp.sum(unit_vec * gradient, axis=-1, keepdims=True)
    return (pooled_grad, block_loss)


def solution(mesh):
    def local(hidden, final_gain, last_row, pair_owner, hard_negatives):
        plan = feature_plan if hidden.shape[1] >= lanes * mesh.shape["pb"] else row_plan
        return plan(hidden, final_gain, last_row, pair_owner, hard_negatives)

    return jax.shard_map(
        local,
        mesh=mesh,
        in_specs=(
            P(("groups", "pb"), None),
            P(),
            P(("groups", "pb"), None),
            P(("groups", "pb"), None),
            P(("groups", "pb"), None),
        ),
        out_specs=(P(("groups", "pb"), None), P(("groups", "pb"))),
        check_vma=False,
    )
```

```python
import functools

import jax
import jax.numpy as jnp
from jax import lax
from jax.experimental import pallas as pl
from jax.experimental.pallas import tpu as pltpu
from jax.sharding import PartitionSpec as P

inverse_temp = 50.0
token_eps = 1e-05
unit_eps = 1e-06
lanes = 128
bound_steps = 256.0
code_steps = 32000.0
mebibyte = 1024 * 1024


def spread(target, at, value):
    count = value.shape[0]
    for half in range(2):
        target[pl.ds(2 * at + half, count, stride=2), :] = value[:, half * lanes : (half + 1) * lanes]


def gathered(source, at, count):
    halves = [source[pl.ds(2 * at + half, count, stride=2), :] for half in range(2)]
    return jnp.concatenate(halves, axis=1)


def row_pair(index):
    return pl.ds(pl.multiple_of(2 * index, 2), 2)


def norm_kernel(
    last_ref,
    hidden_ref,
    gain_ref,
    owner_ref,
    negative_ref,
    normed_ref,
    inv_ref,
    emb_ref,
    fact_ref,
    held,
    normed,
    cast,
    in_sems,
    out_sems,
    emb_sems,
):
    seqs, width = normed_ref.shape
    parts, _, piece = emb_ref.shape
    pairs = owner_ref.shape[1]
    cuts = [slice(part * piece, (part + 1) * piece) for part in range(parts)]
    chunk = width // 4
    chunks = [slice(at, at + chunk) for at in range(0, width, chunk)]
    arrivals = [
        pltpu.make_async_copy(hidden_ref.at[:, cut], held.at[:, cut], in_sems.at[at])
        for at, cut in enumerate(chunks)
    ]
    for arrival in arrivals:
        arrival.start()
    row = lax.broadcasted_iota(jnp.int32, fact_ref.shape, 0)
    spot = lax.broadcasted_iota(jnp.int32, fact_ref.shape, 1)
    facts = jnp.where(row == 0, owner_ref[:1], jnp.where(row == 1, owner_ref[1:2], 0))
    for offset in range(negative_ref.shape[1]):
        present = (negative_ref[0, offset] >= 0).astype(jnp.int32)
        facts = jnp.where((row == 2) & (spot == offset), present, facts)
    fact_ref[...] = facts

    sources = lax.broadcasted_iota(jnp.int32, (seqs, seqs), 0)
    pick = jnp.where(sources == last_ref[...], 1.0, 0.0).astype(jnp.bfloat16)

    def folded(squares):
        return functools.reduce(
            jnp.add, [squares[:, at : at + lanes] for at in range(0, piece, lanes)]
        )

    total = jnp.zeros((seqs, lanes), jnp.float32)
    for part, cut in enumerate(cuts):
        if part % (parts // 4) == 0:
            arrivals[part // (parts // 4)].wait()
        values = lax.dot_general(
            pick, held[:, cut], (((0,), (0,)), ((), ())), preferred_element_type=jnp.float32
        )
        normed[:, cut] = values.astype(jnp.bfloat16)
        total = total + folded(values * values)
    scale = lax.rsqrt(jnp.sum(total, axis=-1, keepdims=True) / width + token_eps)
    total = jnp.zeros((seqs, lanes), jnp.float32)
    for cut in cuts:
        values = normed[:, cut].astype(jnp.float32)
        gain = gain_ref[cut].astype(jnp.float32).reshape(1, piece)
        rounded = (values * scale * gain).astype(jnp.bfloat16)
        normed[:, cut] = rounded
        pooled = rounded.astype(jnp.float32)
        total = total + folded(pooled * pooled)
    departures = [
        pltpu.make_async_copy(normed.at[:, cut], normed_ref.at[:, cut], out_sems.at[at])
        for at, cut in enumerate(chunks)
    ]
    for departure in departures:
        departure.start()
    inverse = lax.rsqrt(jnp.sum(total, axis=-1, keepdims=True) + unit_eps)
    inv_ref[...] = jnp.broadcast_to(inverse, inv_ref.shape)
    for part, cut in enumerate(cuts):
        cast[part] = (normed[:, cut].astype(jnp.float32) * inverse).astype(jnp.bfloat16)
        departures.append(
            pltpu.make_async_copy(cast.at[part], emb_ref.at[part], emb_sems.at[part])
        )
        departures[-1].start()
    for departure in departures:
        departure.wait()


def norm_call(last_row, hidden, gain, owners, hard_negatives, parts):
    seqs, width = hidden.shape
    piece = width // parts
    whole = pl.BlockSpec(memory_space=pltpu.VMEM)
    apart = pl.BlockSpec(memory_space=pl.ANY)
    return pl.pallas_call(
        norm_kernel,
        in_specs=[whole, apart, whole, whole, pl.BlockSpec(memory_space=pltpu.SMEM)],
        out_specs=[apart, whole, apart, whole],
        out_shape=[
            jax.ShapeDtypeStruct((seqs, width), jnp.bfloat16),
            jax.ShapeDtypeStruct((seqs, lanes), jnp.float32),
            jax.ShapeDtypeStruct((parts, seqs, piece), jnp.bfloat16),
            jax.ShapeDtypeStruct((8, owners.shape[1]), jnp.int32),
        ],
        scratch_shapes=[
            pltpu.VMEM((seqs, width), jnp.bfloat16),
            pltpu.VMEM((seqs, width), jnp.bfloat16),
            pltpu.VMEM((parts, seqs, piece), jnp.bfloat16),
            pltpu.SemaphoreType.DMA((4,)),
            pltpu.SemaphoreType.DMA((4,)),
            pltpu.SemaphoreType.DMA((parts,)),
        ],
        compiler_params=pltpu.CompilerParams(vmem_limit_bytes=56 * mebibyte),
        name="norm_rows",
    )(last_row, hidden, gain, owners, hard_negatives)


def score_kernel(
    blocks,
    pairs,
    window,
    *refs,
):
    fact_ref, emb_ref, q_ref, d_ref, mine_ref, other_ref, top_ref, place_ref = refs[:-3]
    wide, picked, picked_too = refs[-3:]
    seqs = emb_ref.shape[1]
    for part in range(blocks):
        spread(wide, part * seqs, emb_ref[part].astype(jnp.float32))

    def place(block, count):
        place_ref[0, block] = block
        for offset in range(window):
            present = fact_ref[block, 2, offset] > 0
            place_ref[offset + 1, block] = jnp.where(present, count, -1)
            count = count + present.astype(jnp.int32)
        return count

    used = lax.fori_loop(0, blocks, place, blocks)
    fine = pairs // blocks

    def clear(spot, carry):
        empty = jnp.zeros((blocks // 2, fine, pairs), jnp.float32)
        at = pl.ds(pl.multiple_of(spot * fine, fine), fine)
        mine_ref[:, at, :] = empty
        other_ref[:, at, :] = empty
        return carry

    lax.fori_loop(used, mine_ref.shape[1] // fine, clear, 0)
    group = 32

    def pick_block(block, rows_at):
        for kind in range(2):
            for base in range(0, pairs, group):
                rows = [
                    wide[row_pair(fact_ref[block, kind, base + k]), :] for k in range(group)
                ]
                for k in range(group):
                    at = 2 * (kind * pairs + base + k)
                    rows_at[at : at + 2, :] = rows[k]
        at = pl.multiple_of(block * pairs, pairs)
        q_ref[pl.ds(at, pairs), :] = gathered(rows_at, 0, pairs).astype(jnp.bfloat16)
        d_ref[pl.ds(at, pairs), :] = gathered(rows_at, pairs, pairs).astype(jnp.bfloat16)

    def pick_blocks(step, carry):
        pick_block(2 * step, picked)
        pick_block(2 * step + 1, picked_too)
        return carry

    ahead = (window + 2) // 2
    lax.fori_loop(0, ahead, pick_blocks, 0)
    even = lax.axis_index("pb") % 2 == 0
    spare = mine_ref.shape[1] // fine - 1

    def score_blocks(step, carry):
        at = pl.multiple_of(step * 2 * pairs, 2 * pairs)
        tiles = inverse_temp * lax.dot_general(
            q_ref[pl.ds(at, 2 * pairs), :],
            d_ref[pl.ds(at, (window + 2) * pairs), :],
            (((1,), (1,)), ((), ())),
            preferred_element_type=jnp.float32,
        )
        top = carry
        for half in range(2):
            for column in range(window + 1):
                spot = place_ref[column, 2 * step + half]
                row = pl.multiple_of(jnp.where(spot >= 0, spot, spare) * fine, fine)
                tile = tiles[
                    half * pairs : (half + 1) * pairs,
                    (half + column) * pairs : (half + column + 1) * pairs,
                ]
                parted = tile.reshape(blocks // 2, 2, fine, pairs)
                first, second = parted[:, 0], parted[:, 1]
                mine_ref[:, pl.ds(row, fine), :] = jnp.where(even, first, second)
                other_ref[:, pl.ds(row, fine), :] = jnp.where(even, second, first)
                size = jnp.maximum(jnp.abs(first), jnp.abs(second))
                top = jnp.maximum(top, jnp.max(size, axis=0))
        return top

    def score_and_pick(step, top):
        top = score_blocks(step - ahead, top)
        pick_blocks(step, 0)
        return top

    top = jnp.zeros((fine, pairs), jnp.float32)
    top = lax.fori_loop(ahead, blocks // 2, score_and_pick, top)
    d_ref[blocks * pairs :, :] = d_ref[: window * pairs, :]
    top_ref[...] = lax.fori_loop(blocks // 2 - ahead, blocks // 2, score_blocks, top)


def score_call(facts, embedded, room, blocks, pairs, window):
    _, seqs, piece = embedded.shape
    fine = pairs // blocks
    whole = pl.BlockSpec(memory_space=pltpu.VMEM)
    scalars = pl.BlockSpec(memory_space=pltpu.SMEM)
    return pl.pallas_call(
        functools.partial(score_kernel, blocks, pairs, window),
        in_specs=[scalars, whole],
        out_specs=[whole, whole, whole, whole, whole, scalars],
        out_shape=[
            jax.ShapeDtypeStruct((blocks * pairs, piece), jnp.bfloat16),
            jax.ShapeDtypeStruct(((blocks + window) * pairs, piece), jnp.bfloat16),
            jax.ShapeDtypeStruct((blocks // 2, (room + 1) * fine, pairs), jnp.float32),
            jax.ShapeDtypeStruct((blocks // 2, (room + 1) * fine, pairs), jnp.float32),
            jax.ShapeDtypeStruct((fine, pairs), jnp.float32),
            jax.ShapeDtypeStruct((window + 1, blocks), jnp.int32),
        ],
        scratch_shapes=[
            pltpu.VMEM((2 * blocks * seqs, lanes), jnp.float32),
            pltpu.VMEM((4 * pairs, lanes), jnp.float32),
            pltpu.VMEM((4 * pairs, lanes), jnp.float32),
        ],
        compiler_params=pltpu.CompilerParams(vmem_limit_bytes=22 * mebibyte),
        name="partial_scores",
    )(facts, embedded)


def merge_kernel(mine_ref, other_ref, top_ref, other_top_ref, own_ref, *code_refs):
    rows, pairs = own_ref.shape
    steps = code_refs[0].shape[0] - 1
    fine = rows // steps // 2
    chip = lax.axis_index("pb") // 2

    def highest(ref):
        return jnp.max(jnp.max(ref[...], axis=1, keepdims=True), axis=0, keepdims=True)

    top = highest(top_ref) + highest(other_top_ref)
    bound = jnp.ceil(top * bound_steps) + 1.0
    scale = code_steps * bound_steps / bound
    own_ref[...] = mine_ref[chip, :rows] + other_ref[chip, :rows]
    for hop, code_ref in enumerate(code_refs):
        target = chip ^ (hop + 1)

        def encode(step, carry):
            at = pl.multiple_of(step * 2 * fine, 2 * fine)
            there = pl.ds(at, 2 * fine)
            codes = jnp.round((mine_ref[target, there, :] + other_ref[target, there, :]) * scale)
            code_ref[step] = codes.astype(jnp.int32).astype(jnp.int16)
            return carry

        lax.fori_loop(0, steps, encode, 0)
        code_ref[steps] = jnp.broadcast_to(bound, (2 * fine, pairs)).astype(jnp.int32).astype(jnp.int16)


def merge_call(mine, other, top, other_top, blocks):
    chips, rows, pairs = mine.shape
    fine = pairs // blocks
    rows = rows - fine
    whole = pl.BlockSpec(memory_space=pltpu.VMEM)
    coded = jax.ShapeDtypeStruct((rows // (2 * fine) + 1, 2 * fine, pairs), jnp.int16)
    return pl.pallas_call(
        merge_kernel,
        in_specs=[whole] * 4,
        out_specs=[whole] * chips,
        out_shape=[jax.ShapeDtypeStruct((rows, pairs), jnp.float32)] + [coded] * (chips - 1),
        compiler_params=pltpu.CompilerParams(vmem_limit_bytes=12 * mebibyte),
        name="merge_scores",
    )(mine, other, top, other_top)


def softmax_kernel(blocks, window, place_ref, own_ref, *refs):
    code_refs, (c_ref, packed, masked) = refs[:-3], refs[-3:]
    room, fine, pairs = packed.shape
    count = blocks * fine
    unit = 1.0 / (code_steps * bound_steps)
    scales = [ref[room // 2].astype(jnp.int32).astype(jnp.float32) * unit for ref in code_refs]

    def decode(step, carry):
        both = own_ref[pl.ds(pl.multiple_of(step * 2 * fine, 2 * fine), 2 * fine), :]
        for ref, scale in zip(code_refs, scales):
            both = both + ref[step].astype(jnp.int32).astype(jnp.float32) * scale
        packed[2 * step] = both[:fine]
        packed[2 * step + 1] = both[fine:]
        return carry

    lax.fori_loop(0, room // 2, decode, 0)
    for block in range(blocks):
        for column in range(window + 1):
            spot = place_ref[column, block]
            tile = packed[jnp.maximum(spot, 0)]
            masked[block * fine : (block + 1) * fine, column * pairs : (column + 1) * pairs] = (
                jnp.where(spot >= 0, tile, -jnp.inf)
            )
    row = lax.broadcasted_iota(jnp.int32, (count, pairs), 0)
    lane = lax.broadcasted_iota(jnp.int32, (count, pairs), 1)
    target = lane == lax.axis_index("pb") * fine + row % fine
    pieces = [masked[:, column * pairs : (column + 1) * pairs] for column in range(window + 1)]
    row_max = jnp.max(functools.reduce(jnp.maximum, pieces), axis=1, keepdims=True)
    total = functools.reduce(jnp.add, [jnp.exp(piece - row_max) for piece in pieces])
    log_total = row_max + jnp.log(jnp.sum(total, axis=1, keepdims=True))
    positive = jnp.sum(jnp.where(target, pieces[0], 0.0), axis=1, keepdims=True)
    for column, piece in enumerate(pieces):
        share = jnp.exp(piece - log_total)
        if column == 0:
            share = share - jnp.where(target, 1.0, 0.0)
        masked[:, column * pairs : (column + 1) * pairs] = inverse_temp * share
    for block in range(blocks):
        for column in range(window + 1):
            spot = place_ref[column, block]

            @pl.when(spot >= 0)
            def _():
                packed[spot] = masked[
                    block * fine : (block + 1) * fine, column * pairs : (column + 1) * pairs
                ]

    for step in range(room // 2):
        both = jnp.concatenate([packed[2 * step], packed[2 * step + 1]], axis=0)
        c_ref[step] = both.astype(jnp.bfloat16)
    losses = jnp.sum(
        jnp.where(lane == row // fine, log_total - positive, 0.0), axis=0, keepdims=True
    )
    coarse = losses.astype(jnp.bfloat16).astype(jnp.float32)
    rank = lax.broadcasted_iota(jnp.int32, (2 * fine, pairs), 0)
    both = jnp.where(rank == 0, coarse, jnp.where(rank == 1, losses - coarse, 0.0))
    c_ref[room // 2] = both.astype(jnp.bfloat16)


def softmax_call(place, own_scores, codes, blocks, window):
    steps, fine, pairs = codes[0].shape
    room, fine = 2 * (steps - 1), fine // 2
    whole = pl.BlockSpec(memory_space=pltpu.VMEM)
    return pl.pallas_call(
        functools.partial(softmax_kernel, blocks, window),
        in_specs=[pl.BlockSpec(memory_space=pltpu.SMEM), whole] + [whole] * len(codes),
        out_specs=whole,
        out_shape=jax.ShapeDtypeStruct((room // 2 + 1, 2 * fine, pairs), jnp.bfloat16),
        scratch_shapes=[
            pltpu.VMEM((room, fine, pairs), jnp.float32),
            pltpu.VMEM((blocks * fine, (window + 1) * pairs), jnp.float32),
        ],
        compiler_params=pltpu.CompilerParams(vmem_limit_bytes=8 * mebibyte),
        name="softmax_rows",
    )(place, own_scores, *codes)


def grad_kernel(
    blocks,
    pairs,
    window,
    fact_ref,
    place_ref,
    q_ref,
    d_ref,
    *refs,
):
    part_refs = refs[:-8]
    out_ref, loss_ref, wide, dsum, picked, picked_too, packed, square = refs[-8:]
    fine = pairs // blocks
    room = packed.shape[1]
    me = lax.axis_index("pb")
    masks = swap_masks(blocks)
    group = 32
    losses = 0.0
    for part in part_refs:
        sent = part[:, room // 2].astype(jnp.float32)
        losses = losses + jnp.sum(sent[:, 0, :] + sent[:, 1, :], axis=0, keepdims=True) / pairs
    lane = lax.broadcasted_iota(jnp.int32, losses.shape, 1)
    mine = jnp.where(lane == me, losses, 0.0)
    loss_ref[...] = jnp.broadcast_to(jnp.sum(mine, axis=1, keepdims=True), loss_ref.shape)
    dsum[...] = jnp.zeros_like(dsum)
    square[...] = jnp.zeros_like(square)

    def unpack(step, carry):
        for part, mask in zip(part_refs, masks):
            both = part[:, step].astype(jnp.float32)
            for at, apart in enumerate(mask):
                packed[me ^ apart, 2 * step] = both[at, :fine]
                packed[me ^ apart, 2 * step + 1] = both[at, fine:]
        return carry

    lax.fori_loop(0, room // 2, unpack, 0)

    def scatter_rows(block, kind, rows_at, start):
        for base in range(0, pairs, group):
            rows = [
                rows_at[2 * (start + base + k) : 2 * (start + base + k + 1), :]
                for k in range(group)
            ]
            for k in range(group):
                wide[row_pair(fact_ref[block, kind, base + k]), :] = rows[k]

    def query_blocks(step, carry):
        for half in range(2):
            for column in range(window + 1):
                spot = place_ref[column, 2 * step + half]
                tile = packed[:, jnp.maximum(spot, 0)].reshape(pairs, pairs)
                square[
                    half * pairs : (half + 1) * pairs,
                    (half + column) * pairs : (half + column + 1) * pairs,
                ] = jnp.where(spot >= 0, tile, 0.0).astype(jnp.bfloat16)
        at = pl.multiple_of(step * 2 * pairs, 2 * pairs)
        there = pl.ds(at, (window + 2) * pairs)
        coefficients = square[...]
        summed = jnp.dot(coefficients, d_ref[there, :], preferred_element_type=jnp.float32)
        spread(picked, 0, summed)
        dsum[there, :] += lax.dot_general(
            coefficients,
            q_ref[pl.ds(at, 2 * pairs), :],
            (((0,), (0,)), ((), ())),
            preferred_element_type=jnp.float32,
        )
        for half in range(2):
            scatter_rows(2 * step + half, 0, picked, half * pairs)
        return carry

    def doc_blocks(step):
        at = pl.multiple_of(step * 2 * pairs, 2 * pairs)
        spread(picked_too, 0, dsum[pl.ds(at, 2 * pairs), :])
        for half in range(2):
            scatter_rows(2 * step + half, 1, picked_too, half * pairs)

    def both_blocks(step, carry):
        doc_blocks(step - 1)
        return query_blocks(step, carry)

    late = window // 2
    lax.fori_loop(0, late + 1, query_blocks, 0)
    lax.fori_loop(late + 1, blocks // 2, both_blocks, 0)
    dsum[: window * pairs, :] += dsum[blocks * pairs :, :]
    for step in (*range(late), blocks // 2 - 1):
        doc_blocks(step)
    slots = out_ref.shape[1]
    for part in range(blocks):
        out_ref[part] = gathered(wide, part * slots, slots).astype(jnp.bfloat16)


def grad_call(facts, place, parts, queries, documents, blocks, pairs, window):
    count, piece = queries.shape
    seqs = 2 * count
    room = 2 * (parts[0].shape[1] - 1)
    whole = pl.BlockSpec(memory_space=pltpu.VMEM)
    scalars = pl.BlockSpec(memory_space=pltpu.SMEM)
    return pl.pallas_call(
        functools.partial(grad_kernel, blocks, pairs, window),
        in_specs=[scalars, scalars, whole, whole] + [whole] * len(parts),
        out_specs=[whole, whole],
        out_shape=[
            jax.ShapeDtypeStruct((blocks, seqs // blocks, piece), jnp.bfloat16),
            jax.ShapeDtypeStruct((1, lanes), jnp.float32),
        ],
        scratch_shapes=[
            pltpu.VMEM((2 * seqs, lanes), jnp.float32),
            pltpu.VMEM(((blocks + window) * pairs, piece), jnp.float32),
            pltpu.VMEM((4 * pairs, lanes), jnp.float32),
            pltpu.VMEM((4 * pairs, lanes), jnp.float32),
            pltpu.VMEM((blocks, room, pairs // blocks, pairs), jnp.float32),
            pltpu.VMEM((2 * pairs, (window + 2) * pairs), jnp.bfloat16),
        ],
        compiler_params=pltpu.CompilerParams(vmem_limit_bytes=26 * mebibyte),
        name="slice_grads",
    )(facts, place, queries, documents, *parts)


def project_kernel(grad_ref, normed_ref, inv_ref, out_ref):
    parts, _, piece = grad_ref.shape
    cuts = [slice(part * piece, (part + 1) * piece) for part in range(parts)]
    inverse = inv_ref[:, :1]
    total = 0.0
    for part, cut in enumerate(cuts):
        unit = normed_ref[:, cut].astype(jnp.float32) * inverse
        total = total + unit * grad_ref[part].astype(jnp.float32)
    along = jnp.sum(total, axis=-1, keepdims=True)
    for part, cut in enumerate(cuts):
        unit = normed_ref[:, cut].astype(jnp.float32) * inverse
        out_ref[:, cut] = grad_ref[part].astype(jnp.float32) - unit * along


def project_call(returned, normed, inverse):
    parts, seqs, piece = returned.shape
    width = normed.shape[1]
    rows = 64
    return pl.pallas_call(
        project_kernel,
        grid=(seqs // rows,),
        in_specs=[
            pl.BlockSpec((parts, rows, piece), lambda i: (0, i, 0)),
            pl.BlockSpec((rows, width), lambda i: (i, 0)),
            pl.BlockSpec((rows, lanes), lambda i: (i, 0)),
        ],
        out_specs=pl.BlockSpec((rows, width), lambda i: (i, 0)),
        out_shape=jax.ShapeDtypeStruct((seqs, width), jnp.float32),
        compiler_params=pltpu.CompilerParams(vmem_limit_bytes=10 * mebibyte),
        name="project_out",
    )(returned, normed, inverse)


def swapped(value, apart):
    pairs = [(at, at ^ apart) for at in range(lax.axis_size("pb"))]
    return lax.ppermute(value, "pb", pairs)


def swap_bits(devices):
    bits = [1 << bit for bit in reversed(range(devices.bit_length() - 1))]
    return bits[:-2], bits[-2], bits[-1]


def swap_masks(devices):
    far, side, last = swap_bits(devices)
    held = [0]
    for apart in far:
        held = held + [mask ^ apart for mask in held]
    held = held + [mask ^ side for mask in held]
    return [held, [mask ^ last for mask in held]]


def gather_all(value):
    far, side, last = swap_bits(lax.axis_size("pb"))
    held = value[None]
    beside = [swapped(held, side)]
    for apart in far:
        arrived = swapped(held, apart)
        beside.append(swapped(arrived, side))
        held = jnp.concatenate([held, arrived], axis=0)
    held = jnp.concatenate([held] + beside, axis=0)
    return [held, swapped(held, last)]


def middle(facts, embedded, room, devices, pairs, window):
    queries, documents, mine, other, top, place = score_call(
        facts, embedded, room, devices, pairs, window
    )
    own_scores, *codes = merge_call(mine, swapped(other, 1), top, swapped(top, 1), devices)
    codes = [swapped(code, 2 * (hop + 1)) for hop, code in enumerate(codes)]
    parts = gather_all(softmax_call(place, own_scores, codes, devices, window))
    grads, loss = grad_call(facts, place, parts, queries, documents, devices, pairs, window)
    return grads, loss[0, :1]


def feature_plan(hidden, final_gain, last_row, pair_owner, hard_negatives):
    devices = lax.axis_size("pb")
    pairs = pair_owner.shape[0]
    window = hard_negatives.shape[1]
    normed, inverse, embedding, known = norm_call(
        last_row, hidden, final_gain, pair_owner.T, hard_negatives, devices
    )
    facts = lax.all_gather(known, "pb", axis=0, tiled=False)
    embedded = lax.all_to_all(embedding, "pb", split_axis=0, concat_axis=0, tiled=True)
    most = devices * (window + 1)
    rooms = [most * part // 20 for part in (10, 11, 12, 13, 14, 16, 20)]
    used = devices + jnp.sum(facts[:, 2, :window])
    level = sum((used > room).astype(jnp.int32) for room in rooms[:-1])
    grads, loss = lax.switch(
        level,
        [
            functools.partial(middle, room=room, devices=devices, pairs=pairs, window=window)
            for room in rooms
        ],
        facts,
        embedded,
    )
    returned = lax.all_to_all(grads, "pb", split_axis=0, concat_axis=0, tiled=True)
    return project_call(returned, normed, inverse), loss


def from_behind(value, axis, steps):
    count = lax.axis_size(axis)
    pairs = [(source, (source + steps) % count) for source in range(count)]
    return lax.ppermute(value, axis, pairs)


def similarity(queries, documents):
    return inverse_temp * lax.dot_general(
        queries, documents, (((1,), (1,)), ((), ())), preferred_element_type=jnp.float32
    )


def transposed(weights, queries):
    return lax.dot_general(
        weights, queries, (((0,), (0,)), ((), ())), preferred_element_type=jnp.float32
    )


def combine_docs(weights, documents):
    return jnp.dot(weights, documents, preferred_element_type=jnp.float32)


def skipped(listed, function, operands, out_shape):
    return lax.cond(
        listed,
        lambda inputs: function(*inputs),
        lambda inputs: jnp.zeros(out_shape, jnp.float32),
        operands,
    )


def row_plan(hidden, final_gain, last_row, pair_owner, hard_negatives):
    values = hidden.astype(jnp.float32)
    scale_row = lax.rsqrt(jnp.mean(values * values, axis=-1, keepdims=True) + token_eps)
    normed = (values * scale_row * final_gain.astype(jnp.float32)).astype(jnp.bfloat16)
    seq_count = last_row.shape[1]
    model_width = hidden.shape[1]
    pooled = normed[last_row[0]].astype(jnp.float32)
    inverse_norm = lax.rsqrt(jnp.sum(pooled * pooled, axis=-1, keepdims=True) + 1e-06)
    unit_vec = pooled * inverse_norm
    embedding = unit_vec.astype(jnp.bfloat16)
    devices = lax.axis_size("pb")
    capacity = 2 * seq_count // devices
    pair_count = pair_owner.shape[0]
    wanted = jnp.concatenate([pair_owner[:, 0], pair_owner[:, 1]])
    holder = wanted // seq_count
    within = wanted % seq_count
    entry_ids = jnp.arange(2 * pair_count, dtype=jnp.int32)
    earlier = (holder[None, :] == holder[:, None]) & (entry_ids[None, :] < entry_ids[:, None])
    position = jnp.sum(earlier.astype(jnp.int32), axis=1)
    request = jnp.full((devices, capacity), -1, jnp.int32).at[holder, position].set(within)
    served = lax.all_to_all(request, "pb", split_axis=0, concat_axis=0, tiled=True)
    outgoing = jnp.where(
        served[:, :, None] >= 0, embedding[jnp.maximum(served, 0)], jnp.zeros((), jnp.bfloat16)
    )
    received = lax.all_to_all(outgoing, "pb", split_axis=0, concat_axis=0, tiled=True)
    gathered = received[holder, position]
    queries = gathered[:pair_count]
    own_docs = gathered[pair_count:]
    listed_ids = hard_negatives[0]
    window = hard_negatives.shape[1]
    listed = [listed_ids[offset] >= 0 for offset in range(window)]
    neighbours = []
    moving = own_docs
    for offset in range(window):
        moving = from_behind(moving, "pb", -1)
        neighbours.append(moving)
    tile_shape = (pair_count, pair_count)
    score_blocks = [similarity(queries, own_docs)]
    for offset in range(window):
        score_blocks.append(
            skipped(listed[offset], similarity, (queries, neighbours[offset]), tile_shape)
        )
    all_scores = jnp.concatenate(score_blocks, axis=1)
    usable = jnp.concatenate(
        [jnp.ones((pair_count,), jnp.bool_)]
        + [jnp.broadcast_to(listed[offset], (pair_count,)) for offset in range(window)]
    )
    masked = jnp.where(usable[None, :], all_scores, -jnp.inf)
    row_max = jnp.max(masked, axis=1, keepdims=True)
    log_total = row_max + jnp.log(jnp.sum(jnp.exp(masked - row_max), axis=1, keepdims=True))
    diagonal = jnp.arange(pair_count, dtype=jnp.int32)
    positive = all_scores[diagonal, diagonal]
    block_loss = jnp.mean(log_total[:, 0] - positive).reshape(1)
    columns = jnp.arange((window + 1) * pair_count, dtype=jnp.int32)
    target = (columns[None, :] == diagonal[:, None]).astype(jnp.float32)
    coefficients = (inverse_temp * (jnp.exp(masked - log_total) - target)).astype(jnp.bfloat16)
    pieces = [
        coefficients[:, offset * pair_count : (offset + 1) * pair_count]
        for offset in range(window + 1)
    ]
    grad_shape = (pair_count, model_width)
    query_sum = combine_docs(pieces[0], own_docs)
    for offset in range(window):
        query_sum = query_sum + skipped(
            listed[offset], combine_docs, (pieces[offset + 1], neighbours[offset]), grad_shape
        )
    query_grad = query_sum.astype(jnp.bfloat16)
    own_part = transposed(pieces[0], queries).astype(jnp.bfloat16)
    partial_value = [
        skipped(listed[offset], transposed, (pieces[offset + 1], queries), grad_shape).astype(
            jnp.bfloat16
        )
        for offset in range(window)
    ]
    running = partial_value[window - 1].astype(jnp.float32)
    for offset in range(window):
        running = from_behind(running, "pb", 1)
        if offset + 1 < window:
            running = running + partial_value[window - 2 - offset].astype(jnp.float32)
    doc_grad = (own_part.astype(jnp.float32) + running).astype(jnp.bfloat16)
    answers = jnp.concatenate([query_grad, doc_grad], axis=0)
    returning = (
        jnp.zeros((devices, capacity, model_width), jnp.bfloat16).at[holder, position].set(answers)
    )
    returned = lax.all_to_all(returning, "pb", split_axis=0, concat_axis=0, tiled=True)
    slot_ids = jnp.where(served >= 0, served, seq_count).reshape(-1)
    emb_grad = (
        jnp.zeros((seq_count, model_width), jnp.bfloat16)
        .at[slot_ids]
        .set(returned.reshape(-1, model_width), mode="drop")
    )
    gradient = emb_grad.astype(jnp.float32)
    pooled_grad = gradient - unit_vec * jnp.sum(unit_vec * gradient, axis=-1, keepdims=True)
    return (pooled_grad, block_loss)


def solution(mesh):
    def local(hidden, final_gain, last_row, pair_owner, hard_negatives):
        plan = feature_plan if hidden.shape[1] >= lanes * mesh.shape["pb"] else row_plan
        return plan(hidden, final_gain, last_row, pair_owner, hard_negatives)

    return jax.shard_map(
        local,
        mesh=mesh,
        in_specs=(
            P(("groups", "pb"), None),
            P(),
            P(("groups", "pb"), None),
            P(("groups", "pb"), None),
            P(("groups", "pb"), None),
        ),
        out_specs=(P(("groups", "pb"), None), P(("groups", "pb"))),
        check_vma=False,
    )
```

```python
import functools

import jax
import jax.numpy as jnp
from jax import lax
from jax.experimental import pallas as pl
from jax.experimental.pallas import tpu as pltpu
from jax.sharding import PartitionSpec as P

inverse_temp = 50.0
token_eps = 1e-05
unit_eps = 1e-06
lanes = 128
bound_steps = 256.0
code_steps = 32000.0
mebibyte = 1024 * 1024


def spread(target, at, value):
    count = value.shape[0]
    for half in range(2):
        target[pl.ds(2 * at + half, count, stride=2), :] = value[:, half * lanes : (half + 1) * lanes]


def gathered(source, at, count):
    halves = [source[pl.ds(2 * at + half, count, stride=2), :] for half in range(2)]
    return jnp.concatenate(halves, axis=1)


def row_pair(index):
    return pl.ds(pl.multiple_of(2 * index, 2), 2)


def norm_kernel(
    last_ref, hidden_ref, gain_ref, owner_ref, negative_ref, normed_ref, inv_ref, emb_ref
):
    seqs, width = normed_ref.shape
    parts, _, piece = emb_ref.shape
    pairs = owner_ref.shape[1]
    cuts = [slice(part * piece, (part + 1) * piece) for part in range(parts)]
    sources = lax.broadcasted_iota(jnp.int32, (seqs, seqs), 0)
    pick = jnp.where(sources == last_ref[...], 1.0, 0.0).astype(jnp.bfloat16)

    def folded(squares):
        return functools.reduce(
            jnp.add, [squares[:, at : at + lanes] for at in range(0, piece, lanes)]
        )

    total = jnp.zeros((seqs, lanes), jnp.float32)
    for cut in cuts:
        values = lax.dot_general(
            pick, hidden_ref[:, cut], (((0,), (0,)), ((), ())), preferred_element_type=jnp.float32
        )
        normed_ref[:, cut] = values.astype(jnp.bfloat16)
        total = total + folded(values * values)
    scale = lax.rsqrt(jnp.sum(total, axis=-1, keepdims=True) / width + token_eps)
    total = jnp.zeros((seqs, lanes), jnp.float32)
    for cut in cuts:
        values = normed_ref[:, cut].astype(jnp.float32)
        gain = gain_ref[cut].astype(jnp.float32).reshape(1, piece)
        normed = (values * scale * gain).astype(jnp.bfloat16)
        normed_ref[:, cut] = normed
        pooled = normed.astype(jnp.float32)
        total = total + folded(pooled * pooled)
    inverse = lax.rsqrt(jnp.sum(total, axis=-1, keepdims=True) + unit_eps)
    inv_ref[...] = jnp.broadcast_to(inverse, inv_ref.shape)

    owners = owner_ref[...].astype(jnp.float32)
    high = jnp.floor(owners * (1.0 / 256.0))
    low = owners - 256.0 * high
    row = lax.broadcasted_iota(jnp.int32, (16, pairs), 0)
    spot = lax.broadcasted_iota(jnp.int32, (16, pairs), 1)
    left = jnp.where(row == 0, low[:1], jnp.where(row == 1, high[:1], 0.0))
    right = jnp.where(row == 0, low[1:2], jnp.where(row == 1, high[1:2], 0.0))
    for offset in range(negative_ref.shape[1]):
        named = (negative_ref[0, offset] >= 0).astype(jnp.float32)
        left = jnp.where((row == 2) & (spot == offset), named, left)
    facts = jnp.concatenate([left, right], axis=1).astype(jnp.bfloat16)

    for part, cut in enumerate(cuts):
        emb_ref[part, :seqs] = (normed_ref[:, cut].astype(jnp.float32) * inverse).astype(jnp.bfloat16)
        emb_ref[part, seqs:] = facts


def norm_call(last_row, hidden, gain, owners, hard_negatives, parts):
    seqs, width = hidden.shape
    piece = width // parts
    whole = pl.BlockSpec(memory_space=pltpu.VMEM)
    return pl.pallas_call(
        norm_kernel,
        in_specs=[whole, whole, whole, whole, pl.BlockSpec(memory_space=pltpu.SMEM)],
        out_specs=[whole] * 3,
        out_shape=[
            jax.ShapeDtypeStruct((seqs, width), jnp.bfloat16),
            jax.ShapeDtypeStruct((seqs, lanes), jnp.float32),
            jax.ShapeDtypeStruct((parts, seqs + 16, piece), jnp.bfloat16),
        ],
        compiler_params=pltpu.CompilerParams(vmem_limit_bytes=56 * mebibyte),
        name="norm_rows",
    )(last_row, hidden, gain, owners, hard_negatives)


def score_kernel(
    blocks,
    pairs,
    window,
    *refs,
):
    emb_ref, q_ref, d_ref, mine_ref, other_ref, top_ref, own_ref, place_ref = refs[:-7]
    wide, picked, picked_too, facts, own, named, sems = refs[-7:]
    seqs = emb_ref.shape[1] - 16
    sent = emb_ref[:, seqs:, :].astype(jnp.float32)
    own_ref[...] = (sent[:, 0, :] + 256.0 * sent[:, 1, :]).astype(jnp.int32)
    facts[...] = sent[:, 2, :lanes].astype(jnp.int32)
    fetches = [
        pltpu.make_async_copy(own_ref, own, sems.at[0]),
        pltpu.make_async_copy(facts, named, sems.at[1]),
    ]
    for fetch in fetches:
        fetch.start()

    for part in range(blocks):
        spread(wide, part * seqs, emb_ref[part, :seqs, :].astype(jnp.float32))
    for fetch in fetches:
        fetch.wait()

    def place(block, count):
        place_ref[0, block] = block
        for offset in range(window):
            present = named[block, offset] > 0
            place_ref[offset + 1, block] = jnp.where(present, count, -1)
            count = count + present.astype(jnp.int32)
        return count

    used = lax.fori_loop(0, blocks, place, blocks)
    fine = pairs // blocks

    def clear(spot, carry):
        empty = jnp.zeros((blocks // 2, fine, pairs), jnp.float32)
        at = pl.ds(pl.multiple_of(spot * fine, fine), fine)
        mine_ref[:, at, :] = empty
        other_ref[:, at, :] = empty
        return carry

    lax.fori_loop(used, mine_ref.shape[1] // fine, clear, 0)
    group = 32

    def pick_block(block, rows_at):
        for base in range(0, 2 * pairs, group):
            rows = [wide[row_pair(own[block, base + k]), :] for k in range(group)]
            for k in range(group):
                rows_at[2 * (base + k) : 2 * (base + k + 1), :] = rows[k]
        at = pl.multiple_of(block * pairs, pairs)
        q_ref[pl.ds(at, pairs), :] = gathered(rows_at, 0, pairs).astype(jnp.bfloat16)
        d_ref[pl.ds(at, pairs), :] = gathered(rows_at, pairs, pairs).astype(jnp.bfloat16)

    ahead = -(-(window + 2) // 2)

    def pick_one(block, carry):
        pick_block(block, picked)
        return carry

    lax.fori_loop(0, 2 * ahead, pick_one, 0)
    even = lax.axis_index("pb") % 2 == 0
    spare = mine_ref.shape[1] // fine - 1

    def score_blocks(step, carry):
        at = pl.multiple_of(step * 2 * pairs, 2 * pairs)
        tiles = inverse_temp * lax.dot_general(
            q_ref[pl.ds(at, 2 * pairs), :],
            d_ref[pl.ds(at, (window + 2) * pairs), :],
            (((1,), (1,)), ((), ())),
            preferred_element_type=jnp.float32,
        )
        top = carry
        for half in range(2):
            for column in range(window + 1):
                spot = place_ref[column, 2 * step + half]
                row = pl.multiple_of(jnp.where(spot >= 0, spot, spare) * fine, fine)
                tile = tiles[
                    half * pairs : (half + 1) * pairs,
                    (half + column) * pairs : (half + column + 1) * pairs,
                ]
                parted = tile.reshape(blocks // 2, 2, fine, pairs)
                first, second = parted[:, 0], parted[:, 1]
                mine_ref[:, pl.ds(row, fine), :] = jnp.where(even, first, second)
                other_ref[:, pl.ds(row, fine), :] = jnp.where(even, second, first)
                size = jnp.maximum(jnp.abs(first), jnp.abs(second))
                top = jnp.maximum(top, jnp.max(size, axis=0))
        return top

    def score_and_pick(step, top):
        top = score_blocks(step - ahead, top)
        pick_block(2 * step, picked)
        pick_block(2 * step + 1, picked_too)
        return top

    top = jnp.zeros((fine, pairs), jnp.float32)
    top = lax.fori_loop(ahead, blocks // 2, score_and_pick, top)
    d_ref[blocks * pairs :, :] = d_ref[: window * pairs, :]
    top_ref[...] = lax.fori_loop(blocks // 2 - ahead, blocks // 2, score_blocks, top)


def score_call(embedded, room, blocks, pairs, window):
    _, rows, piece = embedded.shape
    fine = pairs // blocks
    whole = pl.BlockSpec(memory_space=pltpu.VMEM)
    scalars = pl.BlockSpec(memory_space=pltpu.SMEM)
    return pl.pallas_call(
        functools.partial(score_kernel, blocks, pairs, window),
        in_specs=[whole],
        out_specs=[whole, whole, whole, whole, whole, whole, scalars],
        out_shape=[
            jax.ShapeDtypeStruct((blocks * pairs, piece), jnp.bfloat16),
            jax.ShapeDtypeStruct(((blocks + window) * pairs, piece), jnp.bfloat16),
            jax.ShapeDtypeStruct((blocks // 2, (room + 1) * fine, pairs), jnp.float32),
            jax.ShapeDtypeStruct((blocks // 2, (room + 1) * fine, pairs), jnp.float32),
            jax.ShapeDtypeStruct((fine, pairs), jnp.float32),
            jax.ShapeDtypeStruct((blocks, 2 * pairs), jnp.int32),
            jax.ShapeDtypeStruct((window + 1, blocks), jnp.int32),
        ],
        scratch_shapes=[
            pltpu.VMEM((2 * blocks * (rows - 16), lanes), jnp.float32),
            pltpu.VMEM((4 * pairs, lanes), jnp.float32),
            pltpu.VMEM((4 * pairs, lanes), jnp.float32),
            pltpu.VMEM((blocks, lanes), jnp.int32),
            pltpu.SMEM((blocks, 2 * pairs), jnp.int32),
            pltpu.SMEM((blocks, lanes), jnp.int32),
            pltpu.SemaphoreType.DMA((2,)),
        ],
        compiler_params=pltpu.CompilerParams(vmem_limit_bytes=22 * mebibyte),
        name="partial_scores",
    )(embedded)


def merge_kernel(mine_ref, other_ref, top_ref, other_top_ref, own_ref, *code_refs):
    rows, pairs = own_ref.shape
    steps = code_refs[0].shape[0] - 1
    fine = rows // steps // 2
    chip = lax.axis_index("pb") // 2

    def highest(ref):
        return jnp.max(jnp.max(ref[...], axis=1, keepdims=True), axis=0, keepdims=True)

    top = highest(top_ref) + highest(other_top_ref)
    bound = jnp.ceil(top * bound_steps) + 1.0
    scale = code_steps * bound_steps / bound
    own_ref[...] = mine_ref[chip, :rows] + other_ref[chip, :rows]
    for hop, code_ref in enumerate(code_refs):
        target = chip ^ (hop + 1)

        def encode(step, carry):
            at = pl.multiple_of(step * 2 * fine, 2 * fine)
            there = pl.ds(at, 2 * fine)
            codes = jnp.round((mine_ref[target, there, :] + other_ref[target, there, :]) * scale)
            code_ref[step] = codes.astype(jnp.int32).astype(jnp.int16)
            return carry

        lax.fori_loop(0, steps, encode, 0)
        code_ref[steps] = jnp.broadcast_to(bound, (2 * fine, pairs)).astype(jnp.int32).astype(jnp.int16)


def merge_call(mine, other, top, other_top, blocks):
    chips, rows, pairs = mine.shape
    fine = pairs // blocks
    rows = rows - fine
    whole = pl.BlockSpec(memory_space=pltpu.VMEM)
    coded = jax.ShapeDtypeStruct((rows // (2 * fine) + 1, 2 * fine, pairs), jnp.int16)
    return pl.pallas_call(
        merge_kernel,
        in_specs=[whole] * 4,
        out_specs=[whole] * chips,
        out_shape=[jax.ShapeDtypeStruct((rows, pairs), jnp.float32)] + [coded] * (chips - 1),
        compiler_params=pltpu.CompilerParams(vmem_limit_bytes=12 * mebibyte),
        name="merge_scores",
    )(mine, other, top, other_top)


def softmax_kernel(blocks, window, place_ref, own_ref, *refs):
    code_refs, (c_ref, packed, masked) = refs[:-3], refs[-3:]
    room, fine, pairs = packed.shape
    count = blocks * fine
    unit = 1.0 / (code_steps * bound_steps)
    scales = [ref[room // 2].astype(jnp.int32).astype(jnp.float32) * unit for ref in code_refs]

    def decode(step, carry):
        both = own_ref[pl.ds(pl.multiple_of(step * 2 * fine, 2 * fine), 2 * fine), :]
        for ref, scale in zip(code_refs, scales):
            both = both + ref[step].astype(jnp.int32).astype(jnp.float32) * scale
        packed[2 * step] = both[:fine]
        packed[2 * step + 1] = both[fine:]
        return carry

    lax.fori_loop(0, room // 2, decode, 0)
    for block in range(blocks):
        for column in range(window + 1):
            spot = place_ref[column, block]
            tile = packed[jnp.maximum(spot, 0)]
            masked[block * fine : (block + 1) * fine, column * pairs : (column + 1) * pairs] = (
                jnp.where(spot >= 0, tile, -jnp.inf)
            )
    row = lax.broadcasted_iota(jnp.int32, (count, pairs), 0)
    lane = lax.broadcasted_iota(jnp.int32, (count, pairs), 1)
    target = lane == lax.axis_index("pb") * fine + row % fine
    pieces = [masked[:, column * pairs : (column + 1) * pairs] for column in range(window + 1)]
    row_max = jnp.max(functools.reduce(jnp.maximum, pieces), axis=1, keepdims=True)
    total = functools.reduce(jnp.add, [jnp.exp(piece - row_max) for piece in pieces])
    log_total = row_max + jnp.log(jnp.sum(total, axis=1, keepdims=True))
    positive = jnp.sum(jnp.where(target, pieces[0], 0.0), axis=1, keepdims=True)
    for column, piece in enumerate(pieces):
        share = jnp.exp(piece - log_total)
        if column == 0:
            share = share - jnp.where(target, 1.0, 0.0)
        masked[:, column * pairs : (column + 1) * pairs] = inverse_temp * share
    for block in range(blocks):
        for column in range(window + 1):
            spot = place_ref[column, block]

            @pl.when(spot >= 0)
            def _():
                packed[spot] = masked[
                    block * fine : (block + 1) * fine, column * pairs : (column + 1) * pairs
                ]

    for step in range(room // 2):
        both = jnp.concatenate([packed[2 * step], packed[2 * step + 1]], axis=0)
        c_ref[step] = both.astype(jnp.bfloat16)
    losses = jnp.sum(
        jnp.where(lane == row // fine, log_total - positive, 0.0), axis=0, keepdims=True
    )
    coarse = losses.astype(jnp.bfloat16).astype(jnp.float32)
    rank = lax.broadcasted_iota(jnp.int32, (2 * fine, pairs), 0)
    both = jnp.where(rank == 0, coarse, jnp.where(rank == 1, losses - coarse, 0.0))
    c_ref[room // 2] = both.astype(jnp.bfloat16)


def softmax_call(place, own_scores, codes, blocks, window):
    steps, fine, pairs = codes[0].shape
    room, fine = 2 * (steps - 1), fine // 2
    whole = pl.BlockSpec(memory_space=pltpu.VMEM)
    return pl.pallas_call(
        functools.partial(softmax_kernel, blocks, window),
        in_specs=[pl.BlockSpec(memory_space=pltpu.SMEM), whole] + [whole] * len(codes),
        out_specs=whole,
        out_shape=jax.ShapeDtypeStruct((room // 2 + 1, 2 * fine, pairs), jnp.bfloat16),
        scratch_shapes=[
            pltpu.VMEM((room, fine, pairs), jnp.float32),
            pltpu.VMEM((blocks * fine, (window + 1) * pairs), jnp.float32),
        ],
        compiler_params=pltpu.CompilerParams(vmem_limit_bytes=8 * mebibyte),
        name="softmax_rows",
    )(place, own_scores, *codes)


def grad_kernel(
    blocks,
    pairs,
    window,
    own_ref,
    place_ref,
    q_ref,
    d_ref,
    *refs,
):
    part_refs = refs[:-7]
    out_ref, loss_ref, wide, dsum, picked, packed, square = refs[-7:]
    fine = pairs // blocks
    room = packed.shape[1]
    me = lax.axis_index("pb")
    masks = swap_masks(blocks)
    group = 32
    losses = 0.0
    for part in part_refs:
        sent = part[:, room // 2].astype(jnp.float32)
        losses = losses + jnp.sum(sent[:, 0, :] + sent[:, 1, :], axis=0, keepdims=True) / pairs
    lane = lax.broadcasted_iota(jnp.int32, losses.shape, 1)
    mine = jnp.where(lane == me, losses, 0.0)
    loss_ref[...] = jnp.broadcast_to(jnp.sum(mine, axis=1, keepdims=True), loss_ref.shape)
    dsum[...] = jnp.zeros_like(dsum)
    square[...] = jnp.zeros_like(square)

    def unpack(step, carry):
        for part, mask in zip(part_refs, masks):
            both = part[:, step].astype(jnp.float32)
            for at, apart in enumerate(mask):
                packed[me ^ apart, 2 * step] = both[at, :fine]
                packed[me ^ apart, 2 * step + 1] = both[at, fine:]
        return carry

    lax.fori_loop(0, room // 2, unpack, 0)

    def scatter_rows(block, offset, start):
        for base in range(0, pairs, group):
            rows = [
                picked[2 * (start + base + k) : 2 * (start + base + k + 1), :] for k in range(group)
            ]
            for k in range(group):
                wide[row_pair(own_ref[block, offset + base + k]), :] = rows[k]

    def two_blocks(step, carry):
        for half in range(2):
            for column in range(window + 1):
                spot = place_ref[column, 2 * step + half]
                tile = packed[:, jnp.maximum(spot, 0)].reshape(pairs, pairs)
                square[
                    half * pairs : (half + 1) * pairs,
                    (half + column) * pairs : (half + column + 1) * pairs,
                ] = jnp.where(spot >= 0, tile, 0.0).astype(jnp.bfloat16)
        at = pl.multiple_of(step * 2 * pairs, 2 * pairs)
        there = pl.ds(at, (window + 2) * pairs)
        coefficients = square[...]
        summed = jnp.dot(coefficients, d_ref[there, :], preferred_element_type=jnp.float32)
        spread(picked, 0, summed)
        dsum[there, :] += lax.dot_general(
            coefficients,
            q_ref[pl.ds(at, 2 * pairs), :],
            (((0,), (0,)), ((), ())),
            preferred_element_type=jnp.float32,
        )
        for half in range(2):
            scatter_rows(2 * step + half, 0, half * pairs)
        return carry

    lax.fori_loop(0, blocks // 2, two_blocks, 0)
    dsum[: window * pairs, :] += dsum[blocks * pairs :, :]

    def doc_block(block, carry):
        at = pl.multiple_of(block * pairs, pairs)
        spread(picked, 0, dsum[pl.ds(at, pairs), :])
        scatter_rows(block, pairs, 0)
        return carry

    lax.fori_loop(0, blocks, doc_block, 0)
    slots = out_ref.shape[1]
    for part in range(blocks):
        out_ref[part] = gathered(wide, part * slots, slots).astype(jnp.bfloat16)


def grad_call(own, place, parts, queries, documents, blocks, pairs, window):
    count, piece = queries.shape
    seqs = 2 * count
    room = 2 * (parts[0].shape[1] - 1)
    whole = pl.BlockSpec(memory_space=pltpu.VMEM)
    scalars = pl.BlockSpec(memory_space=pltpu.SMEM)
    return pl.pallas_call(
        functools.partial(grad_kernel, blocks, pairs, window),
        in_specs=[scalars, scalars, whole, whole] + [whole] * len(parts),
        out_specs=[whole, whole],
        out_shape=[
            jax.ShapeDtypeStruct((blocks, seqs // blocks, piece), jnp.bfloat16),
            jax.ShapeDtypeStruct((1, lanes), jnp.float32),
        ],
        scratch_shapes=[
            pltpu.VMEM((2 * seqs, lanes), jnp.float32),
            pltpu.VMEM(((blocks + window) * pairs, piece), jnp.float32),
            pltpu.VMEM((4 * pairs, lanes), jnp.float32),
            pltpu.VMEM((blocks, room, pairs // blocks, pairs), jnp.float32),
            pltpu.VMEM((2 * pairs, (window + 2) * pairs), jnp.bfloat16),
        ],
        compiler_params=pltpu.CompilerParams(vmem_limit_bytes=26 * mebibyte),
        name="slice_grads",
    )(own, place, queries, documents, *parts)


def project_kernel(grad_ref, normed_ref, inv_ref, out_ref):
    parts, _, piece = grad_ref.shape
    cuts = [slice(part * piece, (part + 1) * piece) for part in range(parts)]
    inverse = inv_ref[:, :1]
    total = 0.0
    for part, cut in enumerate(cuts):
        unit = normed_ref[:, cut].astype(jnp.float32) * inverse
        total = total + unit * grad_ref[part].astype(jnp.float32)
    along = jnp.sum(total, axis=-1, keepdims=True)
    for part, cut in enumerate(cuts):
        unit = normed_ref[:, cut].astype(jnp.float32) * inverse
        out_ref[:, cut] = grad_ref[part].astype(jnp.float32) - unit * along


def project_call(returned, normed, inverse):
    parts, seqs, piece = returned.shape
    width = normed.shape[1]
    rows = 64
    return pl.pallas_call(
        project_kernel,
        grid=(seqs // rows,),
        in_specs=[
            pl.BlockSpec((parts, rows, piece), lambda i: (0, i, 0)),
            pl.BlockSpec((rows, width), lambda i: (i, 0)),
            pl.BlockSpec((rows, lanes), lambda i: (i, 0)),
        ],
        out_specs=pl.BlockSpec((rows, width), lambda i: (i, 0)),
        out_shape=jax.ShapeDtypeStruct((seqs, width), jnp.float32),
        compiler_params=pltpu.CompilerParams(vmem_limit_bytes=10 * mebibyte),
        name="project_out",
    )(returned, normed, inverse)


def swapped(value, apart):
    pairs = [(at, at ^ apart) for at in range(lax.axis_size("pb"))]
    return lax.ppermute(value, "pb", pairs)


def swap_bits(devices):
    bits = [1 << bit for bit in reversed(range(devices.bit_length() - 1))]
    return bits[:-2], bits[-2], bits[-1]


def swap_masks(devices):
    far, side, last = swap_bits(devices)
    held = [0]
    for apart in far:
        held = held + [mask ^ apart for mask in held]
    held = held + [mask ^ side for mask in held]
    return [held, [mask ^ last for mask in held]]


def gather_all(value):
    far, side, last = swap_bits(lax.axis_size("pb"))
    held = value[None]
    beside = [swapped(held, side)]
    for apart in far:
        arrived = swapped(held, apart)
        beside.append(swapped(arrived, side))
        held = jnp.concatenate([held, arrived], axis=0)
    held = jnp.concatenate([held] + beside, axis=0)
    return [held, swapped(held, last)]


def middle(embedded, room, devices, pairs, window):
    queries, documents, mine, other, top, own, place = score_call(
        embedded, room, devices, pairs, window
    )
    own_scores, *codes = merge_call(mine, swapped(other, 1), top, swapped(top, 1), devices)
    codes = [swapped(code, 2 * (hop + 1)) for hop, code in enumerate(codes)]
    parts = gather_all(softmax_call(place, own_scores, codes, devices, window))
    grads, loss = grad_call(own, place, parts, queries, documents, devices, pairs, window)
    return grads, loss[0, :1]


def feature_plan(hidden, final_gain, last_row, pair_owner, hard_negatives):
    devices = lax.axis_size("pb")
    seqs, width = hidden.shape
    pairs = pair_owner.shape[0]
    window = hard_negatives.shape[1]
    normed, inverse, embedding = norm_call(
        last_row, hidden, final_gain, pair_owner.T, hard_negatives, devices
    )
    embedded = lax.all_to_all(embedding, "pb", split_axis=0, concat_axis=0, tiled=True)
    most = devices * (window + 1)
    rooms = [most * part // 20 for part in (10, 11, 12, 13, 14, 16, 20)]
    used = devices + jnp.sum(embedded[:, seqs + 2, :window].astype(jnp.float32))
    level = sum((used > room).astype(jnp.int32) for room in rooms[:-1])
    grads, loss = lax.switch(
        level,
        [
            functools.partial(middle, room=room, devices=devices, pairs=pairs, window=window)
            for room in rooms
        ],
        embedded,
    )
    returned = lax.all_to_all(grads, "pb", split_axis=0, concat_axis=0, tiled=True)
    return project_call(returned, normed, inverse), loss


def from_behind(value, axis, steps):
    count = lax.axis_size(axis)
    pairs = [(source, (source + steps) % count) for source in range(count)]
    return lax.ppermute(value, axis, pairs)


def similarity(queries, documents):
    return inverse_temp * lax.dot_general(
        queries, documents, (((1,), (1,)), ((), ())), preferred_element_type=jnp.float32
    )


def transposed(weights, queries):
    return lax.dot_general(
        weights, queries, (((0,), (0,)), ((), ())), preferred_element_type=jnp.float32
    )


def combine_docs(weights, documents):
    return jnp.dot(weights, documents, preferred_element_type=jnp.float32)


def skipped(listed, function, operands, out_shape):
    return lax.cond(
        listed,
        lambda inputs: function(*inputs),
        lambda inputs: jnp.zeros(out_shape, jnp.float32),
        operands,
    )


def row_plan(hidden, final_gain, last_row, pair_owner, hard_negatives):
    values = hidden.astype(jnp.float32)
    scale_row = lax.rsqrt(jnp.mean(values * values, axis=-1, keepdims=True) + token_eps)
    normed = (values * scale_row * final_gain.astype(jnp.float32)).astype(jnp.bfloat16)
    seq_count = last_row.shape[1]
    model_width = hidden.shape[1]
    pooled = normed[last_row[0]].astype(jnp.float32)
    inverse_norm = lax.rsqrt(jnp.sum(pooled * pooled, axis=-1, keepdims=True) + 1e-06)
    unit_vec = pooled * inverse_norm
    embedding = unit_vec.astype(jnp.bfloat16)
    devices = lax.axis_size("pb")
    capacity = 2 * seq_count // devices
    pair_count = pair_owner.shape[0]
    wanted = jnp.concatenate([pair_owner[:, 0], pair_owner[:, 1]])
    holder = wanted // seq_count
    within = wanted % seq_count
    entry_ids = jnp.arange(2 * pair_count, dtype=jnp.int32)
    earlier = (holder[None, :] == holder[:, None]) & (entry_ids[None, :] < entry_ids[:, None])
    position = jnp.sum(earlier.astype(jnp.int32), axis=1)
    request = jnp.full((devices, capacity), -1, jnp.int32).at[holder, position].set(within)
    served = lax.all_to_all(request, "pb", split_axis=0, concat_axis=0, tiled=True)
    outgoing = jnp.where(
        served[:, :, None] >= 0, embedding[jnp.maximum(served, 0)], jnp.zeros((), jnp.bfloat16)
    )
    received = lax.all_to_all(outgoing, "pb", split_axis=0, concat_axis=0, tiled=True)
    gathered = received[holder, position]
    queries = gathered[:pair_count]
    own_docs = gathered[pair_count:]
    listed_ids = hard_negatives[0]
    window = hard_negatives.shape[1]
    listed = [listed_ids[offset] >= 0 for offset in range(window)]
    neighbours = []
    moving = own_docs
    for offset in range(window):
        moving = from_behind(moving, "pb", -1)
        neighbours.append(moving)
    tile_shape = (pair_count, pair_count)
    score_blocks = [similarity(queries, own_docs)]
    for offset in range(window):
        score_blocks.append(
            skipped(listed[offset], similarity, (queries, neighbours[offset]), tile_shape)
        )
    all_scores = jnp.concatenate(score_blocks, axis=1)
    usable = jnp.concatenate(
        [jnp.ones((pair_count,), jnp.bool_)]
        + [jnp.broadcast_to(listed[offset], (pair_count,)) for offset in range(window)]
    )
    masked = jnp.where(usable[None, :], all_scores, -jnp.inf)
    row_max = jnp.max(masked, axis=1, keepdims=True)
    log_total = row_max + jnp.log(jnp.sum(jnp.exp(masked - row_max), axis=1, keepdims=True))
    diagonal = jnp.arange(pair_count, dtype=jnp.int32)
    positive = all_scores[diagonal, diagonal]
    block_loss = jnp.mean(log_total[:, 0] - positive).reshape(1)
    columns = jnp.arange((window + 1) * pair_count, dtype=jnp.int32)
    target = (columns[None, :] == diagonal[:, None]).astype(jnp.float32)
    coefficients = (inverse_temp * (jnp.exp(masked - log_total) - target)).astype(jnp.bfloat16)
    pieces = [
        coefficients[:, offset * pair_count : (offset + 1) * pair_count]
        for offset in range(window + 1)
    ]
    grad_shape = (pair_count, model_width)
    query_sum = combine_docs(pieces[0], own_docs)
    for offset in range(window):
        query_sum = query_sum + skipped(
            listed[offset], combine_docs, (pieces[offset + 1], neighbours[offset]), grad_shape
        )
    query_grad = query_sum.astype(jnp.bfloat16)
    own_part = transposed(pieces[0], queries).astype(jnp.bfloat16)
    partial_value = [
        skipped(listed[offset], transposed, (pieces[offset + 1], queries), grad_shape).astype(
            jnp.bfloat16
        )
        for offset in range(window)
    ]
    running = partial_value[window - 1].astype(jnp.float32)
    for offset in range(window):
        running = from_behind(running, "pb", 1)
        if offset + 1 < window:
            running = running + partial_value[window - 2 - offset].astype(jnp.float32)
    doc_grad = (own_part.astype(jnp.float32) + running).astype(jnp.bfloat16)
    answers = jnp.concatenate([query_grad, doc_grad], axis=0)
    returning = (
        jnp.zeros((devices, capacity, model_width), jnp.bfloat16).at[holder, position].set(answers)
    )
    returned = lax.all_to_all(returning, "pb", split_axis=0, concat_axis=0, tiled=True)
    slot_ids = jnp.where(served >= 0, served, seq_count).reshape(-1)
    emb_grad = (
        jnp.zeros((seq_count, model_width), jnp.bfloat16)
        .at[slot_ids]
        .set(returned.reshape(-1, model_width), mode="drop")
    )
    gradient = emb_grad.astype(jnp.float32)
    pooled_grad = gradient - unit_vec * jnp.sum(unit_vec * gradient, axis=-1, keepdims=True)
    return (pooled_grad, block_loss)


def solution(mesh):
    def local(hidden, final_gain, last_row, pair_owner, hard_negatives):
        plan = feature_plan if hidden.shape[1] >= lanes * mesh.shape["pb"] else row_plan
        return plan(hidden, final_gain, last_row, pair_owner, hard_negatives)

    return jax.shard_map(
        local,
        mesh=mesh,
        in_specs=(
            P(("groups", "pb"), None),
            P(),
            P(("groups", "pb"), None),
            P(("groups", "pb"), None),
            P(("groups", "pb"), None),
        ),
        out_specs=(P(("groups", "pb"), None), P(("groups", "pb"))),
        check_vma=False,
    )
```

```python
import functools

import jax
import jax.numpy as jnp
from jax import lax
from jax.experimental import pallas as pl
from jax.experimental.pallas import tpu as pltpu
from jax.sharding import PartitionSpec as P

inverse_temp = 50.0
token_eps = 1e-05
unit_eps = 1e-06
lanes = 128
bound_steps = 256.0
code_steps = 32000.0
mebibyte = 1024 * 1024


def spread(target, at, value):
    count = value.shape[0]
    for half in range(2):
        target[pl.ds(2 * at + half, count, stride=2), :] = value[:, half * lanes : (half + 1) * lanes]


def gathered(source, at, count):
    halves = [source[pl.ds(2 * at + half, count, stride=2), :] for half in range(2)]
    return jnp.concatenate(halves, axis=1)


def row_pair(index):
    return pl.ds(pl.multiple_of(2 * index, 2), 2)


def norm_kernel(
    last_ref, hidden_ref, gain_ref, owner_ref, negative_ref, normed_ref, inv_ref, emb_ref
):
    seqs, width = normed_ref.shape
    parts, _, piece = emb_ref.shape
    pairs = owner_ref.shape[1]
    cuts = [slice(part * piece, (part + 1) * piece) for part in range(parts)]
    sources = lax.broadcasted_iota(jnp.int32, (seqs, seqs), 0)
    pick = jnp.where(sources == last_ref[...], 1.0, 0.0).astype(jnp.bfloat16)

    def folded(squares):
        return functools.reduce(
            jnp.add, [squares[:, at : at + lanes] for at in range(0, piece, lanes)]
        )

    total = jnp.zeros((seqs, lanes), jnp.float32)
    for cut in cuts:
        values = lax.dot_general(
            pick, hidden_ref[:, cut], (((0,), (0,)), ((), ())), preferred_element_type=jnp.float32
        )
        normed_ref[:, cut] = values.astype(jnp.bfloat16)
        total = total + folded(values * values)
    scale = lax.rsqrt(jnp.sum(total, axis=-1, keepdims=True) / width + token_eps)
    total = jnp.zeros((seqs, lanes), jnp.float32)
    for cut in cuts:
        values = normed_ref[:, cut].astype(jnp.float32)
        gain = gain_ref[cut].astype(jnp.float32).reshape(1, piece)
        normed = (values * scale * gain).astype(jnp.bfloat16)
        normed_ref[:, cut] = normed
        pooled = normed.astype(jnp.float32)
        total = total + folded(pooled * pooled)
    inverse = lax.rsqrt(jnp.sum(total, axis=-1, keepdims=True) + unit_eps)
    inv_ref[...] = jnp.broadcast_to(inverse, inv_ref.shape)

    owners = owner_ref[...].astype(jnp.float32)
    high = jnp.floor(owners * (1.0 / 256.0))
    low = owners - 256.0 * high
    row = lax.broadcasted_iota(jnp.int32, (16, pairs), 0)
    spot = lax.broadcasted_iota(jnp.int32, (16, pairs), 1)
    left = jnp.where(row == 0, low[:1], jnp.where(row == 1, high[:1], 0.0))
    right = jnp.where(row == 0, low[1:2], jnp.where(row == 1, high[1:2], 0.0))
    for offset in range(negative_ref.shape[1]):
        named = (negative_ref[0, offset] >= 0).astype(jnp.float32)
        left = jnp.where((row == 2) & (spot == offset), named, left)
    facts = jnp.concatenate([left, right], axis=1).astype(jnp.bfloat16)

    for part, cut in enumerate(cuts):
        emb_ref[part, :seqs] = (normed_ref[:, cut].astype(jnp.float32) * inverse).astype(jnp.bfloat16)
        emb_ref[part, seqs:] = facts


def norm_call(last_row, hidden, gain, owners, hard_negatives, parts):
    seqs, width = hidden.shape
    piece = width // parts
    whole = pl.BlockSpec(memory_space=pltpu.VMEM)
    return pl.pallas_call(
        norm_kernel,
        in_specs=[whole, whole, whole, whole, pl.BlockSpec(memory_space=pltpu.SMEM)],
        out_specs=[whole] * 3,
        out_shape=[
            jax.ShapeDtypeStruct((seqs, width), jnp.bfloat16),
            jax.ShapeDtypeStruct((seqs, lanes), jnp.float32),
            jax.ShapeDtypeStruct((parts, seqs + 16, piece), jnp.bfloat16),
        ],
        compiler_params=pltpu.CompilerParams(vmem_limit_bytes=56 * mebibyte),
        name="norm_rows",
    )(last_row, hidden, gain, owners, hard_negatives)


def score_kernel(
    blocks,
    pairs,
    window,
    *refs,
):
    emb_ref, q_ref, d_ref, mine_ref, other_ref, top_ref, own_ref, place_ref = refs[:-7]
    wide, picked, picked_too, facts, own, named, sems = refs[-7:]
    seqs = emb_ref.shape[1] - 16
    sent = emb_ref[:, seqs:, :].astype(jnp.float32)
    own_ref[...] = (sent[:, 0, :] + 256.0 * sent[:, 1, :]).astype(jnp.int32)
    facts[...] = sent[:, 2, :lanes].astype(jnp.int32)
    fetches = [
        pltpu.make_async_copy(own_ref, own, sems.at[0]),
        pltpu.make_async_copy(facts, named, sems.at[1]),
    ]
    for fetch in fetches:
        fetch.start()

    for part in range(blocks):
        spread(wide, part * seqs, emb_ref[part, :seqs, :].astype(jnp.float32))
    for fetch in fetches:
        fetch.wait()

    def place(block, count):
        place_ref[0, block] = block
        for offset in range(window):
            present = named[block, offset] > 0
            place_ref[offset + 1, block] = jnp.where(present, count, -1)
            count = count + present.astype(jnp.int32)
        return count

    used = lax.fori_loop(0, blocks, place, blocks)
    fine = pairs // blocks

    def clear(spot, carry):
        empty = jnp.zeros((blocks // 2, fine, pairs), jnp.float32)
        at = pl.ds(pl.multiple_of(spot * fine, fine), fine)
        mine_ref[:, at, :] = empty
        other_ref[:, at, :] = empty
        return carry

    lax.fori_loop(used, mine_ref.shape[1] // fine, clear, 0)
    group = 32

    def pick_block(block, rows_at):
        for base in range(0, 2 * pairs, group):
            rows = [wide[row_pair(own[block, base + k]), :] for k in range(group)]
            for k in range(group):
                rows_at[2 * (base + k) : 2 * (base + k + 1), :] = rows[k]
        at = pl.multiple_of(block * pairs, pairs)
        q_ref[pl.ds(at, pairs), :] = gathered(rows_at, 0, pairs).astype(jnp.bfloat16)
        d_ref[pl.ds(at, pairs), :] = gathered(rows_at, pairs, pairs).astype(jnp.bfloat16)

    ahead = -(-(window + 2) // 2)

    def pick_one(block, carry):
        pick_block(block, picked)
        return carry

    lax.fori_loop(0, 2 * ahead, pick_one, 0)
    even = lax.axis_index("pb") % 2 == 0
    spare = mine_ref.shape[1] // fine - 1

    def score_blocks(step, carry):
        at = pl.multiple_of(step * 2 * pairs, 2 * pairs)
        tiles = inverse_temp * lax.dot_general(
            q_ref[pl.ds(at, 2 * pairs), :],
            d_ref[pl.ds(at, (window + 2) * pairs), :],
            (((1,), (1,)), ((), ())),
            preferred_element_type=jnp.float32,
        )
        top = carry
        for half in range(2):
            for column in range(window + 1):
                spot = place_ref[column, 2 * step + half]
                row = pl.multiple_of(jnp.where(spot >= 0, spot, spare) * fine, fine)
                tile = tiles[
                    half * pairs : (half + 1) * pairs,
                    (half + column) * pairs : (half + column + 1) * pairs,
                ]
                parted = tile.reshape(blocks // 2, 2, fine, pairs)
                first, second = parted[:, 0], parted[:, 1]
                mine_ref[:, pl.ds(row, fine), :] = jnp.where(even, first, second)
                other_ref[:, pl.ds(row, fine), :] = jnp.where(even, second, first)
                size = jnp.maximum(jnp.abs(first), jnp.abs(second))
                top = jnp.maximum(top, jnp.max(size, axis=0))
        return top

    def score_and_pick(step, top):
        top = score_blocks(step - ahead, top)
        pick_block(2 * step, picked)
        pick_block(2 * step + 1, picked_too)
        return top

    top = jnp.zeros((fine, pairs), jnp.float32)
    top = lax.fori_loop(ahead, blocks // 2, score_and_pick, top)
    d_ref[blocks * pairs :, :] = d_ref[: window * pairs, :]
    top_ref[...] = lax.fori_loop(blocks // 2 - ahead, blocks // 2, score_blocks, top)


def score_call(embedded, room, blocks, pairs, window):
    _, rows, piece = embedded.shape
    fine = pairs // blocks
    whole = pl.BlockSpec(memory_space=pltpu.VMEM)
    scalars = pl.BlockSpec(memory_space=pltpu.SMEM)
    return pl.pallas_call(
        functools.partial(score_kernel, blocks, pairs, window),
        in_specs=[whole],
        out_specs=[whole, whole, whole, whole, whole, whole, scalars],
        out_shape=[
            jax.ShapeDtypeStruct((blocks * pairs, piece), jnp.bfloat16),
            jax.ShapeDtypeStruct(((blocks + window) * pairs, piece), jnp.bfloat16),
            jax.ShapeDtypeStruct((blocks // 2, (room + 1) * fine, pairs), jnp.float32),
            jax.ShapeDtypeStruct((blocks // 2, (room + 1) * fine, pairs), jnp.float32),
            jax.ShapeDtypeStruct((fine, pairs), jnp.float32),
            jax.ShapeDtypeStruct((blocks, 2 * pairs), jnp.int32),
            jax.ShapeDtypeStruct((window + 1, blocks), jnp.int32),
        ],
        scratch_shapes=[
            pltpu.VMEM((2 * blocks * (rows - 16), lanes), jnp.float32),
            pltpu.VMEM((4 * pairs, lanes), jnp.float32),
            pltpu.VMEM((4 * pairs, lanes), jnp.float32),
            pltpu.VMEM((blocks, lanes), jnp.int32),
            pltpu.SMEM((blocks, 2 * pairs), jnp.int32),
            pltpu.SMEM((blocks, lanes), jnp.int32),
            pltpu.SemaphoreType.DMA((2,)),
        ],
        compiler_params=pltpu.CompilerParams(vmem_limit_bytes=22 * mebibyte),
        name="partial_scores",
    )(embedded)


def merge_kernel(mine_ref, other_ref, top_ref, other_top_ref, own_ref, *code_refs):
    rows, pairs = own_ref.shape
    steps = code_refs[0].shape[0] - 1
    fine = rows // steps // 2
    chip = lax.axis_index("pb") // 2

    def highest(ref):
        return jnp.max(jnp.max(ref[...], axis=1, keepdims=True), axis=0, keepdims=True)

    top = highest(top_ref) + highest(other_top_ref)
    bound = jnp.ceil(top * bound_steps) + 1.0
    scale = code_steps * bound_steps / bound
    own_ref[...] = mine_ref[chip, :rows] + other_ref[chip, :rows]
    for hop, code_ref in enumerate(code_refs):
        target = chip ^ (hop + 1)

        def encode(step, carry):
            at = pl.multiple_of(step * 2 * fine, 2 * fine)
            there = pl.ds(at, 2 * fine)
            codes = jnp.round((mine_ref[target, there, :] + other_ref[target, there, :]) * scale)
            code_ref[step] = codes.astype(jnp.int32).astype(jnp.int16)
            return carry

        lax.fori_loop(0, steps, encode, 0)
        code_ref[steps] = jnp.broadcast_to(bound, (2 * fine, pairs)).astype(jnp.int32).astype(jnp.int16)


def merge_call(mine, other, top, other_top, blocks):
    chips, rows, pairs = mine.shape
    fine = pairs // blocks
    rows = rows - fine
    whole = pl.BlockSpec(memory_space=pltpu.VMEM)
    coded = jax.ShapeDtypeStruct((rows // (2 * fine) + 1, 2 * fine, pairs), jnp.int16)
    return pl.pallas_call(
        merge_kernel,
        in_specs=[whole] * 4,
        out_specs=[whole] * chips,
        out_shape=[jax.ShapeDtypeStruct((rows, pairs), jnp.float32)] + [coded] * (chips - 1),
        compiler_params=pltpu.CompilerParams(vmem_limit_bytes=12 * mebibyte),
        name="merge_scores",
    )(mine, other, top, other_top)


def softmax_kernel(blocks, window, place_ref, own_ref, *refs):
    code_refs, (c_ref, packed, masked) = refs[:-3], refs[-3:]
    room, fine, pairs = packed.shape
    count = blocks * fine
    unit = 1.0 / (code_steps * bound_steps)
    scales = [ref[room // 2].astype(jnp.int32).astype(jnp.float32) * unit for ref in code_refs]

    def decode(step, carry):
        both = own_ref[pl.ds(pl.multiple_of(step * 2 * fine, 2 * fine), 2 * fine), :]
        for ref, scale in zip(code_refs, scales):
            both = both + ref[step].astype(jnp.int32).astype(jnp.float32) * scale
        packed[2 * step] = both[:fine]
        packed[2 * step + 1] = both[fine:]
        return carry

    lax.fori_loop(0, room // 2, decode, 0)
    for block in range(blocks):
        for column in range(window + 1):
            spot = place_ref[column, block]
            tile = packed[jnp.maximum(spot, 0)]
            masked[block * fine : (block + 1) * fine, column * pairs : (column + 1) * pairs] = (
                jnp.where(spot >= 0, tile, -jnp.inf)
            )
    row = lax.broadcasted_iota(jnp.int32, (count, pairs), 0)
    lane = lax.broadcasted_iota(jnp.int32, (count, pairs), 1)
    target = lane == lax.axis_index("pb") * fine + row % fine
    pieces = [masked[:, column * pairs : (column + 1) * pairs] for column in range(window + 1)]
    row_max = jnp.max(functools.reduce(jnp.maximum, pieces), axis=1, keepdims=True)
    total = functools.reduce(jnp.add, [jnp.exp(piece - row_max) for piece in pieces])
    log_total = row_max + jnp.log(jnp.sum(total, axis=1, keepdims=True))
    positive = jnp.sum(jnp.where(target, pieces[0], 0.0), axis=1, keepdims=True)
    for column, piece in enumerate(pieces):
        share = jnp.exp(piece - log_total)
        if column == 0:
            share = share - jnp.where(target, 1.0, 0.0)
        masked[:, column * pairs : (column + 1) * pairs] = inverse_temp * share
    for block in range(blocks):
        for column in range(window + 1):
            spot = place_ref[column, block]

            @pl.when(spot >= 0)
            def _():
                packed[spot] = masked[
                    block * fine : (block + 1) * fine, column * pairs : (column + 1) * pairs
                ]

    for step in range(room // 2):
        both = jnp.concatenate([packed[2 * step], packed[2 * step + 1]], axis=0)
        c_ref[step] = both.astype(jnp.bfloat16)
    losses = jnp.sum(
        jnp.where(lane == row // fine, log_total - positive, 0.0), axis=0, keepdims=True
    )
    coarse = losses.astype(jnp.bfloat16).astype(jnp.float32)
    rank = lax.broadcasted_iota(jnp.int32, (2 * fine, pairs), 0)
    both = jnp.where(rank == 0, coarse, jnp.where(rank == 1, losses - coarse, 0.0))
    c_ref[room // 2] = both.astype(jnp.bfloat16)


def softmax_call(place, own_scores, codes, blocks, window):
    steps, fine, pairs = codes[0].shape
    room, fine = 2 * (steps - 1), fine // 2
    whole = pl.BlockSpec(memory_space=pltpu.VMEM)
    return pl.pallas_call(
        functools.partial(softmax_kernel, blocks, window),
        in_specs=[pl.BlockSpec(memory_space=pltpu.SMEM), whole] + [whole] * len(codes),
        out_specs=whole,
        out_shape=jax.ShapeDtypeStruct((room // 2 + 1, 2 * fine, pairs), jnp.bfloat16),
        scratch_shapes=[
            pltpu.VMEM((room, fine, pairs), jnp.float32),
            pltpu.VMEM((blocks * fine, (window + 1) * pairs), jnp.float32),
        ],
        compiler_params=pltpu.CompilerParams(vmem_limit_bytes=8 * mebibyte),
        name="softmax_rows",
    )(place, own_scores, *codes)


def grad_kernel(
    blocks,
    pairs,
    window,
    own_ref,
    place_ref,
    q_ref,
    d_ref,
    *refs,
):
    part_refs = refs[:-7]
    out_ref, loss_ref, wide, dsum, picked, packed, square = refs[-7:]
    fine = pairs // blocks
    room = packed.shape[1]
    me = lax.axis_index("pb")
    masks = swap_masks(blocks)
    group = 32
    losses = 0.0
    for part in part_refs:
        sent = part[:, room // 2].astype(jnp.float32)
        losses = losses + jnp.sum(sent[:, 0, :] + sent[:, 1, :], axis=0, keepdims=True) / pairs
    lane = lax.broadcasted_iota(jnp.int32, losses.shape, 1)
    mine = jnp.where(lane == me, losses, 0.0)
    loss_ref[...] = jnp.broadcast_to(jnp.sum(mine, axis=1, keepdims=True), loss_ref.shape)
    dsum[...] = jnp.zeros_like(dsum)
    square[...] = jnp.zeros_like(square)

    def unpack(step, carry):
        for part, mask in zip(part_refs, masks):
            both = part[:, step].astype(jnp.float32)
            for at, apart in enumerate(mask):
                packed[me ^ apart, 2 * step] = both[at, :fine]
                packed[me ^ apart, 2 * step + 1] = both[at, fine:]
        return carry

    lax.fori_loop(0, room // 2, unpack, 0)

    def scatter_rows(block, offset, start):
        for base in range(0, pairs, group):
            rows = [
                picked[2 * (start + base + k) : 2 * (start + base + k + 1), :] for k in range(group)
            ]
            for k in range(group):
                wide[row_pair(own_ref[block, offset + base + k]), :] = rows[k]

    def two_blocks(step, carry):
        for half in range(2):
            for column in range(window + 1):
                spot = place_ref[column, 2 * step + half]
                tile = packed[:, jnp.maximum(spot, 0)].reshape(pairs, pairs)
                square[
                    half * pairs : (half + 1) * pairs,
                    (half + column) * pairs : (half + column + 1) * pairs,
                ] = jnp.where(spot >= 0, tile, 0.0).astype(jnp.bfloat16)
        at = pl.multiple_of(step * 2 * pairs, 2 * pairs)
        there = pl.ds(at, (window + 2) * pairs)
        coefficients = square[...]
        summed = jnp.dot(coefficients, d_ref[there, :], preferred_element_type=jnp.float32)
        spread(picked, 0, summed)
        dsum[there, :] += lax.dot_general(
            coefficients,
            q_ref[pl.ds(at, 2 * pairs), :],
            (((0,), (0,)), ((), ())),
            preferred_element_type=jnp.float32,
        )
        for half in range(2):
            scatter_rows(2 * step + half, 0, half * pairs)
        return carry

    lax.fori_loop(0, blocks // 2, two_blocks, 0)
    dsum[: window * pairs, :] += dsum[blocks * pairs :, :]

    def doc_block(block, carry):
        at = pl.multiple_of(block * pairs, pairs)
        spread(picked, 0, dsum[pl.ds(at, pairs), :])
        scatter_rows(block, pairs, 0)
        return carry

    lax.fori_loop(0, blocks, doc_block, 0)
    slots = out_ref.shape[1]
    for part in range(blocks):
        out_ref[part] = gathered(wide, part * slots, slots).astype(jnp.bfloat16)


def grad_call(own, place, parts, queries, documents, blocks, pairs, window):
    count, piece = queries.shape
    seqs = 2 * count
    room = 2 * (parts[0].shape[1] - 1)
    whole = pl.BlockSpec(memory_space=pltpu.VMEM)
    scalars = pl.BlockSpec(memory_space=pltpu.SMEM)
    return pl.pallas_call(
        functools.partial(grad_kernel, blocks, pairs, window),
        in_specs=[scalars, scalars, whole, whole] + [whole] * len(parts),
        out_specs=[whole, whole],
        out_shape=[
            jax.ShapeDtypeStruct((blocks, seqs // blocks, piece), jnp.bfloat16),
            jax.ShapeDtypeStruct((1, lanes), jnp.float32),
        ],
        scratch_shapes=[
            pltpu.VMEM((2 * seqs, lanes), jnp.float32),
            pltpu.VMEM(((blocks + window) * pairs, piece), jnp.float32),
            pltpu.VMEM((4 * pairs, lanes), jnp.float32),
            pltpu.VMEM((blocks, room, pairs // blocks, pairs), jnp.float32),
            pltpu.VMEM((2 * pairs, (window + 2) * pairs), jnp.bfloat16),
        ],
        compiler_params=pltpu.CompilerParams(vmem_limit_bytes=26 * mebibyte),
        name="slice_grads",
    )(own, place, queries, documents, *parts)


def project_kernel(grad_ref, normed_ref, inv_ref, out_ref):
    parts, _, piece = grad_ref.shape
    cuts = [slice(part * piece, (part + 1) * piece) for part in range(parts)]
    inverse = inv_ref[:, :1]
    total = 0.0
    for part, cut in enumerate(cuts):
        unit = normed_ref[:, cut].astype(jnp.float32) * inverse
        total = total + unit * grad_ref[part].astype(jnp.float32)
    along = jnp.sum(total, axis=-1, keepdims=True)
    for part, cut in enumerate(cuts):
        unit = normed_ref[:, cut].astype(jnp.float32) * inverse
        out_ref[:, cut] = grad_ref[part].astype(jnp.float32) - unit * along


def project_call(returned, normed, inverse):
    parts, seqs, piece = returned.shape
    width = normed.shape[1]
    rows = 64
    return pl.pallas_call(
        project_kernel,
        grid=(seqs // rows,),
        in_specs=[
            pl.BlockSpec((parts, rows, piece), lambda i: (0, i, 0)),
            pl.BlockSpec((rows, width), lambda i: (i, 0)),
            pl.BlockSpec((rows, lanes), lambda i: (i, 0)),
        ],
        out_specs=pl.BlockSpec((rows, width), lambda i: (i, 0)),
        out_shape=jax.ShapeDtypeStruct((seqs, width), jnp.float32),
        compiler_params=pltpu.CompilerParams(vmem_limit_bytes=10 * mebibyte),
        name="project_out",
    )(returned, normed, inverse)


def swapped(value, apart):
    pairs = [(at, at ^ apart) for at in range(lax.axis_size("pb"))]
    return lax.ppermute(value, "pb", pairs)


def swap_bits(devices):
    bits = [1 << bit for bit in reversed(range(devices.bit_length() - 1))]
    return bits[:-2], bits[-2], bits[-1]


def swap_masks(devices):
    far, side, last = swap_bits(devices)
    held = [0]
    for apart in far:
        held = held + [mask ^ apart for mask in held]
    held = held + [mask ^ side for mask in held]
    return [held, [mask ^ last for mask in held]]


def gather_all(value):
    far, side, last = swap_bits(lax.axis_size("pb"))
    held = value[None]
    beside = [swapped(held, side)]
    for apart in far:
        arrived = swapped(held, apart)
        beside.append(swapped(arrived, side))
        held = jnp.concatenate([held, arrived], axis=0)
    held = jnp.concatenate([held] + beside, axis=0)
    return [held, swapped(held, last)]


def middle(embedded, room, devices, pairs, window):
    queries, documents, mine, other, top, own, place = score_call(
        embedded, room, devices, pairs, window
    )
    own_scores, *codes = merge_call(mine, swapped(other, 1), top, swapped(top, 1), devices)
    codes = [swapped(code, 2 * (hop + 1)) for hop, code in enumerate(codes)]
    parts = gather_all(softmax_call(place, own_scores, codes, devices, window))
    grads, loss = grad_call(own, place, parts, queries, documents, devices, pairs, window)
    return grads, loss[0, :1]


def feature_plan(hidden, final_gain, last_row, pair_owner, hard_negatives):
    devices = lax.axis_size("pb")
    seqs, width = hidden.shape
    pairs = pair_owner.shape[0]
    window = hard_negatives.shape[1]
    normed, inverse, embedding = norm_call(
        last_row, hidden, final_gain, pair_owner.T, hard_negatives, devices
    )
    embedded = lax.all_to_all(embedding, "pb", split_axis=0, concat_axis=0, tiled=True)
    most = devices * (window + 1)
    rooms = [most * part // 20 for part in (11, 12, 13, 15, 20)]
    used = devices + jnp.sum(embedded[:, seqs + 2, :window].astype(jnp.float32))
    level = sum((used > room).astype(jnp.int32) for room in rooms[:-1])
    grads, loss = lax.switch(
        level,
        [
            functools.partial(middle, room=room, devices=devices, pairs=pairs, window=window)
            for room in rooms
        ],
        embedded,
    )
    returned = lax.all_to_all(grads, "pb", split_axis=0, concat_axis=0, tiled=True)
    return project_call(returned, normed, inverse), loss


def from_behind(value, axis, steps):
    count = lax.axis_size(axis)
    pairs = [(source, (source + steps) % count) for source in range(count)]
    return lax.ppermute(value, axis, pairs)


def similarity(queries, documents):
    return inverse_temp * lax.dot_general(
        queries, documents, (((1,), (1,)), ((), ())), preferred_element_type=jnp.float32
    )


def transposed(weights, queries):
    return lax.dot_general(
        weights, queries, (((0,), (0,)), ((), ())), preferred_element_type=jnp.float32
    )


def combine_docs(weights, documents):
    return jnp.dot(weights, documents, preferred_element_type=jnp.float32)


def skipped(listed, function, operands, out_shape):
    return lax.cond(
        listed,
        lambda inputs: function(*inputs),
        lambda inputs: jnp.zeros(out_shape, jnp.float32),
        operands,
    )


def row_plan(hidden, final_gain, last_row, pair_owner, hard_negatives):
    values = hidden.astype(jnp.float32)
    scale_row = lax.rsqrt(jnp.mean(values * values, axis=-1, keepdims=True) + token_eps)
    normed = (values * scale_row * final_gain.astype(jnp.float32)).astype(jnp.bfloat16)
    seq_count = last_row.shape[1]
    model_width = hidden.shape[1]
    pooled = normed[last_row[0]].astype(jnp.float32)
    inverse_norm = lax.rsqrt(jnp.sum(pooled * pooled, axis=-1, keepdims=True) + 1e-06)
    unit_vec = pooled * inverse_norm
    embedding = unit_vec.astype(jnp.bfloat16)
    devices = lax.axis_size("pb")
    capacity = 2 * seq_count // devices
    pair_count = pair_owner.shape[0]
    wanted = jnp.concatenate([pair_owner[:, 0], pair_owner[:, 1]])
    holder = wanted // seq_count
    within = wanted % seq_count
    entry_ids = jnp.arange(2 * pair_count, dtype=jnp.int32)
    earlier = (holder[None, :] == holder[:, None]) & (entry_ids[None, :] < entry_ids[:, None])
    position = jnp.sum(earlier.astype(jnp.int32), axis=1)
    request = jnp.full((devices, capacity), -1, jnp.int32).at[holder, position].set(within)
    served = lax.all_to_all(request, "pb", split_axis=0, concat_axis=0, tiled=True)
    outgoing = jnp.where(
        served[:, :, None] >= 0, embedding[jnp.maximum(served, 0)], jnp.zeros((), jnp.bfloat16)
    )
    received = lax.all_to_all(outgoing, "pb", split_axis=0, concat_axis=0, tiled=True)
    gathered = received[holder, position]
    queries = gathered[:pair_count]
    own_docs = gathered[pair_count:]
    listed_ids = hard_negatives[0]
    window = hard_negatives.shape[1]
    listed = [listed_ids[offset] >= 0 for offset in range(window)]
    neighbours = []
    moving = own_docs
    for offset in range(window):
        moving = from_behind(moving, "pb", -1)
        neighbours.append(moving)
    tile_shape = (pair_count, pair_count)
    score_blocks = [similarity(queries, own_docs)]
    for offset in range(window):
        score_blocks.append(
            skipped(listed[offset], similarity, (queries, neighbours[offset]), tile_shape)
        )
    all_scores = jnp.concatenate(score_blocks, axis=1)
    usable = jnp.concatenate(
        [jnp.ones((pair_count,), jnp.bool_)]
        + [jnp.broadcast_to(listed[offset], (pair_count,)) for offset in range(window)]
    )
    masked = jnp.where(usable[None, :], all_scores, -jnp.inf)
    row_max = jnp.max(masked, axis=1, keepdims=True)
    log_total = row_max + jnp.log(jnp.sum(jnp.exp(masked - row_max), axis=1, keepdims=True))
    diagonal = jnp.arange(pair_count, dtype=jnp.int32)
    positive = all_scores[diagonal, diagonal]
    block_loss = jnp.mean(log_total[:, 0] - positive).reshape(1)
    columns = jnp.arange((window + 1) * pair_count, dtype=jnp.int32)
    target = (columns[None, :] == diagonal[:, None]).astype(jnp.float32)
    coefficients = (inverse_temp * (jnp.exp(masked - log_total) - target)).astype(jnp.bfloat16)
    pieces = [
        coefficients[:, offset * pair_count : (offset + 1) * pair_count]
        for offset in range(window + 1)
    ]
    grad_shape = (pair_count, model_width)
    query_sum = combine_docs(pieces[0], own_docs)
    for offset in range(window):
        query_sum = query_sum + skipped(
            listed[offset], combine_docs, (pieces[offset + 1], neighbours[offset]), grad_shape
        )
    query_grad = query_sum.astype(jnp.bfloat16)
    own_part = transposed(pieces[0], queries).astype(jnp.bfloat16)
    partial_value = [
        skipped(listed[offset], transposed, (pieces[offset + 1], queries), grad_shape).astype(
            jnp.bfloat16
        )
        for offset in range(window)
    ]
    running = partial_value[window - 1].astype(jnp.float32)
    for offset in range(window):
        running = from_behind(running, "pb", 1)
        if offset + 1 < window:
            running = running + partial_value[window - 2 - offset].astype(jnp.float32)
    doc_grad = (own_part.astype(jnp.float32) + running).astype(jnp.bfloat16)
    answers = jnp.concatenate([query_grad, doc_grad], axis=0)
    returning = (
        jnp.zeros((devices, capacity, model_width), jnp.bfloat16).at[holder, position].set(answers)
    )
    returned = lax.all_to_all(returning, "pb", split_axis=0, concat_axis=0, tiled=True)
    slot_ids = jnp.where(served >= 0, served, seq_count).reshape(-1)
    emb_grad = (
        jnp.zeros((seq_count, model_width), jnp.bfloat16)
        .at[slot_ids]
        .set(returned.reshape(-1, model_width), mode="drop")
    )
    gradient = emb_grad.astype(jnp.float32)
    pooled_grad = gradient - unit_vec * jnp.sum(unit_vec * gradient, axis=-1, keepdims=True)
    return (pooled_grad, block_loss)


def solution(mesh):
    def local(hidden, final_gain, last_row, pair_owner, hard_negatives):
        plan = feature_plan if hidden.shape[1] >= lanes * mesh.shape["pb"] else row_plan
        return plan(hidden, final_gain, last_row, pair_owner, hard_negatives)

    return jax.shard_map(
        local,
        mesh=mesh,
        in_specs=(
            P(("groups", "pb"), None),
            P(),
            P(("groups", "pb"), None),
            P(("groups", "pb"), None),
            P(("groups", "pb"), None),
        ),
        out_specs=(P(("groups", "pb"), None), P(("groups", "pb"))),
        check_vma=False,
    )
```

```python
import functools

import jax
import jax.numpy as jnp
from jax import lax
from jax.experimental import pallas as pl
from jax.experimental.pallas import tpu as pltpu
from jax.sharding import PartitionSpec as P

inverse_temp = 50.0
token_eps = 1e-05
unit_eps = 1e-06
lanes = 128
bound_steps = 256.0
code_steps = 32000.0
mebibyte = 1024 * 1024


def spread(target, at, value):
    count = value.shape[0]
    for half in range(2):
        target[pl.ds(2 * at + half, count, stride=2), :] = value[:, half * lanes : (half + 1) * lanes]


def gathered(source, at, count):
    halves = [source[pl.ds(2 * at + half, count, stride=2), :] for half in range(2)]
    return jnp.concatenate(halves, axis=1)


def row_pair(place):
    return pl.ds(pl.multiple_of(place, 2), 2)


def norm_kernel(
    last_ref, hidden_ref, gain_ref, owner_ref, negative_ref, normed_ref, inv_ref, emb_ref
):
    seqs, width = normed_ref.shape
    parts, _, piece = emb_ref.shape
    pairs = owner_ref.shape[1]
    cuts = [slice(part * piece, (part + 1) * piece) for part in range(parts)]
    sources = lax.broadcasted_iota(jnp.int32, (seqs, seqs), 0)
    pick = jnp.where(sources == last_ref[...], 1.0, 0.0).astype(jnp.bfloat16)

    def folded(squares):
        return functools.reduce(
            jnp.add, [squares[:, at : at + lanes] for at in range(0, piece, lanes)]
        )

    total = jnp.zeros((seqs, lanes), jnp.float32)
    for cut in cuts:
        values = lax.dot_general(
            pick, hidden_ref[:, cut], (((0,), (0,)), ((), ())), preferred_element_type=jnp.float32
        )
        normed_ref[:, cut] = values.astype(jnp.bfloat16)
        total = total + folded(values * values)
    scale = lax.rsqrt(jnp.sum(total, axis=-1, keepdims=True) / width + token_eps)
    total = jnp.zeros((seqs, lanes), jnp.float32)
    for cut in cuts:
        values = normed_ref[:, cut].astype(jnp.float32)
        gain = gain_ref[cut].astype(jnp.float32).reshape(1, piece)
        normed = (values * scale * gain).astype(jnp.bfloat16)
        normed_ref[:, cut] = normed
        pooled = normed.astype(jnp.float32)
        total = total + folded(pooled * pooled)
    inverse = lax.rsqrt(jnp.sum(total, axis=-1, keepdims=True) + unit_eps)
    inv_ref[...] = jnp.broadcast_to(inverse, inv_ref.shape)

    owners = owner_ref[...].astype(jnp.float32)
    high = jnp.floor(owners * (1.0 / 256.0))
    low = owners - 256.0 * high
    row = lax.broadcasted_iota(jnp.int32, (16, pairs), 0)
    spot = lax.broadcasted_iota(jnp.int32, (16, pairs), 1)
    left = jnp.where(row == 0, low[:1], jnp.where(row == 1, high[:1], 0.0))
    right = jnp.where(row == 0, low[1:2], jnp.where(row == 1, high[1:2], 0.0))
    for offset in range(negative_ref.shape[1]):
        named = (negative_ref[0, offset] >= 0).astype(jnp.float32)
        left = jnp.where((row == 2) & (spot == offset), named, left)
    facts = jnp.concatenate([left, right], axis=1).astype(jnp.bfloat16)

    for part, cut in enumerate(cuts):
        emb_ref[part, :seqs] = (normed_ref[:, cut].astype(jnp.float32) * inverse).astype(jnp.bfloat16)
        emb_ref[part, seqs:] = facts


def norm_call(last_row, hidden, gain, owners, hard_negatives, parts):
    seqs, width = hidden.shape
    piece = width // parts
    whole = pl.BlockSpec(memory_space=pltpu.VMEM)
    return pl.pallas_call(
        norm_kernel,
        in_specs=[whole, whole, whole, whole, pl.BlockSpec(memory_space=pltpu.SMEM)],
        out_specs=[whole] * 3,
        out_shape=[
            jax.ShapeDtypeStruct((seqs, width), jnp.bfloat16),
            jax.ShapeDtypeStruct((seqs, lanes), jnp.float32),
            jax.ShapeDtypeStruct((parts, seqs + 16, piece), jnp.bfloat16),
        ],
        compiler_params=pltpu.CompilerParams(vmem_limit_bytes=56 * mebibyte),
        name="norm_rows",
    )(last_row, hidden, gain, owners, hard_negatives)


def score_kernel(
    blocks,
    pairs,
    window,
    *refs,
):
    emb_ref, q_ref, d_ref, mine_ref, other_ref, top_ref, own_ref, place_ref = refs[:-7]
    wide, picked, picked_too, facts, own, named, sems = refs[-7:]
    seqs = emb_ref.shape[1] - 16
    sent = emb_ref[:, seqs:, :].astype(jnp.float32)
    own_ref[...] = (2.0 * sent[:, 0, :] + 512.0 * sent[:, 1, :]).astype(jnp.int32)
    facts[...] = sent[:, 2, :lanes].astype(jnp.int32)
    fetches = [
        pltpu.make_async_copy(own_ref, own, sems.at[0]),
        pltpu.make_async_copy(facts, named, sems.at[1]),
    ]
    for fetch in fetches:
        fetch.start()

    for part in range(blocks):
        spread(wide, part * seqs, emb_ref[part, :seqs, :].astype(jnp.float32))
    for fetch in fetches:
        fetch.wait()

    def place(block, count):
        place_ref[0, block] = block
        for offset in range(window):
            present = named[block, offset] > 0
            place_ref[offset + 1, block] = jnp.where(present, count, -1)
            count = count + present.astype(jnp.int32)
        return count

    used = lax.fori_loop(0, blocks, place, blocks)
    fine = pairs // blocks

    def clear(spot, carry):
        empty = jnp.zeros((blocks // 2, fine, pairs), jnp.float32)
        at = pl.ds(pl.multiple_of(spot * fine, fine), fine)
        mine_ref[:, at, :] = empty
        other_ref[:, at, :] = empty
        return carry

    lax.fori_loop(used, mine_ref.shape[1] // fine, clear, 0)
    group = 32

    def pick_block(block, rows_at):
        for base in range(0, 2 * pairs, group):
            rows = [wide[row_pair(own[block, base + k]), :] for k in range(group)]
            for k in range(group):
                rows_at[2 * (base + k) : 2 * (base + k + 1), :] = rows[k]
        at = pl.multiple_of(block * pairs, pairs)
        q_ref[pl.ds(at, pairs), :] = gathered(rows_at, 0, pairs).astype(jnp.bfloat16)
        d_ref[pl.ds(at, pairs), :] = gathered(rows_at, pairs, pairs).astype(jnp.bfloat16)

    ahead = -(-(window + 2) // 2)

    def pick_one(block, carry):
        pick_block(block, picked)
        return carry

    lax.fori_loop(0, 2 * ahead, pick_one, 0)
    even = lax.axis_index("pb") % 2 == 0
    spare = mine_ref.shape[1] // fine - 1

    def score_blocks(step, carry):
        at = pl.multiple_of(step * 2 * pairs, 2 * pairs)
        tiles = inverse_temp * lax.dot_general(
            q_ref[pl.ds(at, 2 * pairs), :],
            d_ref[pl.ds(at, (window + 2) * pairs), :],
            (((1,), (1,)), ((), ())),
            preferred_element_type=jnp.float32,
        )
        top = carry
        for half in range(2):
            for column in range(window + 1):
                spot = place_ref[column, 2 * step + half]
                row = pl.multiple_of(jnp.where(spot >= 0, spot, spare) * fine, fine)
                tile = tiles[
                    half * pairs : (half + 1) * pairs,
                    (half + column) * pairs : (half + column + 1) * pairs,
                ]
                parted = tile.reshape(blocks // 2, 2, fine, pairs)
                first, second = parted[:, 0], parted[:, 1]
                mine_ref[:, pl.ds(row, fine), :] = jnp.where(even, first, second)
                other_ref[:, pl.ds(row, fine), :] = jnp.where(even, second, first)
                size = jnp.maximum(jnp.abs(first), jnp.abs(second))
                top = jnp.maximum(top, jnp.max(size, axis=0))
        return top

    def score_and_pick(step, top):
        top = score_blocks(step - ahead, top)
        pick_block(2 * step, picked)
        pick_block(2 * step + 1, picked_too)
        return top

    top = jnp.zeros((fine, pairs), jnp.float32)
    top = lax.fori_loop(ahead, blocks // 2, score_and_pick, top)
    d_ref[blocks * pairs :, :] = d_ref[: window * pairs, :]
    top_ref[...] = lax.fori_loop(blocks // 2 - ahead, blocks // 2, score_blocks, top)


def score_call(embedded, room, blocks, pairs, window):
    _, rows, piece = embedded.shape
    fine = pairs // blocks
    whole = pl.BlockSpec(memory_space=pltpu.VMEM)
    scalars = pl.BlockSpec(memory_space=pltpu.SMEM)
    return pl.pallas_call(
        functools.partial(score_kernel, blocks, pairs, window),
        in_specs=[whole],
        out_specs=[whole, whole, whole, whole, whole, whole, scalars],
        out_shape=[
            jax.ShapeDtypeStruct((blocks * pairs, piece), jnp.bfloat16),
            jax.ShapeDtypeStruct(((blocks + window) * pairs, piece), jnp.bfloat16),
            jax.ShapeDtypeStruct((blocks // 2, (room + 1) * fine, pairs), jnp.float32),
            jax.ShapeDtypeStruct((blocks // 2, (room + 1) * fine, pairs), jnp.float32),
            jax.ShapeDtypeStruct((fine, pairs), jnp.float32),
            jax.ShapeDtypeStruct((blocks, 2 * pairs), jnp.int32),
            jax.ShapeDtypeStruct((window + 1, blocks), jnp.int32),
        ],
        scratch_shapes=[
            pltpu.VMEM((2 * blocks * (rows - 16), lanes), jnp.float32),
            pltpu.VMEM((4 * pairs, lanes), jnp.float32),
            pltpu.VMEM((4 * pairs, lanes), jnp.float32),
            pltpu.VMEM((blocks, lanes), jnp.int32),
            pltpu.SMEM((blocks, 2 * pairs), jnp.int32),
            pltpu.SMEM((blocks, lanes), jnp.int32),
            pltpu.SemaphoreType.DMA((2,)),
        ],
        compiler_params=pltpu.CompilerParams(vmem_limit_bytes=22 * mebibyte),
        name="partial_scores",
    )(embedded)


def merge_kernel(mine_ref, other_ref, top_ref, other_top_ref, own_ref, *code_refs):
    rows, pairs = own_ref.shape
    steps = code_refs[0].shape[0] - 1
    fine = rows // steps // 2
    chip = lax.axis_index("pb") // 2

    def highest(ref):
        return jnp.max(jnp.max(ref[...], axis=1, keepdims=True), axis=0, keepdims=True)

    top = highest(top_ref) + highest(other_top_ref)
    bound = jnp.ceil(top * bound_steps) + 1.0
    scale = code_steps * bound_steps / bound
    own_ref[...] = mine_ref[chip, :rows] + other_ref[chip, :rows]
    for hop, code_ref in enumerate(code_refs):
        target = chip ^ (hop + 1)

        def encode(step, carry):
            at = pl.multiple_of(step * 2 * fine, 2 * fine)
            there = pl.ds(at, 2 * fine)
            codes = jnp.round((mine_ref[target, there, :] + other_ref[target, there, :]) * scale)
            code_ref[step] = codes.astype(jnp.int32).astype(jnp.int16)
            return carry

        lax.fori_loop(0, steps, encode, 0)
        code_ref[steps] = jnp.broadcast_to(bound, (2 * fine, pairs)).astype(jnp.int32).astype(jnp.int16)


def merge_call(mine, other, top, other_top, blocks):
    chips, rows, pairs = mine.shape
    fine = pairs // blocks
    rows = rows - fine
    whole = pl.BlockSpec(memory_space=pltpu.VMEM)
    coded = jax.ShapeDtypeStruct((rows // (2 * fine) + 1, 2 * fine, pairs), jnp.int16)
    return pl.pallas_call(
        merge_kernel,
        in_specs=[whole] * 4,
        out_specs=[whole] * chips,
        out_shape=[jax.ShapeDtypeStruct((rows, pairs), jnp.float32)] + [coded] * (chips - 1),
        compiler_params=pltpu.CompilerParams(vmem_limit_bytes=12 * mebibyte),
        name="merge_scores",
    )(mine, other, top, other_top)


def softmax_kernel(blocks, window, place_ref, own_ref, *refs):
    code_refs, (c_ref, packed, masked) = refs[:-3], refs[-3:]
    room, fine, pairs = packed.shape
    count = blocks * fine
    unit = 1.0 / (code_steps * bound_steps)
    scales = [ref[room // 2].astype(jnp.int32).astype(jnp.float32) * unit for ref in code_refs]

    def decode(step, carry):
        both = own_ref[pl.ds(pl.multiple_of(step * 2 * fine, 2 * fine), 2 * fine), :]
        for ref, scale in zip(code_refs, scales):
            both = both + ref[step].astype(jnp.int32).astype(jnp.float32) * scale
        packed[2 * step] = both[:fine]
        packed[2 * step + 1] = both[fine:]
        return carry

    lax.fori_loop(0, room // 2, decode, 0)
    for block in range(blocks):
        for column in range(window + 1):
            spot = place_ref[column, block]
            tile = packed[jnp.maximum(spot, 0)]
            masked[block * fine : (block + 1) * fine, column * pairs : (column + 1) * pairs] = (
                jnp.where(spot >= 0, tile, -jnp.inf)
            )
    row = lax.broadcasted_iota(jnp.int32, (count, pairs), 0)
    lane = lax.broadcasted_iota(jnp.int32, (count, pairs), 1)
    target = lane == lax.axis_index("pb") * fine + row % fine
    pieces = [masked[:, column * pairs : (column + 1) * pairs] for column in range(window + 1)]
    row_max = jnp.max(functools.reduce(jnp.maximum, pieces), axis=1, keepdims=True)
    total = functools.reduce(jnp.add, [jnp.exp(piece - row_max) for piece in pieces])
    log_total = row_max + jnp.log(jnp.sum(total, axis=1, keepdims=True))
    positive = jnp.sum(jnp.where(target, pieces[0], 0.0), axis=1, keepdims=True)
    for column, piece in enumerate(pieces):
        share = jnp.exp(piece - log_total)
        if column == 0:
            share = share - jnp.where(target, 1.0, 0.0)
        masked[:, column * pairs : (column + 1) * pairs] = inverse_temp * share
    for block in range(blocks):
        for column in range(window + 1):
            spot = place_ref[column, block]

            @pl.when(spot >= 0)
            def _():
                packed[spot] = masked[
                    block * fine : (block + 1) * fine, column * pairs : (column + 1) * pairs
                ]

    for step in range(room // 2):
        both = jnp.concatenate([packed[2 * step], packed[2 * step + 1]], axis=0)
        c_ref[step] = both.astype(jnp.bfloat16)
    losses = jnp.sum(
        jnp.where(lane == row // fine, log_total - positive, 0.0), axis=0, keepdims=True
    )
    coarse = losses.astype(jnp.bfloat16).astype(jnp.float32)
    rank = lax.broadcasted_iota(jnp.int32, (2 * fine, pairs), 0)
    both = jnp.where(rank == 0, coarse, jnp.where(rank == 1, losses - coarse, 0.0))
    c_ref[room // 2] = both.astype(jnp.bfloat16)


def softmax_call(place, own_scores, codes, blocks, window):
    steps, fine, pairs = codes[0].shape
    room, fine = 2 * (steps - 1), fine // 2
    whole = pl.BlockSpec(memory_space=pltpu.VMEM)
    return pl.pallas_call(
        functools.partial(softmax_kernel, blocks, window),
        in_specs=[pl.BlockSpec(memory_space=pltpu.SMEM), whole] + [whole] * len(codes),
        out_specs=whole,
        out_shape=jax.ShapeDtypeStruct((room // 2 + 1, 2 * fine, pairs), jnp.bfloat16),
        scratch_shapes=[
            pltpu.VMEM((room, fine, pairs), jnp.float32),
            pltpu.VMEM((blocks * fine, (window + 1) * pairs), jnp.float32),
        ],
        compiler_params=pltpu.CompilerParams(vmem_limit_bytes=8 * mebibyte),
        name="softmax_rows",
    )(place, own_scores, *codes)


def grad_kernel(
    blocks,
    pairs,
    window,
    own_ref,
    place_ref,
    q_ref,
    d_ref,
    *refs,
):
    part_refs = refs[:-7]
    out_ref, loss_ref, wide, dsum, picked, packed, square = refs[-7:]
    fine = pairs // blocks
    room = packed.shape[1]
    me = lax.axis_index("pb")
    masks = swap_masks(blocks)
    group = 32
    losses = 0.0
    for part in part_refs:
        sent = part[:, room // 2].astype(jnp.float32)
        losses = losses + jnp.sum(sent[:, 0, :] + sent[:, 1, :], axis=0, keepdims=True) / pairs
    lane = lax.broadcasted_iota(jnp.int32, losses.shape, 1)
    mine = jnp.where(lane == me, losses, 0.0)
    loss_ref[...] = jnp.broadcast_to(jnp.sum(mine, axis=1, keepdims=True), loss_ref.shape)
    dsum[...] = jnp.zeros_like(dsum)
    square[...] = jnp.zeros_like(square)

    def unpack(step, carry):
        for part, mask in zip(part_refs, masks):
            both = part[:, step].astype(jnp.float32)
            for at, apart in enumerate(mask):
                packed[me ^ apart, 2 * step] = both[at, :fine]
                packed[me ^ apart, 2 * step + 1] = both[at, fine:]
        return carry

    lax.fori_loop(0, room // 2, unpack, 0)

    def scatter_rows(block, offset, start):
        for base in range(0, pairs, group):
            rows = [
                picked[2 * (start + base + k) : 2 * (start + base + k + 1), :] for k in range(group)
            ]
            for k in range(group):
                wide[row_pair(own_ref[block, offset + base + k]), :] = rows[k]

    def two_blocks(step, carry):
        for half in range(2):
            for column in range(window + 1):
                spot = place_ref[column, 2 * step + half]
                tile = packed[:, jnp.maximum(spot, 0)].reshape(pairs, pairs)
                square[
                    half * pairs : (half + 1) * pairs,
                    (half + column) * pairs : (half + column + 1) * pairs,
                ] = jnp.where(spot >= 0, tile, 0.0).astype(jnp.bfloat16)
        at = pl.multiple_of(step * 2 * pairs, 2 * pairs)
        there = pl.ds(at, (window + 2) * pairs)
        coefficients = square[...]
        summed = jnp.dot(coefficients, d_ref[there, :], preferred_element_type=jnp.float32)
        spread(picked, 0, summed)
        dsum[there, :] += lax.dot_general(
            coefficients,
            q_ref[pl.ds(at, 2 * pairs), :],
            (((0,), (0,)), ((), ())),
            preferred_element_type=jnp.float32,
        )
        for half in range(2):
            scatter_rows(2 * step + half, 0, half * pairs)
        return carry

    lax.fori_loop(0, blocks // 2, two_blocks, 0)
    dsum[: window * pairs, :] += dsum[blocks * pairs :, :]

    def doc_block(block, carry):
        at = pl.multiple_of(block * pairs, pairs)
        spread(picked, 0, dsum[pl.ds(at, pairs), :])
        scatter_rows(block, pairs, 0)
        return carry

    lax.fori_loop(0, blocks, doc_block, 0)
    slots = out_ref.shape[1]
    for part in range(blocks):
        out_ref[part] = gathered(wide, part * slots, slots).astype(jnp.bfloat16)


def grad_call(own, place, parts, queries, documents, blocks, pairs, window):
    count, piece = queries.shape
    seqs = 2 * count
    room = 2 * (parts[0].shape[1] - 1)
    whole = pl.BlockSpec(memory_space=pltpu.VMEM)
    scalars = pl.BlockSpec(memory_space=pltpu.SMEM)
    return pl.pallas_call(
        functools.partial(grad_kernel, blocks, pairs, window),
        in_specs=[scalars, scalars, whole, whole] + [whole] * len(parts),
        out_specs=[whole, whole],
        out_shape=[
            jax.ShapeDtypeStruct((blocks, seqs // blocks, piece), jnp.bfloat16),
            jax.ShapeDtypeStruct((1, lanes), jnp.float32),
        ],
        scratch_shapes=[
            pltpu.VMEM((2 * seqs, lanes), jnp.float32),
            pltpu.VMEM(((blocks + window) * pairs, piece), jnp.float32),
            pltpu.VMEM((4 * pairs, lanes), jnp.float32),
            pltpu.VMEM((blocks, room, pairs // blocks, pairs), jnp.float32),
            pltpu.VMEM((2 * pairs, (window + 2) * pairs), jnp.bfloat16),
        ],
        compiler_params=pltpu.CompilerParams(vmem_limit_bytes=26 * mebibyte),
        name="slice_grads",
    )(own, place, queries, documents, *parts)


def project_kernel(grad_ref, normed_ref, inv_ref, out_ref):
    parts, _, piece = grad_ref.shape
    cuts = [slice(part * piece, (part + 1) * piece) for part in range(parts)]
    inverse = inv_ref[:, :1]
    total = 0.0
    for part, cut in enumerate(cuts):
        unit = normed_ref[:, cut].astype(jnp.float32) * inverse
        total = total + unit * grad_ref[part].astype(jnp.float32)
    along = jnp.sum(total, axis=-1, keepdims=True)
    for part, cut in enumerate(cuts):
        unit = normed_ref[:, cut].astype(jnp.float32) * inverse
        out_ref[:, cut] = grad_ref[part].astype(jnp.float32) - unit * along


def project_call(returned, normed, inverse):
    parts, seqs, piece = returned.shape
    width = normed.shape[1]
    rows = 64
    return pl.pallas_call(
        project_kernel,
        grid=(seqs // rows,),
        in_specs=[
            pl.BlockSpec((parts, rows, piece), lambda i: (0, i, 0)),
            pl.BlockSpec((rows, width), lambda i: (i, 0)),
            pl.BlockSpec((rows, lanes), lambda i: (i, 0)),
        ],
        out_specs=pl.BlockSpec((rows, width), lambda i: (i, 0)),
        out_shape=jax.ShapeDtypeStruct((seqs, width), jnp.float32),
        compiler_params=pltpu.CompilerParams(vmem_limit_bytes=10 * mebibyte),
        name="project_out",
    )(returned, normed, inverse)


def swapped(value, apart):
    pairs = [(at, at ^ apart) for at in range(lax.axis_size("pb"))]
    return lax.ppermute(value, "pb", pairs)


def swap_bits(devices):
    bits = [1 << bit for bit in reversed(range(devices.bit_length() - 1))]
    return bits[:-2], bits[-2], bits[-1]


def swap_masks(devices):
    far, side, last = swap_bits(devices)
    held = [0]
    for apart in far:
        held = held + [mask ^ apart for mask in held]
    held = held + [mask ^ side for mask in held]
    return [held, [mask ^ last for mask in held]]


def gather_all(value):
    far, side, last = swap_bits(lax.axis_size("pb"))
    held = value[None]
    beside, latest = [], held
    for apart in far:
        arrived = swapped(held, apart)
        beside.append(swapped(latest, side))
        held = jnp.concatenate([held, arrived], axis=0)
        latest = arrived
    beside.append(swapped(latest, side))
    held = jnp.concatenate([held] + beside, axis=0)
    return [held, swapped(held, last)]


def middle(embedded, room, devices, pairs, window):
    queries, documents, mine, other, top, own, place = score_call(
        embedded, room, devices, pairs, window
    )
    own_scores, *codes = merge_call(mine, swapped(other, 1), top, swapped(top, 1), devices)
    codes = [swapped(codes[hop], 2 * (hop + 1)) for hop in reversed(range(len(codes)))]
    parts = gather_all(softmax_call(place, own_scores, codes, devices, window))
    grads, loss = grad_call(own, place, parts, queries, documents, devices, pairs, window)
    return grads, loss[0, :1]


def feature_plan(hidden, final_gain, last_row, pair_owner, hard_negatives):
    devices = lax.axis_size("pb")
    seqs, width = hidden.shape
    pairs = pair_owner.shape[0]
    window = hard_negatives.shape[1]
    normed, inverse, embedding = norm_call(
        last_row, hidden, final_gain, pair_owner.T, hard_negatives, devices
    )
    embedded = lax.all_to_all(embedding, "pb", split_axis=0, concat_axis=0, tiled=True)
    most = devices * (window + 1)
    rooms = [most * part // 20 for part in (11, 12, 13, 15, 20)]
    used = devices + jnp.sum(embedded[:, seqs + 2, :window].astype(jnp.float32))
    level = sum((used > room).astype(jnp.int32) for room in rooms[:-1])
    grads, loss = lax.switch(
        level,
        [
            functools.partial(middle, room=room, devices=devices, pairs=pairs, window=window)
            for room in rooms
        ],
        embedded,
    )
    returned = lax.all_to_all(grads, "pb", split_axis=0, concat_axis=0, tiled=True)
    return project_call(returned, normed, inverse), loss


def from_behind(value, axis, steps):
    count = lax.axis_size(axis)
    pairs = [(source, (source + steps) % count) for source in range(count)]
    return lax.ppermute(value, axis, pairs)


def similarity(queries, documents):
    return inverse_temp * lax.dot_general(
        queries, documents, (((1,), (1,)), ((), ())), preferred_element_type=jnp.float32
    )


def transposed(weights, queries):
    return lax.dot_general(
        weights, queries, (((0,), (0,)), ((), ())), preferred_element_type=jnp.float32
    )


def combine_docs(weights, documents):
    return jnp.dot(weights, documents, preferred_element_type=jnp.float32)


def skipped(listed, function, operands, out_shape):
    return lax.cond(
        listed,
        lambda inputs: function(*inputs),
        lambda inputs: jnp.zeros(out_shape, jnp.float32),
        operands,
    )


def row_plan(hidden, final_gain, last_row, pair_owner, hard_negatives):
    values = hidden.astype(jnp.float32)
    scale_row = lax.rsqrt(jnp.mean(values * values, axis=-1, keepdims=True) + token_eps)
    normed = (values * scale_row * final_gain.astype(jnp.float32)).astype(jnp.bfloat16)
    seq_count = last_row.shape[1]
    model_width = hidden.shape[1]
    pooled = normed[last_row[0]].astype(jnp.float32)
    inverse_norm = lax.rsqrt(jnp.sum(pooled * pooled, axis=-1, keepdims=True) + 1e-06)
    unit_vec = pooled * inverse_norm
    embedding = unit_vec.astype(jnp.bfloat16)
    devices = lax.axis_size("pb")
    capacity = 2 * seq_count // devices
    pair_count = pair_owner.shape[0]
    wanted = jnp.concatenate([pair_owner[:, 0], pair_owner[:, 1]])
    holder = wanted // seq_count
    within = wanted % seq_count
    entry_ids = jnp.arange(2 * pair_count, dtype=jnp.int32)
    earlier = (holder[None, :] == holder[:, None]) & (entry_ids[None, :] < entry_ids[:, None])
    position = jnp.sum(earlier.astype(jnp.int32), axis=1)
    request = jnp.full((devices, capacity), -1, jnp.int32).at[holder, position].set(within)
    served = lax.all_to_all(request, "pb", split_axis=0, concat_axis=0, tiled=True)
    outgoing = jnp.where(
        served[:, :, None] >= 0, embedding[jnp.maximum(served, 0)], jnp.zeros((), jnp.bfloat16)
    )
    received = lax.all_to_all(outgoing, "pb", split_axis=0, concat_axis=0, tiled=True)
    gathered = received[holder, position]
    queries = gathered[:pair_count]
    own_docs = gathered[pair_count:]
    listed_ids = hard_negatives[0]
    window = hard_negatives.shape[1]
    listed = [listed_ids[offset] >= 0 for offset in range(window)]
    neighbours = []
    moving = own_docs
    for offset in range(window):
        moving = from_behind(moving, "pb", -1)
        neighbours.append(moving)
    tile_shape = (pair_count, pair_count)
    score_blocks = [similarity(queries, own_docs)]
    for offset in range(window):
        score_blocks.append(
            skipped(listed[offset], similarity, (queries, neighbours[offset]), tile_shape)
        )
    all_scores = jnp.concatenate(score_blocks, axis=1)
    usable = jnp.concatenate(
        [jnp.ones((pair_count,), jnp.bool_)]
        + [jnp.broadcast_to(listed[offset], (pair_count,)) for offset in range(window)]
    )
    masked = jnp.where(usable[None, :], all_scores, -jnp.inf)
    row_max = jnp.max(masked, axis=1, keepdims=True)
    log_total = row_max + jnp.log(jnp.sum(jnp.exp(masked - row_max), axis=1, keepdims=True))
    diagonal = jnp.arange(pair_count, dtype=jnp.int32)
    positive = all_scores[diagonal, diagonal]
    block_loss = jnp.mean(log_total[:, 0] - positive).reshape(1)
    columns = jnp.arange((window + 1) * pair_count, dtype=jnp.int32)
    target = (columns[None, :] == diagonal[:, None]).astype(jnp.float32)
    coefficients = (inverse_temp * (jnp.exp(masked - log_total) - target)).astype(jnp.bfloat16)
    pieces = [
        coefficients[:, offset * pair_count : (offset + 1) * pair_count]
        for offset in range(window + 1)
    ]
    grad_shape = (pair_count, model_width)
    query_sum = combine_docs(pieces[0], own_docs)
    for offset in range(window):
        query_sum = query_sum + skipped(
            listed[offset], combine_docs, (pieces[offset + 1], neighbours[offset]), grad_shape
        )
    query_grad = query_sum.astype(jnp.bfloat16)
    own_part = transposed(pieces[0], queries).astype(jnp.bfloat16)
    partial_value = [
        skipped(listed[offset], transposed, (pieces[offset + 1], queries), grad_shape).astype(
            jnp.bfloat16
        )
        for offset in range(window)
    ]
    running = partial_value[window - 1].astype(jnp.float32)
    for offset in range(window):
        running = from_behind(running, "pb", 1)
        if offset + 1 < window:
            running = running + partial_value[window - 2 - offset].astype(jnp.float32)
    doc_grad = (own_part.astype(jnp.float32) + running).astype(jnp.bfloat16)
    answers = jnp.concatenate([query_grad, doc_grad], axis=0)
    returning = (
        jnp.zeros((devices, capacity, model_width), jnp.bfloat16).at[holder, position].set(answers)
    )
    returned = lax.all_to_all(returning, "pb", split_axis=0, concat_axis=0, tiled=True)
    slot_ids = jnp.where(served >= 0, served, seq_count).reshape(-1)
    emb_grad = (
        jnp.zeros((seq_count, model_width), jnp.bfloat16)
        .at[slot_ids]
        .set(returned.reshape(-1, model_width), mode="drop")
    )
    gradient = emb_grad.astype(jnp.float32)
    pooled_grad = gradient - unit_vec * jnp.sum(unit_vec * gradient, axis=-1, keepdims=True)
    return (pooled_grad, block_loss)


def solution(mesh):
    def local(hidden, final_gain, last_row, pair_owner, hard_negatives):
        plan = feature_plan if hidden.shape[1] >= lanes * mesh.shape["pb"] else row_plan
        return plan(hidden, final_gain, last_row, pair_owner, hard_negatives)

    return jax.shard_map(
        local,
        mesh=mesh,
        in_specs=(
            P(("groups", "pb"), None),
            P(),
            P(("groups", "pb"), None),
            P(("groups", "pb"), None),
            P(("groups", "pb"), None),
        ),
        out_specs=(P(("groups", "pb"), None), P(("groups", "pb"))),
        check_vma=False,
    )
```

```python
import functools

import jax
import jax.numpy as jnp
from jax import lax
from jax.experimental import pallas as pl
from jax.experimental.pallas import tpu as pltpu
from jax.sharding import PartitionSpec as P

inverse_temp = 50.0
token_eps = 1e-05
unit_eps = 1e-06
lanes = 128
bound_steps = 256.0
code_steps = 32000.0
mebibyte = 1024 * 1024


def peer_order(devices):
    return [device for pair in zip(range(devices // 2), range(devices // 2, devices)) for device in pair]


def exchange(blocks):
    order = peer_order(blocks.shape[0])
    return lax.all_to_all(
        blocks, "pb", split_axis=0, concat_axis=0, axis_index_groups=[order], tiled=True
    )


def spread(target, at, value):
    count = value.shape[0]
    for half in range(2):
        target[pl.ds(2 * at + half, count, stride=2), :] = value[:, half * lanes : (half + 1) * lanes]


def gathered(source, at, count):
    halves = [source[pl.ds(2 * at + half, count, stride=2), :] for half in range(2)]
    return jnp.concatenate(halves, axis=1)


def row_pair(place):
    return pl.ds(pl.multiple_of(place, 2), 2)


def norm_kernel(
    last_ref, hidden_ref, gain_ref, owner_ref, negative_ref, normed_ref, inv_ref, emb_ref
):
    seqs, width = normed_ref.shape
    parts, _, piece = emb_ref.shape
    pairs = owner_ref.shape[1]
    cuts = [slice(part * piece, (part + 1) * piece) for part in range(parts)]
    sources = lax.broadcasted_iota(jnp.int32, (seqs, seqs), 0)
    pick = jnp.where(sources == last_ref[...], 1.0, 0.0).astype(jnp.bfloat16)

    def folded(squares):
        return functools.reduce(
            jnp.add, [squares[:, at : at + lanes] for at in range(0, piece, lanes)]
        )

    total = jnp.zeros((seqs, lanes), jnp.float32)
    for cut in cuts:
        values = lax.dot_general(
            pick, hidden_ref[:, cut], (((0,), (0,)), ((), ())), preferred_element_type=jnp.float32
        )
        normed_ref[:, cut] = values.astype(jnp.bfloat16)
        total = total + folded(values * values)
    scale = lax.rsqrt(jnp.sum(total, axis=-1, keepdims=True) / width + token_eps)
    total = jnp.zeros((seqs, lanes), jnp.float32)
    for cut in cuts:
        values = normed_ref[:, cut].astype(jnp.float32)
        gain = gain_ref[cut].astype(jnp.float32).reshape(1, piece)
        normed = (values * scale * gain).astype(jnp.bfloat16)
        normed_ref[:, cut] = normed
        pooled = normed.astype(jnp.float32)
        total = total + folded(pooled * pooled)
    inverse = lax.rsqrt(jnp.sum(total, axis=-1, keepdims=True) + unit_eps)
    inv_ref[...] = jnp.broadcast_to(inverse, inv_ref.shape)

    owners = owner_ref[...].astype(jnp.float32)
    high = jnp.floor(owners * (1.0 / 256.0))
    low = owners - 256.0 * high
    row = lax.broadcasted_iota(jnp.int32, (16, pairs), 0)
    spot = lax.broadcasted_iota(jnp.int32, (16, pairs), 1)
    left = jnp.where(row == 0, low[:1], jnp.where(row == 1, high[:1], 0.0))
    right = jnp.where(row == 0, low[1:2], jnp.where(row == 1, high[1:2], 0.0))
    for offset in range(negative_ref.shape[1]):
        named = (negative_ref[0, offset] >= 0).astype(jnp.float32)
        left = jnp.where((row == 2) & (spot == offset), named, left)
    facts = jnp.concatenate([left, right], axis=1).astype(jnp.bfloat16)

    for slot, part in enumerate(peer_order(parts)):
        values = normed_ref[:, cuts[part]].astype(jnp.float32)
        emb_ref[slot, :seqs] = (values * inverse).astype(jnp.bfloat16)
        emb_ref[slot, seqs:] = facts


def norm_call(last_row, hidden, gain, owners, hard_negatives, parts):
    seqs, width = hidden.shape
    piece = width // parts
    whole = pl.BlockSpec(memory_space=pltpu.VMEM)
    return pl.pallas_call(
        norm_kernel,
        in_specs=[whole, whole, whole, whole, pl.BlockSpec(memory_space=pltpu.SMEM)],
        out_specs=[whole] * 3,
        out_shape=[
            jax.ShapeDtypeStruct((seqs, width), jnp.bfloat16),
            jax.ShapeDtypeStruct((seqs, lanes), jnp.float32),
            jax.ShapeDtypeStruct((parts, seqs + 16, piece), jnp.bfloat16),
        ],
        compiler_params=pltpu.CompilerParams(vmem_limit_bytes=56 * mebibyte),
        name="norm_rows",
    )(last_row, hidden, gain, owners, hard_negatives)


def score_kernel(
    blocks,
    pairs,
    window,
    *refs,
):
    emb_ref, q_ref, d_ref, mine_ref, other_ref, top_ref, own_ref, place_ref = refs[:-7]
    wide, picked, picked_too, facts, own, named, sems = refs[-7:]
    seqs = emb_ref.shape[1] - 16
    sent = emb_ref[:, seqs:, :].astype(jnp.float32)
    places = (2.0 * sent[:, 0, :] + 512.0 * sent[:, 1, :]).astype(jnp.int32)
    flags = sent[:, 2, :lanes].astype(jnp.int32)
    order = peer_order(blocks)
    for slot, block in enumerate(order):
        own_ref[block : block + 1, :] = places[slot : slot + 1]
        facts[block : block + 1, :] = flags[slot : slot + 1]
    fetches = [
        pltpu.make_async_copy(own_ref, own, sems.at[0]),
        pltpu.make_async_copy(facts, named, sems.at[1]),
    ]
    for fetch in fetches:
        fetch.start()

    for slot, part in enumerate(order):
        spread(wide, part * seqs, emb_ref[slot, :seqs, :].astype(jnp.float32))
    for fetch in fetches:
        fetch.wait()

    def place(block, count):
        place_ref[0, block] = block
        for offset in range(window):
            present = named[block, offset] > 0
            place_ref[offset + 1, block] = jnp.where(present, count, -1)
            count = count + present.astype(jnp.int32)
        return count

    used = lax.fori_loop(0, blocks, place, blocks)
    fine = pairs // blocks

    def clear(spot, carry):
        empty = jnp.zeros((blocks // 2, fine, pairs), jnp.float32)
        at = pl.ds(pl.multiple_of(spot * fine, fine), fine)
        mine_ref[:, at, :] = empty
        other_ref[:, at, :] = empty
        return carry

    lax.fori_loop(used, mine_ref.shape[1] // fine, clear, 0)
    group = 32

    def pick_block(block, rows_at):
        for base in range(0, 2 * pairs, group):
            rows = [wide[row_pair(own[block, base + k]), :] for k in range(group)]
            for k in range(group):
                rows_at[2 * (base + k) : 2 * (base + k + 1), :] = rows[k]
        at = pl.multiple_of(block * pairs, pairs)
        q_ref[pl.ds(at, pairs), :] = gathered(rows_at, 0, pairs).astype(jnp.bfloat16)
        d_ref[pl.ds(at, pairs), :] = gathered(rows_at, pairs, pairs).astype(jnp.bfloat16)

    ahead = -(-(window + 2) // 2)

    def pick_one(block, carry):
        pick_block(block, picked)
        return carry

    lax.fori_loop(0, 2 * ahead, pick_one, 0)
    even = lax.axis_index("pb") % 2 == 0
    spare = mine_ref.shape[1] // fine - 1

    def score_blocks(step, carry):
        at = pl.multiple_of(step * 2 * pairs, 2 * pairs)
        tiles = inverse_temp * lax.dot_general(
            q_ref[pl.ds(at, 2 * pairs), :],
            d_ref[pl.ds(at, (window + 2) * pairs), :],
            (((1,), (1,)), ((), ())),
            preferred_element_type=jnp.float32,
        )
        top = carry
        for half in range(2):
            for column in range(window + 1):
                spot = place_ref[column, 2 * step + half]
                row = pl.multiple_of(jnp.where(spot >= 0, spot, spare) * fine, fine)
                tile = tiles[
                    half * pairs : (half + 1) * pairs,
                    (half + column) * pairs : (half + column + 1) * pairs,
                ]
                parted = tile.reshape(blocks // 2, 2, fine, pairs)
                first, second = parted[:, 0], parted[:, 1]
                mine_ref[:, pl.ds(row, fine), :] = jnp.where(even, first, second)
                other_ref[:, pl.ds(row, fine), :] = jnp.where(even, second, first)
                size = jnp.maximum(jnp.abs(first), jnp.abs(second))
                top = jnp.maximum(top, jnp.max(size, axis=0))
        return top

    def score_and_pick(step, top):
        top = score_blocks(step - ahead, top)
        pick_block(2 * step, picked)
        pick_block(2 * step + 1, picked_too)
        return top

    top = jnp.zeros((fine, pairs), jnp.float32)
    top = lax.fori_loop(ahead, blocks // 2, score_and_pick, top)
    d_ref[blocks * pairs :, :] = d_ref[: window * pairs, :]
    top_ref[...] = lax.fori_loop(blocks // 2 - ahead, blocks // 2, score_blocks, top)


def score_call(embedded, room, blocks, pairs, window):
    _, rows, piece = embedded.shape
    fine = pairs // blocks
    whole = pl.BlockSpec(memory_space=pltpu.VMEM)
    scalars = pl.BlockSpec(memory_space=pltpu.SMEM)
    return pl.pallas_call(
        functools.partial(score_kernel, blocks, pairs, window),
        in_specs=[whole],
        out_specs=[whole, whole, whole, whole, whole, whole, scalars],
        out_shape=[
            jax.ShapeDtypeStruct((blocks * pairs, piece), jnp.bfloat16),
            jax.ShapeDtypeStruct(((blocks + window) * pairs, piece), jnp.bfloat16),
            jax.ShapeDtypeStruct((blocks // 2, (room + 1) * fine, pairs), jnp.float32),
            jax.ShapeDtypeStruct((blocks // 2, (room + 1) * fine, pairs), jnp.float32),
            jax.ShapeDtypeStruct((fine, pairs), jnp.float32),
            jax.ShapeDtypeStruct((blocks, 2 * pairs), jnp.int32),
            jax.ShapeDtypeStruct((window + 1, blocks), jnp.int32),
        ],
        scratch_shapes=[
            pltpu.VMEM((2 * blocks * (rows - 16), lanes), jnp.float32),
            pltpu.VMEM((4 * pairs, lanes), jnp.float32),
            pltpu.VMEM((4 * pairs, lanes), jnp.float32),
            pltpu.VMEM((blocks, lanes), jnp.int32),
            pltpu.SMEM((blocks, 2 * pairs), jnp.int32),
            pltpu.SMEM((blocks, lanes), jnp.int32),
            pltpu.SemaphoreType.DMA((2,)),
        ],
        compiler_params=pltpu.CompilerParams(vmem_limit_bytes=22 * mebibyte),
        name="partial_scores",
    )(embedded)


def merge_kernel(mine_ref, other_ref, top_ref, other_top_ref, own_ref, *code_refs):
    rows, pairs = own_ref.shape
    steps = code_refs[0].shape[0] - 1
    fine = rows // steps // 2
    chip = lax.axis_index("pb") // 2

    def highest(ref):
        return jnp.max(jnp.max(ref[...], axis=1, keepdims=True), axis=0, keepdims=True)

    top = highest(top_ref) + highest(other_top_ref)
    bound = jnp.ceil(top * bound_steps) + 1.0
    scale = code_steps * bound_steps / bound
    own_ref[...] = mine_ref[chip, :rows] + other_ref[chip, :rows]
    for hop, code_ref in enumerate(code_refs):
        target = chip ^ (hop + 1)

        def encode(step, carry):
            at = pl.multiple_of(step * 2 * fine, 2 * fine)
            there = pl.ds(at, 2 * fine)
            codes = jnp.round((mine_ref[target, there, :] + other_ref[target, there, :]) * scale)
            code_ref[step] = codes.astype(jnp.int32).astype(jnp.int16)
            return carry

        lax.fori_loop(0, steps, encode, 0)
        code_ref[steps] = jnp.broadcast_to(bound, (2 * fine, pairs)).astype(jnp.int32).astype(jnp.int16)


def merge_call(mine, other, top, other_top, blocks):
    chips, rows, pairs = mine.shape
    fine = pairs // blocks
    rows = rows - fine
    whole = pl.BlockSpec(memory_space=pltpu.VMEM)
    coded = jax.ShapeDtypeStruct((rows // (2 * fine) + 1, 2 * fine, pairs), jnp.int16)
    return pl.pallas_call(
        merge_kernel,
        in_specs=[whole] * 4,
        out_specs=[whole] * chips,
        out_shape=[jax.ShapeDtypeStruct((rows, pairs), jnp.float32)] + [coded] * (chips - 1),
        compiler_params=pltpu.CompilerParams(vmem_limit_bytes=12 * mebibyte),
        name="merge_scores",
    )(mine, other, top, other_top)


def softmax_kernel(blocks, window, place_ref, own_ref, *refs):
    code_refs, (c_ref, packed, masked) = refs[:-3], refs[-3:]
    room, fine, pairs = packed.shape
    count = blocks * fine
    unit = 1.0 / (code_steps * bound_steps)
    scales = [ref[room // 2].astype(jnp.int32).astype(jnp.float32) * unit for ref in code_refs]

    def decode(step, carry):
        both = own_ref[pl.ds(pl.multiple_of(step * 2 * fine, 2 * fine), 2 * fine), :]
        for ref, scale in zip(code_refs, scales):
            both = both + ref[step].astype(jnp.int32).astype(jnp.float32) * scale
        packed[2 * step] = both[:fine]
        packed[2 * step + 1] = both[fine:]
        return carry

    lax.fori_loop(0, room // 2, decode, 0)
    for block in range(blocks):
        for column in range(window + 1):
            spot = place_ref[column, block]
            tile = packed[jnp.maximum(spot, 0)]
            masked[block * fine : (block + 1) * fine, column * pairs : (column + 1) * pairs] = (
                jnp.where(spot >= 0, tile, -jnp.inf)
            )
    row = lax.broadcasted_iota(jnp.int32, (count, pairs), 0)
    lane = lax.broadcasted_iota(jnp.int32, (count, pairs), 1)
    target = lane == lax.axis_index("pb") * fine + row % fine
    pieces = [masked[:, column * pairs : (column + 1) * pairs] for column in range(window + 1)]
    row_max = jnp.max(functools.reduce(jnp.maximum, pieces), axis=1, keepdims=True)
    total = functools.reduce(jnp.add, [jnp.exp(piece - row_max) for piece in pieces])
    log_total = row_max + jnp.log(jnp.sum(total, axis=1, keepdims=True))
    positive = jnp.sum(jnp.where(target, pieces[0], 0.0), axis=1, keepdims=True)
    for column, piece in enumerate(pieces):
        share = jnp.exp(piece - log_total)
        if column == 0:
            share = share - jnp.where(target, 1.0, 0.0)
        masked[:, column * pairs : (column + 1) * pairs] = inverse_temp * share
    for block in range(blocks):
        for column in range(window + 1):
            spot = place_ref[column, block]

            @pl.when(spot >= 0)
            def _():
                packed[spot] = masked[
                    block * fine : (block + 1) * fine, column * pairs : (column + 1) * pairs
                ]

    for step in range(room // 2):
        both = jnp.concatenate([packed[2 * step], packed[2 * step + 1]], axis=0)
        c_ref[step] = both.astype(jnp.bfloat16)
    losses = jnp.sum(
        jnp.where(lane == row // fine, log_total - positive, 0.0), axis=0, keepdims=True
    )
    coarse = losses.astype(jnp.bfloat16).astype(jnp.float32)
    rank = lax.broadcasted_iota(jnp.int32, (2 * fine, pairs), 0)
    both = jnp.where(rank == 0, coarse, jnp.where(rank == 1, losses - coarse, 0.0))
    c_ref[room // 2] = both.astype(jnp.bfloat16)


def softmax_call(place, own_scores, codes, blocks, window):
    steps, fine, pairs = codes[0].shape
    room, fine = 2 * (steps - 1), fine // 2
    whole = pl.BlockSpec(memory_space=pltpu.VMEM)
    return pl.pallas_call(
        functools.partial(softmax_kernel, blocks, window),
        in_specs=[pl.BlockSpec(memory_space=pltpu.SMEM), whole] + [whole] * len(codes),
        out_specs=whole,
        out_shape=jax.ShapeDtypeStruct((room // 2 + 1, 2 * fine, pairs), jnp.bfloat16),
        scratch_shapes=[
            pltpu.VMEM((room, fine, pairs), jnp.float32),
            pltpu.VMEM((blocks * fine, (window + 1) * pairs), jnp.float32),
        ],
        compiler_params=pltpu.CompilerParams(vmem_limit_bytes=8 * mebibyte),
        name="softmax_rows",
    )(place, own_scores, *codes)


def grad_kernel(
    blocks,
    pairs,
    window,
    own_ref,
    place_ref,
    q_ref,
    d_ref,
    *refs,
):
    part_refs = refs[:-7]
    out_ref, loss_ref, wide, dsum, picked, packed, square = refs[-7:]
    fine = pairs // blocks
    room = packed.shape[1]
    me = lax.axis_index("pb")
    masks = swap_masks(blocks)
    group = 32
    losses = 0.0
    for part in part_refs:
        sent = part[:, room // 2].astype(jnp.float32)
        losses = losses + jnp.sum(sent[:, 0, :] + sent[:, 1, :], axis=0, keepdims=True) / pairs
    lane = lax.broadcasted_iota(jnp.int32, losses.shape, 1)
    mine = jnp.where(lane == me, losses, 0.0)
    loss_ref[...] = jnp.broadcast_to(jnp.sum(mine, axis=1, keepdims=True), loss_ref.shape)
    dsum[...] = jnp.zeros_like(dsum)
    square[...] = jnp.zeros_like(square)

    def unpack(step, carry):
        for part, mask in zip(part_refs, masks):
            both = part[:, step].astype(jnp.float32)
            for at, apart in enumerate(mask):
                packed[me ^ apart, 2 * step] = both[at, :fine]
                packed[me ^ apart, 2 * step + 1] = both[at, fine:]
        return carry

    lax.fori_loop(0, room // 2, unpack, 0)

    def scatter_rows(block, offset, start):
        for base in range(0, pairs, group):
            rows = [
                picked[2 * (start + base + k) : 2 * (start + base + k + 1), :] for k in range(group)
            ]
            for k in range(group):
                wide[row_pair(own_ref[block, offset + base + k]), :] = rows[k]

    def two_blocks(step, carry):
        for half in range(2):
            for column in range(window + 1):
                spot = place_ref[column, 2 * step + half]
                tile = packed[:, jnp.maximum(spot, 0)].reshape(pairs, pairs)
                square[
                    half * pairs : (half + 1) * pairs,
                    (half + column) * pairs : (half + column + 1) * pairs,
                ] = jnp.where(spot >= 0, tile, 0.0).astype(jnp.bfloat16)
        at = pl.multiple_of(step * 2 * pairs, 2 * pairs)
        there = pl.ds(at, (window + 2) * pairs)
        coefficients = square[...]
        summed = jnp.dot(coefficients, d_ref[there, :], preferred_element_type=jnp.float32)
        spread(picked, 0, summed)
        dsum[there, :] += lax.dot_general(
            coefficients,
            q_ref[pl.ds(at, 2 * pairs), :],
            (((0,), (0,)), ((), ())),
            preferred_element_type=jnp.float32,
        )
        for half in range(2):
            scatter_rows(2 * step + half, 0, half * pairs)
        return carry

    lax.fori_loop(0, blocks // 2, two_blocks, 0)
    dsum[: window * pairs, :] += dsum[blocks * pairs :, :]

    def doc_block(block, carry):
        at = pl.multiple_of(block * pairs, pairs)
        spread(picked, 0, dsum[pl.ds(at, pairs), :])
        scatter_rows(block, pairs, 0)
        return carry

    lax.fori_loop(0, blocks, doc_block, 0)
    slots = out_ref.shape[1]
    for slot, part in enumerate(peer_order(blocks)):
        out_ref[slot] = gathered(wide, part * slots, slots).astype(jnp.bfloat16)


def grad_call(own, place, parts, queries, documents, blocks, pairs, window):
    count, piece = queries.shape
    seqs = 2 * count
    room = 2 * (parts[0].shape[1] - 1)
    whole = pl.BlockSpec(memory_space=pltpu.VMEM)
    scalars = pl.BlockSpec(memory_space=pltpu.SMEM)
    return pl.pallas_call(
        functools.partial(grad_kernel, blocks, pairs, window),
        in_specs=[scalars, scalars, whole, whole] + [whole] * len(parts),
        out_specs=[whole, whole],
        out_shape=[
            jax.ShapeDtypeStruct((blocks, seqs // blocks, piece), jnp.bfloat16),
            jax.ShapeDtypeStruct((1, lanes), jnp.float32),
        ],
        scratch_shapes=[
            pltpu.VMEM((2 * seqs, lanes), jnp.float32),
            pltpu.VMEM(((blocks + window) * pairs, piece), jnp.float32),
            pltpu.VMEM((4 * pairs, lanes), jnp.float32),
            pltpu.VMEM((blocks, room, pairs // blocks, pairs), jnp.float32),
            pltpu.VMEM((2 * pairs, (window + 2) * pairs), jnp.bfloat16),
        ],
        compiler_params=pltpu.CompilerParams(vmem_limit_bytes=26 * mebibyte),
        name="slice_grads",
    )(own, place, queries, documents, *parts)


def project_kernel(grad_ref, normed_ref, inv_ref, out_ref):
    parts, _, piece = grad_ref.shape
    cuts = [slice(part * piece, (part + 1) * piece) for part in peer_order(parts)]
    inverse = inv_ref[:, :1]
    total = 0.0
    for part, cut in enumerate(cuts):
        unit = normed_ref[:, cut].astype(jnp.float32) * inverse
        total = total + unit * grad_ref[part].astype(jnp.float32)
    along = jnp.sum(total, axis=-1, keepdims=True)
    for part, cut in enumerate(cuts):
        unit = normed_ref[:, cut].astype(jnp.float32) * inverse
        out_ref[:, cut] = grad_ref[part].astype(jnp.float32) - unit * along


def project_call(returned, normed, inverse):
    parts, seqs, piece = returned.shape
    width = normed.shape[1]
    rows = 64
    return pl.pallas_call(
        project_kernel,
        grid=(seqs // rows,),
        in_specs=[
            pl.BlockSpec((parts, rows, piece), lambda i: (0, i, 0)),
            pl.BlockSpec((rows, width), lambda i: (i, 0)),
            pl.BlockSpec((rows, lanes), lambda i: (i, 0)),
        ],
        out_specs=pl.BlockSpec((rows, width), lambda i: (i, 0)),
        out_shape=jax.ShapeDtypeStruct((seqs, width), jnp.float32),
        compiler_params=pltpu.CompilerParams(vmem_limit_bytes=10 * mebibyte),
        name="project_out",
    )(returned, normed, inverse)


def swapped(value, apart):
    pairs = [(at, at ^ apart) for at in range(lax.axis_size("pb"))]
    return lax.ppermute(value, "pb", pairs)


def swap_bits(devices):
    bits = [1 << bit for bit in reversed(range(devices.bit_length() - 1))]
    return bits[:-2], bits[-2], bits[-1]


def swap_masks(devices):
    far, side, last = swap_bits(devices)
    held = [0]
    for apart in far:
        held = held + [mask ^ apart for mask in held]
    held = held + [mask ^ side for mask in held]
    return [held, [mask ^ last for mask in held]]


def gather_all(value):
    far, side, last = swap_bits(lax.axis_size("pb"))
    held = value[None]
    beside, latest = [], held
    for apart in far:
        arrived = swapped(held, apart)
        beside.append(swapped(latest, side))
        held = jnp.concatenate([held, arrived], axis=0)
        latest = arrived
    beside.append(swapped(latest, side))
    held = jnp.concatenate([held] + beside, axis=0)
    return [held, swapped(held, last)]


def middle(embedded, room, devices, pairs, window):
    queries, documents, mine, other, top, own, place = score_call(
        embedded, room, devices, pairs, window
    )
    own_scores, *codes = merge_call(mine, swapped(other, 1), top, swapped(top, 1), devices)
    codes = [swapped(codes[hop], 2 * (hop + 1)) for hop in reversed(range(len(codes)))]
    parts = gather_all(softmax_call(place, own_scores, codes, devices, window))
    grads, loss = grad_call(own, place, parts, queries, documents, devices, pairs, window)
    return grads, loss[0, :1]


def feature_plan(hidden, final_gain, last_row, pair_owner, hard_negatives):
    devices = lax.axis_size("pb")
    seqs, width = hidden.shape
    pairs = pair_owner.shape[0]
    window = hard_negatives.shape[1]
    normed, inverse, embedding = norm_call(
        last_row, hidden, final_gain, pair_owner.T, hard_negatives, devices
    )
    embedded = exchange(embedding)
    most = devices * (window + 1)
    rooms = [most * part // 20 for part in (11, 12, 13, 15, 20)]
    used = devices + jnp.sum(embedded[:, seqs + 2, :window].astype(jnp.float32))
    level = sum((used > room).astype(jnp.int32) for room in rooms[:-1])
    grads, loss = lax.switch(
        level,
        [
            functools.partial(middle, room=room, devices=devices, pairs=pairs, window=window)
            for room in rooms
        ],
        embedded,
    )
    returned = exchange(grads)
    return project_call(returned, normed, inverse), loss


def from_behind(value, axis, steps):
    count = lax.axis_size(axis)
    pairs = [(source, (source + steps) % count) for source in range(count)]
    return lax.ppermute(value, axis, pairs)


def similarity(queries, documents):
    return inverse_temp * lax.dot_general(
        queries, documents, (((1,), (1,)), ((), ())), preferred_element_type=jnp.float32
    )


def transposed(weights, queries):
    return lax.dot_general(
        weights, queries, (((0,), (0,)), ((), ())), preferred_element_type=jnp.float32
    )


def combine_docs(weights, documents):
    return jnp.dot(weights, documents, preferred_element_type=jnp.float32)


def skipped(listed, function, operands, out_shape):
    return lax.cond(
        listed,
        lambda inputs: function(*inputs),
        lambda inputs: jnp.zeros(out_shape, jnp.float32),
        operands,
    )


def row_plan(hidden, final_gain, last_row, pair_owner, hard_negatives):
    values = hidden.astype(jnp.float32)
    scale_row = lax.rsqrt(jnp.mean(values * values, axis=-1, keepdims=True) + token_eps)
    normed = (values * scale_row * final_gain.astype(jnp.float32)).astype(jnp.bfloat16)
    seq_count = last_row.shape[1]
    model_width = hidden.shape[1]
    pooled = normed[last_row[0]].astype(jnp.float32)
    inverse_norm = lax.rsqrt(jnp.sum(pooled * pooled, axis=-1, keepdims=True) + 1e-06)
    unit_vec = pooled * inverse_norm
    embedding = unit_vec.astype(jnp.bfloat16)
    devices = lax.axis_size("pb")
    capacity = 2 * seq_count // devices
    pair_count = pair_owner.shape[0]
    wanted = jnp.concatenate([pair_owner[:, 0], pair_owner[:, 1]])
    holder = wanted // seq_count
    within = wanted % seq_count
    entry_ids = jnp.arange(2 * pair_count, dtype=jnp.int32)
    earlier = (holder[None, :] == holder[:, None]) & (entry_ids[None, :] < entry_ids[:, None])
    position = jnp.sum(earlier.astype(jnp.int32), axis=1)
    request = jnp.full((devices, capacity), -1, jnp.int32).at[holder, position].set(within)
    served = lax.all_to_all(request, "pb", split_axis=0, concat_axis=0, tiled=True)
    outgoing = jnp.where(
        served[:, :, None] >= 0, embedding[jnp.maximum(served, 0)], jnp.zeros((), jnp.bfloat16)
    )
    received = lax.all_to_all(outgoing, "pb", split_axis=0, concat_axis=0, tiled=True)
    gathered = received[holder, position]
    queries = gathered[:pair_count]
    own_docs = gathered[pair_count:]
    listed_ids = hard_negatives[0]
    window = hard_negatives.shape[1]
    listed = [listed_ids[offset] >= 0 for offset in range(window)]
    neighbours = []
    moving = own_docs
    for offset in range(window):
        moving = from_behind(moving, "pb", -1)
        neighbours.append(moving)
    tile_shape = (pair_count, pair_count)
    score_blocks = [similarity(queries, own_docs)]
    for offset in range(window):
        score_blocks.append(
            skipped(listed[offset], similarity, (queries, neighbours[offset]), tile_shape)
        )
    all_scores = jnp.concatenate(score_blocks, axis=1)
    usable = jnp.concatenate(
        [jnp.ones((pair_count,), jnp.bool_)]
        + [jnp.broadcast_to(listed[offset], (pair_count,)) for offset in range(window)]
    )
    masked = jnp.where(usable[None, :], all_scores, -jnp.inf)
    row_max = jnp.max(masked, axis=1, keepdims=True)
    log_total = row_max + jnp.log(jnp.sum(jnp.exp(masked - row_max), axis=1, keepdims=True))
    diagonal = jnp.arange(pair_count, dtype=jnp.int32)
    positive = all_scores[diagonal, diagonal]
    block_loss = jnp.mean(log_total[:, 0] - positive).reshape(1)
    columns = jnp.arange((window + 1) * pair_count, dtype=jnp.int32)
    target = (columns[None, :] == diagonal[:, None]).astype(jnp.float32)
    coefficients = (inverse_temp * (jnp.exp(masked - log_total) - target)).astype(jnp.bfloat16)
    pieces = [
        coefficients[:, offset * pair_count : (offset + 1) * pair_count]
        for offset in range(window + 1)
    ]
    grad_shape = (pair_count, model_width)
    query_sum = combine_docs(pieces[0], own_docs)
    for offset in range(window):
        query_sum = query_sum + skipped(
            listed[offset], combine_docs, (pieces[offset + 1], neighbours[offset]), grad_shape
        )
    query_grad = query_sum.astype(jnp.bfloat16)
    own_part = transposed(pieces[0], queries).astype(jnp.bfloat16)
    partial_value = [
        skipped(listed[offset], transposed, (pieces[offset + 1], queries), grad_shape).astype(
            jnp.bfloat16
        )
        for offset in range(window)
    ]
    running = partial_value[window - 1].astype(jnp.float32)
    for offset in range(window):
        running = from_behind(running, "pb", 1)
        if offset + 1 < window:
            running = running + partial_value[window - 2 - offset].astype(jnp.float32)
    doc_grad = (own_part.astype(jnp.float32) + running).astype(jnp.bfloat16)
    answers = jnp.concatenate([query_grad, doc_grad], axis=0)
    returning = (
        jnp.zeros((devices, capacity, model_width), jnp.bfloat16).at[holder, position].set(answers)
    )
    returned = lax.all_to_all(returning, "pb", split_axis=0, concat_axis=0, tiled=True)
    slot_ids = jnp.where(served >= 0, served, seq_count).reshape(-1)
    emb_grad = (
        jnp.zeros((seq_count, model_width), jnp.bfloat16)
        .at[slot_ids]
        .set(returned.reshape(-1, model_width), mode="drop")
    )
    gradient = emb_grad.astype(jnp.float32)
    pooled_grad = gradient - unit_vec * jnp.sum(unit_vec * gradient, axis=-1, keepdims=True)
    return (pooled_grad, block_loss)


def solution(mesh):
    def local(hidden, final_gain, last_row, pair_owner, hard_negatives):
        plan = feature_plan if hidden.shape[1] >= lanes * mesh.shape["pb"] else row_plan
        return plan(hidden, final_gain, last_row, pair_owner, hard_negatives)

    return jax.shard_map(
        local,
        mesh=mesh,
        in_specs=(
            P(("groups", "pb"), None),
            P(),
            P(("groups", "pb"), None),
            P(("groups", "pb"), None),
            P(("groups", "pb"), None),
        ),
        out_specs=(P(("groups", "pb"), None), P(("groups", "pb"))),
        check_vma=False,
    )
```

```python
import functools

import jax
import jax.numpy as jnp
from jax import lax
from jax.experimental import pallas as pl
from jax.experimental.pallas import tpu as pltpu
from jax.sharding import PartitionSpec as P

inverse_temp = 50.0
token_eps = 1e-05
unit_eps = 1e-06
lanes = 128
bound_steps = 256.0
code_steps = 32000.0
score_limit = 51.0
mebibyte = 1024 * 1024


def spread(target, at, value):
    count = value.shape[0]
    for half in range(2):
        target[pl.ds(2 * at + half, count, stride=2), :] = value[:, half * lanes : (half + 1) * lanes]


def gathered(source, at, count):
    halves = [source[pl.ds(2 * at + half, count, stride=2), :] for half in range(2)]
    return jnp.concatenate(halves, axis=1)


def row_pair(place):
    return pl.ds(pl.multiple_of(place, 2), 2)


def norm_kernel(
    last_ref, hidden_ref, gain_ref, owner_ref, negative_ref, normed_ref, inv_ref, emb_ref
):
    seqs, width = normed_ref.shape
    parts, _, piece = emb_ref.shape
    pairs = owner_ref.shape[1]
    cuts = [slice(part * piece, (part + 1) * piece) for part in range(parts)]
    sources = lax.broadcasted_iota(jnp.int32, (seqs, seqs), 0)
    pick = jnp.where(sources == last_ref[...], 1.0, 0.0).astype(jnp.bfloat16)

    def folded(squares):
        return functools.reduce(
            jnp.add, [squares[:, at : at + lanes] for at in range(0, piece, lanes)]
        )

    total = jnp.zeros((seqs, lanes), jnp.float32)
    for cut in cuts:
        values = lax.dot_general(
            pick, hidden_ref[:, cut], (((0,), (0,)), ((), ())), preferred_element_type=jnp.float32
        )
        normed_ref[:, cut] = values.astype(jnp.bfloat16)
        total = total + folded(values * values)
    scale = lax.rsqrt(jnp.sum(total, axis=-1, keepdims=True) / width + token_eps)
    total = jnp.zeros((seqs, lanes), jnp.float32)
    for cut in cuts:
        values = normed_ref[:, cut].astype(jnp.float32)
        gain = gain_ref[cut].astype(jnp.float32).reshape(1, piece)
        normed = (values * scale * gain).astype(jnp.bfloat16)
        normed_ref[:, cut] = normed
        pooled = normed.astype(jnp.float32)
        total = total + folded(pooled * pooled)
    inverse = lax.rsqrt(jnp.sum(total, axis=-1, keepdims=True) + unit_eps)
    inv_ref[...] = jnp.broadcast_to(inverse, inv_ref.shape)

    owners = owner_ref[...].astype(jnp.float32)
    high = jnp.floor(owners * (1.0 / 256.0))
    low = owners - 256.0 * high
    row = lax.broadcasted_iota(jnp.int32, (8, pairs), 0)
    spot = lax.broadcasted_iota(jnp.int32, (8, pairs), 1)
    left = jnp.where(row == 0, low[:1], jnp.where(row == 1, high[:1], 0.0))
    right = jnp.where(row == 0, low[1:2], jnp.where(row == 1, high[1:2], 0.0))
    for offset in range(negative_ref.shape[1]):
        named = (negative_ref[0, offset] >= 0).astype(jnp.float32)
        left = jnp.where((row == 2) & (spot == offset), named, left)
    facts = jnp.concatenate([left, right], axis=1).astype(jnp.bfloat16)

    for part, cut in enumerate(cuts):
        emb_ref[part, :seqs] = (normed_ref[:, cut].astype(jnp.float32) * inverse).astype(jnp.bfloat16)
        emb_ref[part, seqs:] = facts


def norm_call(last_row, hidden, gain, owners, hard_negatives, parts):
    seqs, width = hidden.shape
    piece = width // parts
    whole = pl.BlockSpec(memory_space=pltpu.VMEM)
    return pl.pallas_call(
        norm_kernel,
        in_specs=[whole, whole, whole, whole, pl.BlockSpec(memory_space=pltpu.SMEM)],
        out_specs=[whole] * 3,
        out_shape=[
            jax.ShapeDtypeStruct((seqs, width), jnp.bfloat16),
            jax.ShapeDtypeStruct((seqs, lanes), jnp.float32),
            jax.ShapeDtypeStruct((parts, seqs + 8, piece), jnp.bfloat16),
        ],
        compiler_params=pltpu.CompilerParams(vmem_limit_bytes=56 * mebibyte),
        name="norm_rows",
    )(last_row, hidden, gain, owners, hard_negatives)


def score_kernel(
    blocks,
    pairs,
    window,
    *refs,
):
    emb_ref, q_ref, d_ref, mine_ref, other_ref, top_ref, own_ref, place_ref = refs[:-7]
    wide, picked, picked_too, facts, own, named, sems = refs[-7:]
    seqs = emb_ref.shape[1] - 8
    sent = emb_ref[:, seqs:, :].astype(jnp.float32)
    own_ref[...] = (2.0 * sent[:, 0, :] + 512.0 * sent[:, 1, :]).astype(jnp.int32)
    facts[...] = sent[:, 2, :lanes].astype(jnp.int32)
    fetches = [
        pltpu.make_async_copy(own_ref, own, sems.at[0]),
        pltpu.make_async_copy(facts, named, sems.at[1]),
    ]
    for fetch in fetches:
        fetch.start()

    for part in range(blocks):
        spread(wide, part * seqs, emb_ref[part, :seqs, :].astype(jnp.float32))
    for fetch in fetches:
        fetch.wait()

    def place(block, count):
        place_ref[0, block] = block
        for offset in range(window):
            present = named[block, offset] > 0
            place_ref[offset + 1, block] = jnp.where(present, count, -1)
            count = count + present.astype(jnp.int32)
        return count

    used = lax.fori_loop(0, blocks, place, blocks)
    fine = pairs // blocks

    def clear(spot, carry):
        empty = jnp.zeros((blocks // 2, fine, pairs), jnp.float32)
        at = pl.ds(pl.multiple_of(spot * fine, fine), fine)
        mine_ref[:, at, :] = empty
        other_ref[:, at, :] = empty
        return carry

    lax.fori_loop(used, mine_ref.shape[1] // fine, clear, 0)
    group = 32

    def pick_block(block, rows_at):
        for base in range(0, 2 * pairs, group):
            rows = [wide[row_pair(own[block, base + k]), :] for k in range(group)]
            for k in range(group):
                rows_at[2 * (base + k) : 2 * (base + k + 1), :] = rows[k]
        at = pl.multiple_of(block * pairs, pairs)
        q_ref[pl.ds(at, pairs), :] = gathered(rows_at, 0, pairs).astype(jnp.bfloat16)
        d_ref[pl.ds(at, pairs), :] = gathered(rows_at, pairs, pairs).astype(jnp.bfloat16)

    ahead = -(-(window + 2) // 2)

    def pick_one(block, carry):
        pick_block(block, picked)
        return carry

    lax.fori_loop(0, 2 * ahead, pick_one, 0)
    even = lax.axis_index("pb") % 2 == 0
    spare = mine_ref.shape[1] // fine - 1

    def score_blocks(step, carry):
        at = pl.multiple_of(step * 2 * pairs, 2 * pairs)
        tiles = inverse_temp * lax.dot_general(
            q_ref[pl.ds(at, 2 * pairs), :],
            d_ref[pl.ds(at, (window + 2) * pairs), :],
            (((1,), (1,)), ((), ())),
            preferred_element_type=jnp.float32,
        )
        top = carry
        for half in range(2):
            for column in range(window + 1):
                spot = place_ref[column, 2 * step + half]
                row = pl.multiple_of(jnp.where(spot >= 0, spot, spare) * fine, fine)
                tile = tiles[
                    half * pairs : (half + 1) * pairs,
                    (half + column) * pairs : (half + column + 1) * pairs,
                ]
                parted = tile.reshape(blocks // 2, 2, fine, pairs)
                first, second = parted[:, 0], parted[:, 1]
                mine_ref[:, pl.ds(row, fine), :] = jnp.where(even, first, second)
                other_ref[:, pl.ds(row, fine), :] = jnp.where(even, second, first)
                size = jnp.maximum(jnp.abs(first), jnp.abs(second))
                top = jnp.maximum(top, jnp.max(size, axis=0))
        return top

    def score_and_pick(step, top):
        top = score_blocks(step - ahead, top)
        pick_block(2 * step, picked)
        pick_block(2 * step + 1, picked_too)
        return top

    top = jnp.zeros((fine, pairs), jnp.float32)
    top = lax.fori_loop(ahead, blocks // 2, score_and_pick, top)
    d_ref[blocks * pairs :, :] = d_ref[: window * pairs, :]
    top_ref[...] = lax.fori_loop(blocks // 2 - ahead, blocks // 2, score_blocks, top)


def score_call(embedded, room, blocks, pairs, window):
    _, rows, piece = embedded.shape
    fine = pairs // blocks
    whole = pl.BlockSpec(memory_space=pltpu.VMEM)
    scalars = pl.BlockSpec(memory_space=pltpu.SMEM)
    return pl.pallas_call(
        functools.partial(score_kernel, blocks, pairs, window),
        in_specs=[whole],
        out_specs=[whole, whole, whole, whole, whole, whole, scalars],
        out_shape=[
            jax.ShapeDtypeStruct((blocks * pairs, piece), jnp.bfloat16),
            jax.ShapeDtypeStruct(((blocks + window) * pairs, piece), jnp.bfloat16),
            jax.ShapeDtypeStruct((blocks // 2, (room + 1) * fine, pairs), jnp.float32),
            jax.ShapeDtypeStruct((blocks // 2, (room + 1) * fine, pairs), jnp.float32),
            jax.ShapeDtypeStruct((fine, pairs), jnp.float32),
            jax.ShapeDtypeStruct((blocks, 2 * pairs), jnp.int32),
            jax.ShapeDtypeStruct((window + 1, blocks), jnp.int32),
        ],
        scratch_shapes=[
            pltpu.VMEM((2 * blocks * (rows - 8), lanes), jnp.float32),
            pltpu.VMEM((4 * pairs, lanes), jnp.float32),
            pltpu.VMEM((4 * pairs, lanes), jnp.float32),
            pltpu.VMEM((blocks, lanes), jnp.int32),
            pltpu.SMEM((blocks, 2 * pairs), jnp.int32),
            pltpu.SMEM((blocks, lanes), jnp.int32),
            pltpu.SemaphoreType.DMA((2,)),
        ],
        compiler_params=pltpu.CompilerParams(vmem_limit_bytes=22 * mebibyte),
        name="partial_scores",
    )(embedded)


def coded(values, scale):
    return jnp.round(values * scale).astype(jnp.int32).astype(jnp.int16)


def decoded(codes, scale):
    return codes.astype(jnp.int32).astype(jnp.float32) * scale


def highest(values):
    return jnp.max(jnp.max(values, axis=1, keepdims=True), axis=0, keepdims=True)


def merge_kernel(mine_ref, other_ref, top_ref, other_top_ref, own_ref, *code_refs):
    _, rows, pairs = own_ref.shape
    steps = code_refs[0].shape[1] - 1
    fine = rows // steps // 2
    chip = lax.axis_index("pb") // 2
    across = mine_ref.shape[0] // 2
    top = jnp.minimum(highest(top_ref[...]) + highest(other_top_ref[...]), score_limit)
    bound = jnp.ceil(top * bound_steps) + 1.0
    scale = code_steps * bound_steps / bound
    sent_bound = jnp.broadcast_to(bound, (2 * fine, pairs)).astype(jnp.int32).astype(jnp.int16)
    for which in range(2):
        target = chip ^ (which * across)
        own_ref[which] = mine_ref[target, :rows] + other_ref[target, :rows]
        for hop, code_ref in enumerate(code_refs):
            near = target ^ (hop + 1)

            def encode(step, carry):
                there = pl.ds(pl.multiple_of(step * 2 * fine, 2 * fine), 2 * fine)
                values = mine_ref[near, there, :] + other_ref[near, there, :]
                code_ref[which, step] = coded(values, scale)
                return carry

            lax.fori_loop(0, steps, encode, 0)
            code_ref[which, steps] = sent_bound


def merge_call(mine, other, top, other_top, blocks):
    chips, rows, pairs = mine.shape
    fine = pairs // blocks
    rows = rows - fine
    whole = pl.BlockSpec(memory_space=pltpu.VMEM)
    codes = jax.ShapeDtypeStruct((2, rows // (2 * fine) + 1, 2 * fine, pairs), jnp.int16)
    near = chips // 2 - 1
    return pl.pallas_call(
        merge_kernel,
        in_specs=[whole] * 4,
        out_specs=[whole] * (near + 1),
        out_shape=[jax.ShapeDtypeStruct((2, rows, pairs), jnp.float32)] + [codes] * near,
        compiler_params=pltpu.CompilerParams(vmem_limit_bytes=12 * mebibyte),
        name="merge_scores",
    )(mine, other, top, other_top)


def half_kernel(own_ref, *refs):
    near_refs, (sum_ref, code_ref, sums) = refs[:-3], refs[-3:]
    steps, deep, pairs = code_ref.shape
    steps = steps - 1
    unit = 1.0 / (code_steps * bound_steps)
    scales = [decoded(ref[0, steps], unit) for ref in near_refs]

    def add(step, top):
        there = pl.ds(pl.multiple_of(step * deep, deep), deep)
        here, over = own_ref[0, there, :], own_ref[1, there, :]
        for ref, scale in zip(near_refs, scales):
            here = here + decoded(ref[0, step], scale)
            over = over + decoded(ref[1, step], scale)
        sum_ref[there, :] = here
        sums[there, :] = over
        return jnp.maximum(top, jnp.abs(over))

    top = lax.fori_loop(0, steps, add, jnp.zeros((deep, pairs), jnp.float32))
    bound = jnp.ceil(highest(top) * bound_steps) + 1.0
    scale = code_steps * bound_steps / bound

    def encode(step, carry):
        there = pl.ds(pl.multiple_of(step * deep, deep), deep)
        code_ref[step] = coded(sums[there, :], scale)
        return carry

    lax.fori_loop(0, steps, encode, 0)
    code_ref[steps] = jnp.broadcast_to(bound, (deep, pairs)).astype(jnp.int32).astype(jnp.int16)


def half_call(own, near):
    _, rows, pairs = own.shape
    whole = pl.BlockSpec(memory_space=pltpu.VMEM)
    return pl.pallas_call(
        half_kernel,
        in_specs=[whole] * (1 + len(near)),
        out_specs=[whole, whole],
        out_shape=[
            jax.ShapeDtypeStruct((rows, pairs), jnp.float32),
            jax.ShapeDtypeStruct(near[0].shape[1:], jnp.int16),
        ],
        scratch_shapes=[pltpu.VMEM((rows, pairs), jnp.float32)],
        compiler_params=pltpu.CompilerParams(vmem_limit_bytes=8 * mebibyte),
        name="half_scores",
    )(own, *near)


def softmax_kernel(blocks, window, place_ref, own_ref, *refs):
    code_refs, (c_ref, packed, masked) = refs[:-3], refs[-3:]
    room, fine, pairs = packed.shape
    count = blocks * fine
    unit = 1.0 / (code_steps * bound_steps)
    scales = [ref[room // 2].astype(jnp.int32).astype(jnp.float32) * unit for ref in code_refs]

    def decode(step, carry):
        both = own_ref[pl.ds(pl.multiple_of(step * 2 * fine, 2 * fine), 2 * fine), :]
        for ref, scale in zip(code_refs, scales):
            both = both + ref[step].astype(jnp.int32).astype(jnp.float32) * scale
        packed[2 * step] = both[:fine]
        packed[2 * step + 1] = both[fine:]
        return carry

    lax.fori_loop(0, room // 2, decode, 0)
    for block in range(blocks):
        for column in range(window + 1):
            spot = place_ref[column, block]
            tile = packed[jnp.maximum(spot, 0)]
            masked[block * fine : (block + 1) * fine, column * pairs : (column + 1) * pairs] = (
                jnp.where(spot >= 0, tile, -jnp.inf)
            )
    row = lax.broadcasted_iota(jnp.int32, (count, pairs), 0)
    lane = lax.broadcasted_iota(jnp.int32, (count, pairs), 1)
    target = lane == lax.axis_index("pb") * fine + row % fine
    pieces = [masked[:, column * pairs : (column + 1) * pairs] for column in range(window + 1)]
    row_max = jnp.max(functools.reduce(jnp.maximum, pieces), axis=1, keepdims=True)
    total = functools.reduce(jnp.add, [jnp.exp(piece - row_max) for piece in pieces])
    log_total = row_max + jnp.log(jnp.sum(total, axis=1, keepdims=True))
    positive = jnp.sum(jnp.where(target, pieces[0], 0.0), axis=1, keepdims=True)
    for column, piece in enumerate(pieces):
        share = jnp.exp(piece - log_total)
        if column == 0:
            share = share - jnp.where(target, 1.0, 0.0)
        masked[:, column * pairs : (column + 1) * pairs] = inverse_temp * share
    for block in range(blocks):
        for column in range(window + 1):
            spot = place_ref[column, block]

            @pl.when(spot >= 0)
            def _():
                packed[spot] = masked[
                    block * fine : (block + 1) * fine, column * pairs : (column + 1) * pairs
                ]

    for step in range(room // 2):
        both = jnp.concatenate([packed[2 * step], packed[2 * step + 1]], axis=0)
        c_ref[step] = both.astype(jnp.bfloat16)
    losses = jnp.sum(
        jnp.where(lane == row // fine, log_total - positive, 0.0), axis=0, keepdims=True
    )
    coarse = losses.astype(jnp.bfloat16).astype(jnp.float32)
    rank = lax.broadcasted_iota(jnp.int32, (2 * fine, pairs), 0)
    both = jnp.where(rank == 0, coarse, jnp.where(rank == 1, losses - coarse, 0.0))
    c_ref[room // 2] = both.astype(jnp.bfloat16)


def softmax_call(place, own_scores, codes, blocks, window):
    steps, fine, pairs = codes[0].shape
    room, fine = 2 * (steps - 1), fine // 2
    whole = pl.BlockSpec(memory_space=pltpu.VMEM)
    return pl.pallas_call(
        functools.partial(softmax_kernel, blocks, window),
        in_specs=[pl.BlockSpec(memory_space=pltpu.SMEM), whole] + [whole] * len(codes),
        out_specs=whole,
        out_shape=jax.ShapeDtypeStruct((room // 2 + 1, 2 * fine, pairs), jnp.bfloat16),
        scratch_shapes=[
            pltpu.VMEM((room, fine, pairs), jnp.float32),
            pltpu.VMEM((blocks * fine, (window + 1) * pairs), jnp.float32),
        ],
        compiler_params=pltpu.CompilerParams(vmem_limit_bytes=8 * mebibyte),
        name="softmax_rows",
    )(place, own_scores, *codes)


def grad_kernel(
    blocks,
    pairs,
    window,
    own_ref,
    place_ref,
    q_ref,
    d_ref,
    *refs,
):
    part_refs = refs[:-7]
    out_ref, loss_ref, wide, dsum, picked, packed, square = refs[-7:]
    fine = pairs // blocks
    room = packed.shape[1]
    me = lax.axis_index("pb")
    masks = swap_masks(blocks)
    group = 32
    losses = 0.0
    for part in part_refs:
        sent = part[:, room // 2].astype(jnp.float32)
        losses = losses + jnp.sum(sent[:, 0, :] + sent[:, 1, :], axis=0, keepdims=True) / pairs
    lane = lax.broadcasted_iota(jnp.int32, losses.shape, 1)
    mine = jnp.where(lane == me, losses, 0.0)
    loss_ref[...] = jnp.broadcast_to(jnp.sum(mine, axis=1, keepdims=True), loss_ref.shape)
    dsum[...] = jnp.zeros_like(dsum)
    square[...] = jnp.zeros_like(square)

    def unpack(step, carry):
        for part, mask in zip(part_refs, masks):
            both = part[:, step].astype(jnp.float32)
            for at, apart in enumerate(mask):
                packed[me ^ apart, 2 * step] = both[at, :fine]
                packed[me ^ apart, 2 * step + 1] = both[at, fine:]
        return carry

    lax.fori_loop(0, room // 2, unpack, 0)

    def scatter_rows(block, offset, start):
        for base in range(0, pairs, group):
            rows = [
                picked[2 * (start + base + k) : 2 * (start + base + k + 1), :] for k in range(group)
            ]
            for k in range(group):
                wide[row_pair(own_ref[block, offset + base + k]), :] = rows[k]

    def two_blocks(step, carry):
        for half in range(2):
            for column in range(window + 1):
                spot = place_ref[column, 2 * step + half]
                tile = packed[:, jnp.maximum(spot, 0)].reshape(pairs, pairs)
                square[
                    half * pairs : (half + 1) * pairs,
                    (half + column) * pairs : (half + column + 1) * pairs,
                ] = jnp.where(spot >= 0, tile, 0.0).astype(jnp.bfloat16)
        at = pl.multiple_of(step * 2 * pairs, 2 * pairs)
        there = pl.ds(at, (window + 2) * pairs)
        coefficients = square[...]
        summed = jnp.dot(coefficients, d_ref[there, :], preferred_element_type=jnp.float32)
        spread(picked, 0, summed)
        dsum[there, :] += lax.dot_general(
            coefficients,
            q_ref[pl.ds(at, 2 * pairs), :],
            (((0,), (0,)), ((), ())),
            preferred_element_type=jnp.float32,
        )
        for half in range(2):
            scatter_rows(2 * step + half, 0, half * pairs)
        return carry

    lax.fori_loop(0, blocks // 2, two_blocks, 0)
    dsum[: window * pairs, :] += dsum[blocks * pairs :, :]

    def doc_block(block, carry):
        at = pl.multiple_of(block * pairs, pairs)
        spread(picked, 0, dsum[pl.ds(at, pairs), :])
        scatter_rows(block, pairs, 0)
        return carry

    lax.fori_loop(0, blocks, doc_block, 0)
    slots = out_ref.shape[1]
    for part in range(blocks):
        out_ref[part] = gathered(wide, part * slots, slots).astype(jnp.bfloat16)


def grad_call(own, place, parts, queries, documents, blocks, pairs, window):
    count, piece = queries.shape
    seqs = 2 * count
    room = 2 * (parts[0].shape[1] - 1)
    whole = pl.BlockSpec(memory_space=pltpu.VMEM)
    scalars = pl.BlockSpec(memory_space=pltpu.SMEM)
    return pl.pallas_call(
        functools.partial(grad_kernel, blocks, pairs, window),
        in_specs=[scalars, scalars, whole, whole] + [whole] * len(parts),
        out_specs=[whole, whole],
        out_shape=[
            jax.ShapeDtypeStruct((blocks, seqs // blocks, piece), jnp.bfloat16),
            jax.ShapeDtypeStruct((1, lanes), jnp.float32),
        ],
        scratch_shapes=[
            pltpu.VMEM((2 * seqs, lanes), jnp.float32),
            pltpu.VMEM(((blocks + window) * pairs, piece), jnp.float32),
            pltpu.VMEM((4 * pairs, lanes), jnp.float32),
            pltpu.VMEM((blocks, room, pairs // blocks, pairs), jnp.float32),
            pltpu.VMEM((2 * pairs, (window + 2) * pairs), jnp.bfloat16),
        ],
        compiler_params=pltpu.CompilerParams(vmem_limit_bytes=26 * mebibyte),
        name="slice_grads",
    )(own, place, queries, documents, *parts)


def project_kernel(grad_ref, normed_ref, inv_ref, out_ref):
    parts, _, piece = grad_ref.shape
    cuts = [slice(part * piece, (part + 1) * piece) for part in range(parts)]
    inverse = inv_ref[:, :1]
    total = 0.0
    for part, cut in enumerate(cuts):
        unit = normed_ref[:, cut].astype(jnp.float32) * inverse
        total = total + unit * grad_ref[part].astype(jnp.float32)
    along = jnp.sum(total, axis=-1, keepdims=True)
    for part, cut in enumerate(cuts):
        unit = normed_ref[:, cut].astype(jnp.float32) * inverse
        out_ref[:, cut] = grad_ref[part].astype(jnp.float32) - unit * along


def project_call(returned, normed, inverse):
    parts, seqs, piece = returned.shape
    width = normed.shape[1]
    rows = 64
    return pl.pallas_call(
        project_kernel,
        grid=(seqs // rows,),
        in_specs=[
            pl.BlockSpec((parts, rows, piece), lambda i: (0, i, 0)),
            pl.BlockSpec((rows, width), lambda i: (i, 0)),
            pl.BlockSpec((rows, lanes), lambda i: (i, 0)),
        ],
        out_specs=pl.BlockSpec((rows, width), lambda i: (i, 0)),
        out_shape=jax.ShapeDtypeStruct((seqs, width), jnp.float32),
        compiler_params=pltpu.CompilerParams(vmem_limit_bytes=10 * mebibyte),
        name="project_out",
    )(returned, normed, inverse)


def swapped(value, apart):
    pairs = [(at, at ^ apart) for at in range(lax.axis_size("pb"))]
    return lax.ppermute(value, "pb", pairs)


def swap_bits(devices):
    bits = [1 << bit for bit in reversed(range(devices.bit_length() - 1))]
    return bits[:-2], bits[-2], bits[-1]


def swap_masks(devices):
    far, side, last = swap_bits(devices)
    held = [0]
    for apart in far:
        held = held + [mask ^ apart for mask in held]
    held = held + [mask ^ side for mask in held]
    return [held, [mask ^ last for mask in held]]


def gather_all(value):
    far, side, last = swap_bits(lax.axis_size("pb"))
    held = value[None]
    beside, latest = [], held
    for apart in far:
        arrived = swapped(held, apart)
        beside.append(swapped(latest, side))
        held = jnp.concatenate([held, arrived], axis=0)
        latest = arrived
    beside.append(swapped(latest, side))
    held = jnp.concatenate([held] + beside, axis=0)
    return [held, swapped(held, last)]


def middle(embedded, room, devices, pairs, window):
    queries, documents, mine, other, top, own, place = score_call(
        embedded, room, devices, pairs, window
    )
    own_scores, *codes = merge_call(mine, swapped(other, 1), top, swapped(top, 1), devices)
    near = [swapped(codes[hop], 2 * (hop + 1)) for hop in reversed(range(len(codes)))]
    own_scores, over = half_call(own_scores, near)
    codes = [swapped(over, devices // 2)]
    parts = gather_all(softmax_call(place, own_scores, codes, devices, window))
    grads, loss = grad_call(own, place, parts, queries, documents, devices, pairs, window)
    return grads, loss[0, :1]


def feature_plan(hidden, final_gain, last_row, pair_owner, hard_negatives):
    devices = lax.axis_size("pb")
    seqs, width = hidden.shape
    pairs = pair_owner.shape[0]
    window = hard_negatives.shape[1]
    normed, inverse, embedding = norm_call(
        last_row, hidden, final_gain, pair_owner.T, hard_negatives, devices
    )
    embedded = lax.all_to_all(embedding, "pb", split_axis=0, concat_axis=0, tiled=True)
    most = devices * (window + 1)
    rooms = [most * part // 20 for part in (11, 12, 13, 15, 20)]
    used = devices + jnp.sum(embedded[:, seqs + 2, :window].astype(jnp.float32))
    level = sum((used > room).astype(jnp.int32) for room in rooms[:-1])
    grads, loss = lax.switch(
        level,
        [
            functools.partial(middle, room=room, devices=devices, pairs=pairs, window=window)
            for room in rooms
        ],
        embedded,
    )
    returned = lax.all_to_all(grads, "pb", split_axis=0, concat_axis=0, tiled=True)
    return project_call(returned, normed, inverse), loss


def from_behind(value, axis, steps):
    count = lax.axis_size(axis)
    pairs = [(source, (source + steps) % count) for source in range(count)]
    return lax.ppermute(value, axis, pairs)


def similarity(queries, documents):
    return inverse_temp * lax.dot_general(
        queries, documents, (((1,), (1,)), ((), ())), preferred_element_type=jnp.float32
    )


def transposed(weights, queries):
    return lax.dot_general(
        weights, queries, (((0,), (0,)), ((), ())), preferred_element_type=jnp.float32
    )


def combine_docs(weights, documents):
    return jnp.dot(weights, documents, preferred_element_type=jnp.float32)


def skipped(listed, function, operands, out_shape):
    return lax.cond(
        listed,
        lambda inputs: function(*inputs),
        lambda inputs: jnp.zeros(out_shape, jnp.float32),
        operands,
    )


def row_plan(hidden, final_gain, last_row, pair_owner, hard_negatives):
    values = hidden.astype(jnp.float32)
    scale_row = lax.rsqrt(jnp.mean(values * values, axis=-1, keepdims=True) + token_eps)
    normed = (values * scale_row * final_gain.astype(jnp.float32)).astype(jnp.bfloat16)
    seq_count = last_row.shape[1]
    model_width = hidden.shape[1]
    pooled = normed[last_row[0]].astype(jnp.float32)
    inverse_norm = lax.rsqrt(jnp.sum(pooled * pooled, axis=-1, keepdims=True) + 1e-06)
    unit_vec = pooled * inverse_norm
    embedding = unit_vec.astype(jnp.bfloat16)
    devices = lax.axis_size("pb")
    capacity = 2 * seq_count // devices
    pair_count = pair_owner.shape[0]
    wanted = jnp.concatenate([pair_owner[:, 0], pair_owner[:, 1]])
    holder = wanted // seq_count
    within = wanted % seq_count
    entry_ids = jnp.arange(2 * pair_count, dtype=jnp.int32)
    earlier = (holder[None, :] == holder[:, None]) & (entry_ids[None, :] < entry_ids[:, None])
    position = jnp.sum(earlier.astype(jnp.int32), axis=1)
    request = jnp.full((devices, capacity), -1, jnp.int32).at[holder, position].set(within)
    served = lax.all_to_all(request, "pb", split_axis=0, concat_axis=0, tiled=True)
    outgoing = jnp.where(
        served[:, :, None] >= 0, embedding[jnp.maximum(served, 0)], jnp.zeros((), jnp.bfloat16)
    )
    received = lax.all_to_all(outgoing, "pb", split_axis=0, concat_axis=0, tiled=True)
    gathered = received[holder, position]
    queries = gathered[:pair_count]
    own_docs = gathered[pair_count:]
    listed_ids = hard_negatives[0]
    window = hard_negatives.shape[1]
    listed = [listed_ids[offset] >= 0 for offset in range(window)]
    neighbours = []
    moving = own_docs
    for offset in range(window):
        moving = from_behind(moving, "pb", -1)
        neighbours.append(moving)
    tile_shape = (pair_count, pair_count)
    score_blocks = [similarity(queries, own_docs)]
    for offset in range(window):
        score_blocks.append(
            skipped(listed[offset], similarity, (queries, neighbours[offset]), tile_shape)
        )
    all_scores = jnp.concatenate(score_blocks, axis=1)
    usable = jnp.concatenate(
        [jnp.ones((pair_count,), jnp.bool_)]
        + [jnp.broadcast_to(listed[offset], (pair_count,)) for offset in range(window)]
    )
    masked = jnp.where(usable[None, :], all_scores, -jnp.inf)
    row_max = jnp.max(masked, axis=1, keepdims=True)
    log_total = row_max + jnp.log(jnp.sum(jnp.exp(masked - row_max), axis=1, keepdims=True))
    diagonal = jnp.arange(pair_count, dtype=jnp.int32)
    positive = all_scores[diagonal, diagonal]
    block_loss = jnp.mean(log_total[:, 0] - positive).reshape(1)
    columns = jnp.arange((window + 1) * pair_count, dtype=jnp.int32)
    target = (columns[None, :] == diagonal[:, None]).astype(jnp.float32)
    coefficients = (inverse_temp * (jnp.exp(masked - log_total) - target)).astype(jnp.bfloat16)
    pieces = [
        coefficients[:, offset * pair_count : (offset + 1) * pair_count]
        for offset in range(window + 1)
    ]
    grad_shape = (pair_count, model_width)
    query_sum = combine_docs(pieces[0], own_docs)
    for offset in range(window):
        query_sum = query_sum + skipped(
            listed[offset], combine_docs, (pieces[offset + 1], neighbours[offset]), grad_shape
        )
    query_grad = query_sum.astype(jnp.bfloat16)
    own_part = transposed(pieces[0], queries).astype(jnp.bfloat16)
    partial_value = [
        skipped(listed[offset], transposed, (pieces[offset + 1], queries), grad_shape).astype(
            jnp.bfloat16
        )
        for offset in range(window)
    ]
    running = partial_value[window - 1].astype(jnp.float32)
    for offset in range(window):
        running = from_behind(running, "pb", 1)
        if offset + 1 < window:
            running = running + partial_value[window - 2 - offset].astype(jnp.float32)
    doc_grad = (own_part.astype(jnp.float32) + running).astype(jnp.bfloat16)
    answers = jnp.concatenate([query_grad, doc_grad], axis=0)
    returning = (
        jnp.zeros((devices, capacity, model_width), jnp.bfloat16).at[holder, position].set(answers)
    )
    returned = lax.all_to_all(returning, "pb", split_axis=0, concat_axis=0, tiled=True)
    slot_ids = jnp.where(served >= 0, served, seq_count).reshape(-1)
    emb_grad = (
        jnp.zeros((seq_count, model_width), jnp.bfloat16)
        .at[slot_ids]
        .set(returned.reshape(-1, model_width), mode="drop")
    )
    gradient = emb_grad.astype(jnp.float32)
    pooled_grad = gradient - unit_vec * jnp.sum(unit_vec * gradient, axis=-1, keepdims=True)
    return (pooled_grad, block_loss)


def solution(mesh):
    def local(hidden, final_gain, last_row, pair_owner, hard_negatives):
        plan = feature_plan if hidden.shape[1] >= lanes * mesh.shape["pb"] else row_plan
        return plan(hidden, final_gain, last_row, pair_owner, hard_negatives)

    return jax.shard_map(
        local,
        mesh=mesh,
        in_specs=(
            P(("groups", "pb"), None),
            P(),
            P(("groups", "pb"), None),
            P(("groups", "pb"), None),
            P(("groups", "pb"), None),
        ),
        out_specs=(P(("groups", "pb"), None), P(("groups", "pb"))),
        check_vma=False,
    )
```

```python
import functools

import jax
import jax.numpy as jnp
from jax import lax
from jax.experimental import pallas as pl
from jax.experimental.pallas import tpu as pltpu
from jax.sharding import PartitionSpec as P

inverse_temp = 50.0
token_eps = 1e-05
unit_eps = 1e-06
lanes = 128
bound_steps = 256.0
code_steps = 32000.0
score_limit = 51.0
mebibyte = 1024 * 1024


def spread(target, at, value):
    count = value.shape[0]
    for half in range(2):
        target[pl.ds(2 * at + half, count, stride=2), :] = value[:, half * lanes : (half + 1) * lanes]


def gathered(source, at, count):
    halves = [source[pl.ds(2 * at + half, count, stride=2), :] for half in range(2)]
    return jnp.concatenate(halves, axis=1)


def row_pair(place):
    return pl.ds(pl.multiple_of(place, 2), 2)


def norm_kernel(
    last_ref, hidden_ref, gain_ref, owner_ref, negative_ref, normed_ref, inv_ref, emb_ref
):
    seqs, width = normed_ref.shape
    parts, _, piece = emb_ref.shape
    pairs = owner_ref.shape[1]
    cuts = [slice(part * piece, (part + 1) * piece) for part in range(parts)]
    sources = lax.broadcasted_iota(jnp.int32, (seqs, seqs), 0)
    pick = jnp.where(sources == last_ref[...], 1.0, 0.0).astype(jnp.bfloat16)

    def folded(squares):
        return functools.reduce(
            jnp.add, [squares[:, at : at + lanes] for at in range(0, piece, lanes)]
        )

    total = jnp.zeros((seqs, lanes), jnp.float32)
    for cut in cuts:
        values = lax.dot_general(
            pick, hidden_ref[:, cut], (((0,), (0,)), ((), ())), preferred_element_type=jnp.float32
        )
        normed_ref[:, cut] = values.astype(jnp.bfloat16)
        total = total + folded(values * values)
    scale = lax.rsqrt(jnp.sum(total, axis=-1, keepdims=True) / width + token_eps)
    total = jnp.zeros((seqs, lanes), jnp.float32)
    for cut in cuts:
        values = normed_ref[:, cut].astype(jnp.float32)
        gain = gain_ref[cut].astype(jnp.float32).reshape(1, piece)
        normed = (values * scale * gain).astype(jnp.bfloat16)
        normed_ref[:, cut] = normed
        pooled = normed.astype(jnp.float32)
        total = total + folded(pooled * pooled)
    inverse = lax.rsqrt(jnp.sum(total, axis=-1, keepdims=True) + unit_eps)
    inv_ref[...] = jnp.broadcast_to(inverse, inv_ref.shape)

    owners = owner_ref[...].astype(jnp.float32)
    high = jnp.floor(owners * (1.0 / 256.0))
    low = owners - 256.0 * high
    row = lax.broadcasted_iota(jnp.int32, (8, pairs), 0)
    spot = lax.broadcasted_iota(jnp.int32, (8, pairs), 1)
    left = jnp.where(row == 0, low[:1], jnp.where(row == 1, high[:1], 0.0))
    right = jnp.where(row == 0, low[1:2], jnp.where(row == 1, high[1:2], 0.0))
    for offset in range(negative_ref.shape[1]):
        named = (negative_ref[0, offset] >= 0).astype(jnp.float32)
        left = jnp.where((row == 2) & (spot == offset), named, left)
    facts = jnp.concatenate([left, right], axis=1).astype(jnp.bfloat16)

    for part, cut in enumerate(cuts):
        emb_ref[part, :seqs] = (normed_ref[:, cut].astype(jnp.float32) * inverse).astype(jnp.bfloat16)
        emb_ref[part, seqs:] = facts


def norm_call(last_row, hidden, gain, owners, hard_negatives, parts):
    seqs, width = hidden.shape
    piece = width // parts
    whole = pl.BlockSpec(memory_space=pltpu.VMEM)
    return pl.pallas_call(
        norm_kernel,
        in_specs=[whole, whole, whole, whole, pl.BlockSpec(memory_space=pltpu.SMEM)],
        out_specs=[whole] * 3,
        out_shape=[
            jax.ShapeDtypeStruct((seqs, width), jnp.bfloat16),
            jax.ShapeDtypeStruct((seqs, lanes), jnp.float32),
            jax.ShapeDtypeStruct((parts, seqs + 8, piece), jnp.bfloat16),
        ],
        compiler_params=pltpu.CompilerParams(vmem_limit_bytes=56 * mebibyte),
        name="norm_rows",
    )(last_row, hidden, gain, owners, hard_negatives)


def score_kernel(
    blocks,
    pairs,
    window,
    *refs,
):
    emb_ref, q_ref, d_ref, mine_ref, other_ref, top_ref, own_ref, place_ref = refs[:-7]
    wide, picked, picked_too, facts, own, named, sems = refs[-7:]
    seqs = emb_ref.shape[1] - 8
    sent = emb_ref[:, seqs:, :].astype(jnp.float32)
    own_ref[...] = (2.0 * sent[:, 0, :] + 512.0 * sent[:, 1, :]).astype(jnp.int32)
    facts[...] = sent[:, 2, :lanes].astype(jnp.int32)
    fetches = [
        pltpu.make_async_copy(own_ref, own, sems.at[0]),
        pltpu.make_async_copy(facts, named, sems.at[1]),
    ]
    for fetch in fetches:
        fetch.start()

    for part in range(blocks):
        spread(wide, part * seqs, emb_ref[part, :seqs, :].astype(jnp.float32))
    for fetch in fetches:
        fetch.wait()

    def place(block, count):
        place_ref[0, block] = block
        for offset in range(window):
            present = named[block, offset] > 0
            place_ref[offset + 1, block] = jnp.where(present, count, -1)
            count = count + present.astype(jnp.int32)
        return count

    used = lax.fori_loop(0, blocks, place, blocks)
    fine = pairs // blocks

    def clear(spot, carry):
        empty = jnp.zeros((blocks // 2, fine, pairs), jnp.float32)
        at = pl.ds(pl.multiple_of(spot * fine, fine), fine)
        mine_ref[:, at, :] = empty
        other_ref[:, at, :] = empty
        return carry

    lax.fori_loop(used, mine_ref.shape[1] // fine, clear, 0)
    group = 32

    def pick_block(block, rows_at):
        for base in range(0, 2 * pairs, group):
            rows = [wide[row_pair(own[block, base + k]), :] for k in range(group)]
            for k in range(group):
                rows_at[2 * (base + k) : 2 * (base + k + 1), :] = rows[k]
        at = pl.multiple_of(block * pairs, pairs)
        q_ref[pl.ds(at, pairs), :] = gathered(rows_at, 0, pairs).astype(jnp.bfloat16)
        d_ref[pl.ds(at, pairs), :] = gathered(rows_at, pairs, pairs).astype(jnp.bfloat16)

    ahead = -(-(window + 2) // 2)

    def pick_one(block, carry):
        pick_block(block, picked)
        return carry

    lax.fori_loop(0, 2 * ahead, pick_one, 0)
    even = lax.axis_index("pb") % 2 == 0
    spare = mine_ref.shape[1] // fine - 1

    def score_blocks(step, carry):
        at = pl.multiple_of(step * 2 * pairs, 2 * pairs)
        tiles = inverse_temp * lax.dot_general(
            q_ref[pl.ds(at, 2 * pairs), :],
            d_ref[pl.ds(at, (window + 2) * pairs), :],
            (((1,), (1,)), ((), ())),
            preferred_element_type=jnp.float32,
        )
        top = carry
        for half in range(2):
            for column in range(window + 1):
                spot = place_ref[column, 2 * step + half]
                row = pl.multiple_of(jnp.where(spot >= 0, spot, spare) * fine, fine)
                tile = tiles[
                    half * pairs : (half + 1) * pairs,
                    (half + column) * pairs : (half + column + 1) * pairs,
                ]
                parted = tile.reshape(blocks // 2, 2, fine, pairs)
                first, second = parted[:, 0], parted[:, 1]
                mine_ref[:, pl.ds(row, fine), :] = jnp.where(even, first, second)
                other_ref[:, pl.ds(row, fine), :] = jnp.where(even, second, first)
                size = jnp.maximum(jnp.abs(first), jnp.abs(second))
                top = jnp.maximum(top, jnp.max(size, axis=0))
        return top

    def score_and_pick(step, top):
        top = score_blocks(step - ahead, top)
        pick_block(2 * step, picked)
        pick_block(2 * step + 1, picked_too)
        return top

    top = jnp.zeros((fine, pairs), jnp.float32)
    top = lax.fori_loop(ahead, blocks // 2, score_and_pick, top)
    d_ref[blocks * pairs :, :] = d_ref[: window * pairs, :]
    top_ref[...] = lax.fori_loop(blocks // 2 - ahead, blocks // 2, score_blocks, top)


def score_call(embedded, room, blocks, pairs, window):
    _, rows, piece = embedded.shape
    fine = pairs // blocks
    whole = pl.BlockSpec(memory_space=pltpu.VMEM)
    scalars = pl.BlockSpec(memory_space=pltpu.SMEM)
    return pl.pallas_call(
        functools.partial(score_kernel, blocks, pairs, window),
        in_specs=[whole],
        out_specs=[whole, whole, whole, whole, whole, whole, scalars],
        out_shape=[
            jax.ShapeDtypeStruct((blocks * pairs, piece), jnp.bfloat16),
            jax.ShapeDtypeStruct(((blocks + window) * pairs, piece), jnp.bfloat16),
            jax.ShapeDtypeStruct((blocks // 2, (room + 1) * fine, pairs), jnp.float32),
            jax.ShapeDtypeStruct((blocks // 2, (room + 1) * fine, pairs), jnp.float32),
            jax.ShapeDtypeStruct((fine, pairs), jnp.float32),
            jax.ShapeDtypeStruct((blocks, 2 * pairs), jnp.int32),
            jax.ShapeDtypeStruct((window + 1, blocks), jnp.int32),
        ],
        scratch_shapes=[
            pltpu.VMEM((2 * blocks * (rows - 8), lanes), jnp.float32),
            pltpu.VMEM((4 * pairs, lanes), jnp.float32),
            pltpu.VMEM((4 * pairs, lanes), jnp.float32),
            pltpu.VMEM((blocks, lanes), jnp.int32),
            pltpu.SMEM((blocks, 2 * pairs), jnp.int32),
            pltpu.SMEM((blocks, lanes), jnp.int32),
            pltpu.SemaphoreType.DMA((2,)),
        ],
        compiler_params=pltpu.CompilerParams(vmem_limit_bytes=22 * mebibyte),
        name="partial_scores",
    )(embedded)


def coded(values, scale):
    return jnp.round(values * scale).astype(jnp.int32).astype(jnp.int16)


def decoded(codes, scale):
    return codes.astype(jnp.int32).astype(jnp.float32) * scale


def highest(values):
    return jnp.max(jnp.max(values, axis=1, keepdims=True), axis=0, keepdims=True)


def merge_kernel(mine_ref, other_ref, top_ref, other_top_ref, own_ref, *code_refs):
    _, rows, pairs = own_ref.shape
    steps = code_refs[0].shape[1] - 1
    fine = rows // steps // 2
    chip = lax.axis_index("pb") // 2
    across = mine_ref.shape[0] // 2
    top = jnp.minimum(highest(top_ref[...]) + highest(other_top_ref[...]), score_limit)
    bound = jnp.ceil(top * bound_steps) + 1.0
    scale = code_steps * bound_steps / bound
    sent_bound = jnp.broadcast_to(bound, (2 * fine, pairs)).astype(jnp.int32).astype(jnp.int16)
    for which in range(2):
        target = chip ^ (which * across)
        own_ref[which] = mine_ref[target, :rows] + other_ref[target, :rows]
        for hop, code_ref in enumerate(code_refs):
            near = target ^ (hop + 1)

            def encode(step, carry):
                there = pl.ds(pl.multiple_of(step * 2 * fine, 2 * fine), 2 * fine)
                values = mine_ref[near, there, :] + other_ref[near, there, :]
                code_ref[which, step] = coded(values, scale)
                return carry

            lax.fori_loop(0, steps, encode, 0)
            code_ref[which, steps] = sent_bound


def merge_call(mine, other, top, other_top, blocks):
    chips, rows, pairs = mine.shape
    fine = pairs // blocks
    rows = rows - fine
    whole = pl.BlockSpec(memory_space=pltpu.VMEM)
    codes = jax.ShapeDtypeStruct((2, rows // (2 * fine) + 1, 2 * fine, pairs), jnp.int16)
    near = chips // 2 - 1
    return pl.pallas_call(
        merge_kernel,
        in_specs=[whole] * 4,
        out_specs=[whole] * (near + 1),
        out_shape=[jax.ShapeDtypeStruct((2, rows, pairs), jnp.float32)] + [codes] * near,
        compiler_params=pltpu.CompilerParams(vmem_limit_bytes=12 * mebibyte),
        name="merge_scores",
    )(mine, other, top, other_top)


def half_kernel(own_ref, *refs):
    near_refs, (sum_ref, code_ref, sums) = refs[:-3], refs[-3:]
    steps, deep, pairs = code_ref.shape
    steps = steps - 1
    unit = 1.0 / (code_steps * bound_steps)
    scales = [decoded(ref[0, steps], unit) for ref in near_refs]

    def add(step, top):
        there = pl.ds(pl.multiple_of(step * deep, deep), deep)
        here, over = own_ref[0, there, :], own_ref[1, there, :]
        for ref, scale in zip(near_refs, scales):
            here = here + decoded(ref[0, step], scale)
            over = over + decoded(ref[1, step], scale)
        sum_ref[there, :] = here
        sums[there, :] = over
        return jnp.maximum(top, jnp.abs(over))

    top = lax.fori_loop(0, steps, add, jnp.zeros((deep, pairs), jnp.float32))
    bound = jnp.ceil(highest(top) * bound_steps) + 1.0
    scale = code_steps * bound_steps / bound

    def encode(step, carry):
        there = pl.ds(pl.multiple_of(step * deep, deep), deep)
        code_ref[step] = coded(sums[there, :], scale)
        return carry

    lax.fori_loop(0, steps, encode, 0)
    code_ref[steps] = jnp.broadcast_to(bound, (deep, pairs)).astype(jnp.int32).astype(jnp.int16)


def half_call(own, near):
    _, rows, pairs = own.shape
    whole = pl.BlockSpec(memory_space=pltpu.VMEM)
    return pl.pallas_call(
        half_kernel,
        in_specs=[whole] * (1 + len(near)),
        out_specs=[whole, whole],
        out_shape=[
            jax.ShapeDtypeStruct((rows, pairs), jnp.float32),
            jax.ShapeDtypeStruct(near[0].shape[1:], jnp.int16),
        ],
        scratch_shapes=[pltpu.VMEM((rows, pairs), jnp.float32)],
        compiler_params=pltpu.CompilerParams(vmem_limit_bytes=8 * mebibyte),
        name="half_scores",
    )(own, *near)


def softmax_kernel(blocks, window, place_ref, own_ref, *refs):
    code_refs, (c_ref, packed, masked) = refs[:-3], refs[-3:]
    room, fine, pairs = packed.shape
    count = blocks * fine
    unit = 1.0 / (code_steps * bound_steps)
    scales = [ref[room // 2].astype(jnp.int32).astype(jnp.float32) * unit for ref in code_refs]

    def decode(step, carry):
        both = own_ref[pl.ds(pl.multiple_of(step * 2 * fine, 2 * fine), 2 * fine), :]
        for ref, scale in zip(code_refs, scales):
            both = both + ref[step].astype(jnp.int32).astype(jnp.float32) * scale
        packed[2 * step] = both[:fine]
        packed[2 * step + 1] = both[fine:]
        return carry

    lax.fori_loop(0, room // 2, decode, 0)
    for block in range(blocks):
        for column in range(window + 1):
            spot = place_ref[column, block]
            tile = packed[jnp.maximum(spot, 0)]
            masked[block * fine : (block + 1) * fine, column * pairs : (column + 1) * pairs] = (
                jnp.where(spot >= 0, tile, -jnp.inf)
            )
    row = lax.broadcasted_iota(jnp.int32, (count, pairs), 0)
    lane = lax.broadcasted_iota(jnp.int32, (count, pairs), 1)
    target = lane == lax.axis_index("pb") * fine + row % fine
    pieces = [masked[:, column * pairs : (column + 1) * pairs] for column in range(window + 1)]
    row_max = jnp.max(functools.reduce(jnp.maximum, pieces), axis=1, keepdims=True)
    total = functools.reduce(jnp.add, [jnp.exp(piece - row_max) for piece in pieces])
    log_total = row_max + jnp.log(jnp.sum(total, axis=1, keepdims=True))
    positive = jnp.sum(jnp.where(target, pieces[0], 0.0), axis=1, keepdims=True)
    for column, piece in enumerate(pieces):
        share = jnp.exp(piece - log_total)
        if column == 0:
            share = share - jnp.where(target, 1.0, 0.0)
        masked[:, column * pairs : (column + 1) * pairs] = inverse_temp * share
    for block in range(blocks):
        for column in range(window + 1):
            spot = place_ref[column, block]

            @pl.when(spot >= 0)
            def _():
                packed[spot] = masked[
                    block * fine : (block + 1) * fine, column * pairs : (column + 1) * pairs
                ]

    for step in range(room // 2):
        both = jnp.concatenate([packed[2 * step], packed[2 * step + 1]], axis=0)
        c_ref[step] = both.astype(jnp.bfloat16)
    losses = jnp.sum(
        jnp.where(lane == row // fine, log_total - positive, 0.0), axis=0, keepdims=True
    )
    coarse = losses.astype(jnp.bfloat16).astype(jnp.float32)
    rank = lax.broadcasted_iota(jnp.int32, (2 * fine, pairs), 0)
    both = jnp.where(rank == 0, coarse, jnp.where(rank == 1, losses - coarse, 0.0))
    c_ref[room // 2] = both.astype(jnp.bfloat16)


def softmax_call(place, own_scores, codes, blocks, window):
    steps, fine, pairs = codes[0].shape
    room, fine = 2 * (steps - 1), fine // 2
    whole = pl.BlockSpec(memory_space=pltpu.VMEM)
    return pl.pallas_call(
        functools.partial(softmax_kernel, blocks, window),
        in_specs=[pl.BlockSpec(memory_space=pltpu.SMEM), whole] + [whole] * len(codes),
        out_specs=whole,
        out_shape=jax.ShapeDtypeStruct((room // 2 + 1, 2 * fine, pairs), jnp.bfloat16),
        scratch_shapes=[
            pltpu.VMEM((room, fine, pairs), jnp.float32),
            pltpu.VMEM((blocks * fine, (window + 1) * pairs), jnp.float32),
        ],
        compiler_params=pltpu.CompilerParams(vmem_limit_bytes=8 * mebibyte),
        name="softmax_rows",
    )(place, own_scores, *codes)


def grad_kernel(
    blocks,
    pairs,
    window,
    own_ref,
    place_ref,
    q_ref,
    d_ref,
    *refs,
):
    part_refs = refs[:-7]
    out_ref, loss_ref, wide, dsum, picked, packed, square = refs[-7:]
    fine = pairs // blocks
    room = packed.shape[1]
    me = lax.axis_index("pb")
    masks = swap_masks(blocks)
    group = 32
    losses = 0.0
    for part in part_refs:
        sent = part[:, room // 2].astype(jnp.float32)
        losses = losses + jnp.sum(sent[:, 0, :] + sent[:, 1, :], axis=0, keepdims=True) / pairs
    lane = lax.broadcasted_iota(jnp.int32, losses.shape, 1)
    mine = jnp.where(lane == me, losses, 0.0)
    loss_ref[...] = jnp.broadcast_to(jnp.sum(mine, axis=1, keepdims=True), loss_ref.shape)
    dsum[...] = jnp.zeros_like(dsum)
    square[...] = jnp.zeros_like(square)

    def unpack(step, carry):
        for part, mask in zip(part_refs, masks):
            both = part[:, step].astype(jnp.float32)
            for at, apart in enumerate(mask):
                packed[me ^ apart, 2 * step] = both[at, :fine]
                packed[me ^ apart, 2 * step + 1] = both[at, fine:]
        return carry

    lax.fori_loop(0, room // 2, unpack, 0)

    def scatter_rows(block, offset, start):
        for base in range(0, pairs, group):
            rows = [
                picked[2 * (start + base + k) : 2 * (start + base + k + 1), :] for k in range(group)
            ]
            for k in range(group):
                wide[row_pair(own_ref[block, offset + base + k]), :] = rows[k]

    def two_blocks(step, carry):
        for half in range(2):
            for column in range(window + 1):
                spot = place_ref[column, 2 * step + half]
                tile = packed[:, jnp.maximum(spot, 0)].reshape(pairs, pairs)
                square[
                    half * pairs : (half + 1) * pairs,
                    (half + column) * pairs : (half + column + 1) * pairs,
                ] = jnp.where(spot >= 0, tile, 0.0).astype(jnp.bfloat16)
        at = pl.multiple_of(step * 2 * pairs, 2 * pairs)
        there = pl.ds(at, (window + 2) * pairs)
        coefficients = square[...]
        summed = jnp.dot(coefficients, d_ref[there, :], preferred_element_type=jnp.float32)
        spread(picked, 0, summed)
        dsum[there, :] += lax.dot_general(
            coefficients,
            q_ref[pl.ds(at, 2 * pairs), :],
            (((0,), (0,)), ((), ())),
            preferred_element_type=jnp.float32,
        )
        for half in range(2):
            scatter_rows(2 * step + half, 0, half * pairs)
        return carry

    lax.fori_loop(0, blocks // 2, two_blocks, 0)
    dsum[: window * pairs, :] += dsum[blocks * pairs :, :]

    def doc_block(block, carry):
        at = pl.multiple_of(block * pairs, pairs)
        spread(picked, 0, dsum[pl.ds(at, pairs), :])
        scatter_rows(block, pairs, 0)
        return carry

    lax.fori_loop(0, blocks, doc_block, 0)
    slots = out_ref.shape[1]
    for part in range(blocks):
        out_ref[part] = gathered(wide, part * slots, slots).astype(jnp.bfloat16)


def grad_call(own, place, parts, queries, documents, blocks, pairs, window):
    count, piece = queries.shape
    seqs = 2 * count
    room = 2 * (parts[0].shape[1] - 1)
    whole = pl.BlockSpec(memory_space=pltpu.VMEM)
    scalars = pl.BlockSpec(memory_space=pltpu.SMEM)
    return pl.pallas_call(
        functools.partial(grad_kernel, blocks, pairs, window),
        in_specs=[scalars, scalars, whole, whole] + [whole] * len(parts),
        out_specs=[whole, whole],
        out_shape=[
            jax.ShapeDtypeStruct((blocks, seqs // blocks, piece), jnp.bfloat16),
            jax.ShapeDtypeStruct((1, lanes), jnp.float32),
        ],
        scratch_shapes=[
            pltpu.VMEM((2 * seqs, lanes), jnp.float32),
            pltpu.VMEM(((blocks + window) * pairs, piece), jnp.float32),
            pltpu.VMEM((4 * pairs, lanes), jnp.float32),
            pltpu.VMEM((blocks, room, pairs // blocks, pairs), jnp.float32),
            pltpu.VMEM((2 * pairs, (window + 2) * pairs), jnp.bfloat16),
        ],
        compiler_params=pltpu.CompilerParams(vmem_limit_bytes=26 * mebibyte),
        name="slice_grads",
    )(own, place, queries, documents, *parts)


def project_kernel(grad_ref, normed_ref, inv_ref, out_ref):
    parts, _, piece = grad_ref.shape
    cuts = [slice(part * piece, (part + 1) * piece) for part in range(parts)]
    inverse = inv_ref[:, :1]
    total = 0.0
    for part, cut in enumerate(cuts):
        unit = normed_ref[:, cut].astype(jnp.float32) * inverse
        total = total + unit * grad_ref[part].astype(jnp.float32)
    along = jnp.sum(total, axis=-1, keepdims=True)
    for part, cut in enumerate(cuts):
        unit = normed_ref[:, cut].astype(jnp.float32) * inverse
        out_ref[:, cut] = grad_ref[part].astype(jnp.float32) - unit * along


def project_call(returned, normed, inverse):
    parts, seqs, piece = returned.shape
    width = normed.shape[1]
    rows = 64
    return pl.pallas_call(
        project_kernel,
        grid=(seqs // rows,),
        in_specs=[
            pl.BlockSpec((parts, rows, piece), lambda i: (0, i, 0)),
            pl.BlockSpec((rows, width), lambda i: (i, 0)),
            pl.BlockSpec((rows, lanes), lambda i: (i, 0)),
        ],
        out_specs=pl.BlockSpec((rows, width), lambda i: (i, 0)),
        out_shape=jax.ShapeDtypeStruct((seqs, width), jnp.float32),
        compiler_params=pltpu.CompilerParams(vmem_limit_bytes=10 * mebibyte),
        name="project_out",
    )(returned, normed, inverse)


def swapped(value, apart):
    pairs = [(at, at ^ apart) for at in range(lax.axis_size("pb"))]
    return lax.ppermute(value, "pb", pairs)


def near_hops(devices):
    return [2 * hop for hop in reversed(range(1, devices // 4))]


def swap_masks(devices):
    near = [0] + near_hops(devices)
    held = near + [mask ^ (devices // 2) for mask in near]
    return [held, [mask ^ 1 for mask in held]]


def gather_all(value):
    devices = lax.axis_size("pb")
    own = value[None]
    across = swapped(own, devices // 2)
    held = [own] + [swapped(own, hop) for hop in near_hops(devices)]
    held += [across] + [swapped(across, hop) for hop in near_hops(devices)]
    held = jnp.concatenate(held, axis=0)
    return [held, swapped(held, 1)]


def middle(embedded, room, devices, pairs, window):
    queries, documents, mine, other, top, own, place = score_call(
        embedded, room, devices, pairs, window
    )
    own_scores, *codes = merge_call(mine, swapped(other, 1), top, swapped(top, 1), devices)
    near = [swapped(codes[hop], 2 * (hop + 1)) for hop in reversed(range(len(codes)))]
    own_scores, over = half_call(own_scores, near)
    codes = [swapped(over, devices // 2)]
    parts = gather_all(softmax_call(place, own_scores, codes, devices, window))
    grads, loss = grad_call(own, place, parts, queries, documents, devices, pairs, window)
    return grads, loss[0, :1]


def feature_plan(hidden, final_gain, last_row, pair_owner, hard_negatives):
    devices = lax.axis_size("pb")
    seqs, width = hidden.shape
    pairs = pair_owner.shape[0]
    window = hard_negatives.shape[1]
    normed, inverse, embedding = norm_call(
        last_row, hidden, final_gain, pair_owner.T, hard_negatives, devices
    )
    embedded = lax.all_to_all(embedding, "pb", split_axis=0, concat_axis=0, tiled=True)
    most = devices * (window + 1)
    rooms = [most * part // 20 for part in (11, 12, 13, 15, 20)]
    used = devices + jnp.sum(embedded[:, seqs + 2, :window].astype(jnp.float32))
    level = sum((used > room).astype(jnp.int32) for room in rooms[:-1])
    grads, loss = lax.switch(
        level,
        [
            functools.partial(middle, room=room, devices=devices, pairs=pairs, window=window)
            for room in rooms
        ],
        embedded,
    )
    returned = lax.all_to_all(grads, "pb", split_axis=0, concat_axis=0, tiled=True)
    return project_call(returned, normed, inverse), loss


def from_behind(value, axis, steps):
    count = lax.axis_size(axis)
    pairs = [(source, (source + steps) % count) for source in range(count)]
    return lax.ppermute(value, axis, pairs)


def similarity(queries, documents):
    return inverse_temp * lax.dot_general(
        queries, documents, (((1,), (1,)), ((), ())), preferred_element_type=jnp.float32
    )


def transposed(weights, queries):
    return lax.dot_general(
        weights, queries, (((0,), (0,)), ((), ())), preferred_element_type=jnp.float32
    )


def combine_docs(weights, documents):
    return jnp.dot(weights, documents, preferred_element_type=jnp.float32)


def skipped(listed, function, operands, out_shape):
    return lax.cond(
        listed,
        lambda inputs: function(*inputs),
        lambda inputs: jnp.zeros(out_shape, jnp.float32),
        operands,
    )


def row_plan(hidden, final_gain, last_row, pair_owner, hard_negatives):
    values = hidden.astype(jnp.float32)
    scale_row = lax.rsqrt(jnp.mean(values * values, axis=-1, keepdims=True) + token_eps)
    normed = (values * scale_row * final_gain.astype(jnp.float32)).astype(jnp.bfloat16)
    seq_count = last_row.shape[1]
    model_width = hidden.shape[1]
    pooled = normed[last_row[0]].astype(jnp.float32)
    inverse_norm = lax.rsqrt(jnp.sum(pooled * pooled, axis=-1, keepdims=True) + 1e-06)
    unit_vec = pooled * inverse_norm
    embedding = unit_vec.astype(jnp.bfloat16)
    devices = lax.axis_size("pb")
    capacity = 2 * seq_count // devices
    pair_count = pair_owner.shape[0]
    wanted = jnp.concatenate([pair_owner[:, 0], pair_owner[:, 1]])
    holder = wanted // seq_count
    within = wanted % seq_count
    entry_ids = jnp.arange(2 * pair_count, dtype=jnp.int32)
    earlier = (holder[None, :] == holder[:, None]) & (entry_ids[None, :] < entry_ids[:, None])
    position = jnp.sum(earlier.astype(jnp.int32), axis=1)
    request = jnp.full((devices, capacity), -1, jnp.int32).at[holder, position].set(within)
    served = lax.all_to_all(request, "pb", split_axis=0, concat_axis=0, tiled=True)
    outgoing = jnp.where(
        served[:, :, None] >= 0, embedding[jnp.maximum(served, 0)], jnp.zeros((), jnp.bfloat16)
    )
    received = lax.all_to_all(outgoing, "pb", split_axis=0, concat_axis=0, tiled=True)
    gathered = received[holder, position]
    queries = gathered[:pair_count]
    own_docs = gathered[pair_count:]
    listed_ids = hard_negatives[0]
    window = hard_negatives.shape[1]
    listed = [listed_ids[offset] >= 0 for offset in range(window)]
    neighbours = []
    moving = own_docs
    for offset in range(window):
        moving = from_behind(moving, "pb", -1)
        neighbours.append(moving)
    tile_shape = (pair_count, pair_count)
    score_blocks = [similarity(queries, own_docs)]
    for offset in range(window):
        score_blocks.append(
            skipped(listed[offset], similarity, (queries, neighbours[offset]), tile_shape)
        )
    all_scores = jnp.concatenate(score_blocks, axis=1)
    usable = jnp.concatenate(
        [jnp.ones((pair_count,), jnp.bool_)]
        + [jnp.broadcast_to(listed[offset], (pair_count,)) for offset in range(window)]
    )
    masked = jnp.where(usable[None, :], all_scores, -jnp.inf)
    row_max = jnp.max(masked, axis=1, keepdims=True)
    log_total = row_max + jnp.log(jnp.sum(jnp.exp(masked - row_max), axis=1, keepdims=True))
    diagonal = jnp.arange(pair_count, dtype=jnp.int32)
    positive = all_scores[diagonal, diagonal]
    block_loss = jnp.mean(log_total[:, 0] - positive).reshape(1)
    columns = jnp.arange((window + 1) * pair_count, dtype=jnp.int32)
    target = (columns[None, :] == diagonal[:, None]).astype(jnp.float32)
    coefficients = (inverse_temp * (jnp.exp(masked - log_total) - target)).astype(jnp.bfloat16)
    pieces = [
        coefficients[:, offset * pair_count : (offset + 1) * pair_count]
        for offset in range(window + 1)
    ]
    grad_shape = (pair_count, model_width)
    query_sum = combine_docs(pieces[0], own_docs)
    for offset in range(window):
        query_sum = query_sum + skipped(
            listed[offset], combine_docs, (pieces[offset + 1], neighbours[offset]), grad_shape
        )
    query_grad = query_sum.astype(jnp.bfloat16)
    own_part = transposed(pieces[0], queries).astype(jnp.bfloat16)
    partial_value = [
        skipped(listed[offset], transposed, (pieces[offset + 1], queries), grad_shape).astype(
            jnp.bfloat16
        )
        for offset in range(window)
    ]
    running = partial_value[window - 1].astype(jnp.float32)
    for offset in range(window):
        running = from_behind(running, "pb", 1)
        if offset + 1 < window:
            running = running + partial_value[window - 2 - offset].astype(jnp.float32)
    doc_grad = (own_part.astype(jnp.float32) + running).astype(jnp.bfloat16)
    answers = jnp.concatenate([query_grad, doc_grad], axis=0)
    returning = (
        jnp.zeros((devices, capacity, model_width), jnp.bfloat16).at[holder, position].set(answers)
    )
    returned = lax.all_to_all(returning, "pb", split_axis=0, concat_axis=0, tiled=True)
    slot_ids = jnp.where(served >= 0, served, seq_count).reshape(-1)
    emb_grad = (
        jnp.zeros((seq_count, model_width), jnp.bfloat16)
        .at[slot_ids]
        .set(returned.reshape(-1, model_width), mode="drop")
    )
    gradient = emb_grad.astype(jnp.float32)
    pooled_grad = gradient - unit_vec * jnp.sum(unit_vec * gradient, axis=-1, keepdims=True)
    return (pooled_grad, block_loss)


def solution(mesh):
    def local(hidden, final_gain, last_row, pair_owner, hard_negatives):
        plan = feature_plan if hidden.shape[1] >= lanes * mesh.shape["pb"] else row_plan
        return plan(hidden, final_gain, last_row, pair_owner, hard_negatives)

    return jax.shard_map(
        local,
        mesh=mesh,
        in_specs=(
            P(("groups", "pb"), None),
            P(),
            P(("groups", "pb"), None),
            P(("groups", "pb"), None),
            P(("groups", "pb"), None),
        ),
        out_specs=(P(("groups", "pb"), None), P(("groups", "pb"))),
        check_vma=False,
    )
```

```python
import functools

import jax
import jax.numpy as jnp
from jax import lax
from jax.experimental import pallas as pl
from jax.experimental.pallas import tpu as pltpu
from jax.sharding import PartitionSpec as P

inverse_temp = 50.0
token_eps = 1e-05
unit_eps = 1e-06
lanes = 128
bound_steps = 256.0
code_steps = 32000.0
score_limit = 51.0
mebibyte = 1024 * 1024


def spread(target, at, value):
    count = value.shape[0]
    for half in range(2):
        target[pl.ds(2 * at + half, count, stride=2), :] = value[:, half * lanes : (half + 1) * lanes]


def gathered(source, at, count):
    halves = [source[pl.ds(2 * at + half, count, stride=2), :] for half in range(2)]
    return jnp.concatenate(halves, axis=1)


def row_pair(place):
    return pl.ds(pl.multiple_of(place, 2), 2)


def norm_kernel(
    last_ref, hidden_ref, gain_ref, owner_ref, negative_ref, normed_ref, inv_ref, emb_ref
):
    seqs, width = normed_ref.shape
    parts, _, piece = emb_ref.shape
    pairs = owner_ref.shape[1]
    cuts = [slice(part * piece, (part + 1) * piece) for part in range(parts)]
    sources = lax.broadcasted_iota(jnp.int32, (seqs, seqs), 0)
    pick = jnp.where(sources == last_ref[...], 1.0, 0.0).astype(jnp.bfloat16)

    def folded(squares):
        return functools.reduce(
            jnp.add, [squares[:, at : at + lanes] for at in range(0, piece, lanes)]
        )

    total = jnp.zeros((seqs, lanes), jnp.float32)
    for cut in cuts:
        values = lax.dot_general(
            pick, hidden_ref[:, cut], (((0,), (0,)), ((), ())), preferred_element_type=jnp.float32
        )
        normed_ref[:, cut] = values.astype(jnp.bfloat16)
        total = total + folded(values * values)
    scale = lax.rsqrt(jnp.sum(total, axis=-1, keepdims=True) / width + token_eps)
    total = jnp.zeros((seqs, lanes), jnp.float32)
    for cut in cuts:
        values = normed_ref[:, cut].astype(jnp.float32)
        gain = gain_ref[cut].astype(jnp.float32).reshape(1, piece)
        normed = (values * scale * gain).astype(jnp.bfloat16)
        normed_ref[:, cut] = normed
        pooled = normed.astype(jnp.float32)
        total = total + folded(pooled * pooled)
    inverse = lax.rsqrt(jnp.sum(total, axis=-1, keepdims=True) + unit_eps)
    inv_ref[...] = jnp.broadcast_to(inverse, inv_ref.shape)

    owners = owner_ref[...].astype(jnp.float32)
    high = jnp.floor(owners * (1.0 / 256.0))
    low = owners - 256.0 * high
    row = lax.broadcasted_iota(jnp.int32, (8, pairs), 0)
    spot = lax.broadcasted_iota(jnp.int32, (8, pairs), 1)
    left = jnp.where(row == 0, low[:1], jnp.where(row == 1, high[:1], 0.0))
    right = jnp.where(row == 0, low[1:2], jnp.where(row == 1, high[1:2], 0.0))
    for offset in range(negative_ref.shape[1]):
        named = (negative_ref[0, offset] >= 0).astype(jnp.float32)
        left = jnp.where((row == 2) & (spot == offset), named, left)
    facts = jnp.concatenate([left, right], axis=1).astype(jnp.bfloat16)

    for part, cut in enumerate(cuts):
        emb_ref[part, :seqs] = (normed_ref[:, cut].astype(jnp.float32) * inverse).astype(jnp.bfloat16)
        emb_ref[part, seqs:] = facts


def norm_call(last_row, hidden, gain, owners, hard_negatives, parts):
    seqs, width = hidden.shape
    piece = width // parts
    whole = pl.BlockSpec(memory_space=pltpu.VMEM)
    return pl.pallas_call(
        norm_kernel,
        in_specs=[whole, whole, whole, whole, pl.BlockSpec(memory_space=pltpu.SMEM)],
        out_specs=[whole] * 3,
        out_shape=[
            jax.ShapeDtypeStruct((seqs, width), jnp.bfloat16),
            jax.ShapeDtypeStruct((seqs, lanes), jnp.float32),
            jax.ShapeDtypeStruct((parts, seqs + 8, piece), jnp.bfloat16),
        ],
        compiler_params=pltpu.CompilerParams(vmem_limit_bytes=56 * mebibyte),
        name="norm_rows",
    )(last_row, hidden, gain, owners, hard_negatives)


def score_kernel(
    blocks,
    pairs,
    window,
    *refs,
):
    emb_ref, q_ref, d_ref, mine_ref, other_ref, top_ref, own_ref, place_ref = refs[:-7]
    wide, picked, picked_too, facts, own, named, sems = refs[-7:]
    seqs = emb_ref.shape[1] - 8
    sent = emb_ref[:, seqs:, :].astype(jnp.float32)
    own_ref[...] = (2.0 * sent[:, 0, :] + 512.0 * sent[:, 1, :]).astype(jnp.int32)
    facts[...] = sent[:, 2, :lanes].astype(jnp.int32)
    fetches = [
        pltpu.make_async_copy(own_ref, own, sems.at[0]),
        pltpu.make_async_copy(facts, named, sems.at[1]),
    ]
    for fetch in fetches:
        fetch.start()

    for part in range(blocks):
        spread(wide, part * seqs, emb_ref[part, :seqs, :].astype(jnp.float32))
    for fetch in fetches:
        fetch.wait()

    def place(block, count):
        place_ref[0, block] = block
        for offset in range(window):
            present = named[block, offset] > 0
            place_ref[offset + 1, block] = jnp.where(present, count, -1)
            count = count + present.astype(jnp.int32)
        return count

    used = lax.fori_loop(0, blocks, place, blocks)
    fine = pairs // blocks

    def clear(spot, carry):
        empty = jnp.zeros((blocks // 2, fine, pairs), jnp.float32)
        at = pl.ds(pl.multiple_of(spot * fine, fine), fine)
        mine_ref[:, at, :] = empty
        other_ref[:, at, :] = empty
        return carry

    lax.fori_loop(used, mine_ref.shape[1] // fine, clear, 0)
    group = 32

    def pick_block(block, rows_at):
        for base in range(0, 2 * pairs, group):
            rows = [wide[row_pair(own[block, base + k]), :] for k in range(group)]
            for k in range(group):
                rows_at[2 * (base + k) : 2 * (base + k + 1), :] = rows[k]
        at = pl.multiple_of(block * pairs, pairs)
        q_ref[pl.ds(at, pairs), :] = gathered(rows_at, 0, pairs).astype(jnp.bfloat16)
        d_ref[pl.ds(at, pairs), :] = gathered(rows_at, pairs, pairs).astype(jnp.bfloat16)

    ahead = -(-(window + 2) // 2)

    def pick_one(block, carry):
        pick_block(block, picked)
        return carry

    lax.fori_loop(0, 2 * ahead, pick_one, 0)
    even = lax.axis_index("pb") % 2 == 0
    spare = mine_ref.shape[1] // fine - 1

    def score_blocks(step, carry):
        at = pl.multiple_of(step * 2 * pairs, 2 * pairs)
        tiles = inverse_temp * lax.dot_general(
            q_ref[pl.ds(at, 2 * pairs), :],
            d_ref[pl.ds(at, (window + 2) * pairs), :],
            (((1,), (1,)), ((), ())),
            preferred_element_type=jnp.float32,
        )
        top = carry
        for half in range(2):
            for column in range(window + 1):
                spot = place_ref[column, 2 * step + half]
                row = pl.multiple_of(jnp.where(spot >= 0, spot, spare) * fine, fine)
                tile = tiles[
                    half * pairs : (half + 1) * pairs,
                    (half + column) * pairs : (half + column + 1) * pairs,
                ]
                parted = tile.reshape(blocks // 2, 2, fine, pairs)
                first, second = parted[:, 0], parted[:, 1]
                mine_ref[:, pl.ds(row, fine), :] = jnp.where(even, first, second)
                other_ref[:, pl.ds(row, fine), :] = jnp.where(even, second, first)
                size = jnp.maximum(jnp.abs(first), jnp.abs(second))
                top = jnp.maximum(top, jnp.max(size, axis=0))
        return top

    def score_and_pick(step, top):
        top = score_blocks(step - ahead, top)
        pick_block(2 * step, picked)
        pick_block(2 * step + 1, picked_too)
        return top

    top = jnp.zeros((fine, pairs), jnp.float32)
    top = lax.fori_loop(ahead, blocks // 2, score_and_pick, top)
    d_ref[blocks * pairs :, :] = d_ref[: window * pairs, :]
    top_ref[...] = lax.fori_loop(blocks // 2 - ahead, blocks // 2, score_blocks, top)


def score_call(embedded, room, blocks, pairs, window):
    _, rows, piece = embedded.shape
    fine = pairs // blocks
    whole = pl.BlockSpec(memory_space=pltpu.VMEM)
    scalars = pl.BlockSpec(memory_space=pltpu.SMEM)
    return pl.pallas_call(
        functools.partial(score_kernel, blocks, pairs, window),
        in_specs=[whole],
        out_specs=[whole, whole, whole, whole, whole, whole, scalars],
        out_shape=[
            jax.ShapeDtypeStruct((blocks * pairs, piece), jnp.bfloat16),
            jax.ShapeDtypeStruct(((blocks + window) * pairs, piece), jnp.bfloat16),
            jax.ShapeDtypeStruct((blocks // 2, (room + 1) * fine, pairs), jnp.float32),
            jax.ShapeDtypeStruct((blocks // 2, (room + 1) * fine, pairs), jnp.float32),
            jax.ShapeDtypeStruct((fine, pairs), jnp.float32),
            jax.ShapeDtypeStruct((blocks, 2 * pairs), jnp.int32),
            jax.ShapeDtypeStruct((window + 1, blocks), jnp.int32),
        ],
        scratch_shapes=[
            pltpu.VMEM((2 * blocks * (rows - 8), lanes), jnp.float32),
            pltpu.VMEM((4 * pairs, lanes), jnp.float32),
            pltpu.VMEM((4 * pairs, lanes), jnp.float32),
            pltpu.VMEM((blocks, lanes), jnp.int32),
            pltpu.SMEM((blocks, 2 * pairs), jnp.int32),
            pltpu.SMEM((blocks, lanes), jnp.int32),
            pltpu.SemaphoreType.DMA((2,)),
        ],
        compiler_params=pltpu.CompilerParams(vmem_limit_bytes=22 * mebibyte),
        name="partial_scores",
    )(embedded)


def coded(values, scale):
    return jnp.round(values * scale).astype(jnp.int32).astype(jnp.int16)


def decoded(codes, scale):
    return codes.astype(jnp.int32).astype(jnp.float32) * scale


def highest(values):
    return jnp.max(jnp.max(values, axis=1, keepdims=True), axis=0, keepdims=True)


def merge_kernel(mine_ref, other_ref, top_ref, other_top_ref, own_ref, over_ref, *code_refs):
    rows, pairs = own_ref.shape
    steps = code_refs[0].shape[0] - 1
    fine = rows // steps // 2
    chip = lax.axis_index("pb") // 2
    across = mine_ref.shape[0] // 2
    top = jnp.minimum(highest(top_ref[...]) + highest(other_top_ref[...]), score_limit)
    bound = jnp.ceil(top * bound_steps) + 1.0
    scale = code_steps * bound_steps / bound
    sent_bound = jnp.broadcast_to(bound, (2 * fine, pairs)).astype(jnp.int32).astype(jnp.int16)
    near = len(code_refs) // 2
    for target, sum_ref, refs in (
        (chip ^ across, over_ref, code_refs[:near]),
        (chip, own_ref, code_refs[near:]),
    ):
        sum_ref[...] = mine_ref[target, :rows] + other_ref[target, :rows]
        for hop, code_ref in enumerate(refs):
            whose = target ^ (hop + 1)

            def encode(step, carry):
                there = pl.ds(pl.multiple_of(step * 2 * fine, 2 * fine), 2 * fine)
                values = mine_ref[whose, there, :] + other_ref[whose, there, :]
                code_ref[step] = coded(values, scale)
                return carry

            lax.fori_loop(0, steps, encode, 0)
            code_ref[steps] = sent_bound


def merge_call(mine, other, top, other_top, blocks):
    chips, rows, pairs = mine.shape
    fine = pairs // blocks
    rows = rows - fine
    whole = pl.BlockSpec(memory_space=pltpu.VMEM)
    codes = jax.ShapeDtypeStruct((rows // (2 * fine) + 1, 2 * fine, pairs), jnp.int16)
    near = chips // 2 - 1
    return pl.pallas_call(
        merge_kernel,
        in_specs=[whole] * 4,
        out_specs=[whole] * (2 * near + 2),
        out_shape=[jax.ShapeDtypeStruct((rows, pairs), jnp.float32)] * 2 + [codes] * (2 * near),
        compiler_params=pltpu.CompilerParams(vmem_limit_bytes=12 * mebibyte),
        name="merge_scores",
    )(mine, other, top, other_top)


def half_kernel(over_ref, *refs):
    near_refs, (code_ref, sums) = refs[:-2], refs[-2:]
    steps, deep, pairs = code_ref.shape
    steps = steps - 1
    unit = 1.0 / (code_steps * bound_steps)
    scales = [decoded(ref[steps], unit) for ref in near_refs]

    def add(step, top):
        there = pl.ds(pl.multiple_of(step * deep, deep), deep)
        over = over_ref[there, :]
        for ref, scale in zip(near_refs, scales):
            over = over + decoded(ref[step], scale)
        sums[there, :] = over
        return jnp.maximum(top, jnp.abs(over))

    top = lax.fori_loop(0, steps, add, jnp.zeros((deep, pairs), jnp.float32))
    bound = jnp.ceil(highest(top) * bound_steps) + 1.0
    scale = code_steps * bound_steps / bound

    def encode(step, carry):
        there = pl.ds(pl.multiple_of(step * deep, deep), deep)
        code_ref[step] = coded(sums[there, :], scale)
        return carry

    lax.fori_loop(0, steps, encode, 0)
    code_ref[steps] = jnp.broadcast_to(bound, (deep, pairs)).astype(jnp.int32).astype(jnp.int16)


def half_call(over, near):
    whole = pl.BlockSpec(memory_space=pltpu.VMEM)
    return pl.pallas_call(
        half_kernel,
        in_specs=[whole] * (1 + len(near)),
        out_specs=whole,
        out_shape=jax.ShapeDtypeStruct(near[0].shape, jnp.int16),
        scratch_shapes=[pltpu.VMEM(over.shape, jnp.float32)],
        compiler_params=pltpu.CompilerParams(vmem_limit_bytes=8 * mebibyte),
        name="half_scores",
    )(over, *near)


def softmax_kernel(blocks, window, place_ref, own_ref, *refs):
    code_refs, (c_ref, packed, masked) = refs[:-3], refs[-3:]
    room, fine, pairs = packed.shape
    count = blocks * fine
    unit = 1.0 / (code_steps * bound_steps)
    scales = [ref[room // 2].astype(jnp.int32).astype(jnp.float32) * unit for ref in code_refs]

    def decode(step, carry):
        both = own_ref[pl.ds(pl.multiple_of(step * 2 * fine, 2 * fine), 2 * fine), :]
        for ref, scale in zip(code_refs, scales):
            both = both + ref[step].astype(jnp.int32).astype(jnp.float32) * scale
        packed[2 * step] = both[:fine]
        packed[2 * step + 1] = both[fine:]
        return carry

    lax.fori_loop(0, room // 2, decode, 0)
    for block in range(blocks):
        for column in range(window + 1):
            spot = place_ref[column, block]
            tile = packed[jnp.maximum(spot, 0)]
            masked[block * fine : (block + 1) * fine, column * pairs : (column + 1) * pairs] = (
                jnp.where(spot >= 0, tile, -jnp.inf)
            )
    row = lax.broadcasted_iota(jnp.int32, (count, pairs), 0)
    lane = lax.broadcasted_iota(jnp.int32, (count, pairs), 1)
    target = lane == lax.axis_index("pb") * fine + row % fine
    pieces = [masked[:, column * pairs : (column + 1) * pairs] for column in range(window + 1)]
    row_max = jnp.max(functools.reduce(jnp.maximum, pieces), axis=1, keepdims=True)
    total = functools.reduce(jnp.add, [jnp.exp(piece - row_max) for piece in pieces])
    log_total = row_max + jnp.log(jnp.sum(total, axis=1, keepdims=True))
    positive = jnp.sum(jnp.where(target, pieces[0], 0.0), axis=1, keepdims=True)
    for column, piece in enumerate(pieces):
        share = jnp.exp(piece - log_total)
        if column == 0:
            share = share - jnp.where(target, 1.0, 0.0)
        masked[:, column * pairs : (column + 1) * pairs] = inverse_temp * share
    for block in range(blocks):
        for column in range(window + 1):
            spot = place_ref[column, block]

            @pl.when(spot >= 0)
            def _():
                packed[spot] = masked[
                    block * fine : (block + 1) * fine, column * pairs : (column + 1) * pairs
                ]

    for step in range(room // 2):
        both = jnp.concatenate([packed[2 * step], packed[2 * step + 1]], axis=0)
        c_ref[step] = both.astype(jnp.bfloat16)
    losses = jnp.sum(
        jnp.where(lane == row // fine, log_total - positive, 0.0), axis=0, keepdims=True
    )
    coarse = losses.astype(jnp.bfloat16).astype(jnp.float32)
    rank = lax.broadcasted_iota(jnp.int32, (2 * fine, pairs), 0)
    both = jnp.where(rank == 0, coarse, jnp.where(rank == 1, losses - coarse, 0.0))
    c_ref[room // 2] = both.astype(jnp.bfloat16)


def softmax_call(place, own_scores, codes, blocks, window):
    steps, fine, pairs = codes[0].shape
    room, fine = 2 * (steps - 1), fine // 2
    whole = pl.BlockSpec(memory_space=pltpu.VMEM)
    return pl.pallas_call(
        functools.partial(softmax_kernel, blocks, window),
        in_specs=[pl.BlockSpec(memory_space=pltpu.SMEM), whole] + [whole] * len(codes),
        out_specs=whole,
        out_shape=jax.ShapeDtypeStruct((room // 2 + 1, 2 * fine, pairs), jnp.bfloat16),
        scratch_shapes=[
            pltpu.VMEM((room, fine, pairs), jnp.float32),
            pltpu.VMEM((blocks * fine, (window + 1) * pairs), jnp.float32),
        ],
        compiler_params=pltpu.CompilerParams(vmem_limit_bytes=8 * mebibyte),
        name="softmax_rows",
    )(place, own_scores, *codes)


def grad_kernel(
    blocks,
    pairs,
    window,
    own_ref,
    place_ref,
    q_ref,
    d_ref,
    *refs,
):
    part_refs = refs[:-7]
    out_ref, loss_ref, wide, dsum, picked, packed, square = refs[-7:]
    fine = pairs // blocks
    room = packed.shape[1]
    me = lax.axis_index("pb")
    masks = swap_masks(blocks)
    group = 32
    losses = 0.0
    for part in part_refs:
        sent = part[:, room // 2].astype(jnp.float32)
        losses = losses + jnp.sum(sent[:, 0, :] + sent[:, 1, :], axis=0, keepdims=True) / pairs
    lane = lax.broadcasted_iota(jnp.int32, losses.shape, 1)
    mine = jnp.where(lane == me, losses, 0.0)
    loss_ref[...] = jnp.broadcast_to(jnp.sum(mine, axis=1, keepdims=True), loss_ref.shape)
    dsum[...] = jnp.zeros_like(dsum)
    square[...] = jnp.zeros_like(square)

    def unpack(step, carry):
        for part, mask in zip(part_refs, masks):
            both = part[:, step].astype(jnp.float32)
            for at, apart in enumerate(mask):
                packed[me ^ apart, 2 * step] = both[at, :fine]
                packed[me ^ apart, 2 * step + 1] = both[at, fine:]
        return carry

    lax.fori_loop(0, room // 2, unpack, 0)

    def scatter_rows(block, offset, start):
        for base in range(0, pairs, group):
            rows = [
                picked[2 * (start + base + k) : 2 * (start + base + k + 1), :] for k in range(group)
            ]
            for k in range(group):
                wide[row_pair(own_ref[block, offset + base + k]), :] = rows[k]

    def two_blocks(step, carry):
        for half in range(2):
            for column in range(window + 1):
                spot = place_ref[column, 2 * step + half]
                tile = packed[:, jnp.maximum(spot, 0)].reshape(pairs, pairs)
                square[
                    half * pairs : (half + 1) * pairs,
                    (half + column) * pairs : (half + column + 1) * pairs,
                ] = jnp.where(spot >= 0, tile, 0.0).astype(jnp.bfloat16)
        at = pl.multiple_of(step * 2 * pairs, 2 * pairs)
        there = pl.ds(at, (window + 2) * pairs)
        coefficients = square[...]
        summed = jnp.dot(coefficients, d_ref[there, :], preferred_element_type=jnp.float32)
        spread(picked, 0, summed)
        dsum[there, :] += lax.dot_general(
            coefficients,
            q_ref[pl.ds(at, 2 * pairs), :],
            (((0,), (0,)), ((), ())),
            preferred_element_type=jnp.float32,
        )
        for half in range(2):
            scatter_rows(2 * step + half, 0, half * pairs)
        return carry

    lax.fori_loop(0, blocks // 2, two_blocks, 0)
    dsum[: window * pairs, :] += dsum[blocks * pairs :, :]

    def doc_block(block, carry):
        at = pl.multiple_of(block * pairs, pairs)
        spread(picked, 0, dsum[pl.ds(at, pairs), :])
        scatter_rows(block, pairs, 0)
        return carry

    lax.fori_loop(0, blocks, doc_block, 0)
    slots = out_ref.shape[1]
    for part in range(blocks):
        out_ref[part] = gathered(wide, part * slots, slots).astype(jnp.bfloat16)


def grad_call(own, place, parts, queries, documents, blocks, pairs, window):
    count, piece = queries.shape
    seqs = 2 * count
    room = 2 * (parts[0].shape[1] - 1)
    whole = pl.BlockSpec(memory_space=pltpu.VMEM)
    scalars = pl.BlockSpec(memory_space=pltpu.SMEM)
    return pl.pallas_call(
        functools.partial(grad_kernel, blocks, pairs, window),
        in_specs=[scalars, scalars, whole, whole] + [whole] * len(parts),
        out_specs=[whole, whole],
        out_shape=[
            jax.ShapeDtypeStruct((blocks, seqs // blocks, piece), jnp.bfloat16),
            jax.ShapeDtypeStruct((1, lanes), jnp.float32),
        ],
        scratch_shapes=[
            pltpu.VMEM((2 * seqs, lanes), jnp.float32),
            pltpu.VMEM(((blocks + window) * pairs, piece), jnp.float32),
            pltpu.VMEM((4 * pairs, lanes), jnp.float32),
            pltpu.VMEM((blocks, room, pairs // blocks, pairs), jnp.float32),
            pltpu.VMEM((2 * pairs, (window + 2) * pairs), jnp.bfloat16),
        ],
        compiler_params=pltpu.CompilerParams(vmem_limit_bytes=26 * mebibyte),
        name="slice_grads",
    )(own, place, queries, documents, *parts)


def project_kernel(grad_ref, normed_ref, inv_ref, out_ref):
    parts, _, piece = grad_ref.shape
    cuts = [slice(part * piece, (part + 1) * piece) for part in range(parts)]
    inverse = inv_ref[:, :1]
    total = 0.0
    for part, cut in enumerate(cuts):
        unit = normed_ref[:, cut].astype(jnp.float32) * inverse
        total = total + unit * grad_ref[part].astype(jnp.float32)
    along = jnp.sum(total, axis=-1, keepdims=True)
    for part, cut in enumerate(cuts):
        unit = normed_ref[:, cut].astype(jnp.float32) * inverse
        out_ref[:, cut] = grad_ref[part].astype(jnp.float32) - unit * along


def project_call(returned, normed, inverse):
    parts, seqs, piece = returned.shape
    width = normed.shape[1]
    rows = 64
    return pl.pallas_call(
        project_kernel,
        grid=(seqs // rows,),
        in_specs=[
            pl.BlockSpec((parts, rows, piece), lambda i: (0, i, 0)),
            pl.BlockSpec((rows, width), lambda i: (i, 0)),
            pl.BlockSpec((rows, lanes), lambda i: (i, 0)),
        ],
        out_specs=pl.BlockSpec((rows, width), lambda i: (i, 0)),
        out_shape=jax.ShapeDtypeStruct((seqs, width), jnp.float32),
        compiler_params=pltpu.CompilerParams(vmem_limit_bytes=10 * mebibyte),
        name="project_out",
    )(returned, normed, inverse)


def swapped(value, apart):
    pairs = [(at, at ^ apart) for at in range(lax.axis_size("pb"))]
    return lax.ppermute(value, "pb", pairs)


def near_hops(devices):
    return [2 * hop for hop in reversed(range(1, devices // 4))]


def swap_masks(devices):
    near = [0] + near_hops(devices)
    held = near + [mask ^ (devices // 2) for mask in near]
    return [held, [mask ^ 1 for mask in held]]


def gather_all(value):
    devices = lax.axis_size("pb")
    own = value[None]
    across = swapped(own, devices // 2)
    held = [own] + [swapped(own, hop) for hop in near_hops(devices)]
    held += [across] + [swapped(across, hop) for hop in near_hops(devices)]
    held = jnp.concatenate(held, axis=0)
    return [held, swapped(held, 1)]


def middle(embedded, room, devices, pairs, window):
    queries, documents, mine, other, top, own, place = score_call(
        embedded, room, devices, pairs, window
    )
    own_scores, over, *codes = merge_call(mine, swapped(other, 1), top, swapped(top, 1), devices)
    hops = near_hops(devices)
    half = len(hops)
    far = [swapped(codes[hop // 2 - 1], hop) for hop in hops]
    near = [swapped(codes[half + hop // 2 - 1], hop) for hop in hops]
    codes = near + [swapped(half_call(over, far), devices // 2)]
    parts = gather_all(softmax_call(place, own_scores, codes, devices, window))
    grads, loss = grad_call(own, place, parts, queries, documents, devices, pairs, window)
    return grads, loss[0, :1]


def feature_plan(hidden, final_gain, last_row, pair_owner, hard_negatives):
    devices = lax.axis_size("pb")
    seqs, width = hidden.shape
    pairs = pair_owner.shape[0]
    window = hard_negatives.shape[1]
    normed, inverse, embedding = norm_call(
        last_row, hidden, final_gain, pair_owner.T, hard_negatives, devices
    )
    embedded = lax.all_to_all(embedding, "pb", split_axis=0, concat_axis=0, tiled=True)
    most = devices * (window + 1)
    rooms = [most * part // 20 for part in (11, 12, 13, 15, 20)]
    used = devices + jnp.sum(embedded[:, seqs + 2, :window].astype(jnp.float32))
    level = sum((used > room).astype(jnp.int32) for room in rooms[:-1])
    grads, loss = lax.switch(
        level,
        [
            functools.partial(middle, room=room, devices=devices, pairs=pairs, window=window)
            for room in rooms
        ],
        embedded,
    )
    returned = lax.all_to_all(grads, "pb", split_axis=0, concat_axis=0, tiled=True)
    return project_call(returned, normed, inverse), loss


def from_behind(value, axis, steps):
    count = lax.axis_size(axis)
    pairs = [(source, (source + steps) % count) for source in range(count)]
    return lax.ppermute(value, axis, pairs)


def similarity(queries, documents):
    return inverse_temp * lax.dot_general(
        queries, documents, (((1,), (1,)), ((), ())), preferred_element_type=jnp.float32
    )


def transposed(weights, queries):
    return lax.dot_general(
        weights, queries, (((0,), (0,)), ((), ())), preferred_element_type=jnp.float32
    )


def combine_docs(weights, documents):
    return jnp.dot(weights, documents, preferred_element_type=jnp.float32)


def skipped(listed, function, operands, out_shape):
    return lax.cond(
        listed,
        lambda inputs: function(*inputs),
        lambda inputs: jnp.zeros(out_shape, jnp.float32),
        operands,
    )


def row_plan(hidden, final_gain, last_row, pair_owner, hard_negatives):
    values = hidden.astype(jnp.float32)
    scale_row = lax.rsqrt(jnp.mean(values * values, axis=-1, keepdims=True) + token_eps)
    normed = (values * scale_row * final_gain.astype(jnp.float32)).astype(jnp.bfloat16)
    seq_count = last_row.shape[1]
    model_width = hidden.shape[1]
    pooled = normed[last_row[0]].astype(jnp.float32)
    inverse_norm = lax.rsqrt(jnp.sum(pooled * pooled, axis=-1, keepdims=True) + 1e-06)
    unit_vec = pooled * inverse_norm
    embedding = unit_vec.astype(jnp.bfloat16)
    devices = lax.axis_size("pb")
    capacity = 2 * seq_count // devices
    pair_count = pair_owner.shape[0]
    wanted = jnp.concatenate([pair_owner[:, 0], pair_owner[:, 1]])
    holder = wanted // seq_count
    within = wanted % seq_count
    entry_ids = jnp.arange(2 * pair_count, dtype=jnp.int32)
    earlier = (holder[None, :] == holder[:, None]) & (entry_ids[None, :] < entry_ids[:, None])
    position = jnp.sum(earlier.astype(jnp.int32), axis=1)
    request = jnp.full((devices, capacity), -1, jnp.int32).at[holder, position].set(within)
    served = lax.all_to_all(request, "pb", split_axis=0, concat_axis=0, tiled=True)
    outgoing = jnp.where(
        served[:, :, None] >= 0, embedding[jnp.maximum(served, 0)], jnp.zeros((), jnp.bfloat16)
    )
    received = lax.all_to_all(outgoing, "pb", split_axis=0, concat_axis=0, tiled=True)
    gathered = received[holder, position]
    queries = gathered[:pair_count]
    own_docs = gathered[pair_count:]
    listed_ids = hard_negatives[0]
    window = hard_negatives.shape[1]
    listed = [listed_ids[offset] >= 0 for offset in range(window)]
    neighbours = []
    moving = own_docs
    for offset in range(window):
        moving = from_behind(moving, "pb", -1)
        neighbours.append(moving)
    tile_shape = (pair_count, pair_count)
    score_blocks = [similarity(queries, own_docs)]
    for offset in range(window):
        score_blocks.append(
            skipped(listed[offset], similarity, (queries, neighbours[offset]), tile_shape)
        )
    all_scores = jnp.concatenate(score_blocks, axis=1)
    usable = jnp.concatenate(
        [jnp.ones((pair_count,), jnp.bool_)]
        + [jnp.broadcast_to(listed[offset], (pair_count,)) for offset in range(window)]
    )
    masked = jnp.where(usable[None, :], all_scores, -jnp.inf)
    row_max = jnp.max(masked, axis=1, keepdims=True)
    log_total = row_max + jnp.log(jnp.sum(jnp.exp(masked - row_max), axis=1, keepdims=True))
    diagonal = jnp.arange(pair_count, dtype=jnp.int32)
    positive = all_scores[diagonal, diagonal]
    block_loss = jnp.mean(log_total[:, 0] - positive).reshape(1)
    columns = jnp.arange((window + 1) * pair_count, dtype=jnp.int32)
    target = (columns[None, :] == diagonal[:, None]).astype(jnp.float32)
    coefficients = (inverse_temp * (jnp.exp(masked - log_total) - target)).astype(jnp.bfloat16)
    pieces = [
        coefficients[:, offset * pair_count : (offset + 1) * pair_count]
        for offset in range(window + 1)
    ]
    grad_shape = (pair_count, model_width)
    query_sum = combine_docs(pieces[0], own_docs)
    for offset in range(window):
        query_sum = query_sum + skipped(
            listed[offset], combine_docs, (pieces[offset + 1], neighbours[offset]), grad_shape
        )
    query_grad = query_sum.astype(jnp.bfloat16)
    own_part = transposed(pieces[0], queries).astype(jnp.bfloat16)
    partial_value = [
        skipped(listed[offset], transposed, (pieces[offset + 1], queries), grad_shape).astype(
            jnp.bfloat16
        )
        for offset in range(window)
    ]
    running = partial_value[window - 1].astype(jnp.float32)
    for offset in range(window):
        running = from_behind(running, "pb", 1)
        if offset + 1 < window:
            running = running + partial_value[window - 2 - offset].astype(jnp.float32)
    doc_grad = (own_part.astype(jnp.float32) + running).astype(jnp.bfloat16)
    answers = jnp.concatenate([query_grad, doc_grad], axis=0)
    returning = (
        jnp.zeros((devices, capacity, model_width), jnp.bfloat16).at[holder, position].set(answers)
    )
    returned = lax.all_to_all(returning, "pb", split_axis=0, concat_axis=0, tiled=True)
    slot_ids = jnp.where(served >= 0, served, seq_count).reshape(-1)
    emb_grad = (
        jnp.zeros((seq_count, model_width), jnp.bfloat16)
        .at[slot_ids]
        .set(returned.reshape(-1, model_width), mode="drop")
    )
    gradient = emb_grad.astype(jnp.float32)
    pooled_grad = gradient - unit_vec * jnp.sum(unit_vec * gradient, axis=-1, keepdims=True)
    return (pooled_grad, block_loss)


def solution(mesh):
    def local(hidden, final_gain, last_row, pair_owner, hard_negatives):
        plan = feature_plan if hidden.shape[1] >= lanes * mesh.shape["pb"] else row_plan
        return plan(hidden, final_gain, last_row, pair_owner, hard_negatives)

    return jax.shard_map(
        local,
        mesh=mesh,
        in_specs=(
            P(("groups", "pb"), None),
            P(),
            P(("groups", "pb"), None),
            P(("groups", "pb"), None),
            P(("groups", "pb"), None),
        ),
        out_specs=(P(("groups", "pb"), None), P(("groups", "pb"))),
        check_vma=False,
    )
```

```python
import functools

import jax
import jax.numpy as jnp
from jax import lax
from jax.experimental import pallas as pl
from jax.experimental.pallas import tpu as pltpu
from jax.sharding import PartitionSpec as P

inverse_temp = 50.0
token_eps = 1e-05
unit_eps = 1e-06
lanes = 128
bound_steps = 256.0
code_steps = 32000.0
score_limit = 51.0
mebibyte = 1024 * 1024


def spread(target, at, value):
    count = value.shape[0]
    for half in range(2):
        target[pl.ds(2 * at + half, count, stride=2), :] = value[:, half * lanes : (half + 1) * lanes]


def gathered(source, at, count):
    halves = [source[pl.ds(2 * at + half, count, stride=2), :] for half in range(2)]
    return jnp.concatenate(halves, axis=1)


def row_pair(place):
    return pl.ds(pl.multiple_of(place, 2), 2)


def norm_kernel(
    last_ref, hidden_ref, gain_ref, owner_ref, negative_ref, normed_ref, inv_ref, emb_ref
):
    seqs, width = normed_ref.shape
    parts, _, piece = emb_ref.shape
    pairs = owner_ref.shape[1]
    cuts = [slice(part * piece, (part + 1) * piece) for part in range(parts)]
    sources = lax.broadcasted_iota(jnp.int32, (seqs, seqs), 0)
    pick = jnp.where(sources == last_ref[...], 1.0, 0.0).astype(jnp.bfloat16)

    def folded(squares):
        return functools.reduce(
            jnp.add, [squares[:, at : at + lanes] for at in range(0, piece, lanes)]
        )

    total = jnp.zeros((seqs, lanes), jnp.float32)
    for cut in cuts:
        values = lax.dot_general(
            pick, hidden_ref[:, cut], (((0,), (0,)), ((), ())), preferred_element_type=jnp.float32
        )
        normed_ref[:, cut] = values.astype(jnp.bfloat16)
        total = total + folded(values * values)
    scale = lax.rsqrt(jnp.sum(total, axis=-1, keepdims=True) / width + token_eps)
    total = jnp.zeros((seqs, lanes), jnp.float32)
    for cut in cuts:
        values = normed_ref[:, cut].astype(jnp.float32)
        gain = gain_ref[cut].astype(jnp.float32).reshape(1, piece)
        normed = (values * scale * gain).astype(jnp.bfloat16)
        normed_ref[:, cut] = normed
        pooled = normed.astype(jnp.float32)
        total = total + folded(pooled * pooled)
    inverse = lax.rsqrt(jnp.sum(total, axis=-1, keepdims=True) + unit_eps)
    inv_ref[...] = jnp.broadcast_to(inverse, inv_ref.shape)

    owners = owner_ref[...].astype(jnp.float32)
    high = jnp.floor(owners * (1.0 / 256.0))
    low = owners - 256.0 * high
    row = lax.broadcasted_iota(jnp.int32, (8, pairs), 0)
    spot = lax.broadcasted_iota(jnp.int32, (8, pairs), 1)
    left = jnp.where(row == 0, low[:1], jnp.where(row == 1, high[:1], 0.0))
    right = jnp.where(row == 0, low[1:2], jnp.where(row == 1, high[1:2], 0.0))
    for offset in range(negative_ref.shape[1]):
        named = (negative_ref[0, offset] >= 0).astype(jnp.float32)
        left = jnp.where((row == 2) & (spot == offset), named, left)
    facts = jnp.concatenate([left, right], axis=1).astype(jnp.bfloat16)

    for part, cut in enumerate(cuts):
        emb_ref[part, :seqs] = (normed_ref[:, cut].astype(jnp.float32) * inverse).astype(jnp.bfloat16)
        emb_ref[part, seqs:] = facts


def norm_call(last_row, hidden, gain, owners, hard_negatives, parts):
    seqs, width = hidden.shape
    piece = width // parts
    whole = pl.BlockSpec(memory_space=pltpu.VMEM)
    return pl.pallas_call(
        norm_kernel,
        in_specs=[whole, whole, whole, whole, pl.BlockSpec(memory_space=pltpu.SMEM)],
        out_specs=[whole] * 3,
        out_shape=[
            jax.ShapeDtypeStruct((seqs, width), jnp.bfloat16),
            jax.ShapeDtypeStruct((seqs, lanes), jnp.float32),
            jax.ShapeDtypeStruct((parts, seqs + 8, piece), jnp.bfloat16),
        ],
        compiler_params=pltpu.CompilerParams(vmem_limit_bytes=56 * mebibyte),
        name="norm_rows",
    )(last_row, hidden, gain, owners, hard_negatives)


def score_kernel(
    blocks,
    pairs,
    window,
    *refs,
):
    emb_ref, q_ref, d_ref, mine_ref, other_ref, top_ref, own_ref, place_ref = refs[:-7]
    wide, picked, picked_too, facts, own, named, sems = refs[-7:]
    seqs = emb_ref.shape[1] - 8
    sent = emb_ref[:, seqs:, :].astype(jnp.float32)
    own_ref[...] = (2.0 * sent[:, 0, :] + 512.0 * sent[:, 1, :]).astype(jnp.int32)
    facts[...] = sent[:, 2, :lanes].astype(jnp.int32)
    fetches = [
        pltpu.make_async_copy(own_ref, own, sems.at[0]),
        pltpu.make_async_copy(facts, named, sems.at[1]),
    ]
    for fetch in fetches:
        fetch.start()

    for part in range(blocks):
        spread(wide, part * seqs, emb_ref[part, :seqs, :].astype(jnp.float32))
    for fetch in fetches:
        fetch.wait()

    def place(block, count):
        place_ref[0, block] = block
        for offset in range(window):
            present = named[block, offset] > 0
            place_ref[offset + 1, block] = jnp.where(present, count, -1)
            count = count + present.astype(jnp.int32)
        return count

    used = lax.fori_loop(0, blocks, place, blocks)
    fine = pairs // blocks

    def clear(spot, carry):
        empty = jnp.zeros((blocks // 2, fine, pairs), jnp.float32)
        at = pl.ds(pl.multiple_of(spot * fine, fine), fine)
        mine_ref[:, at, :] = empty
        other_ref[:, at, :] = empty
        return carry

    lax.fori_loop(used, mine_ref.shape[1] // fine, clear, 0)
    group = 32

    def pick_block(block, rows_at):
        for base in range(0, 2 * pairs, group):
            rows = [wide[row_pair(own[block, base + k]), :] for k in range(group)]
            for k in range(group):
                rows_at[2 * (base + k) : 2 * (base + k + 1), :] = rows[k]
        at = pl.multiple_of(block * pairs, pairs)
        q_ref[pl.ds(at, pairs), :] = gathered(rows_at, 0, pairs).astype(jnp.bfloat16)
        d_ref[pl.ds(at, pairs), :] = gathered(rows_at, pairs, pairs).astype(jnp.bfloat16)

    ahead = -(-(window + 2) // 2)

    def pick_one(block, carry):
        pick_block(block, picked)
        return carry

    lax.fori_loop(0, 2 * ahead, pick_one, 0)
    even = lax.axis_index("pb") % 2 == 0
    spare = mine_ref.shape[1] // fine - 1

    def score_blocks(step, carry):
        at = pl.multiple_of(step * 2 * pairs, 2 * pairs)
        tiles = inverse_temp * lax.dot_general(
            q_ref[pl.ds(at, 2 * pairs), :],
            d_ref[pl.ds(at, (window + 2) * pairs), :],
            (((1,), (1,)), ((), ())),
            preferred_element_type=jnp.float32,
        )
        top = carry
        for half in range(2):
            for column in range(window + 1):
                spot = place_ref[column, 2 * step + half]
                row = pl.multiple_of(jnp.where(spot >= 0, spot, spare) * fine, fine)
                tile = tiles[
                    half * pairs : (half + 1) * pairs,
                    (half + column) * pairs : (half + column + 1) * pairs,
                ]
                parted = tile.reshape(blocks // 2, 2, fine, pairs)
                first, second = parted[:, 0], parted[:, 1]
                mine_ref[:, pl.ds(row, fine), :] = jnp.where(even, first, second)
                other_ref[:, pl.ds(row, fine), :] = jnp.where(even, second, first)
                size = jnp.maximum(jnp.abs(first), jnp.abs(second))
                top = jnp.maximum(top, jnp.max(size, axis=0))
        return top

    def score_and_pick(step, top):
        top = score_blocks(step - ahead, top)
        pick_block(2 * step, picked)
        pick_block(2 * step + 1, picked_too)
        return top

    top = jnp.zeros((fine, pairs), jnp.float32)
    top = lax.fori_loop(ahead, blocks // 2, score_and_pick, top)
    d_ref[blocks * pairs :, :] = d_ref[: window * pairs, :]
    top_ref[...] = lax.fori_loop(blocks // 2 - ahead, blocks // 2, score_blocks, top)


def score_call(embedded, room, blocks, pairs, window):
    _, rows, piece = embedded.shape
    fine = pairs // blocks
    whole = pl.BlockSpec(memory_space=pltpu.VMEM)
    scalars = pl.BlockSpec(memory_space=pltpu.SMEM)
    return pl.pallas_call(
        functools.partial(score_kernel, blocks, pairs, window),
        in_specs=[whole],
        out_specs=[whole, whole, whole, whole, whole, whole, scalars],
        out_shape=[
            jax.ShapeDtypeStruct((blocks * pairs, piece), jnp.bfloat16),
            jax.ShapeDtypeStruct(((blocks + window) * pairs, piece), jnp.bfloat16),
            jax.ShapeDtypeStruct((blocks // 2, (room + 1) * fine, pairs), jnp.float32),
            jax.ShapeDtypeStruct((blocks // 2, (room + 1) * fine, pairs), jnp.float32),
            jax.ShapeDtypeStruct((fine, pairs), jnp.float32),
            jax.ShapeDtypeStruct((blocks, 2 * pairs), jnp.int32),
            jax.ShapeDtypeStruct((window + 1, blocks), jnp.int32),
        ],
        scratch_shapes=[
            pltpu.VMEM((2 * blocks * (rows - 8), lanes), jnp.float32),
            pltpu.VMEM((4 * pairs, lanes), jnp.float32),
            pltpu.VMEM((4 * pairs, lanes), jnp.float32),
            pltpu.VMEM((blocks, lanes), jnp.int32),
            pltpu.SMEM((blocks, 2 * pairs), jnp.int32),
            pltpu.SMEM((blocks, lanes), jnp.int32),
            pltpu.SemaphoreType.DMA((2,)),
        ],
        compiler_params=pltpu.CompilerParams(vmem_limit_bytes=22 * mebibyte),
        name="partial_scores",
    )(embedded)


def coded(values, scale):
    return jnp.round(values * scale).astype(jnp.int32).astype(jnp.int16)


def decoded(codes, scale):
    return codes.astype(jnp.int32).astype(jnp.float32) * scale


def highest(values):
    return jnp.max(jnp.max(values, axis=1, keepdims=True), axis=0, keepdims=True)


def merge_kernel(mine_ref, other_ref, top_ref, other_top_ref, own_ref, over_ref, *code_refs):
    rows, pairs = own_ref.shape
    steps = code_refs[0].shape[0] - 1
    fine = rows // steps // 2
    chip = lax.axis_index("pb") // 2
    across = mine_ref.shape[0] // 2
    top = jnp.minimum(highest(top_ref[...]) + highest(other_top_ref[...]), score_limit)
    bound = jnp.ceil(top * bound_steps) + 1.0
    scale = code_steps * bound_steps / bound
    sent_bound = jnp.broadcast_to(bound, (2 * fine, pairs)).astype(jnp.int32).astype(jnp.int16)
    near = len(code_refs) // 2
    for target, sum_ref, refs in (
        (chip ^ across, over_ref, code_refs[:near]),
        (chip, own_ref, code_refs[near:]),
    ):
        sum_ref[...] = mine_ref[target, :rows] + other_ref[target, :rows]
        for hop, code_ref in enumerate(refs):
            whose = target ^ (hop + 1)

            def encode(step, carry):
                there = pl.ds(pl.multiple_of(step * 2 * fine, 2 * fine), 2 * fine)
                values = mine_ref[whose, there, :] + other_ref[whose, there, :]
                code_ref[step] = coded(values, scale)
                return carry

            lax.fori_loop(0, steps, encode, 0)
            code_ref[steps] = sent_bound


def merge_call(mine, other, top, other_top, blocks):
    chips, rows, pairs = mine.shape
    fine = pairs // blocks
    rows = rows - fine
    whole = pl.BlockSpec(memory_space=pltpu.VMEM)
    codes = jax.ShapeDtypeStruct((rows // (2 * fine) + 1, 2 * fine, pairs), jnp.int16)
    near = chips // 2 - 1
    return pl.pallas_call(
        merge_kernel,
        in_specs=[whole] * 4,
        out_specs=[whole] * (2 * near + 2),
        out_shape=[jax.ShapeDtypeStruct((rows, pairs), jnp.float32)] * 2 + [codes] * (2 * near),
        compiler_params=pltpu.CompilerParams(vmem_limit_bytes=12 * mebibyte),
        name="merge_scores",
    )(mine, other, top, other_top)


def half_kernel(over_ref, *refs):
    near_refs, (code_ref, sums) = refs[:-2], refs[-2:]
    steps, deep, pairs = code_ref.shape
    steps = steps - 1
    unit = 1.0 / (code_steps * bound_steps)
    scales = [decoded(ref[steps], unit) for ref in near_refs]

    def add(step, top):
        there = pl.ds(pl.multiple_of(step * deep, deep), deep)
        over = over_ref[there, :]
        for ref, scale in zip(near_refs, scales):
            over = over + decoded(ref[step], scale)
        sums[there, :] = over
        return jnp.maximum(top, jnp.abs(over))

    top = lax.fori_loop(0, steps, add, jnp.zeros((deep, pairs), jnp.float32))
    bound = jnp.ceil(highest(top) * bound_steps) + 1.0
    scale = code_steps * bound_steps / bound

    def encode(step, carry):
        there = pl.ds(pl.multiple_of(step * deep, deep), deep)
        code_ref[step] = coded(sums[there, :], scale)
        return carry

    lax.fori_loop(0, steps, encode, 0)
    code_ref[steps] = jnp.broadcast_to(bound, (deep, pairs)).astype(jnp.int32).astype(jnp.int16)


def half_call(over, near):
    whole = pl.BlockSpec(memory_space=pltpu.VMEM)
    return pl.pallas_call(
        half_kernel,
        in_specs=[whole] * (1 + len(near)),
        out_specs=whole,
        out_shape=jax.ShapeDtypeStruct(near[0].shape, jnp.int16),
        scratch_shapes=[pltpu.VMEM(over.shape, jnp.float32)],
        compiler_params=pltpu.CompilerParams(vmem_limit_bytes=8 * mebibyte),
        name="half_scores",
    )(over, *near)


def softmax_kernel(blocks, window, place_ref, own_ref, *refs):
    code_refs, (c_ref, packed, masked) = refs[:-3], refs[-3:]
    room, fine, pairs = packed.shape
    count = blocks * fine
    unit = 1.0 / (code_steps * bound_steps)
    scales = [ref[room // 2].astype(jnp.int32).astype(jnp.float32) * unit for ref in code_refs]

    def decode(step, carry):
        both = own_ref[pl.ds(pl.multiple_of(step * 2 * fine, 2 * fine), 2 * fine), :]
        for ref, scale in zip(code_refs, scales):
            both = both + ref[step].astype(jnp.int32).astype(jnp.float32) * scale
        packed[2 * step] = both[:fine]
        packed[2 * step + 1] = both[fine:]
        return carry

    lax.fori_loop(0, room // 2, decode, 0)
    for block in range(blocks):
        for column in range(window + 1):
            spot = place_ref[column, block]
            tile = packed[jnp.maximum(spot, 0)]
            masked[block * fine : (block + 1) * fine, column * pairs : (column + 1) * pairs] = (
                jnp.where(spot >= 0, tile, -jnp.inf)
            )
    row = lax.broadcasted_iota(jnp.int32, (count, pairs), 0)
    lane = lax.broadcasted_iota(jnp.int32, (count, pairs), 1)
    target = lane == lax.axis_index("pb") * fine + row % fine
    pieces = [masked[:, column * pairs : (column + 1) * pairs] for column in range(window + 1)]
    row_max = jnp.max(functools.reduce(jnp.maximum, pieces), axis=1, keepdims=True)
    total = functools.reduce(jnp.add, [jnp.exp(piece - row_max) for piece in pieces])
    log_total = row_max + jnp.log(jnp.sum(total, axis=1, keepdims=True))
    positive = jnp.sum(jnp.where(target, pieces[0], 0.0), axis=1, keepdims=True)
    for column, piece in enumerate(pieces):
        share = jnp.exp(piece - log_total)
        if column == 0:
            share = share - jnp.where(target, 1.0, 0.0)
        masked[:, column * pairs : (column + 1) * pairs] = inverse_temp * share
    for block in range(blocks):
        for column in range(window + 1):
            spot = place_ref[column, block]

            @pl.when(spot >= 0)
            def _():
                packed[spot] = masked[
                    block * fine : (block + 1) * fine, column * pairs : (column + 1) * pairs
                ]

    for step in range(room // 2):
        both = jnp.concatenate([packed[2 * step], packed[2 * step + 1]], axis=0)
        c_ref[step] = both.astype(jnp.bfloat16)
    losses = jnp.sum(
        jnp.where(lane == row // fine, log_total - positive, 0.0), axis=0, keepdims=True
    )
    coarse = losses.astype(jnp.bfloat16).astype(jnp.float32)
    rank = lax.broadcasted_iota(jnp.int32, (2 * fine, pairs), 0)
    both = jnp.where(rank == 0, coarse, jnp.where(rank == 1, losses - coarse, 0.0))
    c_ref[room // 2] = both.astype(jnp.bfloat16)


def softmax_call(place, own_scores, codes, blocks, window):
    steps, fine, pairs = codes[0].shape
    room, fine = 2 * (steps - 1), fine // 2
    whole = pl.BlockSpec(memory_space=pltpu.VMEM)
    return pl.pallas_call(
        functools.partial(softmax_kernel, blocks, window),
        in_specs=[pl.BlockSpec(memory_space=pltpu.SMEM), whole] + [whole] * len(codes),
        out_specs=whole,
        out_shape=jax.ShapeDtypeStruct((room // 2 + 1, 2 * fine, pairs), jnp.bfloat16),
        scratch_shapes=[
            pltpu.VMEM((room, fine, pairs), jnp.float32),
            pltpu.VMEM((blocks * fine, (window + 1) * pairs), jnp.float32),
        ],
        compiler_params=pltpu.CompilerParams(vmem_limit_bytes=8 * mebibyte),
        name="softmax_rows",
    )(place, own_scores, *codes)


def grad_kernel(
    blocks,
    pairs,
    window,
    own_ref,
    place_ref,
    q_ref,
    d_ref,
    *refs,
):
    part_refs = refs[:-7]
    out_ref, loss_ref, wide, dsum, picked, packed, square = refs[-7:]
    fine = pairs // blocks
    room = packed.shape[1]
    me = lax.axis_index("pb")
    masks = swap_masks(blocks)
    group = 32
    losses = 0.0
    for part in part_refs:
        sent = part[:, room // 2].astype(jnp.float32)
        losses = losses + jnp.sum(sent[:, 0, :] + sent[:, 1, :], axis=0, keepdims=True) / pairs
    lane = lax.broadcasted_iota(jnp.int32, losses.shape, 1)
    mine = jnp.where(lane == me, losses, 0.0)
    loss_ref[...] = jnp.broadcast_to(jnp.sum(mine, axis=1, keepdims=True), loss_ref.shape)
    dsum[...] = jnp.zeros_like(dsum)
    square[...] = jnp.zeros_like(square)

    def unpack(step, carry):
        for part, mask in zip(part_refs, masks):
            both = part[:, step].astype(jnp.float32)
            for at, apart in enumerate(mask):
                packed[me ^ apart, 2 * step] = both[at, :fine]
                packed[me ^ apart, 2 * step + 1] = both[at, fine:]
        return carry

    lax.fori_loop(0, room // 2, unpack, 0)

    def scatter_rows(block, offset, start):
        for base in range(0, pairs, group):
            rows = [
                picked[2 * (start + base + k) : 2 * (start + base + k + 1), :] for k in range(group)
            ]
            for k in range(group):
                wide[row_pair(own_ref[block, offset + base + k]), :] = rows[k]

    def two_blocks(step, carry):
        for half in range(2):
            for column in range(window + 1):
                spot = place_ref[column, 2 * step + half]
                tile = packed[:, jnp.maximum(spot, 0)].reshape(pairs, pairs)
                square[
                    half * pairs : (half + 1) * pairs,
                    (half + column) * pairs : (half + column + 1) * pairs,
                ] = jnp.where(spot >= 0, tile, 0.0).astype(jnp.bfloat16)
        at = pl.multiple_of(step * 2 * pairs, 2 * pairs)
        there = pl.ds(at, (window + 2) * pairs)
        coefficients = square[...]
        summed = jnp.dot(coefficients, d_ref[there, :], preferred_element_type=jnp.float32)
        spread(picked, 0, summed)
        dsum[there, :] += lax.dot_general(
            coefficients,
            q_ref[pl.ds(at, 2 * pairs), :],
            (((0,), (0,)), ((), ())),
            preferred_element_type=jnp.float32,
        )
        for half in range(2):
            scatter_rows(2 * step + half, 0, half * pairs)
        return carry

    lax.fori_loop(0, blocks // 2, two_blocks, 0)
    dsum[: window * pairs, :] += dsum[blocks * pairs :, :]

    def doc_block(block, carry):
        at = pl.multiple_of(block * pairs, pairs)
        spread(picked, 0, dsum[pl.ds(at, pairs), :])
        scatter_rows(block, pairs, 0)
        return carry

    lax.fori_loop(0, blocks, doc_block, 0)
    slots = out_ref.shape[1]
    for part in range(blocks):
        out_ref[part] = gathered(wide, part * slots, slots).astype(jnp.bfloat16)


def grad_call(own, place, parts, queries, documents, blocks, pairs, window):
    count, piece = queries.shape
    seqs = 2 * count
    room = 2 * (parts[0].shape[1] - 1)
    whole = pl.BlockSpec(memory_space=pltpu.VMEM)
    scalars = pl.BlockSpec(memory_space=pltpu.SMEM)
    return pl.pallas_call(
        functools.partial(grad_kernel, blocks, pairs, window),
        in_specs=[scalars, scalars, whole, whole] + [whole] * len(parts),
        out_specs=[whole, whole],
        out_shape=[
            jax.ShapeDtypeStruct((blocks, seqs // blocks, piece), jnp.bfloat16),
            jax.ShapeDtypeStruct((1, lanes), jnp.float32),
        ],
        scratch_shapes=[
            pltpu.VMEM((2 * seqs, lanes), jnp.float32),
            pltpu.VMEM(((blocks + window) * pairs, piece), jnp.float32),
            pltpu.VMEM((4 * pairs, lanes), jnp.float32),
            pltpu.VMEM((blocks, room, pairs // blocks, pairs), jnp.float32),
            pltpu.VMEM((2 * pairs, (window + 2) * pairs), jnp.bfloat16),
        ],
        compiler_params=pltpu.CompilerParams(vmem_limit_bytes=26 * mebibyte),
        name="slice_grads",
    )(own, place, queries, documents, *parts)


def project_kernel(grad_ref, normed_ref, inv_ref, out_ref):
    parts, _, piece = grad_ref.shape
    cuts = [slice(part * piece, (part + 1) * piece) for part in range(parts)]
    inverse = inv_ref[:, :1]
    total = 0.0
    for part, cut in enumerate(cuts):
        unit = normed_ref[:, cut].astype(jnp.float32) * inverse
        total = total + unit * grad_ref[part].astype(jnp.float32)
    along = jnp.sum(total, axis=-1, keepdims=True)
    for part, cut in enumerate(cuts):
        unit = normed_ref[:, cut].astype(jnp.float32) * inverse
        out_ref[:, cut] = grad_ref[part].astype(jnp.float32) - unit * along


def project_call(returned, normed, inverse):
    parts, seqs, piece = returned.shape
    width = normed.shape[1]
    rows = 64
    return pl.pallas_call(
        project_kernel,
        grid=(seqs // rows,),
        in_specs=[
            pl.BlockSpec((parts, rows, piece), lambda i: (0, i, 0)),
            pl.BlockSpec((rows, width), lambda i: (i, 0)),
            pl.BlockSpec((rows, lanes), lambda i: (i, 0)),
        ],
        out_specs=pl.BlockSpec((rows, width), lambda i: (i, 0)),
        out_shape=jax.ShapeDtypeStruct((seqs, width), jnp.float32),
        compiler_params=pltpu.CompilerParams(vmem_limit_bytes=10 * mebibyte),
        name="project_out",
    )(returned, normed, inverse)


def swapped(value, apart):
    pairs = [(at, at ^ apart) for at in range(lax.axis_size("pb"))]
    return lax.ppermute(value, "pb", pairs)


def near_hops(devices):
    return [2 * hop for hop in reversed(range(1, devices // 4))]


def swap_masks(devices):
    near = [0] + near_hops(devices)
    held = [near, [mask ^ (devices // 2) for mask in near]]
    return held + [[mask ^ 1 for mask in part] for part in held]


def gather_all(value):
    devices = lax.axis_size("pb")
    own = value[None]
    across = swapped(own, devices // 2)
    held = [
        jnp.concatenate([part] + [swapped(part, hop) for hop in near_hops(devices)], axis=0)
        for part in (own, across)
    ]
    return held + [swapped(part, 1) for part in held]


def middle(embedded, room, devices, pairs, window):
    queries, documents, mine, other, top, own, place = score_call(
        embedded, room, devices, pairs, window
    )
    own_scores, over, *codes = merge_call(mine, swapped(other, 1), top, swapped(top, 1), devices)
    hops = near_hops(devices)
    half = len(hops)
    far = [swapped(codes[hop // 2 - 1], hop) for hop in hops]
    near = [swapped(codes[half + hop // 2 - 1], hop) for hop in hops]
    codes = near + [swapped(half_call(over, far), devices // 2)]
    parts = gather_all(softmax_call(place, own_scores, codes, devices, window))
    grads, loss = grad_call(own, place, parts, queries, documents, devices, pairs, window)
    return grads, loss[0, :1]


def feature_plan(hidden, final_gain, last_row, pair_owner, hard_negatives):
    devices = lax.axis_size("pb")
    seqs, width = hidden.shape
    pairs = pair_owner.shape[0]
    window = hard_negatives.shape[1]
    normed, inverse, embedding = norm_call(
        last_row, hidden, final_gain, pair_owner.T, hard_negatives, devices
    )
    embedded = lax.all_to_all(embedding, "pb", split_axis=0, concat_axis=0, tiled=True)
    most = devices * (window + 1)
    rooms = [most * part // 20 for part in (11, 12, 13, 15, 20)]
    used = devices + jnp.sum(embedded[:, seqs + 2, :window].astype(jnp.float32))
    level = sum((used > room).astype(jnp.int32) for room in rooms[:-1])
    grads, loss = lax.switch(
        level,
        [
            functools.partial(middle, room=room, devices=devices, pairs=pairs, window=window)
            for room in rooms
        ],
        embedded,
    )
    returned = lax.all_to_all(grads, "pb", split_axis=0, concat_axis=0, tiled=True)
    return project_call(returned, normed, inverse), loss


def from_behind(value, axis, steps):
    count = lax.axis_size(axis)
    pairs = [(source, (source + steps) % count) for source in range(count)]
    return lax.ppermute(value, axis, pairs)


def similarity(queries, documents):
    return inverse_temp * lax.dot_general(
        queries, documents, (((1,), (1,)), ((), ())), preferred_element_type=jnp.float32
    )


def transposed(weights, queries):
    return lax.dot_general(
        weights, queries, (((0,), (0,)), ((), ())), preferred_element_type=jnp.float32
    )


def combine_docs(weights, documents):
    return jnp.dot(weights, documents, preferred_element_type=jnp.float32)


def skipped(listed, function, operands, out_shape):
    return lax.cond(
        listed,
        lambda inputs: function(*inputs),
        lambda inputs: jnp.zeros(out_shape, jnp.float32),
        operands,
    )


def row_plan(hidden, final_gain, last_row, pair_owner, hard_negatives):
    values = hidden.astype(jnp.float32)
    scale_row = lax.rsqrt(jnp.mean(values * values, axis=-1, keepdims=True) + token_eps)
    normed = (values * scale_row * final_gain.astype(jnp.float32)).astype(jnp.bfloat16)
    seq_count = last_row.shape[1]
    model_width = hidden.shape[1]
    pooled = normed[last_row[0]].astype(jnp.float32)
    inverse_norm = lax.rsqrt(jnp.sum(pooled * pooled, axis=-1, keepdims=True) + 1e-06)
    unit_vec = pooled * inverse_norm
    embedding = unit_vec.astype(jnp.bfloat16)
    devices = lax.axis_size("pb")
    capacity = 2 * seq_count // devices
    pair_count = pair_owner.shape[0]
    wanted = jnp.concatenate([pair_owner[:, 0], pair_owner[:, 1]])
    holder = wanted // seq_count
    within = wanted % seq_count
    entry_ids = jnp.arange(2 * pair_count, dtype=jnp.int32)
    earlier = (holder[None, :] == holder[:, None]) & (entry_ids[None, :] < entry_ids[:, None])
    position = jnp.sum(earlier.astype(jnp.int32), axis=1)
    request = jnp.full((devices, capacity), -1, jnp.int32).at[holder, position].set(within)
    served = lax.all_to_all(request, "pb", split_axis=0, concat_axis=0, tiled=True)
    outgoing = jnp.where(
        served[:, :, None] >= 0, embedding[jnp.maximum(served, 0)], jnp.zeros((), jnp.bfloat16)
    )
    received = lax.all_to_all(outgoing, "pb", split_axis=0, concat_axis=0, tiled=True)
    gathered = received[holder, position]
    queries = gathered[:pair_count]
    own_docs = gathered[pair_count:]
    listed_ids = hard_negatives[0]
    window = hard_negatives.shape[1]
    listed = [listed_ids[offset] >= 0 for offset in range(window)]
    neighbours = []
    moving = own_docs
    for offset in range(window):
        moving = from_behind(moving, "pb", -1)
        neighbours.append(moving)
    tile_shape = (pair_count, pair_count)
    score_blocks = [similarity(queries, own_docs)]
    for offset in range(window):
        score_blocks.append(
            skipped(listed[offset], similarity, (queries, neighbours[offset]), tile_shape)
        )
    all_scores = jnp.concatenate(score_blocks, axis=1)
    usable = jnp.concatenate(
        [jnp.ones((pair_count,), jnp.bool_)]
        + [jnp.broadcast_to(listed[offset], (pair_count,)) for offset in range(window)]
    )
    masked = jnp.where(usable[None, :], all_scores, -jnp.inf)
    row_max = jnp.max(masked, axis=1, keepdims=True)
    log_total = row_max + jnp.log(jnp.sum(jnp.exp(masked - row_max), axis=1, keepdims=True))
    diagonal = jnp.arange(pair_count, dtype=jnp.int32)
    positive = all_scores[diagonal, diagonal]
    block_loss = jnp.mean(log_total[:, 0] - positive).reshape(1)
    columns = jnp.arange((window + 1) * pair_count, dtype=jnp.int32)
    target = (columns[None, :] == diagonal[:, None]).astype(jnp.float32)
    coefficients = (inverse_temp * (jnp.exp(masked - log_total) - target)).astype(jnp.bfloat16)
    pieces = [
        coefficients[:, offset * pair_count : (offset + 1) * pair_count]
        for offset in range(window + 1)
    ]
    grad_shape = (pair_count, model_width)
    query_sum = combine_docs(pieces[0], own_docs)
    for offset in range(window):
        query_sum = query_sum + skipped(
            listed[offset], combine_docs, (pieces[offset + 1], neighbours[offset]), grad_shape
        )
    query_grad = query_sum.astype(jnp.bfloat16)
    own_part = transposed(pieces[0], queries).astype(jnp.bfloat16)
    partial_value = [
        skipped(listed[offset], transposed, (pieces[offset + 1], queries), grad_shape).astype(
            jnp.bfloat16
        )
        for offset in range(window)
    ]
    running = partial_value[window - 1].astype(jnp.float32)
    for offset in range(window):
        running = from_behind(running, "pb", 1)
        if offset + 1 < window:
            running = running + partial_value[window - 2 - offset].astype(jnp.float32)
    doc_grad = (own_part.astype(jnp.float32) + running).astype(jnp.bfloat16)
    answers = jnp.concatenate([query_grad, doc_grad], axis=0)
    returning = (
        jnp.zeros((devices, capacity, model_width), jnp.bfloat16).at[holder, position].set(answers)
    )
    returned = lax.all_to_all(returning, "pb", split_axis=0, concat_axis=0, tiled=True)
    slot_ids = jnp.where(served >= 0, served, seq_count).reshape(-1)
    emb_grad = (
        jnp.zeros((seq_count, model_width), jnp.bfloat16)
        .at[slot_ids]
        .set(returned.reshape(-1, model_width), mode="drop")
    )
    gradient = emb_grad.astype(jnp.float32)
    pooled_grad = gradient - unit_vec * jnp.sum(unit_vec * gradient, axis=-1, keepdims=True)
    return (pooled_grad, block_loss)


def solution(mesh):
    def local(hidden, final_gain, last_row, pair_owner, hard_negatives):
        plan = feature_plan if hidden.shape[1] >= lanes * mesh.shape["pb"] else row_plan
        return plan(hidden, final_gain, last_row, pair_owner, hard_negatives)

    return jax.shard_map(
        local,
        mesh=mesh,
        in_specs=(
            P(("groups", "pb"), None),
            P(),
            P(("groups", "pb"), None),
            P(("groups", "pb"), None),
            P(("groups", "pb"), None),
        ),
        out_specs=(P(("groups", "pb"), None), P(("groups", "pb"))),
        check_vma=False,
    )
```
